32 devices in a mesh: path: 4 (over x, core), ctx: 8 (over z, y).
Axes of the slice: x: 2, y: 2, z: 4, core: 2. Of those that a mesh axis runs over, the one named last changes fastest.
Arguments:
- tokens: int32 [1024], P('ctx'), may hold values from 0 to 511
- sub_pos: int32 [128], P('ctx'), may hold values from 0 to 1023, as said below
- sub_base: int32 [128], P('ctx'), may hold values from 0 to 511
- embed: bfloat16 [512, 4096], replicated, may hold values from -6 to 6
- norm_gain: float32 [4096], replicated, may hold values from 0.1 to 1.9
- fir_taps: bfloat16 [3, 3, 4096], replicated, may hold values from -3.5 to 3.5
- long_filter: float32 [1024, 4096], P(None, 'ctx'), may hold values from -8 to 8
- skip_gain: float32 [4096], P('ctx'), may hold values from 0.5 to 1.5
- cotangent: bfloat16 [1024, 4096], P('ctx'), may hold values from -6 to 6
Outputs:
- path_grad: float32 [1024, 4096], P('ctx', 'path')
- attribution: float32 [1024, 4096], P('ctx', 'path')
The draws below stay inside these ranges and needn't reach their ends.
Inputs may be any that keep to these rules, and one draw needn't show every extreme that they name: `sub_pos`: exactly one substituted position in each aligned block of 8 tokens, so the positions rise strictly.
All inputs are finite; a program needn't handle non-finite values.
Results may differ from the reference program's by a relative error of at most 0.0085.
Values may be sent and summed in bfloat16 or wider, within the bound.
No kernel may reach another device: no remote copies, remote signals or barrier semaphores. Data moves between devices by JAX's collectives and lax.ppermute only.
A program may use at most 192 MiB of HBM per device.

```python
import jax
import jax.numpy as jnp
from jax import lax

D = 4096
VOCAB = 512
FIR_TAPS = 3
TOKENS = 1024
PATHS = 4
SUBS = 128


def substitution_draw(key):
    token_ids = jax.random.randint(jax.random.fold_in(key, 11), (TOKENS,), 0, VOCAB, dtype=jnp.int32)
    offsets = jax.random.randint(jax.random.fold_in(key, 3), (SUBS,), 0, 8, dtype=jnp.int32)
    positions = (jnp.arange(SUBS, dtype=jnp.int32) * 8 + offsets).astype(jnp.int32)
    chosen = jnp.take(token_ids, positions, axis=0)
    partner = ((chosen + VOCAB // 2) % VOCAB).astype(jnp.int32)
    return (token_ids, positions, partner)


def draw_tokens(key, part):
    return substitution_draw(key)[0]


def draw_sub_pos(key, part):
    return substitution_draw(key)[1]


def draw_sub_base(key, part):
    return substitution_draw(key)[2]


def draw_embed(key, part):
    half = VOCAB // 2
    lead_key, extra_key = jax.random.split(jax.random.fold_in(key, 19))
    lead = jnp.clip(jax.random.normal(lead_key, (half, D), jnp.float32), -4.0, 4.0)
    extra = jnp.clip(jax.random.normal(extra_key, (half, D), jnp.float32), -4.0, 4.0)
    partner = -0.5 * lead + 0.1 * extra
    return jnp.concatenate([lead, partner], 0).astype(jnp.bfloat16)


def draw_long_filter(key, part):
    jitter_key, decay_key = jax.random.split(jax.random.fold_in(key, 7))
    jitter = jnp.clip(jax.random.normal(jitter_key, (TOKENS, D), jnp.float32), -6.0, 6.0)
    lowest = 30.0
    decay_len = jnp.exp(jax.random.uniform(decay_key, (D,), jnp.float32, jnp.log(lowest), jnp.log(4.0 * TOKENS)))
    position = jnp.arange(TOKENS, dtype=jnp.float32)[:, None]
    envelope = jnp.exp(-position / decay_len[None, :])
    return jitter * envelope / jnp.sqrt(jnp.sum(envelope * envelope, 0, keepdims=True))


def block_levels(rng, dims, shards, smallest, largest):
    gain, own = 1.0, jax.random.fold_in(rng, 6)
    for dim, shards_of in shards:
        steps = jnp.exp(jax.random.uniform(jax.random.fold_in(own, dim), (shards_of,), jnp.float32, smallest / len(shards), largest / len(shards)))
        gain = gain * jnp.repeat(steps, dims[dim] // shards_of).reshape([-1 if axis == dim else 1 for axis in range(len(dims))])
    return gain


def normal_values(stream_key, shape, scale, bound, cuts=(), kind=jnp.bfloat16):
    result = jax.random.normal(stream_key, shape, jnp.float32) * scale
    if len(cuts) > 0:
        result = block_levels(stream_key, shape, cuts, -0.22, 0.18) * result
    return jnp.clip(result, min=-bound, max=bound).astype(kind)


def setup_inputs(seed: int = 0) -> dict:
    keys = jax.random.split(jax.random.key(seed), 10)
    tokens = draw_tokens(jax.random.fold_in(keys[9], 71), 0)
    sub_pos = draw_sub_pos(jax.random.fold_in(keys[9], 71), 0)
    sub_base = draw_sub_base(jax.random.fold_in(keys[9], 71), 0)
    embed = draw_embed(jax.random.fold_in(keys[9], 71), 0)
    norm_gain = jnp.clip(1.0 + 0.18 * jax.random.normal(keys[4], (D,), jnp.float32), 0.1, 1.9)
    fir_taps = normal_values(keys[5], (3, FIR_TAPS, D), FIR_TAPS ** -0.5, 3.5)
    long_filter = draw_long_filter(jax.random.fold_in(keys[9], 71), 0)
    skip_gain = jnp.clip(0.5 + 1.0 * jax.random.uniform(keys[7], (D,), jnp.float32) ** block_levels(keys[7], (D,), ((0, 8),), -0.2, 0.2), 0.5, 1.5)
    cotangent = normal_values(keys[8], (TOKENS, D), 1.0, 6.0, ((0, 8),))
    return dict(tokens=tokens, sub_pos=sub_pos, sub_base=sub_base, embed=embed, norm_gain=norm_gain, fir_taps=fir_taps, long_filter=long_filter, skip_gain=skip_gain, cotangent=cotangent)


def rounded(value):
    return lax.optimization_barrier(value.astype(jnp.bfloat16)).astype(jnp.float32)

def causal(signal, filters):
    length = signal.shape[0] + filters.shape[0]
    product = jnp.fft.rfft(signal, n=length, axis=0) * jnp.fft.rfft(filters, n=length, axis=0)
    return jnp.fft.irfft(product, n=length, axis=0)[:signal.shape[0]]

def anticausal(signal, filters):
    length = signal.shape[0] + filters.shape[0]
    product = jnp.fft.rfft(signal, n=length, axis=0) * jnp.conj(jnp.fft.rfft(filters, n=length, axis=0))
    return jnp.fft.irfft(product, n=length, axis=0)[:signal.shape[0]]

def reference(tokens, sub_pos, sub_base, embed, norm_gain, fir_taps, long_filter, skip_gain, cotangent):
    base_ids = tokens.at[sub_pos].set(sub_base)
    emb_tok = embed[tokens].astype(jnp.float32)
    emb_base = embed[base_ids].astype(jnp.float32)
    difference = emb_tok - emb_base
    filters = fir_taps.astype(jnp.float32)
    upstream = cotangent.astype(jnp.float32)

    def one_point(total, point):
        alpha = (point.astype(jnp.float32) + 0.5) / PATHS
        inputs = emb_base + alpha * difference
        inv_rms = lax.rsqrt(lax.optimization_barrier(jnp.mean(inputs * inputs, -1, keepdims=True)) + 1e-06)
        normed = rounded(inputs * inv_rms * norm_gain)
        q_feat = causal(normed, filters[0])
        k_feat = causal(normed, filters[1])
        v_feat = causal(normed, filters[2])
        gated = rounded(k_feat * v_feat)
        conv_out = rounded(causal(gated, long_filter) + skip_gain * gated)
        grad_q = rounded(upstream * conv_out)
        grad_y = rounded(upstream * q_feat)
        grad_z = rounded(anticausal(grad_y, long_filter) + skip_gain * grad_y)
        grad_k = rounded(grad_z * v_feat)
        grad_v = rounded(grad_z * k_feat)
        grad_norm = anticausal(grad_q, filters[0]) + anticausal(grad_k, filters[1]) + anticausal(grad_v, filters[2])
        scaled = norm_gain * grad_norm
        grad_in = inv_rms * scaled - inputs * inv_rms ** 3 * lax.optimization_barrier(jnp.mean(inputs * scaled, -1, keepdims=True))
        return (total + grad_in, None)
    total = lax.scan(one_point, jnp.zeros((TOKENS, D), jnp.float32), jnp.arange(PATHS, dtype=jnp.int32))[0]
    path_grad = total / PATHS
    return (path_grad, difference * path_grad)
```

```python
import functools

import jax
import jax.numpy as jnp
import ml_dtypes
import numpy as np
from jax import lax
from jax.experimental import pallas as pl
from jax.experimental.pallas import tpu as pltpu
from jax.sharding import PartitionSpec as P

LANES = 128
GROUP = 8
FREQ_ROWS = 256
CHUNK = 64
EPS = 1e-06
VMEM_BYTES = 50 * 1024 * 1024
F32 = jnp.float32
BF16 = jnp.bfloat16
precise = lax.Precision.HIGH


def angle_tables(length):
    outer_size = 64
    inner_size = length // outer_size
    outer_idx = jnp.arange(outer_size, dtype=jnp.int32)
    inner_idx = jnp.arange(inner_size, dtype=jnp.int32)
    outer_angle = (
        2.0 * jnp.pi / outer_size
        * (outer_idx[:, None] * outer_idx[None, :] % outer_size).astype(F32)
    )
    inner_angle = (
        2.0 * jnp.pi / inner_size
        * (inner_idx[:, None] * inner_idx[None, :] % inner_size).astype(F32)
    )
    twist_angle = (
        2.0 * jnp.pi / length
        * (outer_idx[:, None] * inner_idx[None, :] % length).astype(F32)
    )
    return (outer_angle, inner_angle, twist_angle)


def complex_table(angle, sign):
    cosine = jnp.cos(angle)
    sine = sign * jnp.sin(angle)
    return jnp.stack([jnp.stack([cosine, sine]), jnp.stack([-sine, cosine])])


def twisted(values, angle, sign):
    cosine = jnp.cos(angle)[None, :, :, None]
    sine = sign * jnp.sin(angle)[None, :, :, None]
    real_part = values[:, 0]
    imag_part = values[:, 1]
    return jnp.stack(
        [real_part * cosine - imag_part * sine, real_part * sine + imag_part * cosine], 1
    )


def spectrum(signal):
    batch, half, width = signal.shape
    length = 2 * half
    outer_angle, inner_angle, twist_angle = angle_tables(length)
    outer_size = outer_angle.shape[0]
    inner_size = inner_angle.shape[0]
    folded = signal.reshape(batch, outer_size // 2, inner_size, width)
    used = outer_angle[:, : outer_size // 2]
    outer_table = jnp.stack([jnp.cos(used), -jnp.sin(used)])
    first = jnp.einsum("rka,pabc->prkbc", outer_table, folded, precision=precise)
    turned = twisted(first, twist_angle, -1.0)
    return jnp.einsum(
        "prkbc,rsbm->pskmc", turned, complex_table(inner_angle, -1.0), precision=precise
    )


def inverse(spec):
    batch, parts, outer_size, inner_size, width = spec.shape
    length = outer_size * inner_size
    outer_angle, inner_angle, twist_angle = angle_tables(length)
    back = jnp.einsum("pskmc,stmb->ptkbc", spec, complex_table(inner_angle, 1.0), precision=precise)
    turned = twisted(back, twist_angle, 1.0)
    used = outer_angle[: outer_size // 2]
    outer_table = jnp.stack([jnp.cos(used), -jnp.sin(used)])
    result = jnp.einsum("rak,prkbc->pabc", outer_table, turned, precision=precise)
    return (result / length).reshape(batch, length // 2, width)


def long_conv(signal, filter_spec, skip_gain, adjoint):
    spec = spectrum(signal)
    sig_real = spec[:, 0]
    sig_imag = spec[:, 1]
    filt_real = filter_spec[:, 0]
    filt_imag = filter_spec[:, 1]
    if adjoint:
        prod_real = sig_real * filt_real + sig_imag * filt_imag
        prod_imag = sig_imag * filt_real - sig_real * filt_imag
    else:
        prod_real = sig_real * filt_real - sig_imag * filt_imag
        prod_imag = sig_real * filt_imag + sig_imag * filt_real
    return inverse(jnp.stack([prod_real, prod_imag], 1)) + skip_gain * signal


def rounded(value):
    return value.astype(BF16).astype(F32)


def shifted(values, step):
    zeros = jnp.zeros_like(values[:, : abs(step)])
    if step > 0:
        return jnp.concatenate([zeros, values[:, :-step]], 1)
    return jnp.concatenate([values[:, -step:], zeros], 1)


@functools.lru_cache(maxsize=None)
def dft_tables(length):
    odd = 4 * np.arange(length, dtype=np.int64) + 1
    angle = (odd[:, None] * odd[None, :] % (16 * length)) * (2.0 * np.pi / (16 * length))
    phase = odd * (2.0 * np.pi / (16 * length))
    turn = np.stack([np.cos(phase), np.sin(phase)]).reshape(-1, LANES).astype(np.float32)
    return (
        np.cos(angle).astype(ml_dtypes.bfloat16),
        np.sin(angle).astype(ml_dtypes.bfloat16),
        turn,
    )


def transposed(rows):
    count = rows.shape[0]
    if count < LANES:
        rows = jnp.concatenate([rows, jnp.zeros((LANES - count, LANES), F32)], 0)
    return rows.T


def dot(left, right):
    return jnp.dot(left, right, preferred_element_type=F32)


def table_copies(cos_hbm, sin_hbm, cos_ref, sin_ref, sems):
    copies = []
    for index in range(cos_hbm.shape[0] // FREQ_ROWS):
        rows = pl.ds(index * FREQ_ROWS, FREQ_ROWS)
        copies.append(
            (
                pltpu.make_async_copy(cos_hbm.at[rows], cos_ref.at[rows], sems.at[0, index]),
                pltpu.make_async_copy(sin_hbm.at[rows], sin_ref.at[rows], sems.at[1, index]),
            )
        )
    return copies


def prepare_kernel(
    n_path, filt_hbm, cos_hbm, sin_hbm, embed_hbm, turn_ref,
    spec_ref, vocab_ref,
    filt_ref, cos_ref, sin_ref, embed_ref, parts_ref, sems, table_sems,
):
    length = cos_ref.shape[0]
    vocab, width = embed_ref.shape
    share = filt_ref.shape[1]
    first = pl.multiple_of(lax.axis_index("path") * share, LANES)
    embed_copy = pltpu.make_async_copy(embed_hbm, embed_ref, sems.at[0])
    filt_copy = pltpu.make_async_copy(filt_hbm.at[:, pl.ds(first, share)], filt_ref, sems.at[1])
    tables = table_copies(cos_hbm, sin_hbm, cos_ref, sin_ref, table_sems)
    filt_copy.start()
    embed_copy.start()
    for pair in tables:
        pair[0].start()
        pair[1].start()

    filt_copy.wait()

    @pl.loop(0, length // CHUNK)
    def _(step):
        rows = pl.ds(pl.multiple_of(step * CHUNK, CHUNK), CHUNK)
        value = filt_ref[rows, :]
        high = value.astype(BF16)
        parts_ref[rows, :share] = high
        parts_ref[rows, share:] = (value - high.astype(F32)).astype(BF16)

    embed_copy.wait()

    @pl.loop(0, vocab // 16)
    def _(step):
        rows = pl.ds(pl.multiple_of(step * 16, 16), 16)
        total = jnp.zeros((16, LANES), F32)
        for column in range(width // LANES):
            value = embed_ref[rows, column * LANES : (column + 1) * LANES].astype(F32)
            total = total + value * value
        inv = lax.rsqrt(jnp.sum(total, 1, keepdims=True) / width + EPS)
        inv = jnp.broadcast_to(inv, (16, LANES))
        high = inv.astype(BF16).astype(F32)
        lane = lax.broadcasted_iota(jnp.int32, (16, LANES), 1)
        vocab_ref[rows, :] = jnp.where(lane < LANES // 2, high, inv - high).astype(BF16)

    turn = transposed(turn_ref[...])
    blocks = length // LANES
    for index, pair in enumerate(tables):
        pair[0].wait()
        pair[1].wait()
        rows = pl.ds(index * FREQ_ROWS, FREQ_ROWS)
        real = dot(cos_ref[rows, :], parts_ref[...])
        imag = dot(sin_ref[rows, :], parts_ref[...])
        real = real[:, :share] + real[:, share:]
        imag = imag[:, :share] + imag[:, share:]
        for part in range(FREQ_ROWS // LANES):
            block = index * (FREQ_ROWS // LANES) + part
            cosine = turn[:, block : block + 1] / length
            sine = turn[:, blocks + block : blocks + block + 1] / length
            here = slice(part * LANES, (part + 1) * LANES)
            into = pl.ds(block * LANES, LANES)
            spec_ref[0, into, :] = real[here] * cosine + imag[here] * sine
            spec_ref[1, into, :] = real[here] * sine - imag[here] * cosine


def transform(cos_ref, sin_ref, tables, signal_ref, spec_ref, prod_ref, points, adjoint):
    length = cos_ref.shape[0]
    share = spec_ref.shape[2]
    for index, pair in enumerate(tables):
        pair[0].wait()
        pair[1].wait()
        rows = pl.ds(index * FREQ_ROWS, FREQ_ROWS)
        after = pl.ds(length + index * FREQ_ROWS, FREQ_ROWS)
        real = dot(cos_ref[rows, :], signal_ref[...])
        imag = dot(sin_ref[rows, :], signal_ref[...])
        filt_real = spec_ref[0, rows, :]
        filt_imag = spec_ref[1, rows, :]
        for point in range(points):
            lanes = slice(point * share, (point + 1) * share)
            one, two = real[:, lanes], imag[:, lanes]
            if adjoint:
                prod_ref[rows, lanes] = (one * filt_real - two * filt_imag).astype(BF16)
                prod_ref[after, lanes] = (one * filt_imag + two * filt_real).astype(BF16)
            else:
                prod_ref[rows, lanes] = (one * filt_real + two * filt_imag).astype(BF16)
                prod_ref[after, lanes] = (two * filt_real - one * filt_imag).astype(BF16)


def inverse_rows(cos_ref, sin_ref, prod_ref, rows):
    length = cos_ref.shape[0]
    return dot(cos_ref[rows, :], prod_ref[:length, :]) + dot(sin_ref[rows, :], prod_ref[length:, :])


def forward_kernel(
    points, ids_ref, embed_hbm, vocab_ref, taps_ref, gain_ref, skip_ref, cos_hbm, sin_hbm, spec_hbm,
    conv_ref, q_hbm, k_hbm, v_hbm, inv_hbm, pair_ref, own_ref,
    embed_ref, cos_ref, sin_ref, spec_ref, tok_ref, base_ref, sub_ref, hot_ref, sums_ref, found_ref,
    here_ref, norm_ref, q_ref, k_ref, v_ref, inv_ref, signal_ref, prod_ref, sems, table_sems,
):
    length = cos_ref.shape[0]
    vocab, width = embed_ref.shape
    share = pair_ref.shape[2]
    subs = sub_ref.shape[1]
    per_block = subs * LANES // length
    path, ctx = lax.axis_index("path"), lax.axis_index("ctx")
    n_path = skip_ref.shape[1] // share
    first = pl.multiple_of((ctx * n_path + path) * share, LANES)
    embed_copy = pltpu.make_async_copy(embed_hbm, embed_ref, sems.at[0])
    spec_copy = pltpu.make_async_copy(spec_hbm, spec_ref, sems.at[1])
    tables = table_copies(cos_hbm, sin_hbm, cos_ref, sin_ref, table_sems)
    embed_copy.start()
    spec_copy.start()
    for pair in tables:
        pair[0].start()
        pair[1].start()

    columns = transposed(ids_ref[...].astype(F32))
    for block in range(length // LANES):
        tok_ref[block * LANES : (block + 1) * LANES, :] = jnp.broadcast_to(
            columns[:, 3 * block : 3 * block + 1], (LANES, LANES)
        )
        rows = slice(block * per_block, (block + 1) * per_block)
        for kind in range(2):
            column = columns[:per_block, 3 * block + 1 + kind : 3 * block + 2 + kind]
            sub_ref[kind, rows, :] = jnp.broadcast_to(column, (per_block, LANES))
    within = lax.broadcasted_iota(jnp.int32, (GROUP, LANES), 0)

    @pl.loop(0, subs, unroll=8)
    def _(index):
        rows = pl.ds(pl.multiple_of(index * GROUP, GROUP), GROUP)
        one = pl.ds(index, 1)
        tok = tok_ref[rows, :]
        place = jnp.broadcast_to(sub_ref[0, one, :], (GROUP, LANES)).astype(jnp.int32) - index * GROUP
        put = jnp.broadcast_to(sub_ref[1, one, :], (GROUP, LANES))
        chosen = within == place
        base_ref[rows, :] = jnp.where(chosen, put, tok)
        sub_ref[2, one, :] = jnp.sum(jnp.where(chosen, tok, 0.0), 0, keepdims=True)

    def hot(ids):
        lane = lax.broadcasted_iota(jnp.int32, ids.shape, 1).astype(F32)
        parts = [
            (ids == lane + float(column * LANES)).astype(F32).astype(BF16)
            for column in range(vocab // LANES)
        ]
        return jnp.concatenate(parts, 1)

    for block in range(length // LANES):
        rows = slice(block * LANES, (block + 1) * LANES)
        hot_ref[0, rows, :] = hot(tok_ref[rows, :])
        hot_ref[1, rows, :] = hot(base_ref[rows, :])

    hot_tok = hot(sub_ref[2])
    hot_base = hot(sub_ref[1])
    alphas = [(point + 0.5) / points for point in range(points)]
    sums_ref[...] = jnp.zeros_like(sums_ref)
    embed_copy.wait()
    wide = found_ref.shape[2]

    @pl.loop(0, width // wide)
    def _(step):
        lanes = pl.ds(pl.multiple_of(step * wide, wide), wide)
        found_ref[0] = dot(hot_tok, embed_ref[:, lanes])
        found_ref[1] = dot(hot_base, embed_ref[:, lanes])
        for block in range(subs // GROUP):
            rows = slice(block * GROUP, (block + 1) * GROUP)
            sums = [sums_ref[point, rows, :] for point in range(points)]
            for column in range(wide // LANES):
                cut = slice(column * LANES, (column + 1) * LANES)
                base = found_ref[1, rows, cut]
                diff = found_ref[0, rows, cut] - base
                for point in range(points):
                    value = base + alphas[point] * diff
                    sums[point] = sums[point] + value * value
            for point in range(points):
                sums_ref[point, rows, :] = sums[point]

    for point in range(points):
        mean = jnp.sum(sums_ref[point], 1, keepdims=True) / width
        sums_ref[point] = jnp.broadcast_to(lax.rsqrt(mean + EPS), (subs, LANES))

    mine = embed_ref[:, pl.ds(first, share)]
    looked = dot(hot_ref[0], jnp.concatenate([mine, vocab_ref[...]], 1))
    here_ref[0] = looked[:, :share]
    spread = looked[:, share:]
    here_ref[2] = spread + pltpu.roll(spread, LANES // 2, 1)
    here_ref[1] = dot(hot_ref[1], mine)
    pair_ref[0] = here_ref[0].astype(BF16)
    pair_ref[1] = here_ref[1].astype(BF16)
    own_width = own_ref.shape[2]
    own_rows = pl.ds(pl.multiple_of(ctx * LANES, LANES), LANES)
    own_lanes = pl.ds(pl.multiple_of(path * own_width, LANES), own_width)
    for kind in range(2):
        own_ref[kind] = dot(hot_ref[kind, own_rows, :], embed_ref[:, own_lanes]).astype(BF16)

    norm_ref[:GROUP, :] = jnp.zeros((GROUP, points * share), F32)
    gain = gain_ref[:, pl.ds(first, share)]
    taps = [taps_ref[f, :, pl.ds(first, share)].astype(F32) for f in range(3)]

    @pl.loop(0, length // CHUNK)
    def _(step):
        start = pl.multiple_of(step * CHUNK, CHUNK)
        rows = pl.ds(start, CHUNK)
        base = here_ref[1, rows, :]
        diff = here_ref[0, rows, :] - base
        inv_tok = here_ref[2, rows, :]
        groups = CHUNK // GROUP
        chosen = []
        for group in range(groups):
            index = step * groups + group
            place = jnp.broadcast_to(sub_ref[0, pl.ds(index, 1), :], (GROUP, LANES))
            chosen.append(within == place.astype(jnp.int32) - index * GROUP)
        for point in range(points):
            lanes = slice(point * share, (point + 1) * share)
            inv = jnp.concatenate(
                [
                    jnp.where(
                        chosen[group],
                        jnp.broadcast_to(
                            sums_ref[point, pl.ds(step * groups + group, 1), :], (GROUP, LANES)
                        ),
                        inv_tok[group * GROUP : (group + 1) * GROUP],
                    )
                    for group in range(groups)
                ],
                0,
            )
            inv_ref[rows, lanes] = inv
            now = rounded((base + alphas[point] * diff) * inv * gain)
            norm_ref[pl.ds(start + GROUP, CHUNK), lanes] = now
            window = norm_ref[pl.ds(start, CHUNK + GROUP), lanes]
            back1 = window[GROUP - 1 : GROUP - 1 + CHUNK]
            back2 = window[GROUP - 2 : GROUP - 2 + CHUNK]
            feats = [
                taps[f][0:1] * now + taps[f][1:2] * back1 + taps[f][2:3] * back2 for f in range(3)
            ]
            q_ref[rows, lanes] = feats[0]
            k_ref[rows, lanes] = feats[1]
            v_ref[rows, lanes] = feats[2]
            signal_ref[rows, lanes] = (feats[1] * feats[2]).astype(BF16)

    outs = [
        pltpu.make_async_copy(source, target, sems.at[2 + index])
        for index, (source, target) in enumerate(
            ((q_ref, q_hbm), (k_ref, k_hbm), (v_ref, v_hbm), (inv_ref, inv_hbm))
        )
    ]
    for copy in outs:
        copy.start()

    spec_copy.wait()
    transform(cos_ref, sin_ref, tables, signal_ref, spec_ref, prod_ref, points, False)
    skip = skip_ref[:, pl.ds(pl.multiple_of(path * share, LANES), share)]
    skip = jnp.concatenate([skip] * points, 1)
    for index in range(length // FREQ_ROWS):
        rows = pl.ds(index * FREQ_ROWS, FREQ_ROWS)
        result = inverse_rows(cos_ref, sin_ref, prod_ref, rows)
        conv_ref[rows, :] = (result + skip * signal_ref[rows, :].astype(F32)).astype(BF16)
    for copy in outs:
        copy.wait()


def backward_kernel(
    points, width, cot_ref, pair_ref, taps_ref, gain_ref, skip_ref,
    q_hbm, k_hbm, v_hbm, inv_hbm, conv_hbm, cos_hbm, sin_hbm, spec_hbm,
    grad_ref, part_ref,
    cos_ref, sin_ref, spec_ref, q_ref, k_ref, v_ref, inv_ref, conv_ref, signal_ref, prod_ref,
    tap0_ref, tap1_ref, tap2_ref, sems, table_sems,
):
    length = cos_ref.shape[0]
    share = cot_ref.shape[1]
    path, ctx = lax.axis_index("path"), lax.axis_index("ctx")
    n_path = skip_ref.shape[1] // share
    first = pl.multiple_of((ctx * n_path + path) * share, LANES)
    moves = ((q_hbm, q_ref), (spec_hbm, spec_ref), (conv_hbm, conv_ref), (k_hbm, k_ref), (v_hbm, v_ref), (inv_hbm, inv_ref))
    copies = [
        pltpu.make_async_copy(source, target, sems.at[index])
        for index, (source, target) in enumerate(moves)
    ]
    tables = table_copies(cos_hbm, sin_hbm, cos_ref, sin_ref, table_sems)
    copies[0].start()
    copies[1].start()
    for pair in tables:
        pair[0].start()
        pair[1].start()
    for copy in copies[2:]:
        copy.start()
    copies[0].wait()

    @pl.loop(0, length // CHUNK)
    def _(step):
        rows = pl.ds(pl.multiple_of(step * CHUNK, CHUNK), CHUNK)
        upstream = cot_ref[rows, :].astype(F32)
        for point in range(points):
            lanes = slice(point * share, (point + 1) * share)
            signal_ref[rows, lanes] = (upstream * q_ref[rows, lanes]).astype(BF16)

    copies[1].wait()
    transform(cos_ref, sin_ref, tables, signal_ref, spec_ref, prod_ref, points, True)
    for copy in copies[2:]:
        copy.wait()
    skip = skip_ref[:, pl.ds(pl.multiple_of(path * share, LANES), share)]
    gain = gain_ref[:, pl.ds(first, share)]
    taps = [taps_ref[f, :, pl.ds(first, share)].astype(F32) for f in range(3)]
    taps_refs = (tap0_ref, tap1_ref, tap2_ref)
    for ref in taps_refs:
        ref[length:, :] = jnp.zeros((GROUP, points * share), F32)
    for index in range(length // FREQ_ROWS):
        rows = pl.ds(index * FREQ_ROWS, FREQ_ROWS)
        result = inverse_rows(cos_ref, sin_ref, prod_ref, rows)
        for part in range(FREQ_ROWS // CHUNK):
            rows = pl.ds(index * FREQ_ROWS + part * CHUNK, CHUNK)
            upstream = cot_ref[rows, :].astype(F32)
            for point in range(points):
                lanes = slice(point * share, (point + 1) * share)
                grad_z = rounded(
                    result[part * CHUNK : (part + 1) * CHUNK, lanes]
                    + skip * signal_ref[rows, lanes].astype(F32)
                )
                grads = (
                    rounded(upstream * conv_ref[rows, lanes].astype(F32)),
                    rounded(grad_z * v_ref[rows, lanes]),
                    rounded(grad_z * k_ref[rows, lanes]),
                )
                for tap, ref in enumerate(taps_refs):
                    ref[rows, lanes] = sum(taps[f][tap : tap + 1] * grads[f] for f in range(3))

    alphas = [(point + 0.5) / points for point in range(points)]
    ones = jnp.ones((GROUP, share), F32)

    @pl.loop(0, length // LANES)
    def _(step):
        to_tok, to_base = [], []
        for part in range(LANES // CHUNK):
            start = pl.multiple_of(step * LANES + part * CHUNK, CHUNK)
            rows = pl.ds(start, CHUNK)
            tok = pair_ref[0, rows, :].astype(F32)
            base = pair_ref[1, rows, :].astype(F32)
            diff = tok - base
            total = jnp.zeros((CHUNK, share), F32)
            sum_tok = jnp.zeros((CHUNK, share), F32)
            sum_base = jnp.zeros((CHUNK, share), F32)
            for point in range(points):
                lanes = slice(point * share, (point + 1) * share)
                scaled = gain * (
                    tap0_ref[rows, lanes]
                    + tap1_ref[pl.ds(start, CHUNK + GROUP), lanes][1 : 1 + CHUNK]
                    + tap2_ref[pl.ds(start, CHUNK + GROUP), lanes][2 : 2 + CHUNK]
                )
                inv = inv_ref[rows, lanes]
                along = inv * scaled
                total = total + along
                along = along * (base + alphas[point] * diff) * (inv * inv)
                sum_tok = sum_tok + alphas[point] * along
                sum_base = sum_base + (1.0 - alphas[point]) * along
            grad_ref[rows, :] = total.astype(BF16)
            to_tok.append(sum_tok)
            to_base.append(sum_base)
        for kind, sums in enumerate((to_tok, to_base)):
            row = lax.dot_general(
                ones,
                jnp.concatenate(sums, 0),
                (((1,), (1,)), ((), ())),
                precision=lax.Precision.HIGHEST,
                preferred_element_type=F32,
            )
            part_ref[step, kind : kind + 1, :] = row[:1] / width


def finish_kernel(points, parts_ref, part_ref, own_ref, path_ref, attr_ref):
    n_path, pieces, rows, share = parts_ref.shape
    columns = transposed(part_ref[...])
    to_tok = columns[:, 0:1]
    to_base = columns[:, 1:2]
    for piece in range(pieces):
        for path in range(n_path):
            lanes = slice((piece * n_path + path) * share, (piece * n_path + path + 1) * share)
            tok = own_ref[0, :, lanes].astype(F32)
            base = own_ref[1, :, lanes].astype(F32)
            grad = parts_ref[path, piece].astype(F32) - tok * to_tok - base * to_base
            grad = grad / points
            path_ref[:, lanes] = grad
            attr_ref[:, lanes] = (tok - base) * grad


def any_spec():
    return pl.BlockSpec(memory_space=pl.ANY)


def vmem_spec():
    return pl.BlockSpec(memory_space=pltpu.VMEM)


def call(kernel, ins, outs, scratch, flops, moved):
    return pl.pallas_call(
        kernel,
        in_specs=ins,
        out_specs=[spec for spec, _ in outs],
        out_shape=[shape for _, shape in outs],
        scratch_shapes=scratch,
        compiler_params=pltpu.CompilerParams(vmem_limit_bytes=VMEM_BYTES),
        cost_estimate=pl.CostEstimate(flops=flops, bytes_accessed=moved, transcendentals=0),
    )


def shape(dims, dtype):
    return jax.ShapeDtypeStruct(dims, dtype)


def kernel_body(tokens, sub_pos, sub_base, embed, norm_gain, fir_taps, long_filter, skip_gain, cotangent):
    n_path, n_ctx = lax.axis_size("path"), lax.axis_size("ctx")
    points = n_path
    tok_rows = tokens.shape[0]
    length = tok_rows * n_ctx
    vocab, width = embed.shape
    share = width // (n_path * n_ctx)
    subs = sub_pos.shape[0] * n_ctx
    own_width = width // n_path
    cols = points * share
    cosine, sine, turn = dft_tables(length)

    def padded(values):
        return jnp.pad(values, (0, LANES - values.shape[0]))

    ids = jnp.stack([tokens, padded(sub_pos), padded(sub_base)])
    ids = lax.all_gather(ids, "ctx", axis=0, tiled=True)
    cot = cotangent.reshape(tok_rows, n_ctx, n_path, share)
    cot = lax.dynamic_index_in_dim(cot, lax.axis_index("path"), 2, keepdims=False)
    cot = lax.all_to_all(cot.transpose(1, 0, 2), "ctx", 0, 0, tiled=True)
    cot = cot.reshape(length, share)

    gain = norm_gain.reshape(1, width)
    skip = skip_gain.reshape(1, n_path * share)
    table = [pltpu.VMEM((length, length), BF16)] * 2
    table_sems = pltpu.SemaphoreType.DMA((2, length // FREQ_ROWS))
    dma = pltpu.SemaphoreType.DMA
    transform_flops = 4 * length * length

    spec, vocab_inv = call(
        functools.partial(prepare_kernel, n_path),
        [any_spec()] * 4 + [vmem_spec()],
        [
            (vmem_spec(), shape((2, length, share), F32)),
            (vmem_spec(), shape((vocab, LANES), BF16)),
        ],
        [pltpu.VMEM((length, share), F32)]
        + table
        + [
            pltpu.VMEM((vocab, width), BF16),
            pltpu.VMEM((length, 2 * share), BF16),
            dma((2,)),
            table_sems,
        ],
        2 * transform_flops * share,
        4 * length * length + 2 * vocab * width,
    )(long_filter, cosine, sine, embed, turn)

    wide = 4 * LANES
    conv, q_feat, k_feat, v_feat, inv, pair, own = call(
        functools.partial(forward_kernel, points),
        [vmem_spec(), any_spec()] + [vmem_spec()] * 4 + [any_spec()] * 3,
        [(vmem_spec(), shape((length, cols), BF16))]
        + [(any_spec(), shape((length, cols), F32))] * 4
        + [
            (vmem_spec(), shape((2, length, share), BF16)),
            (vmem_spec(), shape((2, tok_rows, own_width), BF16)),
        ],
        [pltpu.VMEM((vocab, width), BF16)]
        + table
        + [
            pltpu.VMEM((2, length, share), F32),
            pltpu.VMEM((length, LANES), F32),
            pltpu.VMEM((length, LANES), F32),
            pltpu.VMEM((3, subs, LANES), F32),
            pltpu.VMEM((2, length, vocab), BF16),
            pltpu.VMEM((points, subs, LANES), F32),
            pltpu.VMEM((2, subs, wide), F32),
            pltpu.VMEM((3, length, share), F32),
            pltpu.VMEM((GROUP + length, cols), F32),
            pltpu.VMEM((length, cols), F32),
            pltpu.VMEM((length, cols), F32),
            pltpu.VMEM((length, cols), F32),
            pltpu.VMEM((length, cols), F32),
            pltpu.VMEM((length, cols), BF16),
            pltpu.VMEM((2 * length, cols), BF16),
            dma((6,)),
            table_sems,
        ],
        2 * transform_flops * cols,
        4 * length * length + 2 * vocab * width + 16 * length * cols,
    )(ids, embed, vocab_inv, fir_taps, gain, skip, cosine, sine, spec)

    grad, part = call(
        functools.partial(backward_kernel, points, width),
        [vmem_spec()] * 5 + [any_spec()] * 8,
        [
            (vmem_spec(), shape((length, share), BF16)),
            (vmem_spec(), shape((n_ctx, 2, LANES), F32)),
        ],
        table
        + [pltpu.VMEM((2, length, share), F32)]
        + [pltpu.VMEM((length, cols), F32)] * 4
        + [
            pltpu.VMEM((length, cols), BF16),
            pltpu.VMEM((length, cols), BF16),
            pltpu.VMEM((2 * length, cols), BF16),
        ]
        + [pltpu.VMEM((length + GROUP, cols), F32)] * 3
        + [dma((6,)), table_sems],
        2 * transform_flops * cols,
        4 * length * length + 16 * length * cols,
    )(cot, pair, fir_taps, gain, skip, q_feat, k_feat, v_feat, inv, conv, cosine, sine, spec)

    part = lax.psum(part, ("path", "ctx"))
    part = lax.dynamic_index_in_dim(part, lax.axis_index("ctx"), 0, keepdims=False)
    back = lax.all_to_all(grad.reshape(n_ctx, tok_rows, share), "ctx", 0, 0, tiled=True)
    back = back.reshape(n_path, n_ctx // n_path, tok_rows, share)
    back = lax.all_to_all(back, "path", 0, 0, tiled=True)

    out = shape((tok_rows, own_width), F32)
    return tuple(
        call(
            functools.partial(finish_kernel, points),
            [vmem_spec()] * 3,
            [(vmem_spec(), out), (vmem_spec(), out)],
            [],
            8 * tok_rows * own_width,
            14 * tok_rows * own_width,
        )(back, part, own)
    )


def plain_body(tokens, sub_pos, sub_base, embed, norm_gain, fir_taps, long_filter, skip_gain, cotangent):
    n_path, n_ctx = lax.axis_size("path"), lax.axis_size("ctx")
    path, ctx = lax.axis_index("path"), lax.axis_index("ctx")
    points = n_path
    tok_rows = tokens.shape[0]
    length = tok_rows * n_ctx
    width = embed.shape[1]
    share = width // (n_path * n_ctx)
    own_width = width // n_path
    first = (ctx * n_path + path) * share
    alphas = ((jnp.arange(points, dtype=jnp.int32)).astype(F32) + 0.5) / points
    alphas = alphas[:, None, None]

    local = jnp.arange(tok_rows, dtype=jnp.int32)[:, None] + ctx * tok_rows == sub_pos[None, :]
    put = jnp.sum(jnp.where(local, sub_base[None, :], 0), 1)
    base_ids = jnp.where(jnp.any(local, 1), put, tokens)
    rows_tok = jnp.take(embed, tokens, axis=0).astype(F32)
    rows_base = jnp.take(embed, base_ids, axis=0).astype(F32)
    rows_in = rows_base[None] + alphas * (rows_tok - rows_base)[None]
    inv = lax.rsqrt(jnp.mean(rows_in * rows_in, -1) + EPS)
    inv = lax.all_gather(inv, "ctx", axis=1, tiled=True)[:, :, None]
    all_tok = lax.all_gather(tokens, "ctx", tiled=True)
    all_base = lax.all_gather(base_ids, "ctx", tiled=True)

    cot = cotangent.reshape(tok_rows, n_ctx, n_path, share)
    cot = lax.dynamic_index_in_dim(cot, path, 2, keepdims=False)
    cot = lax.all_to_all(cot.transpose(1, 0, 2), "ctx", 0, 0, tiled=True)
    upstream = cot.reshape(1, length, share).astype(F32)
    mine = lax.dynamic_slice_in_dim(embed, first, share, 1)
    gain = lax.dynamic_slice_in_dim(norm_gain, first, share, 0)
    taps = lax.dynamic_slice_in_dim(fir_taps, first, share, 2).astype(F32)
    filt = lax.dynamic_slice_in_dim(long_filter, path * share, share, 1)
    skip = lax.dynamic_slice_in_dim(skip_gain, path * share, share, 0)

    emb_tok = jnp.take(mine, all_tok, axis=0).astype(F32)
    emb_base = jnp.take(mine, all_base, axis=0).astype(F32)
    inputs = emb_base[None] + alphas * (emb_tok - emb_base)[None]
    normed = rounded(inputs * inv * gain)
    q_feat, k_feat, v_feat = (
        taps[f, 0] * normed + taps[f, 1] * shifted(normed, 1) + taps[f, 2] * shifted(normed, 2)
        for f in range(3)
    )
    filter_spec = spectrum(filt[None])
    conv = rounded(long_conv(rounded(k_feat * v_feat), filter_spec, skip, False))
    grad_z = rounded(long_conv(rounded(upstream * q_feat), filter_spec, skip, True))
    grads = (rounded(upstream * conv), rounded(grad_z * v_feat), rounded(grad_z * k_feat))
    by_tap = [sum(taps[f, tap] * grads[f] for f in range(3)) for tap in range(3)]
    scaled = gain * (by_tap[0] + shifted(by_tap[1], -1) + shifted(by_tap[2], -2))
    grad = jnp.sum(inv * scaled, 0).astype(BF16)
    along = jnp.sum(inputs * scaled, -1, keepdims=True) * inv**3 / width
    part = jnp.stack([jnp.sum(alphas * along, 0)[:, 0], jnp.sum((1.0 - alphas) * along, 0)[:, 0]])
    part = lax.psum(part, ("path", "ctx"))
    part = lax.dynamic_slice_in_dim(part, ctx * tok_rows, tok_rows, 1)

    back = lax.all_to_all(grad.reshape(n_ctx, tok_rows, share), "ctx", 0, 0, tiled=True)
    back = back.reshape(n_path, n_ctx // n_path, tok_rows, share)
    back = lax.all_to_all(back, "path", 0, 0, tiled=True).astype(F32)
    back = back.transpose(2, 1, 0, 3).reshape(tok_rows, own_width)
    own_tok = lax.dynamic_slice_in_dim(rows_tok, path * own_width, own_width, 1)
    own_base = lax.dynamic_slice_in_dim(rows_base, path * own_width, own_width, 1)
    grad = (back - own_tok * part[0][:, None] - own_base * part[1][:, None]) / points
    return (grad, (own_tok - own_base) * grad)


def body(tokens, sub_pos, sub_base, embed, *rest):
    n_path, n_ctx = lax.axis_size("path"), lax.axis_size("ctx")
    tok_rows = tokens.shape[0]
    share = embed.shape[1] // (n_path * n_ctx)
    tables = 4 * (tok_rows * n_ctx) ** 2
    fits = share == LANES and tok_rows == LANES and tables <= VMEM_BYTES // 8
    chosen = kernel_body if fits else plain_body
    return chosen(tokens, sub_pos, sub_base, embed, *rest)


def solution(mesh):
    return jax.shard_map(
        body,
        mesh=mesh,
        in_specs=(
            P("ctx"),
            P("ctx"),
            P("ctx"),
            P(),
            P(),
            P(),
            P(None, "ctx"),
            P("ctx"),
            P("ctx", None),
        ),
        out_specs=(P("ctx", "path"), P("ctx", "path")),
        check_vma=False,
    )
```

```python
import functools

import jax
import jax.numpy as jnp
import ml_dtypes
import numpy as np
from jax import lax
from jax.experimental import pallas as pl
from jax.experimental.pallas import tpu as pltpu
from jax.sharding import PartitionSpec as P

LANES = 128
GROUP = 8
FREQ_ROWS = 256
CHUNK = 64
EPS = 1e-06
VMEM_BYTES = 36 * 1024 * 1024
F32 = jnp.float32
BF16 = jnp.bfloat16
precise = lax.Precision.HIGH


def angle_tables(length):
    outer_size = 64
    inner_size = length // outer_size
    outer_idx = jnp.arange(outer_size, dtype=jnp.int32)
    inner_idx = jnp.arange(inner_size, dtype=jnp.int32)
    outer_angle = (
        2.0 * jnp.pi / outer_size
        * (outer_idx[:, None] * outer_idx[None, :] % outer_size).astype(F32)
    )
    inner_angle = (
        2.0 * jnp.pi / inner_size
        * (inner_idx[:, None] * inner_idx[None, :] % inner_size).astype(F32)
    )
    twist_angle = (
        2.0 * jnp.pi / length
        * (outer_idx[:, None] * inner_idx[None, :] % length).astype(F32)
    )
    return (outer_angle, inner_angle, twist_angle)


def complex_table(angle, sign):
    cosine = jnp.cos(angle)
    sine = sign * jnp.sin(angle)
    return jnp.stack([jnp.stack([cosine, sine]), jnp.stack([-sine, cosine])])


def twisted(values, angle, sign):
    cosine = jnp.cos(angle)[None, :, :, None]
    sine = sign * jnp.sin(angle)[None, :, :, None]
    real_part = values[:, 0]
    imag_part = values[:, 1]
    return jnp.stack(
        [real_part * cosine - imag_part * sine, real_part * sine + imag_part * cosine], 1
    )


def spectrum(signal):
    batch, half, width = signal.shape
    length = 2 * half
    outer_angle, inner_angle, twist_angle = angle_tables(length)
    outer_size = outer_angle.shape[0]
    inner_size = inner_angle.shape[0]
    folded = signal.reshape(batch, outer_size // 2, inner_size, width)
    used = outer_angle[:, : outer_size // 2]
    outer_table = jnp.stack([jnp.cos(used), -jnp.sin(used)])
    first = jnp.einsum("rka,pabc->prkbc", outer_table, folded, precision=precise)
    turned = twisted(first, twist_angle, -1.0)
    return jnp.einsum(
        "prkbc,rsbm->pskmc", turned, complex_table(inner_angle, -1.0), precision=precise
    )


def inverse(spec):
    batch, parts, outer_size, inner_size, width = spec.shape
    length = outer_size * inner_size
    outer_angle, inner_angle, twist_angle = angle_tables(length)
    back = jnp.einsum("pskmc,stmb->ptkbc", spec, complex_table(inner_angle, 1.0), precision=precise)
    turned = twisted(back, twist_angle, 1.0)
    used = outer_angle[: outer_size // 2]
    outer_table = jnp.stack([jnp.cos(used), -jnp.sin(used)])
    result = jnp.einsum("rak,prkbc->pabc", outer_table, turned, precision=precise)
    return (result / length).reshape(batch, length // 2, width)


def long_conv(signal, filter_spec, skip_gain, adjoint):
    spec = spectrum(signal)
    sig_real = spec[:, 0]
    sig_imag = spec[:, 1]
    filt_real = filter_spec[:, 0]
    filt_imag = filter_spec[:, 1]
    if adjoint:
        prod_real = sig_real * filt_real + sig_imag * filt_imag
        prod_imag = sig_imag * filt_real - sig_real * filt_imag
    else:
        prod_real = sig_real * filt_real - sig_imag * filt_imag
        prod_imag = sig_real * filt_imag + sig_imag * filt_real
    return inverse(jnp.stack([prod_real, prod_imag], 1)) + skip_gain * signal


def rounded(value):
    return value.astype(BF16).astype(F32)


def shifted(values, step):
    zeros = jnp.zeros_like(values[:, : abs(step)])
    if step > 0:
        return jnp.concatenate([zeros, values[:, :-step]], 1)
    return jnp.concatenate([values[:, -step:], zeros], 1)


@functools.lru_cache(maxsize=None)
def dft_tables(length):
    odd = 4 * np.arange(length, dtype=np.int64) + 1
    angle = (odd[:, None] * odd[None, :] % (16 * length)) * (2.0 * np.pi / (16 * length))
    phase = odd * (2.0 * np.pi / (16 * length))
    turn = np.stack([np.cos(phase), np.sin(phase)]).reshape(-1, LANES).astype(np.float32)
    return (
        np.cos(angle).astype(ml_dtypes.bfloat16),
        np.sin(angle).astype(ml_dtypes.bfloat16),
        turn,
    )


def transposed(rows):
    count = rows.shape[0]
    if count < LANES:
        rows = jnp.concatenate([rows, jnp.zeros((LANES - count, LANES), F32)], 0)
    return rows.T


def dot(left, right):
    return jnp.dot(left, right, preferred_element_type=F32)


def pack_kernel(
    tok_ref, pos_ref, put_ref, skip_ref, cot_hbm, filt_hbm,
    msg_ref, move_ref, ids_ref,
    filt_ref, sems,
):
    dests, rows, share = msg_ref.shape
    tok_rows = cot_hbm.shape[0]
    length = filt_ref.shape[0]
    path = lax.axis_index("path")
    first = path * (dests * share)
    filt_lanes = pl.ds(pl.multiple_of(path * share, LANES), share)
    filt_copy = pltpu.make_async_copy(filt_hbm.at[:, filt_lanes], filt_ref, sems.at[dests])
    copies = []
    for dest in range(dests):
        lanes = pl.ds(pl.multiple_of(first + dest * share, LANES), share)
        copies.append(
            pltpu.make_async_copy(
                cot_hbm.at[:, lanes], msg_ref.at[dest, pl.ds(0, tok_rows)], sems.at[dest]
            )
        )
    for copy in copies:
        copy.start()
    filt_copy.start()

    lists = []
    for ref in (tok_ref, pos_ref, put_ref):
        value = ref[...].astype(F32)
        if value.shape[1] < LANES:
            value = jnp.concatenate([value, jnp.zeros((1, LANES - value.shape[1]), F32)], 1)
        high = jnp.floor(value * (1.0 / 256.0))
        lists += [high, value - 256.0 * high]
    lists.append(jnp.zeros((rows - tok_rows - len(lists), LANES), F32))
    ids = jnp.concatenate(lists, 0)
    ids_ref[...] = ids
    for dest in range(dests):
        msg_ref[dest, tok_rows:, :] = ids.astype(BF16)

    skip = skip_ref[:, filt_lanes]
    one = skip.astype(BF16).astype(F32)
    two = (skip - one).astype(BF16).astype(F32)
    three = skip - one - two
    rest = jnp.zeros((move_ref.shape[0] - length - 3, share), F32)
    move_ref[length:, :] = jnp.concatenate([one, two, three, rest], 0).astype(BF16)
    filt_copy.wait()
    move_ref[:length, :] = filt_ref[...].astype(BF16)
    for copy in copies:
        copy.wait()


def spread_ids(blocks, tok_ref, base_ref, sub_ref):
    per_block = sub_ref.shape[1] // len(blocks)
    rows = []
    for block in blocks:
        rows += [256.0 * block[2 * kind : 2 * kind + 1] + block[2 * kind + 1 : 2 * kind + 2] for kind in range(3)]
    columns = transposed(jnp.concatenate(rows, 0))
    for block in range(len(blocks)):
        tok_ref[block * LANES : (block + 1) * LANES, :] = jnp.broadcast_to(
            columns[:, 3 * block : 3 * block + 1], (LANES, LANES)
        )
        here = slice(block * per_block, (block + 1) * per_block)
        for kind in range(2):
            column = columns[:per_block, 3 * block + 1 + kind : 3 * block + 2 + kind]
            if kind == 0:
                column = column - GROUP * jnp.floor(column * (1.0 / GROUP))
            sub_ref[kind, here, :] = jnp.broadcast_to(column, (per_block, LANES))
    within = lax.broadcasted_iota(jnp.int32, (GROUP, LANES), 0).astype(F32)

    @pl.loop(0, sub_ref.shape[1], unroll=8)
    def _(index):
        rows = pl.ds(pl.multiple_of(index * GROUP, GROUP), GROUP)
        one = pl.ds(index, 1)
        tok = tok_ref[rows, :]
        chosen = within == jnp.broadcast_to(sub_ref[0, one, :], (GROUP, LANES))
        put = jnp.broadcast_to(sub_ref[1, one, :], (GROUP, LANES))
        base_ref[rows, :] = jnp.where(chosen, put, tok)
        sub_ref[2, one, :] = jnp.sum(jnp.where(chosen, tok, 0.0), 0, keepdims=True)


def hot(ids, vocab):
    lane = lax.broadcasted_iota(jnp.int32, ids.shape, 1).astype(F32)
    parts = [
        (ids == lane + float(column * LANES)).astype(F32).astype(BF16)
        for column in range(vocab // LANES)
    ]
    return jnp.concatenate(parts, 1)


def vocab_kernel(ids_ref, embed_ref, vocab_ref, own_ref, tok_ref, base_ref, sub_ref):
    vocab, width = embed_ref.shape

    @pl.loop(0, vocab // 16, unroll=4)
    def _(step):
        rows = pl.ds(pl.multiple_of(step * 16, 16), 16)
        total = jnp.zeros((16, LANES), F32)
        for column in range(width // LANES):
            value = embed_ref[rows, column * LANES : (column + 1) * LANES].astype(F32)
            total = total + value * value
        inv = lax.rsqrt(jnp.sum(total, 1, keepdims=True) / width + EPS)
        inv = jnp.broadcast_to(inv, (16, LANES))
        high = inv.astype(BF16).astype(F32)
        lane = lax.broadcasted_iota(jnp.int32, (16, LANES), 1)
        vocab_ref[rows, :] = jnp.where(lane < LANES // 2, high, inv - high).astype(BF16)

    spread_ids([ids_ref[...]], tok_ref, base_ref, sub_ref)
    own_width = own_ref.shape[2]
    lanes = pl.ds(pl.multiple_of(lax.axis_index("path") * own_width, LANES), own_width)
    own_ref[0] = dot(hot(tok_ref[...], vocab), embed_ref[:, lanes]).astype(BF16)
    own_ref[1] = dot(hot(base_ref[...], vocab), embed_ref[:, lanes]).astype(BF16)


def spectrum_kernel(move_ref, cos_ref, sin_ref, turn_ref, spec_ref):
    length = cos_ref.shape[0]
    turn = transposed(turn_ref[...])
    blocks = length // LANES
    for index in range(length // FREQ_ROWS):
        rows = pl.ds(index * FREQ_ROWS, FREQ_ROWS)
        real = dot(cos_ref[rows, :], move_ref[:length, :])
        imag = dot(sin_ref[rows, :], move_ref[:length, :])
        for part in range(FREQ_ROWS // LANES):
            block = index * (FREQ_ROWS // LANES) + part
            cosine = turn[:, block : block + 1] / length
            sine = turn[:, blocks + block : blocks + block + 1] / length
            here = slice(part * LANES, (part + 1) * LANES)
            into = pl.ds(block * LANES, LANES)
            spec_ref[0, into, :] = real[here] * cosine + imag[here] * sine
            spec_ref[1, into, :] = real[here] * sine - imag[here] * cosine


def transform(cos_ref, sin_ref, signal_ref, spec_ref, prod_ref, points, adjoint):
    length = cos_ref.shape[0]
    share = spec_ref.shape[2]
    for index in range(length // FREQ_ROWS):
        rows = pl.ds(index * FREQ_ROWS, FREQ_ROWS)
        after = pl.ds(length + index * FREQ_ROWS, FREQ_ROWS)
        real = dot(cos_ref[rows, :], signal_ref[...])
        imag = dot(sin_ref[rows, :], signal_ref[...])
        filt_real = spec_ref[0, rows, :]
        filt_imag = spec_ref[1, rows, :]
        for point in range(points):
            lanes = slice(point * share, (point + 1) * share)
            one, two = real[:, lanes], imag[:, lanes]
            if adjoint:
                prod_ref[rows, lanes] = (one * filt_real - two * filt_imag).astype(BF16)
                prod_ref[after, lanes] = (one * filt_imag + two * filt_real).astype(BF16)
            else:
                prod_ref[rows, lanes] = (one * filt_real + two * filt_imag).astype(BF16)
                prod_ref[after, lanes] = (two * filt_real - one * filt_imag).astype(BF16)


def inverse_rows(cos_ref, sin_ref, prod_ref, rows):
    length = cos_ref.shape[0]
    return dot(cos_ref[rows, :], prod_ref[:length, :]) + dot(sin_ref[rows, :], prod_ref[length:, :])


def skip_row(move_ref, length):
    rows = move_ref[length : length + 16, :].astype(F32)
    return rows[0:1] + rows[1:2] + rows[2:3]


def forward_kernel(
    points, msg_ref, move_ref, embed_ref, vocab_ref, taps_ref, gain_ref, cos_ref, sin_ref, spec_ref,
    conv_ref, q_ref, k_ref, v_ref, inv_ref, pair_ref,
    tok_ref, base_ref, sub_ref, hot_ref, sums_ref, found_ref, here_ref, norm_ref, signal_ref, prod_ref,
):
    length = cos_ref.shape[0]
    vocab, width = embed_ref.shape
    share = pair_ref.shape[2]
    subs = sub_ref.shape[1]
    n_ctx = msg_ref.shape[0]
    first = (lax.axis_index("path") * n_ctx + lax.axis_index("ctx")) * share
    first = pl.multiple_of(first, LANES)
    spread_ids([msg_ref[block, LANES:, :].astype(F32) for block in range(n_ctx)], tok_ref, base_ref, sub_ref)
    within = lax.broadcasted_iota(jnp.int32, (GROUP, LANES), 0).astype(F32)
    for block in range(length // LANES):
        rows = slice(block * LANES, (block + 1) * LANES)
        hot_ref[0, rows, :] = hot(tok_ref[rows, :], vocab)
        hot_ref[1, rows, :] = hot(base_ref[rows, :], vocab)

    hot_tok = hot(sub_ref[2], vocab)
    hot_base = hot(sub_ref[1], vocab)
    alphas = [(point + 0.5) / points for point in range(points)]
    sums_ref[...] = jnp.zeros_like(sums_ref)
    wide = found_ref.shape[2]

    @pl.loop(0, width // wide)
    def _(step):
        lanes = pl.ds(pl.multiple_of(step * wide, wide), wide)
        found_ref[0] = dot(hot_tok, embed_ref[:, lanes])
        found_ref[1] = dot(hot_base, embed_ref[:, lanes])
        for block in range(subs // GROUP):
            rows = slice(block * GROUP, (block + 1) * GROUP)
            sums = [sums_ref[point, rows, :] for point in range(points)]
            for column in range(wide // LANES):
                cut = slice(column * LANES, (column + 1) * LANES)
                base = found_ref[1, rows, cut]
                diff = found_ref[0, rows, cut] - base
                for point in range(points):
                    value = base + alphas[point] * diff
                    sums[point] = sums[point] + value * value
            for point in range(points):
                sums_ref[point, rows, :] = sums[point]

    for point in range(points):
        mean = jnp.sum(sums_ref[point], 1, keepdims=True) / width
        sums_ref[point] = jnp.broadcast_to(lax.rsqrt(mean + EPS), (subs, LANES))

    mine = embed_ref[:, pl.ds(first, share)]
    looked = dot(hot_ref[0], jnp.concatenate([mine, vocab_ref[...]], 1))
    here_ref[0] = looked[:, :share]
    spread = looked[:, share:]
    here_ref[2] = spread + pltpu.roll(spread, LANES // 2, 1)
    here_ref[1] = dot(hot_ref[1], mine)
    pair_ref[0] = here_ref[0].astype(BF16)
    pair_ref[1] = here_ref[1].astype(BF16)

    norm_ref[:GROUP, :] = jnp.zeros((GROUP, points * share), F32)
    gain = gain_ref[:, pl.ds(first, share)]
    taps = [taps_ref[f, :, pl.ds(first, share)].astype(F32) for f in range(3)]

    @pl.loop(0, length // CHUNK)
    def _(step):
        start = pl.multiple_of(step * CHUNK, CHUNK)
        rows = pl.ds(start, CHUNK)
        base = here_ref[1, rows, :]
        diff = here_ref[0, rows, :] - base
        inv_tok = here_ref[2, rows, :]
        groups = CHUNK // GROUP
        chosen = []
        for group in range(groups):
            index = step * groups + group
            place = jnp.broadcast_to(sub_ref[0, pl.ds(index, 1), :], (GROUP, LANES))
            chosen.append(within == place)
        for point in range(points):
            lanes = slice(point * share, (point + 1) * share)
            inv = jnp.concatenate(
                [
                    jnp.where(
                        chosen[group],
                        jnp.broadcast_to(
                            sums_ref[point, pl.ds(step * groups + group, 1), :], (GROUP, LANES)
                        ),
                        inv_tok[group * GROUP : (group + 1) * GROUP],
                    )
                    for group in range(groups)
                ],
                0,
            )
            inv_ref[rows, lanes] = inv
            now = rounded((base + alphas[point] * diff) * inv * gain)
            norm_ref[pl.ds(start + GROUP, CHUNK), lanes] = now
            window = norm_ref[pl.ds(start, CHUNK + GROUP), lanes]
            back1 = window[GROUP - 1 : GROUP - 1 + CHUNK]
            back2 = window[GROUP - 2 : GROUP - 2 + CHUNK]
            feats = [
                taps[f][0:1] * now + taps[f][1:2] * back1 + taps[f][2:3] * back2 for f in range(3)
            ]
            q_ref[rows, lanes] = feats[0]
            k_ref[rows, lanes] = feats[1]
            v_ref[rows, lanes] = feats[2]
            signal_ref[rows, lanes] = (feats[1] * feats[2]).astype(BF16)

    transform(cos_ref, sin_ref, signal_ref, spec_ref, prod_ref, points, False)
    skip = jnp.concatenate([skip_row(move_ref, length)] * points, 1)
    for index in range(length // FREQ_ROWS):
        rows = pl.ds(index * FREQ_ROWS, FREQ_ROWS)
        result = inverse_rows(cos_ref, sin_ref, prod_ref, rows)
        conv_ref[rows, :] = (result + skip * signal_ref[rows, :].astype(F32)).astype(BF16)


def backward_kernel(
    points, width, msg_ref, move_ref, pair_ref, taps_ref, gain_ref,
    q_ref, k_ref, v_ref, inv_ref, conv_ref, cos_ref, sin_ref, spec_ref,
    grad_ref, part_ref,
    signal_ref, prod_ref, tap0_ref, tap1_ref, tap2_ref,
):
    length = cos_ref.shape[0]
    share = pair_ref.shape[2]
    n_ctx = msg_ref.shape[0]
    n_path = part_ref.shape[0] // n_ctx
    first = (lax.axis_index("path") * n_ctx + lax.axis_index("ctx")) * share
    first = pl.multiple_of(first, LANES)

    @pl.loop(0, n_ctx)
    def _(block):
        for part in range(LANES // CHUNK):
            rows = pl.ds(pl.multiple_of(block * LANES + part * CHUNK, CHUNK), CHUNK)
            upstream = msg_ref[block, part * CHUNK : (part + 1) * CHUNK, :].astype(F32)
            for point in range(points):
                lanes = slice(point * share, (point + 1) * share)
                signal_ref[rows, lanes] = (upstream * q_ref[rows, lanes]).astype(BF16)

    transform(cos_ref, sin_ref, signal_ref, spec_ref, prod_ref, points, True)
    skip = skip_row(move_ref, length)
    gain = gain_ref[:, pl.ds(first, share)]
    taps = [taps_ref[f, :, pl.ds(first, share)].astype(F32) for f in range(3)]
    taps_refs = (tap0_ref, tap1_ref, tap2_ref)
    for ref in taps_refs:
        ref[length:, :] = jnp.zeros((GROUP, points * share), F32)
    for index in range(length // FREQ_ROWS):
        rows = pl.ds(index * FREQ_ROWS, FREQ_ROWS)
        result = inverse_rows(cos_ref, sin_ref, prod_ref, rows)
        for part in range(FREQ_ROWS // CHUNK):
            start = index * FREQ_ROWS + part * CHUNK
            rows = pl.ds(start, CHUNK)
            inside = start % LANES
            upstream = msg_ref[start // LANES, inside : inside + CHUNK, :].astype(F32)
            for point in range(points):
                lanes = slice(point * share, (point + 1) * share)
                grad_z = rounded(
                    result[part * CHUNK : (part + 1) * CHUNK, lanes]
                    + skip * signal_ref[rows, lanes].astype(F32)
                )
                grads = (
                    rounded(upstream * conv_ref[rows, lanes].astype(F32)),
                    rounded(grad_z * v_ref[rows, lanes]),
                    rounded(grad_z * k_ref[rows, lanes]),
                )
                for tap, ref in enumerate(taps_refs):
                    ref[rows, lanes] = sum(taps[f][tap : tap + 1] * grads[f] for f in range(3))

    alphas = [(point + 0.5) / points for point in range(points)]
    ones = jnp.ones((GROUP, share), F32)

    @pl.loop(0, length // LANES)
    def _(step):
        to_tok, to_base = [], []
        for part in range(LANES // CHUNK):
            start = pl.multiple_of(step * LANES + part * CHUNK, CHUNK)
            rows = pl.ds(start, CHUNK)
            tok = pair_ref[0, rows, :].astype(F32)
            base = pair_ref[1, rows, :].astype(F32)
            diff = tok - base
            total = jnp.zeros((CHUNK, share), F32)
            sum_tok = jnp.zeros((CHUNK, share), F32)
            sum_base = jnp.zeros((CHUNK, share), F32)
            for point in range(points):
                lanes = slice(point * share, (point + 1) * share)
                scaled = gain * (
                    tap0_ref[rows, lanes]
                    + tap1_ref[pl.ds(start, CHUNK + GROUP), lanes][1 : 1 + CHUNK]
                    + tap2_ref[pl.ds(start, CHUNK + GROUP), lanes][2 : 2 + CHUNK]
                )
                inv = inv_ref[rows, lanes]
                along = inv * scaled
                total = total + along
                along = along * (base + alphas[point] * diff) * (inv * inv)
                sum_tok = sum_tok + alphas[point] * along
                sum_base = sum_base + (1.0 - alphas[point]) * along
            grad_ref[rows, :] = total.astype(BF16)
            to_tok.append(sum_tok)
            to_base.append(sum_base)
        for kind, sums in enumerate((to_tok, to_base)):
            row = lax.dot_general(
                ones,
                jnp.concatenate(sums, 0),
                (((1,), (1,)), ((), ())),
                precision=lax.Precision.HIGHEST,
                preferred_element_type=F32,
            )
            for path in range(n_path):
                part_ref[path * n_ctx + step, kind : kind + 1, :] = row[:1] / width


def finish_kernel(points, grad_ref, part_ref, own_ref, path_ref, attr_ref):
    pieces, rows, share = grad_ref.shape
    sums = jnp.sum(part_ref[...], 0)
    columns = transposed(sums)
    to_tok = columns[:, 0:1]
    to_base = columns[:, 1:2]
    for piece in range(pieces):
        lanes = slice(piece * share, (piece + 1) * share)
        tok = own_ref[0, :, lanes].astype(F32)
        base = own_ref[1, :, lanes].astype(F32)
        grad = grad_ref[piece].astype(F32) - tok * to_tok - base * to_base
        grad = grad / points
        path_ref[:, lanes] = grad
        attr_ref[:, lanes] = (tok - base) * grad


def any_spec():
    return pl.BlockSpec(memory_space=pl.ANY)


def vmem_spec():
    return pl.BlockSpec(memory_space=pltpu.VMEM)


def call(kernel, ins, outs, scratch, flops, moved):
    return pl.pallas_call(
        kernel,
        in_specs=ins,
        out_specs=[spec for spec, _ in outs],
        out_shape=[shape for _, shape in outs],
        scratch_shapes=scratch,
        compiler_params=pltpu.CompilerParams(vmem_limit_bytes=VMEM_BYTES),
        cost_estimate=pl.CostEstimate(flops=flops, bytes_accessed=moved, transcendentals=0),
    )


def shape(dims, dtype):
    return jax.ShapeDtypeStruct(dims, dtype)


def kernel_body(tokens, sub_pos, sub_base, embed, norm_gain, fir_taps, long_filter, skip_gain, cotangent):
    n_path, n_ctx = lax.axis_size("path"), lax.axis_size("ctx")
    points = n_path
    tok_rows = tokens.shape[0]
    length = tok_rows * n_ctx
    vocab, width = embed.shape
    share = width // (n_path * n_ctx)
    subs = sub_pos.shape[0] * n_ctx
    own_width = width // n_path
    cols = points * share
    cosine, sine, turn = dft_tables(length)

    dma = pltpu.SemaphoreType.DMA
    transform_flops = 4 * length * length
    spare = 16

    msg, move, ids = call(
        pack_kernel,
        [vmem_spec()] * 4 + [any_spec()] * 2,
        [
            (vmem_spec(), shape((n_ctx, tok_rows + spare, share), BF16)),
            (vmem_spec(), shape((length + spare, share), BF16)),
            (vmem_spec(), shape((spare, LANES), F32)),
        ],
        [pltpu.VMEM((length, share), F32), dma((n_ctx + 1,))],
        length * share,
        8 * length * share,
    )(
        tokens.reshape(1, tok_rows),
        sub_pos.reshape(1, -1),
        sub_base.reshape(1, -1),
        skip_gain.reshape(1, n_path * share),
        cotangent,
        long_filter,
    )
    msg = lax.all_to_all(msg, "ctx", 0, 0, tiled=True)
    route = [(p * n_ctx + c, c * n_path + p) for p in range(n_path) for c in range(n_ctx)]
    move = lax.ppermute(move, ("path", "ctx"), route)

    gain = norm_gain.reshape(1, width)
    vocab_inv, own = call(
        vocab_kernel,
        [vmem_spec()] * 2,
        [
            (vmem_spec(), shape((vocab, LANES), BF16)),
            (vmem_spec(), shape((2, tok_rows, own_width), BF16)),
        ],
        [
            pltpu.VMEM((LANES, LANES), F32),
            pltpu.VMEM((LANES, LANES), F32),
            pltpu.VMEM((3, sub_pos.shape[0], LANES), F32),
        ],
        4 * tok_rows * vocab * own_width,
        2 * vocab * width,
    )(ids, embed)
    spec = call(
        spectrum_kernel,
        [vmem_spec()] * 4,
        [(vmem_spec(), shape((2, length, share), F32))],
        [],
        transform_flops * share,
        4 * length * length,
    )(move, cosine, sine, turn)[0]

    wide = 4 * LANES
    conv, q_feat, k_feat, v_feat, inv, pair = call(
        functools.partial(forward_kernel, points),
        [vmem_spec()] * 9,
        [(vmem_spec(), shape((length, cols), BF16))]
        + [(vmem_spec(), shape((length, cols), F32))] * 4
        + [(vmem_spec(), shape((2, length, share), BF16))],
        [
            pltpu.VMEM((length, LANES), F32),
            pltpu.VMEM((length, LANES), F32),
            pltpu.VMEM((3, subs, LANES), F32),
            pltpu.VMEM((2, length, vocab), BF16),
            pltpu.VMEM((points, subs, LANES), F32),
            pltpu.VMEM((2, subs, wide), F32),
            pltpu.VMEM((3, length, share), F32),
            pltpu.VMEM((GROUP + length, cols), F32),
            pltpu.VMEM((length, cols), BF16),
            pltpu.VMEM((2 * length, cols), BF16),
        ],
        2 * transform_flops * cols,
        4 * length * length + 2 * vocab * width + 16 * length * cols,
    )(msg, move, embed, vocab_inv, fir_taps, gain, cosine, sine, spec)

    grad, part = call(
        functools.partial(backward_kernel, points, width),
        [vmem_spec()] * 13,
        [
            (vmem_spec(), shape((length, share), BF16)),
            (vmem_spec(), shape((n_path * n_ctx, 2, LANES), F32)),
        ],
        [
            pltpu.VMEM((length, cols), BF16),
            pltpu.VMEM((2 * length, cols), BF16),
        ]
        + [pltpu.VMEM((length + GROUP, cols), F32)] * 3,
        2 * transform_flops * cols,
        4 * length * length + 16 * length * cols,
    )(msg, move, pair, fir_taps, gain, q_feat, k_feat, v_feat, inv, conv, cosine, sine, spec)

    part = lax.all_to_all(part, ("path", "ctx"), 0, 0, tiled=True)
    grad = lax.all_to_all(grad.reshape(n_ctx, tok_rows, share), "ctx", 0, 0, tiled=True)
    out = shape((tok_rows, own_width), F32)
    return tuple(
        call(
            functools.partial(finish_kernel, points),
            [vmem_spec()] * 3,
            [(vmem_spec(), out), (vmem_spec(), out)],
            [],
            8 * tok_rows * own_width,
            14 * tok_rows * own_width,
        )(grad, part, own)
    )


def plain_body(tokens, sub_pos, sub_base, embed, norm_gain, fir_taps, long_filter, skip_gain, cotangent):
    n_path, n_ctx = lax.axis_size("path"), lax.axis_size("ctx")
    path, ctx = lax.axis_index("path"), lax.axis_index("ctx")
    points = n_path
    tok_rows = tokens.shape[0]
    length = tok_rows * n_ctx
    width = embed.shape[1]
    share = width // (n_path * n_ctx)
    own_width = width // n_path
    first = (ctx * n_path + path) * share
    alphas = ((jnp.arange(points, dtype=jnp.int32)).astype(F32) + 0.5) / points
    alphas = alphas[:, None, None]

    local = jnp.arange(tok_rows, dtype=jnp.int32)[:, None] + ctx * tok_rows == sub_pos[None, :]
    put = jnp.sum(jnp.where(local, sub_base[None, :], 0), 1)
    base_ids = jnp.where(jnp.any(local, 1), put, tokens)
    rows_tok = jnp.take(embed, tokens, axis=0).astype(F32)
    rows_base = jnp.take(embed, base_ids, axis=0).astype(F32)
    rows_in = rows_base[None] + alphas * (rows_tok - rows_base)[None]
    inv = lax.rsqrt(jnp.mean(rows_in * rows_in, -1) + EPS)
    inv = lax.all_gather(inv, "ctx", axis=1, tiled=True)[:, :, None]
    all_tok = lax.all_gather(tokens, "ctx", tiled=True)
    all_base = lax.all_gather(base_ids, "ctx", tiled=True)

    cot = cotangent.reshape(tok_rows, n_ctx, n_path, share)
    cot = lax.dynamic_index_in_dim(cot, path, 2, keepdims=False)
    cot = lax.all_to_all(cot.transpose(1, 0, 2), "ctx", 0, 0, tiled=True)
    upstream = cot.reshape(1, length, share).astype(F32)
    mine = lax.dynamic_slice_in_dim(embed, first, share, 1)
    gain = lax.dynamic_slice_in_dim(norm_gain, first, share, 0)
    taps = lax.dynamic_slice_in_dim(fir_taps, first, share, 2).astype(F32)
    filt = lax.dynamic_slice_in_dim(long_filter, path * share, share, 1)
    skip = lax.dynamic_slice_in_dim(skip_gain, path * share, share, 0)

    emb_tok = jnp.take(mine, all_tok, axis=0).astype(F32)
    emb_base = jnp.take(mine, all_base, axis=0).astype(F32)
    inputs = emb_base[None] + alphas * (emb_tok - emb_base)[None]
    normed = rounded(inputs * inv * gain)
    q_feat, k_feat, v_feat = (
        taps[f, 0] * normed + taps[f, 1] * shifted(normed, 1) + taps[f, 2] * shifted(normed, 2)
        for f in range(3)
    )
    filter_spec = spectrum(filt[None])
    conv = rounded(long_conv(rounded(k_feat * v_feat), filter_spec, skip, False))
    grad_z = rounded(long_conv(rounded(upstream * q_feat), filter_spec, skip, True))
    grads = (rounded(upstream * conv), rounded(grad_z * v_feat), rounded(grad_z * k_feat))
    by_tap = [sum(taps[f, tap] * grads[f] for f in range(3)) for tap in range(3)]
    scaled = gain * (by_tap[0] + shifted(by_tap[1], -1) + shifted(by_tap[2], -2))
    grad = jnp.sum(inv * scaled, 0).astype(BF16)
    along = jnp.sum(inputs * scaled, -1, keepdims=True) * inv**3 / width
    part = jnp.stack([jnp.sum(alphas * along, 0)[:, 0], jnp.sum((1.0 - alphas) * along, 0)[:, 0]])
    part = lax.psum(part, ("path", "ctx"))
    part = lax.dynamic_slice_in_dim(part, ctx * tok_rows, tok_rows, 1)

    back = lax.all_to_all(grad.reshape(n_ctx, tok_rows, share), "ctx", 0, 0, tiled=True)
    back = back.reshape(n_path, n_ctx // n_path, tok_rows, share)
    back = lax.all_to_all(back, "path", 0, 0, tiled=True).astype(F32)
    back = back.transpose(2, 1, 0, 3).reshape(tok_rows, own_width)
    own_tok = lax.dynamic_slice_in_dim(rows_tok, path * own_width, own_width, 1)
    own_base = lax.dynamic_slice_in_dim(rows_base, path * own_width, own_width, 1)
    grad = (back - own_tok * part[0][:, None] - own_base * part[1][:, None]) / points
    return (grad, (own_tok - own_base) * grad)


def body(tokens, sub_pos, sub_base, embed, *rest):
    n_path, n_ctx = lax.axis_size("path"), lax.axis_size("ctx")
    tok_rows = tokens.shape[0]
    share = embed.shape[1] // (n_path * n_ctx)
    tables = 4 * (tok_rows * n_ctx) ** 2
    fits = share == LANES and tok_rows == LANES and tables <= VMEM_BYTES // 8
    chosen = kernel_body if fits else plain_body
    return chosen(tokens, sub_pos, sub_base, embed, *rest)


def solution(mesh):
    return jax.shard_map(
        body,
        mesh=mesh,
        in_specs=(
            P("ctx"),
            P("ctx"),
            P("ctx"),
            P(),
            P(),
            P(),
            P(None, "ctx"),
            P("ctx"),
            P("ctx", None),
        ),
        out_specs=(P("ctx", "path"), P("ctx", "path")),
        check_vma=False,
    )
```

```python
import functools

import jax
import jax.numpy as jnp
import ml_dtypes
import numpy as np
from jax import lax
from jax.experimental import pallas as pl
from jax.experimental.pallas import tpu as pltpu
from jax.sharding import PartitionSpec as P

LANES = 128
GROUP = 8
FREQ_ROWS = 256
CHUNK = 64
EPS = 1e-06
TABLE_BYTES = 4 * 2**20
F32 = jnp.float32
BF16 = jnp.bfloat16
precise = lax.Precision.HIGH


def angle_tables(length):
    outer_size = 64
    inner_size = length // outer_size
    outer_idx = jnp.arange(outer_size, dtype=jnp.int32)
    inner_idx = jnp.arange(inner_size, dtype=jnp.int32)
    outer_angle = (
        2.0 * jnp.pi / outer_size
        * (outer_idx[:, None] * outer_idx[None, :] % outer_size).astype(F32)
    )
    inner_angle = (
        2.0 * jnp.pi / inner_size
        * (inner_idx[:, None] * inner_idx[None, :] % inner_size).astype(F32)
    )
    twist_angle = (
        2.0 * jnp.pi / length
        * (outer_idx[:, None] * inner_idx[None, :] % length).astype(F32)
    )
    return (outer_angle, inner_angle, twist_angle)


def complex_table(angle, sign):
    cosine = jnp.cos(angle)
    sine = sign * jnp.sin(angle)
    return jnp.stack([jnp.stack([cosine, sine]), jnp.stack([-sine, cosine])])


def twisted(values, angle, sign):
    cosine = jnp.cos(angle)[None, :, :, None]
    sine = sign * jnp.sin(angle)[None, :, :, None]
    real_part = values[:, 0]
    imag_part = values[:, 1]
    return jnp.stack(
        [real_part * cosine - imag_part * sine, real_part * sine + imag_part * cosine], 1
    )


def spectrum(signal):
    batch, half, width = signal.shape
    length = 2 * half
    outer_angle, inner_angle, twist_angle = angle_tables(length)
    outer_size = outer_angle.shape[0]
    inner_size = inner_angle.shape[0]
    folded = signal.reshape(batch, outer_size // 2, inner_size, width)
    used = outer_angle[:, : outer_size // 2]
    outer_table = jnp.stack([jnp.cos(used), -jnp.sin(used)])
    first = jnp.einsum("rka,pabc->prkbc", outer_table, folded, precision=precise)
    turned = twisted(first, twist_angle, -1.0)
    return jnp.einsum(
        "prkbc,rsbm->pskmc", turned, complex_table(inner_angle, -1.0), precision=precise
    )


def inverse(spec):
    batch, parts, outer_size, inner_size, width = spec.shape
    length = outer_size * inner_size
    outer_angle, inner_angle, twist_angle = angle_tables(length)
    back = jnp.einsum("pskmc,stmb->ptkbc", spec, complex_table(inner_angle, 1.0), precision=precise)
    turned = twisted(back, twist_angle, 1.0)
    used = outer_angle[: outer_size // 2]
    outer_table = jnp.stack([jnp.cos(used), -jnp.sin(used)])
    result = jnp.einsum("rak,prkbc->pabc", outer_table, turned, precision=precise)
    return (result / length).reshape(batch, length // 2, width)


def long_conv(signal, filter_spec, skip_gain, adjoint):
    spec = spectrum(signal)
    sig_real = spec[:, 0]
    sig_imag = spec[:, 1]
    filt_real = filter_spec[:, 0]
    filt_imag = filter_spec[:, 1]
    if adjoint:
        prod_real = sig_real * filt_real + sig_imag * filt_imag
        prod_imag = sig_imag * filt_real - sig_real * filt_imag
    else:
        prod_real = sig_real * filt_real - sig_imag * filt_imag
        prod_imag = sig_real * filt_imag + sig_imag * filt_real
    return inverse(jnp.stack([prod_real, prod_imag], 1)) + skip_gain * signal


def rounded(value):
    return value.astype(BF16).astype(F32)


def shifted(values, step):
    zeros = jnp.zeros_like(values[:, : abs(step)])
    if step > 0:
        return jnp.concatenate([zeros, values[:, :-step]], 1)
    return jnp.concatenate([values[:, -step:], zeros], 1)


@functools.lru_cache(maxsize=None)
def dft_tables(length):
    odd = 4 * np.arange(length, dtype=np.int64) + 1
    angle = (odd[:, None] * odd[None, :] % (16 * length)) * (2.0 * np.pi / (16 * length))
    phase = odd * (2.0 * np.pi / (16 * length))
    turn = np.stack([np.cos(phase), np.sin(phase)]).reshape(-1, LANES).astype(np.float32)
    return (
        np.cos(angle).astype(ml_dtypes.bfloat16),
        np.sin(angle).astype(ml_dtypes.bfloat16),
        turn,
    )


def transposed(rows):
    count = rows.shape[0]
    if count < LANES:
        rows = jnp.concatenate([rows, jnp.zeros((LANES - count, LANES), F32)], 0)
    return rows.T


def dot(left, right):
    return jnp.dot(left, right, preferred_element_type=F32)


def pack_kernel(tok_hbm, pos_hbm, put_hbm, cot_hbm, msg_ref, ids_ref, tok_ref, pos_ref, put_ref, sems):
    dests, rows, share = msg_ref.shape
    tok_rows = cot_hbm.shape[0]
    first = lax.axis_index("path") * (dests * share)
    moves = [(tok_hbm, tok_ref), (pos_hbm, pos_ref), (put_hbm, put_ref)]
    for dest in range(dests):
        lanes = pl.ds(pl.multiple_of(first + dest * share, LANES), share)
        moves.append((cot_hbm.at[:, lanes], msg_ref.at[dest, pl.ds(0, tok_rows)]))
    copies = [
        pltpu.make_async_copy(source, target, sems.at[index])
        for index, (source, target) in enumerate(moves)
    ]
    for copy in copies:
        copy.start()
    for copy in copies[:3]:
        copy.wait()
    lists = []
    for ref in (tok_ref, pos_ref, put_ref):
        value = ref[...].astype(F32)
        if value.shape[1] < LANES:
            value = jnp.concatenate([value, jnp.zeros((1, LANES - value.shape[1]), F32)], 1)
        high = jnp.floor(value * (1.0 / 256.0))
        lists += [high, value - 256.0 * high]
    lists.append(jnp.zeros((rows - tok_rows - len(lists), LANES), F32))
    ids = jnp.concatenate(lists, 0)
    ids_ref[...] = ids
    for dest in range(dests):
        msg_ref[dest, tok_rows:, :] = ids.astype(BF16)
    for copy in copies[3:]:
        copy.wait()


def spread_ids(blocks, tok_ref, base_ref, sub_ref):
    per_block = sub_ref.shape[1] // len(blocks)
    rows = []
    for block in blocks:
        rows += [256.0 * block[2 * kind : 2 * kind + 1] + block[2 * kind + 1 : 2 * kind + 2] for kind in range(3)]
    columns = transposed(jnp.concatenate(rows, 0))
    for block in range(len(blocks)):
        tok_ref[block * LANES : (block + 1) * LANES, :] = jnp.broadcast_to(
            columns[:, 3 * block : 3 * block + 1], (LANES, LANES)
        )
        here = slice(block * per_block, (block + 1) * per_block)
        for kind in range(2):
            column = columns[:per_block, 3 * block + 1 + kind : 3 * block + 2 + kind]
            if kind == 0:
                column = column - GROUP * jnp.floor(column * (1.0 / GROUP))
            sub_ref[kind, here, :] = jnp.broadcast_to(column, (per_block, LANES))
    within = lax.broadcasted_iota(jnp.int32, (GROUP, LANES), 0).astype(F32)

    @pl.loop(0, sub_ref.shape[1], unroll=8)
    def _(index):
        rows = pl.ds(pl.multiple_of(index * GROUP, GROUP), GROUP)
        one = pl.ds(index, 1)
        tok = tok_ref[rows, :]
        chosen = within == jnp.broadcast_to(sub_ref[0, one, :], (GROUP, LANES))
        put = jnp.broadcast_to(sub_ref[1, one, :], (GROUP, LANES))
        base_ref[rows, :] = jnp.where(chosen, put, tok)
        sub_ref[2, one, :] = jnp.sum(jnp.where(chosen, tok, 0.0), 0, keepdims=True)


def hot(ids, vocab):
    lane = lax.broadcasted_iota(jnp.int32, ids.shape, 1).astype(F32)
    parts = [
        (ids == lane + float(column * LANES)).astype(F32).astype(BF16)
        for column in range(vocab // LANES)
    ]
    return jnp.concatenate(parts, 1)


def vocab_kernel(
    ids_ref, embed_ref, skip_ref, filt_hbm,
    vocab_ref, own_ref, move_ref,
    tok_ref, base_ref, sub_ref, filt_ref, sem,
):
    length, share = filt_ref.shape
    filt_lanes = pl.ds(pl.multiple_of(lax.axis_index("path") * share, LANES), share)
    filt_copy = pltpu.make_async_copy(filt_hbm.at[:, filt_lanes], filt_ref, sem)
    filt_copy.start()
    vocab, width = embed_ref.shape

    @pl.loop(0, vocab // 16, unroll=4)
    def _(step):
        rows = pl.ds(pl.multiple_of(step * 16, 16), 16)
        total = jnp.zeros((16, LANES), F32)
        for column in range(width // LANES):
            value = embed_ref[rows, column * LANES : (column + 1) * LANES].astype(F32)
            total = total + value * value
        inv = lax.rsqrt(jnp.sum(total, 1, keepdims=True) / width + EPS)
        inv = jnp.broadcast_to(inv, (16, LANES))
        high = inv.astype(BF16).astype(F32)
        lane = lax.broadcasted_iota(jnp.int32, (16, LANES), 1)
        vocab_ref[rows, :] = jnp.where(lane < LANES // 2, high, inv - high).astype(BF16)

    spread_ids([ids_ref[...]], tok_ref, base_ref, sub_ref)
    own_width = own_ref.shape[2]
    lanes = pl.ds(pl.multiple_of(lax.axis_index("path") * own_width, LANES), own_width)
    own_ref[0] = dot(hot(tok_ref[...], vocab), embed_ref[:, lanes]).astype(BF16)
    own_ref[1] = dot(hot(base_ref[...], vocab), embed_ref[:, lanes]).astype(BF16)

    skip = skip_ref[:, filt_lanes]
    one = skip.astype(BF16).astype(F32)
    two = (skip - one).astype(BF16).astype(F32)
    three = skip - one - two
    rest = jnp.zeros((move_ref.shape[0] - length - 3, share), F32)
    move_ref[length:, :] = jnp.concatenate([one, two, three, rest], 0).astype(BF16)
    filt_copy.wait()
    move_ref[:length, :] = filt_ref[...].astype(BF16)


def tie_kernel(msg_ref, move_ref, out_ref):
    pass


def spectrum_kernel(move_ref, cos_ref, sin_ref, turn_ref, spec_ref):
    length = cos_ref.shape[0]
    turn = transposed(turn_ref[...])
    blocks = length // LANES
    for index in range(length // FREQ_ROWS):
        rows = pl.ds(index * FREQ_ROWS, FREQ_ROWS)
        real = dot(cos_ref[rows, :], move_ref[:length, :])
        imag = dot(sin_ref[rows, :], move_ref[:length, :])
        for part in range(FREQ_ROWS // LANES):
            block = index * (FREQ_ROWS // LANES) + part
            cosine = turn[:, block : block + 1] / length
            sine = turn[:, blocks + block : blocks + block + 1] / length
            here = slice(part * LANES, (part + 1) * LANES)
            into = pl.ds(block * LANES, LANES)
            spec_ref[0, into, :] = real[here] * cosine + imag[here] * sine
            spec_ref[1, into, :] = real[here] * sine - imag[here] * cosine


def transform(cos_ref, sin_ref, signal_ref, spec_ref, prod_ref, points, adjoint):
    length = cos_ref.shape[0]
    share = spec_ref.shape[2]
    for index in range(length // FREQ_ROWS):
        rows = pl.ds(index * FREQ_ROWS, FREQ_ROWS)
        after = pl.ds(length + index * FREQ_ROWS, FREQ_ROWS)
        real = dot(cos_ref[rows, :], signal_ref[...])
        imag = dot(sin_ref[rows, :], signal_ref[...])
        filt_real = spec_ref[0, rows, :]
        filt_imag = spec_ref[1, rows, :]
        for point in range(points):
            lanes = slice(point * share, (point + 1) * share)
            one, two = real[:, lanes], imag[:, lanes]
            if adjoint:
                prod_ref[rows, lanes] = (one * filt_real - two * filt_imag).astype(BF16)
                prod_ref[after, lanes] = (one * filt_imag + two * filt_real).astype(BF16)
            else:
                prod_ref[rows, lanes] = (one * filt_real + two * filt_imag).astype(BF16)
                prod_ref[after, lanes] = (two * filt_real - one * filt_imag).astype(BF16)


def inverse_rows(cos_ref, sin_ref, prod_ref, rows):
    length = cos_ref.shape[0]
    return dot(cos_ref[rows, :], prod_ref[:length, :]) + dot(sin_ref[rows, :], prod_ref[length:, :])


def skip_row(move_ref, length):
    rows = move_ref[length : length + 16, :].astype(F32)
    return rows[0:1] + rows[1:2] + rows[2:3]


def feature_kernel(
    points, msg_ref, embed_ref, vocab_ref, taps_ref, gain_ref,
    signal_ref, q_ref, k_ref, v_ref, inv_ref, pair_ref,
    tok_ref, base_ref, sub_ref, hot_ref, sums_ref, found_ref, here_ref, norm_ref,
):
    length = signal_ref.shape[0]
    vocab, width = embed_ref.shape
    share = pair_ref.shape[2]
    subs = sub_ref.shape[1]
    n_ctx = msg_ref.shape[0]
    first = (lax.axis_index("path") * n_ctx + lax.axis_index("ctx")) * share
    first = pl.multiple_of(first, LANES)
    spread_ids([msg_ref[block, LANES:, :].astype(F32) for block in range(n_ctx)], tok_ref, base_ref, sub_ref)
    within = lax.broadcasted_iota(jnp.int32, (GROUP, LANES), 0).astype(F32)
    for block in range(length // LANES):
        rows = slice(block * LANES, (block + 1) * LANES)
        hot_ref[0, rows, :] = hot(tok_ref[rows, :], vocab)
        hot_ref[1, rows, :] = hot(base_ref[rows, :], vocab)

    hot_tok = hot(sub_ref[2], vocab)
    hot_base = hot(sub_ref[1], vocab)
    alphas = [(point + 0.5) / points for point in range(points)]
    sums_ref[...] = jnp.zeros_like(sums_ref)
    wide = found_ref.shape[2]

    @pl.loop(0, width // wide)
    def _(step):
        lanes = pl.ds(pl.multiple_of(step * wide, wide), wide)
        found_ref[0] = dot(hot_tok, embed_ref[:, lanes])
        found_ref[1] = dot(hot_base, embed_ref[:, lanes])
        for block in range(subs // GROUP):
            rows = slice(block * GROUP, (block + 1) * GROUP)
            sums = [sums_ref[point, rows, :] for point in range(points)]
            for column in range(wide // LANES):
                cut = slice(column * LANES, (column + 1) * LANES)
                base = found_ref[1, rows, cut]
                diff = found_ref[0, rows, cut] - base
                for point in range(points):
                    value = base + alphas[point] * diff
                    sums[point] = sums[point] + value * value
            for point in range(points):
                sums_ref[point, rows, :] = sums[point]

    for point in range(points):
        mean = jnp.sum(sums_ref[point], 1, keepdims=True) / width
        sums_ref[point] = jnp.broadcast_to(lax.rsqrt(mean + EPS), (subs, LANES))

    mine = embed_ref[:, pl.ds(first, share)]
    looked = dot(hot_ref[0], jnp.concatenate([mine, vocab_ref[...]], 1))
    here_ref[0] = looked[:, :share]
    spread = looked[:, share:]
    here_ref[2] = spread + pltpu.roll(spread, LANES // 2, 1)
    here_ref[1] = dot(hot_ref[1], mine)
    pair_ref[0] = here_ref[0].astype(BF16)
    pair_ref[1] = here_ref[1].astype(BF16)

    norm_ref[:GROUP, :] = jnp.zeros((GROUP, points * share), F32)
    gain = gain_ref[:, pl.ds(first, share)]
    taps = [taps_ref[f, :, pl.ds(first, share)].astype(F32) for f in range(3)]

    @pl.loop(0, length // CHUNK)
    def _(step):
        start = pl.multiple_of(step * CHUNK, CHUNK)
        rows = pl.ds(start, CHUNK)
        base = here_ref[1, rows, :]
        diff = here_ref[0, rows, :] - base
        inv_tok = here_ref[2, rows, :]
        groups = CHUNK // GROUP
        chosen = []
        for group in range(groups):
            index = step * groups + group
            place = jnp.broadcast_to(sub_ref[0, pl.ds(index, 1), :], (GROUP, LANES))
            chosen.append(within == place)
        for point in range(points):
            lanes = slice(point * share, (point + 1) * share)
            inv = jnp.concatenate(
                [
                    jnp.where(
                        chosen[group],
                        jnp.broadcast_to(
                            sums_ref[point, pl.ds(step * groups + group, 1), :], (GROUP, LANES)
                        ),
                        inv_tok[group * GROUP : (group + 1) * GROUP],
                    )
                    for group in range(groups)
                ],
                0,
            )
            inv_ref[rows, lanes] = inv
            now = rounded((base + alphas[point] * diff) * inv * gain)
            norm_ref[pl.ds(start + GROUP, CHUNK), lanes] = now
            window = norm_ref[pl.ds(start, CHUNK + GROUP), lanes]
            back1 = window[GROUP - 1 : GROUP - 1 + CHUNK]
            back2 = window[GROUP - 2 : GROUP - 2 + CHUNK]
            feats = [
                taps[f][0:1] * now + taps[f][1:2] * back1 + taps[f][2:3] * back2 for f in range(3)
            ]
            q_ref[rows, lanes] = feats[0]
            k_ref[rows, lanes] = feats[1]
            v_ref[rows, lanes] = feats[2]
            signal_ref[rows, lanes] = (feats[1] * feats[2]).astype(BF16)


def forward_kernel(points, signal_ref, move_ref, cos_ref, sin_ref, spec_ref, conv_ref, prod_ref):
    length = cos_ref.shape[0]
    transform(cos_ref, sin_ref, signal_ref, spec_ref, prod_ref, points, False)
    skip = jnp.concatenate([skip_row(move_ref, length)] * points, 1)
    for index in range(length // FREQ_ROWS):
        rows = pl.ds(index * FREQ_ROWS, FREQ_ROWS)
        result = inverse_rows(cos_ref, sin_ref, prod_ref, rows)
        conv_ref[rows, :] = (result + skip * signal_ref[rows, :].astype(F32)).astype(BF16)


def backward_kernel(
    points, width, msg_ref, move_ref, pair_ref, taps_ref, gain_ref,
    q_ref, k_ref, v_ref, inv_ref, conv_ref, cos_ref, sin_ref, spec_ref,
    grad_ref,
    signal_ref, prod_ref, tap0_ref, tap1_ref, tap2_ref,
):
    length = cos_ref.shape[0]
    share = pair_ref.shape[2]
    n_ctx = msg_ref.shape[0]
    first = (lax.axis_index("path") * n_ctx + lax.axis_index("ctx")) * share
    first = pl.multiple_of(first, LANES)

    @pl.loop(0, n_ctx)
    def _(block):
        for part in range(LANES // CHUNK):
            rows = pl.ds(pl.multiple_of(block * LANES + part * CHUNK, CHUNK), CHUNK)
            upstream = msg_ref[block, part * CHUNK : (part + 1) * CHUNK, :].astype(F32)
            for point in range(points):
                lanes = slice(point * share, (point + 1) * share)
                signal_ref[rows, lanes] = (upstream * q_ref[rows, lanes]).astype(BF16)

    transform(cos_ref, sin_ref, signal_ref, spec_ref, prod_ref, points, True)
    skip = skip_row(move_ref, length)
    gain = gain_ref[:, pl.ds(first, share)]
    taps = [taps_ref[f, :, pl.ds(first, share)].astype(F32) for f in range(3)]
    taps_refs = (tap0_ref, tap1_ref, tap2_ref)
    for ref in taps_refs:
        ref[length:, :] = jnp.zeros((GROUP, points * share), F32)
    for index in range(length // FREQ_ROWS):
        rows = pl.ds(index * FREQ_ROWS, FREQ_ROWS)
        result = inverse_rows(cos_ref, sin_ref, prod_ref, rows)
        for part in range(FREQ_ROWS // CHUNK):
            start = index * FREQ_ROWS + part * CHUNK
            rows = pl.ds(start, CHUNK)
            inside = start % LANES
            upstream = msg_ref[start // LANES, inside : inside + CHUNK, :].astype(F32)
            for point in range(points):
                lanes = slice(point * share, (point + 1) * share)
                grad_z = rounded(
                    result[part * CHUNK : (part + 1) * CHUNK, lanes]
                    + skip * signal_ref[rows, lanes].astype(F32)
                )
                grads = (
                    rounded(upstream * conv_ref[rows, lanes].astype(F32)),
                    rounded(grad_z * v_ref[rows, lanes]),
                    rounded(grad_z * k_ref[rows, lanes]),
                )
                for tap, ref in enumerate(taps_refs):
                    ref[rows, lanes] = sum(taps[f][tap : tap + 1] * grads[f] for f in range(3))

    alphas = [(point + 0.5) / points for point in range(points)]
    ones = jnp.ones((GROUP, share), F32)

    @pl.loop(0, length // LANES)
    def _(step):
        to_tok, to_base = [], []
        for part in range(LANES // CHUNK):
            start = pl.multiple_of(step * LANES + part * CHUNK, CHUNK)
            rows = pl.ds(start, CHUNK)
            tok = pair_ref[0, rows, :].astype(F32)
            base = pair_ref[1, rows, :].astype(F32)
            diff = tok - base
            total = jnp.zeros((CHUNK, share), F32)
            sum_tok = jnp.zeros((CHUNK, share), F32)
            sum_base = jnp.zeros((CHUNK, share), F32)
            for point in range(points):
                lanes = slice(point * share, (point + 1) * share)
                scaled = gain * (
                    tap0_ref[rows, lanes]
                    + tap1_ref[pl.ds(start, CHUNK + GROUP), lanes][1 : 1 + CHUNK]
                    + tap2_ref[pl.ds(start, CHUNK + GROUP), lanes][2 : 2 + CHUNK]
                )
                inv = inv_ref[rows, lanes]
                along = inv * scaled
                total = total + along
                along = along * (base + alphas[point] * diff) * (inv * inv)
                sum_tok = sum_tok + alphas[point] * along
                sum_base = sum_base + (1.0 - alphas[point]) * along
            grad_ref[step, part * CHUNK : (part + 1) * CHUNK, :] = total.astype(BF16)
            to_tok.append(sum_tok)
            to_base.append(sum_base)
        sent = []
        for sums in (to_tok, to_base):
            row = lax.dot_general(
                ones,
                jnp.concatenate(sums, 0),
                (((1,), (1,)), ((), ())),
                precision=lax.Precision.HIGHEST,
                preferred_element_type=F32,
            )
            row = row[:1] / width
            high = row.astype(BF16).astype(F32)
            sent += [high, row - high]
        sent.append(jnp.zeros((grad_ref.shape[1] - LANES - len(sent), LANES), F32))
        grad_ref[step, LANES:, :] = jnp.concatenate(sent, 0).astype(BF16)


def partial_kernel(grad_ref, part_ref):
    dests, rows, lanes = part_ref.shape
    spare = sum(grad_ref[block, LANES:, :].astype(F32) for block in range(grad_ref.shape[0]))
    sums = [spare[0:1] + spare[1:2], spare[2:3] + spare[3:4], jnp.zeros((rows - 2, lanes), F32)]
    for dest in range(dests):
        part_ref[dest] = jnp.concatenate(sums, 0)


def finish_kernel(points, grad_ref, part_ref, own_ref, path_ref, attr_ref):
    pieces, _, share = grad_ref.shape
    rows = path_ref.shape[0]
    sums = jnp.sum(part_ref[...], 0)
    columns = transposed(sums)
    to_tok = columns[:, 0:1]
    to_base = columns[:, 1:2]
    for piece in range(pieces):
        lanes = slice(piece * share, (piece + 1) * share)
        tok = own_ref[0, :, lanes].astype(F32)
        base = own_ref[1, :, lanes].astype(F32)
        grad = grad_ref[piece, :rows, :].astype(F32) - tok * to_tok - base * to_base
        grad = grad / points
        path_ref[:, lanes] = grad
        attr_ref[:, lanes] = (tok - base) * grad


def any_spec():
    return pl.BlockSpec(memory_space=pl.ANY)


def vmem_spec():
    return pl.BlockSpec(memory_space=pltpu.VMEM)


def hbm_spec():
    return pl.BlockSpec(memory_space=pltpu.HBM)


def call(kernel, ins, outs, scratch, flops, moved, mebibytes):
    return pl.pallas_call(
        kernel,
        in_specs=ins,
        out_specs=[spec for spec, _ in outs],
        out_shape=[shape for _, shape in outs],
        scratch_shapes=scratch,
        compiler_params=pltpu.CompilerParams(vmem_limit_bytes=mebibytes * 2**20),
        cost_estimate=pl.CostEstimate(flops=flops, bytes_accessed=moved, transcendentals=0),
    )


def shape(dims, dtype):
    return jax.ShapeDtypeStruct(dims, dtype)


def kernel_body(tokens, sub_pos, sub_base, embed, norm_gain, fir_taps, long_filter, skip_gain, cotangent):
    n_path, n_ctx = lax.axis_size("path"), lax.axis_size("ctx")
    points = n_path
    tok_rows = tokens.shape[0]
    length = tok_rows * n_ctx
    vocab, width = embed.shape
    share = width // (n_path * n_ctx)
    subs = sub_pos.shape[0] * n_ctx
    own_width = width // n_path
    cols = points * share
    cosine, sine, turn = dft_tables(length)

    dma = pltpu.SemaphoreType.DMA
    transform_flops = 4 * length * length
    spare = 16

    msg, ids = call(
        pack_kernel,
        [hbm_spec()] * 4,
        [
            (vmem_spec(), shape((n_ctx, tok_rows + spare, share), BF16)),
            (vmem_spec(), shape((spare, LANES), F32)),
        ],
        [
            pltpu.VMEM((1, tok_rows), jnp.int32),
            pltpu.VMEM((1, sub_pos.shape[0]), jnp.int32),
            pltpu.VMEM((1, sub_pos.shape[0]), jnp.int32),
            dma((n_ctx + 3,)),
        ],
        length * share,
        8 * length * share,
        4,
    )(
        tokens.reshape(1, tok_rows),
        sub_pos.reshape(1, -1),
        sub_base.reshape(1, -1),
        cotangent,
    )
    msg = lax.all_to_all(msg, "ctx", 0, 0, tiled=True)

    gain = norm_gain.reshape(1, width)
    vocab_inv, own, move = call(
        vocab_kernel,
        [vmem_spec()] * 3 + [hbm_spec()],
        [
            (vmem_spec(), shape((vocab, LANES), BF16)),
            (vmem_spec(), shape((2, tok_rows, own_width), BF16)),
            (vmem_spec(), shape((length + spare, share), BF16)),
        ],
        [
            pltpu.VMEM((LANES, LANES), F32),
            pltpu.VMEM((LANES, LANES), F32),
            pltpu.VMEM((3, sub_pos.shape[0], LANES), F32),
            pltpu.VMEM((length, share), F32),
            dma,
        ],
        4 * tok_rows * vocab * own_width,
        2 * vocab * width,
        12,
    )(ids, embed, skip_gain.reshape(1, n_path * share), long_filter)

    move = pl.pallas_call(
        tie_kernel,
        in_specs=[any_spec()] * 2,
        out_specs=any_spec(),
        out_shape=shape(move.shape, BF16),
        input_output_aliases={1: 0},
    )(msg, move)
    route = [(p * n_ctx + c, c * n_path + p) for p in range(n_path) for c in range(n_ctx)]
    move = lax.ppermute(move, ("path", "ctx"), route)

    wide = 4 * LANES
    signal, q_feat, k_feat, v_feat, inv, pair = call(
        functools.partial(feature_kernel, points),
        [vmem_spec()] * 5,
        [(vmem_spec(), shape((length, cols), BF16))]
        + [(vmem_spec(), shape((length, cols), F32))] * 4
        + [(vmem_spec(), shape((2, length, share), BF16))],
        [
            pltpu.VMEM((length, LANES), F32),
            pltpu.VMEM((length, LANES), F32),
            pltpu.VMEM((3, subs, LANES), F32),
            pltpu.VMEM((2, length, vocab), BF16),
            pltpu.VMEM((points, subs, LANES), F32),
            pltpu.VMEM((2, subs, wide), F32),
            pltpu.VMEM((3, length, share), F32),
            pltpu.VMEM((GROUP + length, cols), F32),
        ],
        2 * length * vocab * 3 * share,
        2 * vocab * width + 16 * length * cols,
        16,
    )(msg, embed, vocab_inv, fir_taps, gain)
    spec = call(
        spectrum_kernel,
        [vmem_spec()] * 4,
        [(vmem_spec(), shape((2, length, share), F32))],
        [],
        transform_flops * share,
        4 * length * length,
        8,
    )(move, cosine, sine, turn)[0]
    conv = call(
        functools.partial(forward_kernel, points),
        [vmem_spec()] * 5,
        [(vmem_spec(), shape((length, cols), BF16))],
        [pltpu.VMEM((2 * length, cols), BF16)],
        2 * transform_flops * cols,
        4 * length * length,
        10,
    )(signal, move, cosine, sine, spec)[0]

    grad = call(
        functools.partial(backward_kernel, points, width),
        [vmem_spec()] * 13,
        [(vmem_spec(), shape((n_ctx, tok_rows + spare, share), BF16))],
        [
            pltpu.VMEM((length, cols), BF16),
            pltpu.VMEM((2 * length, cols), BF16),
        ]
        + [pltpu.VMEM((length + GROUP, cols), F32)] * 3,
        2 * transform_flops * cols,
        4 * length * length + 16 * length * cols,
        16,
    )(msg, move, pair, fir_taps, gain, q_feat, k_feat, v_feat, inv, conv, cosine, sine, spec)[0]

    grad = lax.all_to_all(grad, "ctx", 0, 0, tiled=True)
    part = call(
        partial_kernel,
        [vmem_spec()],
        [(vmem_spec(), shape((n_path, GROUP, LANES), F32))],
        [],
        spare * LANES * n_ctx,
        2 * spare * LANES * n_ctx,
        4,
    )(grad)[0]
    part = lax.all_to_all(part, "path", 0, 0, tiled=True)
    out = shape((tok_rows, own_width), F32)
    return tuple(
        call(
            functools.partial(finish_kernel, points),
            [vmem_spec()] * 3,
            [(vmem_spec(), out), (vmem_spec(), out)],
            [],
            8 * tok_rows * own_width,
            14 * tok_rows * own_width,
            8,
        )(grad, part, own)
    )


def plain_body(tokens, sub_pos, sub_base, embed, norm_gain, fir_taps, long_filter, skip_gain, cotangent):
    n_path, n_ctx = lax.axis_size("path"), lax.axis_size("ctx")
    path, ctx = lax.axis_index("path"), lax.axis_index("ctx")
    points = n_path
    tok_rows = tokens.shape[0]
    length = tok_rows * n_ctx
    width = embed.shape[1]
    share = width // (n_path * n_ctx)
    own_width = width // n_path
    first = (ctx * n_path + path) * share
    alphas = ((jnp.arange(points, dtype=jnp.int32)).astype(F32) + 0.5) / points
    alphas = alphas[:, None, None]

    local = jnp.arange(tok_rows, dtype=jnp.int32)[:, None] + ctx * tok_rows == sub_pos[None, :]
    put = jnp.sum(jnp.where(local, sub_base[None, :], 0), 1)
    base_ids = jnp.where(jnp.any(local, 1), put, tokens)
    rows_tok = jnp.take(embed, tokens, axis=0).astype(F32)
    rows_base = jnp.take(embed, base_ids, axis=0).astype(F32)
    rows_in = rows_base[None] + alphas * (rows_tok - rows_base)[None]
    inv = lax.rsqrt(jnp.mean(rows_in * rows_in, -1) + EPS)
    inv = lax.all_gather(inv, "ctx", axis=1, tiled=True)[:, :, None]
    all_tok = lax.all_gather(tokens, "ctx", tiled=True)
    all_base = lax.all_gather(base_ids, "ctx", tiled=True)

    cot = cotangent.reshape(tok_rows, n_ctx, n_path, share)
    cot = lax.dynamic_index_in_dim(cot, path, 2, keepdims=False)
    cot = lax.all_to_all(cot.transpose(1, 0, 2), "ctx", 0, 0, tiled=True)
    upstream = cot.reshape(1, length, share).astype(F32)
    mine = lax.dynamic_slice_in_dim(embed, first, share, 1)
    gain = lax.dynamic_slice_in_dim(norm_gain, first, share, 0)
    taps = lax.dynamic_slice_in_dim(fir_taps, first, share, 2).astype(F32)
    filt = lax.dynamic_slice_in_dim(long_filter, path * share, share, 1)
    skip = lax.dynamic_slice_in_dim(skip_gain, path * share, share, 0)

    emb_tok = jnp.take(mine, all_tok, axis=0).astype(F32)
    emb_base = jnp.take(mine, all_base, axis=0).astype(F32)
    inputs = emb_base[None] + alphas * (emb_tok - emb_base)[None]
    normed = rounded(inputs * inv * gain)
    q_feat, k_feat, v_feat = (
        taps[f, 0] * normed + taps[f, 1] * shifted(normed, 1) + taps[f, 2] * shifted(normed, 2)
        for f in range(3)
    )
    filter_spec = spectrum(filt[None])
    conv = rounded(long_conv(rounded(k_feat * v_feat), filter_spec, skip, False))
    grad_z = rounded(long_conv(rounded(upstream * q_feat), filter_spec, skip, True))
    grads = (rounded(upstream * conv), rounded(grad_z * v_feat), rounded(grad_z * k_feat))
    by_tap = [sum(taps[f, tap] * grads[f] for f in range(3)) for tap in range(3)]
    scaled = gain * (by_tap[0] + shifted(by_tap[1], -1) + shifted(by_tap[2], -2))
    grad = jnp.sum(inv * scaled, 0).astype(BF16)
    along = jnp.sum(inputs * scaled, -1, keepdims=True) * inv**3 / width
    part = jnp.stack([jnp.sum(alphas * along, 0)[:, 0], jnp.sum((1.0 - alphas) * along, 0)[:, 0]])
    part = lax.psum(part, ("path", "ctx"))
    part = lax.dynamic_slice_in_dim(part, ctx * tok_rows, tok_rows, 1)

    back = lax.all_to_all(grad.reshape(n_ctx, tok_rows, share), "ctx", 0, 0, tiled=True)
    back = back.reshape(n_path, n_ctx // n_path, tok_rows, share)
    back = lax.all_to_all(back, "path", 0, 0, tiled=True).astype(F32)
    back = back.transpose(2, 1, 0, 3).reshape(tok_rows, own_width)
    own_tok = lax.dynamic_slice_in_dim(rows_tok, path * own_width, own_width, 1)
    own_base = lax.dynamic_slice_in_dim(rows_base, path * own_width, own_width, 1)
    grad = (back - own_tok * part[0][:, None] - own_base * part[1][:, None]) / points
    return (grad, (own_tok - own_base) * grad)


def body(tokens, sub_pos, sub_base, embed, *rest):
    n_path, n_ctx = lax.axis_size("path"), lax.axis_size("ctx")
    tok_rows = tokens.shape[0]
    share = embed.shape[1] // (n_path * n_ctx)
    tables = 4 * (tok_rows * n_ctx) ** 2
    fits = share == LANES and tok_rows == LANES and tables <= TABLE_BYTES
    chosen = kernel_body if fits else plain_body
    return chosen(tokens, sub_pos, sub_base, embed, *rest)


def solution(mesh):
    return jax.shard_map(
        body,
        mesh=mesh,
        in_specs=(
            P("ctx"),
            P("ctx"),
            P("ctx"),
            P(),
            P(),
            P(),
            P(None, "ctx"),
            P("ctx"),
            P("ctx", None),
        ),
        out_specs=(P("ctx", "path"), P("ctx", "path")),
        check_vma=False,
    )
```

```python
import functools

import jax
import jax.numpy as jnp
import ml_dtypes
import numpy as np
from jax import lax
from jax.experimental import pallas as pl
from jax.experimental.pallas import tpu as pltpu
from jax.sharding import PartitionSpec as P

LANES = 128
GROUP = 8
FREQ_ROWS = 256
CHUNK = 32
EPS = 1e-06
TABLE_BYTES = 4 * 2**20
F32 = jnp.float32
BF16 = jnp.bfloat16
precise = lax.Precision.HIGH


def angle_tables(length):
    outer_size = 64
    inner_size = length // outer_size
    outer_idx = jnp.arange(outer_size, dtype=jnp.int32)
    inner_idx = jnp.arange(inner_size, dtype=jnp.int32)
    outer_angle = (
        2.0 * jnp.pi / outer_size
        * (outer_idx[:, None] * outer_idx[None, :] % outer_size).astype(F32)
    )
    inner_angle = (
        2.0 * jnp.pi / inner_size
        * (inner_idx[:, None] * inner_idx[None, :] % inner_size).astype(F32)
    )
    twist_angle = (
        2.0 * jnp.pi / length
        * (outer_idx[:, None] * inner_idx[None, :] % length).astype(F32)
    )
    return (outer_angle, inner_angle, twist_angle)


def complex_table(angle, sign):
    cosine = jnp.cos(angle)
    sine = sign * jnp.sin(angle)
    return jnp.stack([jnp.stack([cosine, sine]), jnp.stack([-sine, cosine])])


def twisted(values, angle, sign):
    cosine = jnp.cos(angle)[None, :, :, None]
    sine = sign * jnp.sin(angle)[None, :, :, None]
    real_part = values[:, 0]
    imag_part = values[:, 1]
    return jnp.stack(
        [real_part * cosine - imag_part * sine, real_part * sine + imag_part * cosine], 1
    )


def spectrum(signal):
    batch, half, width = signal.shape
    length = 2 * half
    outer_angle, inner_angle, twist_angle = angle_tables(length)
    outer_size = outer_angle.shape[0]
    inner_size = inner_angle.shape[0]
    folded = signal.reshape(batch, outer_size // 2, inner_size, width)
    used = outer_angle[:, : outer_size // 2]
    outer_table = jnp.stack([jnp.cos(used), -jnp.sin(used)])
    first = jnp.einsum("rka,pabc->prkbc", outer_table, folded, precision=precise)
    turned = twisted(first, twist_angle, -1.0)
    return jnp.einsum(
        "prkbc,rsbm->pskmc", turned, complex_table(inner_angle, -1.0), precision=precise
    )


def inverse(spec):
    batch, parts, outer_size, inner_size, width = spec.shape
    length = outer_size * inner_size
    outer_angle, inner_angle, twist_angle = angle_tables(length)
    back = jnp.einsum("pskmc,stmb->ptkbc", spec, complex_table(inner_angle, 1.0), precision=precise)
    turned = twisted(back, twist_angle, 1.0)
    used = outer_angle[: outer_size // 2]
    outer_table = jnp.stack([jnp.cos(used), -jnp.sin(used)])
    result = jnp.einsum("rak,prkbc->pabc", outer_table, turned, precision=precise)
    return (result / length).reshape(batch, length // 2, width)


def long_conv(signal, filter_spec, skip_gain, adjoint):
    spec = spectrum(signal)
    sig_real = spec[:, 0]
    sig_imag = spec[:, 1]
    filt_real = filter_spec[:, 0]
    filt_imag = filter_spec[:, 1]
    if adjoint:
        prod_real = sig_real * filt_real + sig_imag * filt_imag
        prod_imag = sig_imag * filt_real - sig_real * filt_imag
    else:
        prod_real = sig_real * filt_real - sig_imag * filt_imag
        prod_imag = sig_real * filt_imag + sig_imag * filt_real
    return inverse(jnp.stack([prod_real, prod_imag], 1)) + skip_gain * signal


def rounded(value):
    return value.astype(BF16).astype(F32)


def shifted(values, step):
    zeros = jnp.zeros_like(values[:, : abs(step)])
    if step > 0:
        return jnp.concatenate([zeros, values[:, :-step]], 1)
    return jnp.concatenate([values[:, -step:], zeros], 1)


@functools.lru_cache(maxsize=None)
def dft_tables(length):
    half = length // 2
    freq = 4 * np.arange(half, dtype=np.int64) + 1
    place = np.arange(half, dtype=np.int64)
    tables = []
    for offset in (0, 1):
        turns = freq[:, None] * (2 * place + offset)[None, :] % (8 * half)
        angle = turns * (2.0 * np.pi / (8 * half))
        cosine = np.cos(angle).astype(ml_dtypes.bfloat16)
        sine = np.sin(angle).astype(ml_dtypes.bfloat16)
        tables.append((np.concatenate([cosine, sine], 0), np.concatenate([cosine.T, sine.T], 1)))
    return (tables[0][0], tables[1][0], tables[0][1], tables[1][1])


def transposed(rows):
    count = rows.shape[0]
    if count < LANES:
        rows = jnp.concatenate([rows, jnp.zeros((LANES - count, LANES), F32)], 0)
    return rows.T


def dot(left, right):
    return jnp.dot(left, right, preferred_element_type=F32)


def exact_dot(left, right, dims):
    return lax.dot_general(
        left, right, (dims, ((), ())), precision=lax.Precision.HIGHEST, preferred_element_type=F32
    )


def iota(dims, axis):
    return lax.broadcasted_iota(jnp.int32, dims, axis)


def even_first():
    row = iota((LANES, LANES), 0)
    half = LANES // 2
    source = jnp.where(row < half, 2 * row, 2 * (row - half) + 1)
    return (iota((LANES, LANES), 1) == source).astype(F32)


def hot(ids, vocab):
    lane = iota(ids.shape, 1).astype(F32)
    parts = [
        (ids == lane + float(column * LANES)).astype(F32).astype(BF16)
        for column in range(vocab // LANES)
    ]
    return jnp.concatenate(parts, 1)


def joined(block, kind):
    return 256.0 * block[2 * kind : 2 * kind + 1] + block[2 * kind + 1 : 2 * kind + 2]


def pack_kernel(
    tok_hbm, pos_hbm, put_hbm, cot_hbm, msg_ref, ids_ref, tok_ref, pos_ref, put_ref, cot_ref, sems
):
    dests, rows, share = msg_ref.shape
    tok_rows = cot_hbm.shape[0]
    n_path = cot_hbm.shape[1] // (dests * share)
    path = lax.axis_index("path")
    moves = [(tok_hbm, tok_ref), (pos_hbm, pos_ref), (put_hbm, put_ref)]
    for dest in range(dests):
        lanes = pl.ds(pl.multiple_of((dest * n_path + path) * share, LANES), share)
        moves.append((cot_hbm.at[:, lanes], cot_ref.at[dest]))
    copies = [
        pltpu.make_async_copy(source, target, sems.at[index])
        for index, (source, target) in enumerate(moves)
    ]
    for copy in copies:
        copy.start()
    order = even_first()
    for copy in copies[:3]:
        copy.wait()
    lists = []
    for ref in (tok_ref, pos_ref, put_ref):
        value = ref[...].astype(F32)
        if value.shape[1] < LANES:
            value = jnp.concatenate([value, jnp.zeros((1, LANES - value.shape[1]), F32)], 1)
        high = jnp.floor(value * (1.0 / 256.0))
        lists += [high, value - 256.0 * high]
    lists.append(jnp.zeros((rows - tok_rows - len(lists), LANES), F32))
    ids = jnp.concatenate(lists, 0)
    ids_ref[...] = ids
    turned = exact_dot(ids, order, ((1,), (1,)))
    ids = jnp.where(iota(ids.shape, 0) < 2, turned, ids).astype(BF16)
    order = order.astype(BF16)
    for dest in range(dests):
        msg_ref[dest, tok_rows:, :] = ids
        copies[3 + dest].wait()
        msg_ref[dest, :tok_rows, :] = dot(order, cot_ref[dest]).astype(BF16)


def vocab_kernel(ids_ref, embed_ref, vocab_ref, own_ref):
    vocab, width = embed_ref.shape

    @pl.loop(0, vocab // 16, unroll=4)
    def _(step):
        rows = pl.ds(pl.multiple_of(step * 16, 16), 16)
        total = jnp.zeros((16, LANES), F32)
        for column in range(width // LANES):
            value = embed_ref[rows, column * LANES : (column + 1) * LANES].astype(F32)
            total = total + value * value
        inv = lax.rsqrt(jnp.sum(total, 1, keepdims=True) / width + EPS)
        inv = jnp.broadcast_to(inv, (16, LANES))
        high = inv.astype(BF16).astype(F32)
        vocab_ref[rows, :] = jnp.where(iota((16, LANES), 1) < LANES // 2, high, inv - high).astype(BF16)

    ids = ids_ref[...]
    columns = transposed(jnp.concatenate([joined(ids, kind) for kind in range(3)], 0))
    tok = jnp.broadcast_to(columns[:, 0:1], (LANES, LANES))
    place = jnp.broadcast_to(joined(ids, 1), (LANES, LANES))
    put = jnp.broadcast_to(joined(ids, 2), (LANES, LANES))
    first = lax.axis_index("ctx") * LANES
    subs = LANES // GROUP
    here = (place == (iota((LANES, LANES), 0) + first).astype(F32)) & (iota((LANES, LANES), 1) < subs)
    found = jnp.max(jnp.where(here, put, -1.0), 1, keepdims=True)
    base = jnp.where(found >= 0.0, found, tok)
    own_width = own_ref.shape[2]
    lanes = pl.ds(pl.multiple_of(lax.axis_index("path") * own_width, LANES), own_width)
    own_ref[0] = dot(hot(tok, vocab), embed_ref[:, lanes]).astype(BF16)
    own_ref[1] = dot(hot(base, vocab), embed_ref[:, lanes]).astype(BF16)


def spectrum_kernel(filt_hbm, even_ref, odd_ref, spec_ref, filt_ref, sem):
    length, share = filt_ref.shape
    half = length // 2
    lanes = pl.ds(pl.multiple_of(lax.axis_index("path") * share, LANES), share)
    copy = pltpu.make_async_copy(filt_hbm.at[:, lanes], filt_ref, sem)
    copy.start()
    copy.wait()
    parts = []
    for offset in range(2):
        value = filt_ref[pl.ds(offset, half, stride=2), :] * (1.0 / length)
        high = value.astype(BF16)
        parts.append(jnp.concatenate([high, (value - high.astype(F32)).astype(BF16)], 1))
    for index in range(half // FREQ_ROWS):
        found = []
        for table, part in ((even_ref, parts[0]), (odd_ref, parts[1])):
            for offset in (0, half):
                both = dot(table[pl.ds(offset + index * FREQ_ROWS, FREQ_ROWS), :], part)
                found.append(both[:, :share] + both[:, share:])
        rows = pl.ds(index * FREQ_ROWS, FREQ_ROWS)
        spec_ref[0, rows, :] = found[0] + found[2]
        spec_ref[1, rows, :] = -found[1] - found[3]
        spec_ref[2, rows, :] = found[0] - found[2]
        spec_ref[3, rows, :] = found[3] - found[1]


def transform(even_ref, odd_ref, signal_ref, spec_ref, prod_ref, points, adjoint):
    half = even_ref.shape[1]
    share = spec_ref.shape[2]
    for index in range(half // FREQ_ROWS):
        rows = pl.ds(index * FREQ_ROWS, FREQ_ROWS)
        after = pl.ds(half + index * FREQ_ROWS, FREQ_ROWS)
        even_real = dot(even_ref[rows, :], signal_ref[:half, :])
        even_imag = dot(even_ref[after, :], signal_ref[:half, :])
        odd_real = dot(odd_ref[rows, :], signal_ref[half:, :])
        odd_imag = dot(odd_ref[after, :], signal_ref[half:, :])
        filt = [spec_ref[part, rows, :] for part in range(4)]
        for point in range(points):
            lanes = slice(point * share, (point + 1) * share)
            prods = []
            for part, sign in ((0, 1.0), (2, -1.0)):
                real = even_real[:, lanes] + sign * odd_real[:, lanes]
                imag = even_imag[:, lanes] + sign * odd_imag[:, lanes]
                if adjoint:
                    prods.append(real * filt[part] - imag * filt[part + 1])
                    prods.append(real * filt[part + 1] + imag * filt[part])
                else:
                    prods.append(real * filt[part] + imag * filt[part + 1])
                    prods.append(imag * filt[part] - real * filt[part + 1])
            sums = (prods[0] + prods[2], prods[1] + prods[3], prods[0] - prods[2], prods[1] - prods[3])
            for part, value in enumerate(sums):
                into = pl.ds(part * half + index * FREQ_ROWS, FREQ_ROWS)
                prod_ref[into, lanes] = value.astype(BF16)


def inverse_rows(back_refs, prod_ref, rows):
    length = 2 * back_refs[0].shape[0]
    return [
        dot(ref[rows, :], prod_ref[offset : offset + length, :])
        for ref, offset in zip(back_refs, (0, length))
    ]


def feature_kernel(
    points, msg_ref, embed_ref, vocab_ref, taps_ref, gain_ref,
    signal_ref, q_ref, k_ref, v_ref, inv_ref, pair_ref,
    hot_ref, sums_ref, found_ref, look_ref, subs_ref, norm_ref,
):
    length = signal_ref.shape[0]
    half = length // 2
    vocab, width = embed_ref.shape
    share = pair_ref.shape[2]
    n_ctx = msg_ref.shape[0]
    block_half = LANES // 2
    per_block = LANES // GROUP
    subs = n_ctx * per_block
    n_path = points
    first = (lax.axis_index("ctx") * n_path + lax.axis_index("path")) * share
    first = pl.multiple_of(first, LANES)

    blocks = [msg_ref[block, LANES:, :].astype(F32) for block in range(n_ctx)]
    toks = transposed(jnp.concatenate([joined(block, 0) for block in blocks], 0))
    for block in range(n_ctx):
        column = jnp.broadcast_to(toks[:, block : block + 1], (LANES, LANES))
        rows = hot(column, vocab)
        hot_ref[block * block_half : (block + 1) * block_half, :] = rows[:block_half]
        hot_ref[half + block * block_half : half + (block + 1) * block_half, :] = rows[block_half:]
    spread = sum(
        blocks[block] if block == 0 else pltpu.roll(blocks[block], block * per_block, 1)
        for block in range(n_ctx)
    )
    place = joined(spread, 1)
    put = joined(spread, 2)
    back = jnp.floor(place * 0.5)
    place = back + (place - 2.0 * back) * half
    columns = transposed(jnp.concatenate([place, put], 0))
    hot_base = hot(jnp.broadcast_to(columns[:, 1:2], (subs, LANES)), vocab)
    pick = jnp.concatenate(
        [
            (columns[:, 0:1] == (iota((subs, LANES), 1) + part * LANES).astype(F32)).astype(F32).astype(BF16)
            for part in range(length // LANES)
        ],
        1,
    )
    hot_tok = dot(pick, hot_ref[...]).astype(BF16)

    alphas = [(point + 0.5) / points for point in range(points)]
    sums_ref[...] = jnp.zeros_like(sums_ref)
    wide = found_ref.shape[2]

    @pl.loop(0, width // wide)
    def _(step):
        lanes = pl.ds(pl.multiple_of(step * wide, wide), wide)
        found_ref[0] = dot(hot_tok, embed_ref[:, lanes])
        found_ref[1] = dot(hot_base, embed_ref[:, lanes])
        for block in range(subs // GROUP):
            rows = slice(block * GROUP, (block + 1) * GROUP)
            sums = [sums_ref[point, rows, :] for point in range(points)]
            for column in range(wide // LANES):
                cut = slice(column * LANES, (column + 1) * LANES)
                base = found_ref[1, rows, cut]
                diff = found_ref[0, rows, cut] - base
                for point in range(points):
                    value = base + alphas[point] * diff
                    sums[point] = sums[point] + value * value
            for point in range(points):
                sums_ref[point, rows, :] = sums[point]

    mine = embed_ref[:, pl.ds(first, share)]
    high = [dot(hot_base, mine), jnp.ones((subs, LANES), F32)]
    low = [jnp.zeros((subs, LANES), F32)] * 2
    for point in range(points):
        mean = jnp.sum(sums_ref[point], 1, keepdims=True) / width
        inv = jnp.broadcast_to(lax.rsqrt(mean + EPS), (subs, LANES))
        high.append(inv.astype(BF16).astype(F32))
        low.append(inv - high[-1])
    held = jnp.concatenate([jnp.concatenate(high, 1), jnp.concatenate(low, 1)], 0).astype(BF16)
    table = jnp.concatenate([mine, vocab_ref[...]], 1)
    for index in range(length // FREQ_ROWS):
        rows = pl.ds(index * FREQ_ROWS, FREQ_ROWS)
        look_ref[rows, :] = dot(hot_ref[rows, :], table)
        row = (iota((FREQ_ROWS, subs), 0) + index * FREQ_ROWS).astype(F32)
        put_here = (row == place[:, :subs]).astype(F32).astype(BF16)
        subs_ref[rows, :] = dot(jnp.concatenate([put_here, put_here], 1), held)

    cols = points * share
    norm_ref[:, :GROUP, :] = jnp.zeros((2, GROUP, cols), F32)
    gain = gain_ref[:, pl.ds(first, share)]
    taps = [taps_ref[f, :, pl.ds(first, share)].astype(F32) for f in range(3)]
    taps = [[taps[f][tap : tap + 1] for tap in range(3)] for f in range(3)]

    @pl.loop(0, half // CHUNK)
    def _(step):
        start = pl.multiple_of(step * CHUNK, CHUNK)
        sides = []
        for side in range(2):
            rows = pl.ds(pl.multiple_of(side * half + start, CHUNK), CHUNK)
            tok = look_ref[rows, :share]
            inv = look_ref[rows, share:]
            inv = inv + pltpu.roll(inv, LANES // 2, 1)
            chosen = subs_ref[rows, share : 2 * share] > 0.5
            base = jnp.where(chosen, subs_ref[rows, :share], tok)
            pair_ref[0, rows, :] = tok.astype(BF16)
            pair_ref[1, rows, :] = base.astype(BF16)
            sides.append((rows, base, tok - base, inv, chosen))
        for point in range(points):
            lanes = slice(point * share, (point + 1) * share)
            nows, backs = [], []
            for side, (rows, base, diff, inv_tok, chosen) in enumerate(sides):
                inv = jnp.where(
                    chosen, subs_ref[rows, (2 + point) * share : (3 + point) * share], inv_tok
                )
                inv_ref[rows, lanes] = inv
                now = rounded((base + alphas[point] * diff) * inv * gain)
                norm_ref[side, pl.ds(start + GROUP, CHUNK), lanes] = now
                window = norm_ref[side, pl.ds(start, CHUNK + GROUP), lanes]
                nows.append(now)
                backs.append(window[GROUP - 1 : GROUP - 1 + CHUNK])
            recent = ((nows[0], backs[1], backs[0]), (nows[1], nows[0], backs[1]))
            for side in range(2):
                rows = sides[side][0]
                feats = [sum(taps[f][tap] * recent[side][tap] for tap in range(3)) for f in range(3)]
                q_ref[rows, lanes] = feats[0]
                k_ref[rows, lanes] = feats[1]
                v_ref[rows, lanes] = feats[2]
                signal_ref[rows, lanes] = (feats[1] * feats[2]).astype(BF16)


def forward_kernel(
    points, signal_ref, skip_ref, even_ref, odd_ref, even_back_ref, odd_back_ref, spec_ref, conv_ref, prod_ref
):
    half = even_ref.shape[1]
    share = spec_ref.shape[2]
    transform(even_ref, odd_ref, signal_ref, spec_ref, prod_ref, points, False)
    skip = skip_ref[:, pl.ds(pl.multiple_of(lax.axis_index("path") * share, LANES), share)]
    skip = jnp.concatenate([skip] * points, 1)
    for index in range(half // FREQ_ROWS):
        found = inverse_rows((even_back_ref, odd_back_ref), prod_ref, pl.ds(index * FREQ_ROWS, FREQ_ROWS))
        for side in range(2):
            rows = pl.ds(side * half + index * FREQ_ROWS, FREQ_ROWS)
            conv_ref[rows, :] = (found[side] + skip * signal_ref[rows, :].astype(F32)).astype(BF16)


def backward_kernel(
    points, width, msg_ref, pair_ref, taps_ref, gain_ref, skip_ref,
    q_ref, k_ref, v_ref, inv_ref, conv_ref, even_ref, odd_ref, even_back_ref, odd_back_ref, spec_ref,
    grad_ref,
    signal_ref, prod_ref, tap0_ref, tap1_ref, tap2_ref,
):
    half = even_ref.shape[1]
    share = pair_ref.shape[2]
    n_ctx = msg_ref.shape[0]
    block_half = LANES // 2
    path = lax.axis_index("path")
    first = pl.multiple_of((lax.axis_index("ctx") * points + path) * share, LANES)

    @pl.loop(0, n_ctx)
    def _(block):
        for side in range(2):
            rows = pl.ds(pl.multiple_of(side * half + block * block_half, block_half), block_half)
            upstream = msg_ref[block, side * block_half : (side + 1) * block_half, :].astype(F32)
            for point in range(points):
                lanes = slice(point * share, (point + 1) * share)
                signal_ref[rows, lanes] = (upstream * q_ref[rows, lanes]).astype(BF16)

    transform(even_ref, odd_ref, signal_ref, spec_ref, prod_ref, points, True)
    skip = skip_ref[:, pl.ds(pl.multiple_of(path * share, LANES), share)]
    gain = gain_ref[:, pl.ds(first, share)]
    taps = [taps_ref[f, :, pl.ds(first, share)].astype(F32) for f in range(3)]
    taps_refs = (tap0_ref, tap1_ref, tap2_ref)
    for ref in taps_refs:
        ref[:, half:, :] = jnp.zeros((2, GROUP, points * share), F32)
    for index in range(half // FREQ_ROWS):
        found = inverse_rows((even_back_ref, odd_back_ref), prod_ref, pl.ds(index * FREQ_ROWS, FREQ_ROWS))
        for side in range(2):
            for part in range(FREQ_ROWS // CHUNK):
                inside = slice(part * CHUNK, (part + 1) * CHUNK)
                start = index * FREQ_ROWS + part * CHUNK
                rows = pl.ds(side * half + start, CHUNK)
                block = start // block_half
                sent = start % block_half + side * block_half
                upstream = msg_ref[block, sent : sent + CHUNK, :].astype(F32)
                for point in range(points):
                    lanes = slice(point * share, (point + 1) * share)
                    grad_z = rounded(
                        found[side][inside, lanes] + skip * signal_ref[rows, lanes].astype(F32)
                    )
                    grads = (
                        rounded(upstream * conv_ref[rows, lanes].astype(F32)),
                        rounded(grad_z * v_ref[rows, lanes]),
                        rounded(grad_z * k_ref[rows, lanes]),
                    )
                    for tap, ref in enumerate(taps_refs):
                        ref[side, pl.ds(start, CHUNK), lanes] = sum(
                            taps[f][tap : tap + 1] * grads[f] for f in range(3)
                        )

    alphas = [(point + 0.5) / points for point in range(points)]
    ones = jnp.ones((GROUP, share), F32)

    @pl.loop(0, n_ctx)
    def _(block):
        to_tok, to_base = [[], []], [[], []]
        for part in range(block_half // CHUNK):
            start = pl.multiple_of(block * block_half + part * CHUNK, CHUNK)
            here = pl.ds(start, CHUNK)
            ahead = pl.ds(start, CHUNK + GROUP)
            sides = []
            for side in range(2):
                rows = pl.ds(pl.multiple_of(side * half + start, CHUNK), CHUNK)
                base = pair_ref[1, rows, :].astype(F32)
                diff = pair_ref[0, rows, :].astype(F32) - base
                sides.append([rows, base, diff] + [jnp.zeros((CHUNK, share), F32)] * 3)
            for point in range(points):
                lanes = slice(point * share, (point + 1) * share)
                even1 = tap1_ref[0, ahead, lanes][1 : 1 + CHUNK]
                even2 = tap2_ref[0, ahead, lanes][1 : 1 + CHUNK]
                odd2 = tap2_ref[1, ahead, lanes][1 : 1 + CHUNK]
                sums = (
                    tap0_ref[0, here, lanes] + tap1_ref[1, here, lanes] + even2,
                    tap0_ref[1, here, lanes] + even1 + odd2,
                )
                for side in range(2):
                    rows, base, diff, total, sum_tok, sum_base = sides[side]
                    inv = inv_ref[rows, lanes]
                    along = inv * (gain * sums[side])
                    total = total + along
                    along = along * (base + alphas[point] * diff) * (inv * inv)
                    sum_tok = sum_tok + alphas[point] * along
                    sum_base = sum_base + (1.0 - alphas[point]) * along
                    sides[side][3:] = [total, sum_tok, sum_base]
            for side in range(2):
                sent = side * block_half + part * CHUNK
                grad_ref[block, sent : sent + CHUNK, :] = sides[side][3].astype(BF16)
                to_tok[side].append(sides[side][4])
                to_base[side].append(sides[side][5])
        sent = []
        for sums in (to_tok, to_base):
            row = exact_dot(ones, jnp.concatenate(sums[0] + sums[1], 0), ((1,), (1,)))
            row = row[:1] / width
            high = row.astype(BF16).astype(F32)
            sent += [high, row - high]
        sent.append(jnp.zeros((grad_ref.shape[1] - LANES - len(sent), LANES), F32))
        grad_ref[block, LANES:, :] = jnp.concatenate(sent, 0).astype(BF16)


def partial_kernel(grad_ref, out_ref):
    dests, rows, _ = out_ref.shape
    n_ctx = grad_ref.shape[0]
    each = n_ctx // dests
    spare = sum(grad_ref[block, LANES:, :].astype(F32) for block in range(n_ctx))
    sums = [spare[0:1] + spare[1:2], spare[2:3] + spare[3:4]]
    sent = []
    for value in sums:
        high = value.astype(BF16).astype(F32)
        sent += [high, value - high]
    sent.append(jnp.zeros((rows - each * LANES - len(sent), LANES), F32))
    sent = jnp.concatenate(sent, 0).astype(BF16)
    for dest in range(dests):
        for piece in range(each):
            out_ref[dest, piece * LANES : (piece + 1) * LANES, :] = grad_ref[dest * each + piece, :LANES, :]
        out_ref[dest, each * LANES :, :] = sent


def finish_kernel(grad_ref, own_ref, path_ref, attr_ref):
    points, rows, share = grad_ref.shape
    pieces = rows // LANES
    spare = sum(grad_ref[path, pieces * LANES :, :].astype(F32) for path in range(points))
    sums = jnp.concatenate([spare[0:1] + spare[1:2], spare[2:3] + spare[3:4], spare[4:10]], 0)
    order = even_first()
    columns = transposed(exact_dot(sums, order, ((1,), (0,))))
    to_tok = columns[:, 0:1]
    to_base = columns[:, 1:2]
    order = order.T.astype(BF16)
    for piece in range(pieces):
        for path in range(points):
            lanes = slice((piece * points + path) * share, (piece * points + path + 1) * share)
            tok = own_ref[0, :, lanes].astype(F32)
            base = own_ref[1, :, lanes].astype(F32)
            grad = dot(order, grad_ref[path, piece * LANES : (piece + 1) * LANES, :])
            grad = (grad - tok * to_tok - base * to_base) / points
            path_ref[:, lanes] = grad
            attr_ref[:, lanes] = (tok - base) * grad


def any_spec():
    return pl.BlockSpec(memory_space=pl.ANY)


def vmem_spec():
    return pl.BlockSpec(memory_space=pltpu.VMEM)


def hbm_spec():
    return pl.BlockSpec(memory_space=pltpu.HBM)


def call(kernel, ins, outs, scratch, flops, moved, mebibytes):
    return pl.pallas_call(
        kernel,
        in_specs=ins,
        out_specs=[spec for spec, _ in outs],
        out_shape=[shape for _, shape in outs],
        scratch_shapes=scratch,
        compiler_params=pltpu.CompilerParams(vmem_limit_bytes=mebibytes * 2**20),
        cost_estimate=pl.CostEstimate(flops=flops, bytes_accessed=moved, transcendentals=0),
    )


def shape(dims, dtype):
    return jax.ShapeDtypeStruct(dims, dtype)


def kernel_body(tokens, sub_pos, sub_base, embed, norm_gain, fir_taps, long_filter, skip_gain, cotangent):
    n_path, n_ctx = lax.axis_size("path"), lax.axis_size("ctx")
    points = n_path
    tok_rows = tokens.shape[0]
    length = tok_rows * n_ctx
    vocab, width = embed.shape
    share = width // (n_path * n_ctx)
    subs = sub_pos.shape[0] * n_ctx
    own_width = width // n_path
    cols = points * share
    half = length // 2
    tables = dft_tables(length)
    dma = pltpu.SemaphoreType.DMA
    transform_flops = 2 * length * length
    spare = 16

    msg, ids = call(
        pack_kernel,
        [hbm_spec()] * 4,
        [
            (vmem_spec(), shape((n_ctx, tok_rows + spare, share), BF16)),
            (vmem_spec(), shape((spare, LANES), F32)),
        ],
        [
            pltpu.VMEM((1, tok_rows), jnp.int32),
            pltpu.VMEM((1, sub_pos.shape[0]), jnp.int32),
            pltpu.VMEM((1, sub_pos.shape[0]), jnp.int32),
            pltpu.VMEM((n_ctx, tok_rows, share), BF16),
            dma((n_ctx + 3,)),
        ],
        length * share,
        8 * length * share,
        4,
    )(
        tokens.reshape(1, tok_rows),
        sub_pos.reshape(1, -1),
        sub_base.reshape(1, -1),
        cotangent,
    )
    msg = lax.all_to_all(msg, "ctx", 0, 0, tiled=True)

    gain = norm_gain.reshape(1, width)
    skip = skip_gain.reshape(1, n_path * share)
    vocab_inv, own = call(
        vocab_kernel,
        [vmem_spec()] * 2,
        [
            (vmem_spec(), shape((vocab, LANES), BF16)),
            (vmem_spec(), shape((2, tok_rows, own_width), BF16)),
        ],
        [],
        4 * tok_rows * vocab * own_width,
        2 * vocab * width,
        8,
    )(ids, embed)
    spec = call(
        spectrum_kernel,
        [hbm_spec()] + [vmem_spec()] * 2,
        [(vmem_spec(), shape((4, half, share), F32))],
        [pltpu.VMEM((length, share), F32), dma],
        transform_flops * share,
        4 * length * length,
        8,
    )(long_filter, tables[0], tables[1])[0]

    wide = 4 * LANES
    signal, q_feat, k_feat, v_feat, inv, pair = call(
        functools.partial(feature_kernel, points),
        [vmem_spec()] * 5,
        [(vmem_spec(), shape((length, cols), BF16))]
        + [(vmem_spec(), shape((length, cols), F32))] * 4
        + [(vmem_spec(), shape((2, length, share), BF16))],
        [
            pltpu.VMEM((length, vocab), BF16),
            pltpu.VMEM((points, subs, LANES), F32),
            pltpu.VMEM((2, subs, wide), F32),
            pltpu.VMEM((length, 2 * share), F32),
            pltpu.VMEM((length, (2 + points) * share), F32),
            pltpu.VMEM((2, GROUP + half, cols), F32),
        ],
        2 * length * vocab * 3 * share,
        2 * vocab * width + 16 * length * cols,
        16,
    )(msg, embed, vocab_inv, fir_taps, gain)
    conv = call(
        functools.partial(forward_kernel, points),
        [vmem_spec()] * 7,
        [(vmem_spec(), shape((length, cols), BF16))],
        [pltpu.VMEM((2 * length, cols), BF16)],
        2 * transform_flops * cols,
        4 * length * length,
        12,
    )(signal, skip, *tables, spec)[0]

    grad = call(
        functools.partial(backward_kernel, points, width),
        [vmem_spec()] * 15,
        [(vmem_spec(), shape((n_ctx, tok_rows + spare, share), BF16))],
        [
            pltpu.VMEM((length, cols), BF16),
            pltpu.VMEM((2 * length, cols), BF16),
        ]
        + [pltpu.VMEM((2, half + GROUP, cols), F32)] * 3,
        2 * transform_flops * cols,
        4 * length * length + 16 * length * cols,
        18,
    )(msg, pair, fir_taps, gain, skip, q_feat, k_feat, v_feat, inv, conv, *tables, spec)[0]

    grad = lax.all_to_all(grad, "ctx", 0, 0, tiled=True)
    each = n_ctx // n_path
    grad = call(
        partial_kernel,
        [vmem_spec()],
        [(vmem_spec(), shape((n_path, each * tok_rows + spare, share), BF16))],
        [],
        spare * LANES * n_ctx,
        4 * length * share,
        4,
    )(grad)[0]
    grad = lax.all_to_all(grad, "path", 0, 0, tiled=True)
    out = shape((tok_rows, own_width), F32)
    return tuple(
        call(
            finish_kernel,
            [vmem_spec()] * 2,
            [(vmem_spec(), out), (vmem_spec(), out)],
            [],
            8 * tok_rows * own_width,
            14 * tok_rows * own_width,
            8,
        )(grad, own)
    )


def plain_body(tokens, sub_pos, sub_base, embed, norm_gain, fir_taps, long_filter, skip_gain, cotangent):
    n_path, n_ctx = lax.axis_size("path"), lax.axis_size("ctx")
    path, ctx = lax.axis_index("path"), lax.axis_index("ctx")
    points = n_path
    tok_rows = tokens.shape[0]
    length = tok_rows * n_ctx
    width = embed.shape[1]
    share = width // (n_path * n_ctx)
    own_width = width // n_path
    first = (ctx * n_path + path) * share
    alphas = ((jnp.arange(points, dtype=jnp.int32)).astype(F32) + 0.5) / points
    alphas = alphas[:, None, None]

    local = jnp.arange(tok_rows, dtype=jnp.int32)[:, None] + ctx * tok_rows == sub_pos[None, :]
    put = jnp.sum(jnp.where(local, sub_base[None, :], 0), 1)
    base_ids = jnp.where(jnp.any(local, 1), put, tokens)
    rows_tok = jnp.take(embed, tokens, axis=0).astype(F32)
    rows_base = jnp.take(embed, base_ids, axis=0).astype(F32)
    rows_in = rows_base[None] + alphas * (rows_tok - rows_base)[None]
    inv = lax.rsqrt(jnp.mean(rows_in * rows_in, -1) + EPS)
    inv = lax.all_gather(inv, "ctx", axis=1, tiled=True)[:, :, None]
    all_tok = lax.all_gather(tokens, "ctx", tiled=True)
    all_base = lax.all_gather(base_ids, "ctx", tiled=True)

    cot = cotangent.reshape(tok_rows, n_ctx, n_path, share)
    cot = lax.dynamic_index_in_dim(cot, path, 2, keepdims=False)
    cot = lax.all_to_all(cot.transpose(1, 0, 2), "ctx", 0, 0, tiled=True)
    upstream = cot.reshape(1, length, share).astype(F32)
    mine = lax.dynamic_slice_in_dim(embed, first, share, 1)
    gain = lax.dynamic_slice_in_dim(norm_gain, first, share, 0)
    taps = lax.dynamic_slice_in_dim(fir_taps, first, share, 2).astype(F32)
    filt = lax.dynamic_slice_in_dim(long_filter, path * share, share, 1)
    skip = lax.dynamic_slice_in_dim(skip_gain, path * share, share, 0)

    emb_tok = jnp.take(mine, all_tok, axis=0).astype(F32)
    emb_base = jnp.take(mine, all_base, axis=0).astype(F32)
    inputs = emb_base[None] + alphas * (emb_tok - emb_base)[None]
    normed = rounded(inputs * inv * gain)
    q_feat, k_feat, v_feat = (
        taps[f, 0] * normed + taps[f, 1] * shifted(normed, 1) + taps[f, 2] * shifted(normed, 2)
        for f in range(3)
    )
    filter_spec = spectrum(filt[None])
    conv = rounded(long_conv(rounded(k_feat * v_feat), filter_spec, skip, False))
    grad_z = rounded(long_conv(rounded(upstream * q_feat), filter_spec, skip, True))
    grads = (rounded(upstream * conv), rounded(grad_z * v_feat), rounded(grad_z * k_feat))
    by_tap = [sum(taps[f, tap] * grads[f] for f in range(3)) for tap in range(3)]
    scaled = gain * (by_tap[0] + shifted(by_tap[1], -1) + shifted(by_tap[2], -2))
    grad = jnp.sum(inv * scaled, 0).astype(BF16)
    along = jnp.sum(inputs * scaled, -1, keepdims=True) * inv**3 / width
    part = jnp.stack([jnp.sum(alphas * along, 0)[:, 0], jnp.sum((1.0 - alphas) * along, 0)[:, 0]])
    part = lax.psum(part, ("path", "ctx"))
    part = lax.dynamic_slice_in_dim(part, ctx * tok_rows, tok_rows, 1)

    back = lax.all_to_all(grad.reshape(n_ctx, tok_rows, share), "ctx", 0, 0, tiled=True)
    back = back.reshape(n_path, n_ctx // n_path, tok_rows, share)
    back = lax.all_to_all(back, "path", 0, 0, tiled=True).astype(F32)
    back = back.transpose(2, 1, 0, 3).reshape(tok_rows, own_width)
    own_tok = lax.dynamic_slice_in_dim(rows_tok, path * own_width, own_width, 1)
    own_base = lax.dynamic_slice_in_dim(rows_base, path * own_width, own_width, 1)
    grad = (back - own_tok * part[0][:, None] - own_base * part[1][:, None]) / points
    return (grad, (own_tok - own_base) * grad)


def body(tokens, sub_pos, sub_base, embed, *rest):
    n_path, n_ctx = lax.axis_size("path"), lax.axis_size("ctx")
    tok_rows = tokens.shape[0]
    share = embed.shape[1] // (n_path * n_ctx)
    tables = 4 * (tok_rows * n_ctx) ** 2
    fits = share == LANES and tok_rows == LANES and n_ctx == GROUP and tables <= TABLE_BYTES
    chosen = kernel_body if fits else plain_body
    return chosen(tokens, sub_pos, sub_base, embed, *rest)


def solution(mesh):
    return jax.shard_map(
        body,
        mesh=mesh,
        in_specs=(
            P("ctx"),
            P("ctx"),
            P("ctx"),
            P(),
            P(),
            P(),
            P(None, "ctx"),
            P("ctx"),
            P("ctx", None),
        ),
        out_specs=(P("ctx", "path"), P("ctx", "path")),
        check_vma=False,
    )
```

```python
import functools

import jax
import jax.numpy as jnp
import ml_dtypes
import numpy as np
from jax import lax
from jax.experimental import pallas as pl
from jax.experimental.pallas import tpu as pltpu
from jax.sharding import PartitionSpec as P

LANES = 128
GROUP = 8
FREQ_ROWS = 256
CHUNK = 32
EPS = 1e-06
CANCEL = 0.004
TABLE_BYTES = 4 * 2**20
F32 = jnp.float32
BF16 = jnp.bfloat16
precise = lax.Precision.HIGH


def angle_tables(length):
    outer_size = 64
    inner_size = length // outer_size
    outer_idx = jnp.arange(outer_size, dtype=jnp.int32)
    inner_idx = jnp.arange(inner_size, dtype=jnp.int32)
    outer_angle = (
        2.0 * jnp.pi / outer_size
        * (outer_idx[:, None] * outer_idx[None, :] % outer_size).astype(F32)
    )
    inner_angle = (
        2.0 * jnp.pi / inner_size
        * (inner_idx[:, None] * inner_idx[None, :] % inner_size).astype(F32)
    )
    twist_angle = (
        2.0 * jnp.pi / length
        * (outer_idx[:, None] * inner_idx[None, :] % length).astype(F32)
    )
    return (outer_angle, inner_angle, twist_angle)


def complex_table(angle, sign):
    cosine = jnp.cos(angle)
    sine = sign * jnp.sin(angle)
    return jnp.stack([jnp.stack([cosine, sine]), jnp.stack([-sine, cosine])])


def twisted(values, angle, sign):
    cosine = jnp.cos(angle)[None, :, :, None]
    sine = sign * jnp.sin(angle)[None, :, :, None]
    real_part = values[:, 0]
    imag_part = values[:, 1]
    return jnp.stack(
        [real_part * cosine - imag_part * sine, real_part * sine + imag_part * cosine], 1
    )


def spectrum(signal):
    batch, half, width = signal.shape
    length = 2 * half
    outer_angle, inner_angle, twist_angle = angle_tables(length)
    outer_size = outer_angle.shape[0]
    inner_size = inner_angle.shape[0]
    folded = signal.reshape(batch, outer_size // 2, inner_size, width)
    used = outer_angle[:, : outer_size // 2]
    outer_table = jnp.stack([jnp.cos(used), -jnp.sin(used)])
    first = jnp.einsum("rka,pabc->prkbc", outer_table, folded, precision=precise)
    turned = twisted(first, twist_angle, -1.0)
    return jnp.einsum(
        "prkbc,rsbm->pskmc", turned, complex_table(inner_angle, -1.0), precision=precise
    )


def inverse(spec):
    batch, parts, outer_size, inner_size, width = spec.shape
    length = outer_size * inner_size
    outer_angle, inner_angle, twist_angle = angle_tables(length)
    back = jnp.einsum("pskmc,stmb->ptkbc", spec, complex_table(inner_angle, 1.0), precision=precise)
    turned = twisted(back, twist_angle, 1.0)
    used = outer_angle[: outer_size // 2]
    outer_table = jnp.stack([jnp.cos(used), -jnp.sin(used)])
    result = jnp.einsum("rak,prkbc->pabc", outer_table, turned, precision=precise)
    return (result / length).reshape(batch, length // 2, width)


def long_conv(signal, filter_spec, skip_gain, adjoint):
    spec = spectrum(signal)
    sig_real = spec[:, 0]
    sig_imag = spec[:, 1]
    filt_real = filter_spec[:, 0]
    filt_imag = filter_spec[:, 1]
    if adjoint:
        prod_real = sig_real * filt_real + sig_imag * filt_imag
        prod_imag = sig_imag * filt_real - sig_real * filt_imag
    else:
        prod_real = sig_real * filt_real - sig_imag * filt_imag
        prod_imag = sig_real * filt_imag + sig_imag * filt_real
    return inverse(jnp.stack([prod_real, prod_imag], 1)) + skip_gain * signal


def rounded(value):
    return value.astype(BF16).astype(F32)


def shifted(values, step):
    zeros = jnp.zeros_like(values[:, : abs(step)])
    if step > 0:
        return jnp.concatenate([zeros, values[:, :-step]], 1)
    return jnp.concatenate([values[:, -step:], zeros], 1)


@functools.lru_cache(maxsize=None)
def dft_tables(length):
    half = length // 2
    freq = 4 * np.arange(half, dtype=np.int64) + 1
    place = np.arange(half, dtype=np.int64)
    tables = []
    for offset in (0, 1):
        turns = freq[:, None] * (2 * place + offset)[None, :] % (8 * half)
        angle = turns * (2.0 * np.pi / (8 * half))
        cosine = np.cos(angle).astype(ml_dtypes.bfloat16)
        sine = np.sin(angle).astype(ml_dtypes.bfloat16)
        tables.append((np.concatenate([cosine, sine], 0), np.concatenate([cosine.T, sine.T], 1)))
    return (tables[0][0], tables[1][0], tables[0][1], tables[1][1])


def transposed(rows):
    count = rows.shape[0]
    if count < LANES:
        rows = jnp.concatenate([rows, jnp.zeros((LANES - count, LANES), F32)], 0)
    return rows.T


def dot(left, right):
    return jnp.dot(left, right, preferred_element_type=F32)


def exact_dot(left, right, dims):
    return lax.dot_general(
        left, right, (dims, ((), ())), precision=lax.Precision.HIGHEST, preferred_element_type=F32
    )


def iota(dims, axis):
    return lax.broadcasted_iota(jnp.int32, dims, axis)


def even_first():
    row = iota((LANES, LANES), 0)
    half = LANES // 2
    source = jnp.where(row < half, 2 * row, 2 * (row - half) + 1)
    return (iota((LANES, LANES), 1) == source).astype(F32)


def hot(ids, vocab):
    lane = iota(ids.shape, 1).astype(F32)
    parts = [
        (ids == lane + float(column * LANES)).astype(F32).astype(BF16)
        for column in range(vocab // LANES)
    ]
    return jnp.concatenate(parts, 1)


def joined(block, kind):
    return 256.0 * block[2 * kind : 2 * kind + 1] + block[2 * kind + 1 : 2 * kind + 2]


def pack_kernel(
    tok_hbm, pos_hbm, put_hbm, cot_hbm, msg_ref, ids_ref, tok_ref, pos_ref, put_ref, cot_ref, sems
):
    dests, rows, share = msg_ref.shape
    tok_rows = cot_hbm.shape[0]
    n_path = cot_hbm.shape[1] // (dests * share)
    path = lax.axis_index("path")
    moves = [(tok_hbm, tok_ref), (pos_hbm, pos_ref), (put_hbm, put_ref)]
    for dest in range(dests):
        lanes = pl.ds(pl.multiple_of((dest * n_path + path) * share, LANES), share)
        moves.append((cot_hbm.at[:, lanes], cot_ref.at[:, pl.ds(dest * share, share)]))
    copies = [
        pltpu.make_async_copy(source, target, sems.at[index])
        for index, (source, target) in enumerate(moves)
    ]
    for copy in copies:
        copy.start()
    order = even_first().astype(BF16)
    for copy in copies[:3]:
        copy.wait()
    lists = []
    for ref in (tok_ref, pos_ref, put_ref):
        value = ref[...].astype(F32)
        if value.shape[1] < LANES:
            value = jnp.concatenate([value, jnp.zeros((1, LANES - value.shape[1]), F32)], 1)
        high = jnp.floor(value * (1.0 / 256.0))
        lists += [high, value - 256.0 * high]
    lists.append(jnp.zeros((rows - tok_rows - len(lists), LANES), F32))
    ids = jnp.concatenate(lists, 0)
    ids_ref[...] = ids
    turned = lax.dot_general(
        ids.astype(BF16), order, (((1,), (1,)), ((), ())), preferred_element_type=F32
    )
    ids = jnp.where(iota(ids.shape, 0) < 2, turned, ids).astype(BF16)
    for dest in range(dests):
        msg_ref[dest, tok_rows:, :] = ids
    for copy in copies[3:]:
        copy.wait()
    turned = dot(order, cot_ref[...]).astype(BF16)
    for dest in range(dests):
        msg_ref[dest, :tok_rows, :] = turned[:, dest * share : (dest + 1) * share]


def vocab_kernel(ids_ref, embed_hbm, gram_ref, table_ref, own_ref, embed_ref, sum_ref, sems):
    vocab, width = embed_ref.shape
    share = table_ref.shape[1] - LANES
    wide = width // sems.shape[0]
    copies = []
    for index in range(sems.shape[0]):
        lanes = pl.ds(index * wide, wide)
        copies.append(
            pltpu.make_async_copy(embed_hbm.at[:, lanes], embed_ref.at[:, lanes], sems.at[index])
        )
        copies[-1].start()
    for index, copy in enumerate(copies):
        copy.wait()
        part = embed_ref[:, index * wide : (index + 1) * wide]
        found = lax.dot_general(part, part, (((1,), (1,)), ((), ())), preferred_element_type=F32)
        if index == 0:
            sum_ref[...] = found
        else:
            sum_ref[...] += found
    n_path = lax.axis_size("path")
    first = (lax.axis_index("ctx") * n_path + lax.axis_index("path")) * share
    table_ref[:, :share] = embed_ref[:, pl.ds(pl.multiple_of(first, LANES), share)]
    same = iota((LANES, LANES), 0) == iota((LANES, LANES), 1)
    for block in range(vocab // LANES):
        rows = slice(block * LANES, (block + 1) * LANES)
        value = sum_ref[rows, :]
        norm = jnp.sum(jnp.where(same, value[:, rows], 0.0), 1, keepdims=True)
        inv = jnp.broadcast_to(lax.rsqrt(norm / width + EPS), (LANES, LANES))
        high = inv.astype(BF16).astype(F32)
        lane = iota((LANES, LANES), 1)
        table_ref[rows, share:] = jnp.where(lane < LANES // 2, high, inv - high).astype(BF16)
        for part in range(3):
            high = value.astype(BF16)
            gram_ref[part * vocab + block * LANES : part * vocab + (block + 1) * LANES, :] = high
            value = value - high.astype(F32)

    ids = ids_ref[...]
    columns = transposed(jnp.concatenate([joined(ids, kind) for kind in range(3)], 0))
    tok = jnp.broadcast_to(columns[:, 0:1], (LANES, LANES))
    place = jnp.broadcast_to(joined(ids, 1), (LANES, LANES))
    put = jnp.broadcast_to(joined(ids, 2), (LANES, LANES))
    first = lax.axis_index("ctx") * LANES
    subs = LANES // GROUP
    here = (place == (iota((LANES, LANES), 0) + first).astype(F32)) & (iota((LANES, LANES), 1) < subs)
    found = jnp.max(jnp.where(here, put, -1.0), 1, keepdims=True)
    base = jnp.where(found >= 0.0, found, tok)
    own_width = own_ref.shape[2]
    lanes = pl.ds(pl.multiple_of(lax.axis_index("path") * own_width, LANES), own_width)
    own_ref[0] = dot(hot(tok, vocab), embed_ref[:, lanes]).astype(BF16)
    own_ref[1] = dot(hot(base, vocab), embed_ref[:, lanes]).astype(BF16)


def spectrum_kernel(filt_hbm, even_ref, odd_ref, spec_ref, filt_ref, sem):
    length, share = filt_ref.shape
    half = length // 2
    lanes = pl.ds(pl.multiple_of(lax.axis_index("path") * share, LANES), share)
    copy = pltpu.make_async_copy(filt_hbm.at[:, lanes], filt_ref, sem)
    copy.start()
    copy.wait()
    parts = []
    for offset in range(2):
        value = filt_ref[pl.ds(offset, half, stride=2), :] * (1.0 / length)
        high = value.astype(BF16)
        parts.append(jnp.concatenate([high, (value - high.astype(F32)).astype(BF16)], 1))
    for index in range(half // FREQ_ROWS):
        found = []
        for table, part in ((even_ref, parts[0]), (odd_ref, parts[1])):
            for offset in (0, half):
                both = dot(table[pl.ds(offset + index * FREQ_ROWS, FREQ_ROWS), :], part)
                found.append(both[:, :share] + both[:, share:])
        rows = pl.ds(index * FREQ_ROWS, FREQ_ROWS)
        spec_ref[0, rows, :] = found[0] + found[2]
        spec_ref[1, rows, :] = -found[1] - found[3]
        spec_ref[2, rows, :] = found[0] - found[2]
        spec_ref[3, rows, :] = found[3] - found[1]


def transform(even_ref, odd_ref, signal_ref, spec_ref, prod_ref, points, adjoint):
    half = even_ref.shape[1]
    share = spec_ref.shape[2]
    for index in range(half // FREQ_ROWS):
        rows = pl.ds(index * FREQ_ROWS, FREQ_ROWS)
        after = pl.ds(half + index * FREQ_ROWS, FREQ_ROWS)
        even_real = dot(even_ref[rows, :], signal_ref[:half, :])
        even_imag = dot(even_ref[after, :], signal_ref[:half, :])
        odd_real = dot(odd_ref[rows, :], signal_ref[half:, :])
        odd_imag = dot(odd_ref[after, :], signal_ref[half:, :])
        filt = [spec_ref[part, rows, :] for part in range(4)]
        for point in range(points):
            lanes = slice(point * share, (point + 1) * share)
            prods = []
            for part, sign in ((0, 1.0), (2, -1.0)):
                real = even_real[:, lanes] + sign * odd_real[:, lanes]
                imag = even_imag[:, lanes] + sign * odd_imag[:, lanes]
                if adjoint:
                    prods.append(real * filt[part] - imag * filt[part + 1])
                    prods.append(real * filt[part + 1] + imag * filt[part])
                else:
                    prods.append(real * filt[part] + imag * filt[part + 1])
                    prods.append(imag * filt[part] - real * filt[part + 1])
            sums = (prods[0] + prods[2], prods[1] + prods[3], prods[0] - prods[2], prods[1] - prods[3])
            for part, value in enumerate(sums):
                into = pl.ds(part * half + index * FREQ_ROWS, FREQ_ROWS)
                prod_ref[into, lanes] = value.astype(BF16)


def inverse_rows(back_refs, prod_ref, rows):
    length = 2 * back_refs[0].shape[0]
    return [
        dot(ref[rows, :], prod_ref[offset : offset + length, :])
        for ref, offset in zip(back_refs, (0, length))
    ]


def feature_kernel(
    points, msg_ref, gram_ref, table_ref, taps_ref, gain_ref, embed_hbm,
    signal_ref, q_ref, k_ref, v_ref, inv_ref, pair_ref,
    hot_ref, embed_ref, sums_ref, found_ref, look_ref, subs_ref, norm_ref, sem,
):
    length = signal_ref.shape[0]
    half = length // 2
    vocab, width = embed_hbm.shape
    share = pair_ref.shape[2]
    n_ctx = msg_ref.shape[0]
    block_half = LANES // 2
    per_block = LANES // GROUP
    subs = n_ctx * per_block
    n_path = points
    first = (lax.axis_index("ctx") * n_path + lax.axis_index("path")) * share
    first = pl.multiple_of(first, LANES)

    blocks = [msg_ref[block, LANES:, :].astype(F32) for block in range(n_ctx)]
    toks = transposed(jnp.concatenate([joined(block, 0) for block in blocks], 0))
    for block in range(n_ctx):
        column = jnp.broadcast_to(toks[:, block : block + 1], (LANES, LANES))
        rows = hot(column, vocab)
        hot_ref[block * block_half : (block + 1) * block_half, :] = rows[:block_half]
        hot_ref[half + block * block_half : half + (block + 1) * block_half, :] = rows[block_half:]
    spread = sum(
        blocks[block] if block == 0 else pltpu.roll(blocks[block], block * per_block, 1)
        for block in range(n_ctx)
    )
    place = joined(spread, 1)
    put = joined(spread, 2)
    back = jnp.floor(place * 0.5)
    place = back + (place - 2.0 * back) * half
    columns = transposed(jnp.concatenate([place, put], 0))
    hot_base = hot(jnp.broadcast_to(columns[:, 1:2], (subs, LANES)), vocab)
    pick = jnp.concatenate(
        [
            (columns[:, 0:1] == (iota((subs, LANES), 1) + part * LANES).astype(F32)).astype(F32).astype(BF16)
            for part in range(length // LANES)
        ],
        1,
    )
    hot_tok = dot(pick, hot_ref[...]).astype(BF16)

    alphas = [(point + 0.5) / points for point in range(points)]
    hots = jnp.concatenate([hot_tok, hot_base], 0)
    found = dot(jnp.concatenate([hots] * 3, 1), gram_ref[...])
    hot_tok32, hot_base32 = hot_tok.astype(F32), hot_base.astype(F32)
    tok_tok = jnp.sum(found[:subs] * hot_tok32, 1, keepdims=True)
    tok_base = jnp.sum(found[:subs] * hot_base32, 1, keepdims=True)
    base_base = jnp.sum(found[subs:] * hot_base32, 1, keepdims=True)
    cancels = jnp.zeros((subs, 1), F32)
    for point in range(points):
        alpha = alphas[point]
        terms = (1.0 - alpha) ** 2 * base_base + alpha**2 * tok_tok
        total = terms + 2.0 * alpha * (1.0 - alpha) * tok_base
        cancels = jnp.maximum(cancels, (total < CANCEL * terms).astype(F32))
        inv = lax.rsqrt(jnp.maximum(total, 0.0) / width + EPS)
        sums_ref[point] = jnp.broadcast_to(inv, (subs, LANES))

    @pl.when(jnp.max(cancels) > 0.5)
    def _():
        copy = pltpu.make_async_copy(embed_hbm, embed_ref, sem)
        copy.start()
        sums_ref[...] = jnp.zeros_like(sums_ref)
        copy.wait()
        wide = found_ref.shape[1]

        @pl.loop(0, width // wide)
        def _(step):
            lanes = pl.ds(pl.multiple_of(step * wide, wide), wide)
            found_ref[...] = dot(hots, embed_ref[:, lanes])
            for block in range(subs // GROUP):
                rows = slice(block * GROUP, (block + 1) * GROUP)
                sums = [sums_ref[point, rows, :] for point in range(points)]
                for column in range(wide // LANES):
                    cut = slice(column * LANES, (column + 1) * LANES)
                    base = found_ref[subs + block * GROUP : subs + (block + 1) * GROUP, cut]
                    diff = found_ref[rows, cut] - base
                    for point in range(points):
                        value = base + alphas[point] * diff
                        sums[point] = sums[point] + value * value
                for point in range(points):
                    sums_ref[point, rows, :] = sums[point]

        for point in range(points):
            mean = jnp.sum(sums_ref[point], 1, keepdims=True) / width
            sums_ref[point] = jnp.broadcast_to(lax.rsqrt(mean + EPS), (subs, LANES))

    high = [dot(hot_base, table_ref[:, :share]), jnp.ones((subs, LANES), F32)]
    low = [jnp.zeros((subs, LANES), F32)] * 2
    for point in range(points):
        inv = sums_ref[point]
        high.append(inv.astype(BF16).astype(F32))
        low.append(inv - high[-1])
    held = jnp.concatenate([jnp.concatenate(high, 1), jnp.concatenate(low, 1)], 0).astype(BF16)
    for index in range(length // FREQ_ROWS):
        rows = pl.ds(index * FREQ_ROWS, FREQ_ROWS)
        look_ref[rows, :] = dot(hot_ref[rows, :], table_ref[...])
        row = (iota((FREQ_ROWS, subs), 0) + index * FREQ_ROWS).astype(F32)
        put_here = (row == place[:, :subs]).astype(F32).astype(BF16)
        subs_ref[rows, :] = dot(jnp.concatenate([put_here, put_here], 1), held)

    cols = points * share
    norm_ref[:, :GROUP, :] = jnp.zeros((2, GROUP, cols), F32)
    gain = gain_ref[:, pl.ds(first, share)]
    taps = [taps_ref[f, :, pl.ds(first, share)].astype(F32) for f in range(3)]
    taps = [[taps[f][tap : tap + 1] for tap in range(3)] for f in range(3)]

    @pl.loop(0, half // CHUNK)
    def _(step):
        start = pl.multiple_of(step * CHUNK, CHUNK)
        sides = []
        for side in range(2):
            rows = pl.ds(pl.multiple_of(side * half + start, CHUNK), CHUNK)
            tok = look_ref[rows, :share]
            inv = look_ref[rows, share:]
            inv = inv + pltpu.roll(inv, LANES // 2, 1)
            chosen = subs_ref[rows, share : 2 * share] > 0.5
            base = jnp.where(chosen, subs_ref[rows, :share], tok)
            pair_ref[0, rows, :] = tok.astype(BF16)
            pair_ref[1, rows, :] = base.astype(BF16)
            sides.append((rows, base, tok - base, inv, chosen))
        for point in range(points):
            lanes = slice(point * share, (point + 1) * share)
            nows, backs = [], []
            for side, (rows, base, diff, inv_tok, chosen) in enumerate(sides):
                inv = jnp.where(
                    chosen, subs_ref[rows, (2 + point) * share : (3 + point) * share], inv_tok
                )
                inv_ref[rows, lanes] = inv
                now = rounded((base + alphas[point] * diff) * inv * gain)
                norm_ref[side, pl.ds(start + GROUP, CHUNK), lanes] = now
                window = norm_ref[side, pl.ds(start, CHUNK + GROUP), lanes]
                nows.append(now)
                backs.append(window[GROUP - 1 : GROUP - 1 + CHUNK])
            recent = ((nows[0], backs[1], backs[0]), (nows[1], nows[0], backs[1]))
            for side in range(2):
                rows = sides[side][0]
                feats = [sum(taps[f][tap] * recent[side][tap] for tap in range(3)) for f in range(3)]
                q_ref[rows, lanes] = feats[0]
                k_ref[rows, lanes] = feats[1]
                v_ref[rows, lanes] = feats[2]
                signal_ref[rows, lanes] = (feats[1] * feats[2]).astype(BF16)


def forward_kernel(
    points, signal_ref, skip_ref, even_ref, odd_ref, even_back_ref, odd_back_ref, spec_ref, conv_ref, prod_ref
):
    half = even_ref.shape[1]
    share = spec_ref.shape[2]
    transform(even_ref, odd_ref, signal_ref, spec_ref, prod_ref, points, False)
    skip = skip_ref[:, pl.ds(pl.multiple_of(lax.axis_index("path") * share, LANES), share)]
    skip = jnp.concatenate([skip] * points, 1)
    for index in range(half // FREQ_ROWS):
        found = inverse_rows((even_back_ref, odd_back_ref), prod_ref, pl.ds(index * FREQ_ROWS, FREQ_ROWS))
        for side in range(2):
            rows = pl.ds(side * half + index * FREQ_ROWS, FREQ_ROWS)
            conv_ref[rows, :] = (found[side] + skip * signal_ref[rows, :].astype(F32)).astype(BF16)


def backward_kernel(
    points, width, msg_ref, pair_ref, taps_ref, gain_ref, skip_ref,
    q_ref, k_ref, v_ref, inv_ref, conv_ref, even_ref, odd_ref, even_back_ref, odd_back_ref, spec_ref,
    grad_ref,
    signal_ref, prod_ref, tap0_ref, tap1_ref, tap2_ref,
):
    half = even_ref.shape[1]
    share = pair_ref.shape[2]
    n_ctx = msg_ref.shape[0]
    block_half = LANES // 2
    path = lax.axis_index("path")
    first = pl.multiple_of((lax.axis_index("ctx") * points + path) * share, LANES)

    @pl.loop(0, n_ctx)
    def _(block):
        for side in range(2):
            rows = pl.ds(pl.multiple_of(side * half + block * block_half, block_half), block_half)
            upstream = msg_ref[block, side * block_half : (side + 1) * block_half, :].astype(F32)
            for point in range(points):
                lanes = slice(point * share, (point + 1) * share)
                signal_ref[rows, lanes] = (upstream * q_ref[rows, lanes]).astype(BF16)

    transform(even_ref, odd_ref, signal_ref, spec_ref, prod_ref, points, True)
    skip = skip_ref[:, pl.ds(pl.multiple_of(path * share, LANES), share)]
    gain = gain_ref[:, pl.ds(first, share)]
    taps = [taps_ref[f, :, pl.ds(first, share)].astype(F32) for f in range(3)]
    taps_refs = (tap0_ref, tap1_ref, tap2_ref)
    for ref in taps_refs:
        ref[:, half:, :] = jnp.zeros((2, GROUP, points * share), F32)
    for index in range(half // FREQ_ROWS):
        found = inverse_rows((even_back_ref, odd_back_ref), prod_ref, pl.ds(index * FREQ_ROWS, FREQ_ROWS))
        for side in range(2):
            for part in range(FREQ_ROWS // CHUNK):
                inside = slice(part * CHUNK, (part + 1) * CHUNK)
                start = index * FREQ_ROWS + part * CHUNK
                rows = pl.ds(side * half + start, CHUNK)
                block = start // block_half
                sent = start % block_half + side * block_half
                upstream = msg_ref[block, sent : sent + CHUNK, :].astype(F32)
                for point in range(points):
                    lanes = slice(point * share, (point + 1) * share)
                    grad_z = found[side][inside, lanes] + skip * signal_ref[rows, lanes].astype(F32)
                    grads = (
                        upstream * conv_ref[rows, lanes].astype(F32),
                        grad_z * v_ref[rows, lanes],
                        grad_z * k_ref[rows, lanes],
                    )
                    for tap, ref in enumerate(taps_refs):
                        ref[side, pl.ds(start, CHUNK), lanes] = sum(
                            taps[f][tap : tap + 1] * grads[f] for f in range(3)
                        )

    alphas = [(point + 0.5) / points for point in range(points)]
    ones = jnp.ones((GROUP, share), F32)

    @pl.loop(0, n_ctx)
    def _(block):
        to_tok, to_base = [[], []], [[], []]
        for part in range(block_half // CHUNK):
            start = pl.multiple_of(block * block_half + part * CHUNK, CHUNK)
            here = pl.ds(start, CHUNK)
            ahead = pl.ds(start, CHUNK + GROUP)
            sides = []
            for side in range(2):
                rows = pl.ds(pl.multiple_of(side * half + start, CHUNK), CHUNK)
                base = pair_ref[1, rows, :].astype(F32)
                diff = pair_ref[0, rows, :].astype(F32) - base
                sides.append([rows, base, diff] + [jnp.zeros((CHUNK, share), F32)] * 3)
            for point in range(points):
                lanes = slice(point * share, (point + 1) * share)
                even1 = tap1_ref[0, ahead, lanes][1 : 1 + CHUNK]
                even2 = tap2_ref[0, ahead, lanes][1 : 1 + CHUNK]
                odd2 = tap2_ref[1, ahead, lanes][1 : 1 + CHUNK]
                sums = (
                    tap0_ref[0, here, lanes] + tap1_ref[1, here, lanes] + even2,
                    tap0_ref[1, here, lanes] + even1 + odd2,
                )
                for side in range(2):
                    rows, base, diff, total, sum_tok, sum_base = sides[side]
                    inv = inv_ref[rows, lanes]
                    along = inv * sums[side]
                    total = total + along
                    along = along * (base + alphas[point] * diff) * (inv * inv)
                    sum_tok = sum_tok + alphas[point] * along
                    sum_base = sum_base + along
                    sides[side][3:] = [total, sum_tok, sum_base]
            for side in range(2):
                sent = side * block_half + part * CHUNK
                grad_ref[block, sent : sent + CHUNK, :] = (gain * sides[side][3]).astype(BF16)
                to_tok[side].append(gain * sides[side][4])
                to_base[side].append(gain * (sides[side][5] - sides[side][4]))
        sent = []
        for sums in (to_tok, to_base):
            row = exact_dot(ones, jnp.concatenate(sums[0] + sums[1], 0), ((1,), (1,)))
            row = row[:1] / width
            high = row.astype(BF16).astype(F32)
            sent += [high, row - high]
        sent.append(jnp.zeros((grad_ref.shape[1] - LANES - len(sent), LANES), F32))
        grad_ref[block, LANES:, :] = jnp.concatenate(sent, 0).astype(BF16)


def partial_kernel(grad_ref, out_ref):
    dests, rows, _ = out_ref.shape
    n_ctx = grad_ref.shape[0]
    each = n_ctx // dests
    spare = sum(grad_ref[block, LANES:, :].astype(F32) for block in range(n_ctx))
    sums = [spare[0:1] + spare[1:2], spare[2:3] + spare[3:4]]
    sent = []
    for value in sums:
        high = value.astype(BF16).astype(F32)
        sent += [high, value - high]
    sent.append(jnp.zeros((rows - each * LANES - len(sent), LANES), F32))
    sent = jnp.concatenate(sent, 0).astype(BF16)
    for dest in range(dests):
        for piece in range(each):
            out_ref[dest, piece * LANES : (piece + 1) * LANES, :] = grad_ref[dest * each + piece, :LANES, :]
        out_ref[dest, each * LANES :, :] = sent


def finish_kernel(grad_ref, own_ref, path_ref, attr_ref):
    points, rows, share = grad_ref.shape
    pieces = rows // LANES
    spare = sum(grad_ref[path, pieces * LANES :, :].astype(F32) for path in range(points))
    sums = jnp.concatenate([spare[0:1] + spare[1:2], spare[2:3] + spare[3:4], spare[4:10]], 0)
    order = even_first()
    columns = transposed(exact_dot(sums, order, ((1,), (0,))))
    to_tok = columns[:, 0:1]
    to_base = columns[:, 1:2]
    order = order.T.astype(BF16)
    for piece in range(pieces):
        for path in range(points):
            lanes = slice((piece * points + path) * share, (piece * points + path + 1) * share)
            tok = own_ref[0, :, lanes].astype(F32)
            base = own_ref[1, :, lanes].astype(F32)
            grad = dot(order, grad_ref[path, piece * LANES : (piece + 1) * LANES, :])
            grad = (grad - tok * to_tok - base * to_base) / points
            path_ref[:, lanes] = grad
            attr_ref[:, lanes] = (tok - base) * grad


def any_spec():
    return pl.BlockSpec(memory_space=pl.ANY)


def vmem_spec():
    return pl.BlockSpec(memory_space=pltpu.VMEM)


def hbm_spec():
    return pl.BlockSpec(memory_space=pltpu.HBM)


def call(kernel, ins, outs, scratch, flops, moved, mebibytes):
    return pl.pallas_call(
        kernel,
        in_specs=ins,
        out_specs=[spec for spec, _ in outs],
        out_shape=[shape for _, shape in outs],
        scratch_shapes=scratch,
        compiler_params=pltpu.CompilerParams(vmem_limit_bytes=mebibytes * 2**20),
        cost_estimate=pl.CostEstimate(flops=flops, bytes_accessed=moved, transcendentals=0),
    )


def shape(dims, dtype):
    return jax.ShapeDtypeStruct(dims, dtype)


def kernel_body(tokens, sub_pos, sub_base, embed, norm_gain, fir_taps, long_filter, skip_gain, cotangent):
    n_path, n_ctx = lax.axis_size("path"), lax.axis_size("ctx")
    points = n_path
    tok_rows = tokens.shape[0]
    length = tok_rows * n_ctx
    vocab, width = embed.shape
    share = width // (n_path * n_ctx)
    subs = sub_pos.shape[0] * n_ctx
    own_width = width // n_path
    cols = points * share
    half = length // 2
    tables = dft_tables(length)
    dma = pltpu.SemaphoreType.DMA
    transform_flops = 2 * length * length
    spare = 16

    msg, ids = call(
        pack_kernel,
        [hbm_spec()] * 4,
        [
            (vmem_spec(), shape((n_ctx, tok_rows + spare, share), BF16)),
            (vmem_spec(), shape((spare, LANES), F32)),
        ],
        [
            pltpu.VMEM((1, tok_rows), jnp.int32),
            pltpu.VMEM((1, sub_pos.shape[0]), jnp.int32),
            pltpu.VMEM((1, sub_pos.shape[0]), jnp.int32),
            pltpu.VMEM((tok_rows, n_ctx * share), BF16),
            dma((n_ctx + 3,)),
        ],
        length * share,
        8 * length * share,
        60,
    )(
        tokens.reshape(1, tok_rows),
        sub_pos.reshape(1, -1),
        sub_base.reshape(1, -1),
        cotangent,
    )
    msg = lax.all_to_all(msg, "ctx", 0, 0, tiled=True)

    gain = norm_gain.reshape(1, width)
    skip = skip_gain.reshape(1, n_path * share)
    gram, table, own = call(
        vocab_kernel,
        [vmem_spec(), hbm_spec()],
        [
            (vmem_spec(), shape((3 * vocab, vocab), BF16)),
            (vmem_spec(), shape((vocab, share + LANES), BF16)),
            (vmem_spec(), shape((2, tok_rows, own_width), BF16)),
        ],
        [pltpu.VMEM((vocab, width), BF16), pltpu.VMEM((vocab, vocab), F32), dma((4,))],
        2 * vocab * vocab * width,
        2 * vocab * width,
        56,
    )(ids, embed)
    spec = call(
        spectrum_kernel,
        [hbm_spec()] + [vmem_spec()] * 2,
        [(vmem_spec(), shape((4, half, share), F32))],
        [pltpu.VMEM((length, share), F32), dma],
        transform_flops * share,
        4 * length * length,
        8,
    )(long_filter, tables[0], tables[1])[0]

    wide = 4 * LANES
    signal, q_feat, k_feat, v_feat, inv, pair = call(
        functools.partial(feature_kernel, points),
        [vmem_spec()] * 5 + [hbm_spec()],
        [(vmem_spec(), shape((length, cols), BF16))]
        + [(vmem_spec(), shape((length, cols), F32))] * 4
        + [(vmem_spec(), shape((2, length, share), BF16))],
        [
            pltpu.VMEM((length, vocab), BF16),
            pltpu.VMEM((vocab, width), BF16),
            pltpu.VMEM((points, subs, LANES), F32),
            pltpu.VMEM((2 * subs, wide), F32),
            pltpu.VMEM((length, 2 * share), F32),
            pltpu.VMEM((length, (2 + points) * share), F32),
            pltpu.VMEM((2, GROUP + half, cols), F32),
            dma,
        ],
        2 * length * vocab * 3 * share,
        2 * vocab * width + 16 * length * cols,
        44,
    )(msg, gram, table, fir_taps, gain, embed)
    conv = call(
        functools.partial(forward_kernel, points),
        [vmem_spec()] * 7,
        [(vmem_spec(), shape((length, cols), BF16))],
        [pltpu.VMEM((2 * length, cols), BF16)],
        2 * transform_flops * cols,
        4 * length * length,
        12,
    )(signal, skip, *tables, spec)[0]

    grad = call(
        functools.partial(backward_kernel, points, width),
        [vmem_spec()] * 15,
        [(vmem_spec(), shape((n_ctx, tok_rows + spare, share), BF16))],
        [
            pltpu.VMEM((length, cols), BF16),
            pltpu.VMEM((2 * length, cols), BF16),
        ]
        + [pltpu.VMEM((2, half + GROUP, cols), F32)] * 3,
        2 * transform_flops * cols,
        4 * length * length + 16 * length * cols,
        18,
    )(msg, pair, fir_taps, gain, skip, q_feat, k_feat, v_feat, inv, conv, *tables, spec)[0]

    grad = lax.all_to_all(grad, "ctx", 0, 0, tiled=True)
    each = n_ctx // n_path
    grad = call(
        partial_kernel,
        [vmem_spec()],
        [(vmem_spec(), shape((n_path, each * tok_rows + spare, share), BF16))],
        [],
        spare * LANES * n_ctx,
        4 * length * share,
        4,
    )(grad)[0]
    grad = lax.all_to_all(grad, "path", 0, 0, tiled=True)
    out = shape((tok_rows, own_width), F32)
    return tuple(
        call(
            finish_kernel,
            [vmem_spec()] * 2,
            [(vmem_spec(), out), (vmem_spec(), out)],
            [],
            8 * tok_rows * own_width,
            14 * tok_rows * own_width,
            8,
        )(grad, own)
    )


def plain_body(tokens, sub_pos, sub_base, embed, norm_gain, fir_taps, long_filter, skip_gain, cotangent):
    n_path, n_ctx = lax.axis_size("path"), lax.axis_size("ctx")
    path, ctx = lax.axis_index("path"), lax.axis_index("ctx")
    points = n_path
    tok_rows = tokens.shape[0]
    length = tok_rows * n_ctx
    width = embed.shape[1]
    share = width // (n_path * n_ctx)
    own_width = width // n_path
    first = (ctx * n_path + path) * share
    alphas = ((jnp.arange(points, dtype=jnp.int32)).astype(F32) + 0.5) / points
    alphas = alphas[:, None, None]

    local = jnp.arange(tok_rows, dtype=jnp.int32)[:, None] + ctx * tok_rows == sub_pos[None, :]
    put = jnp.sum(jnp.where(local, sub_base[None, :], 0), 1)
    base_ids = jnp.where(jnp.any(local, 1), put, tokens)
    rows_tok = jnp.take(embed, tokens, axis=0).astype(F32)
    rows_base = jnp.take(embed, base_ids, axis=0).astype(F32)
    rows_in = rows_base[None] + alphas * (rows_tok - rows_base)[None]
    inv = lax.rsqrt(jnp.mean(rows_in * rows_in, -1) + EPS)
    inv = lax.all_gather(inv, "ctx", axis=1, tiled=True)[:, :, None]
    all_tok = lax.all_gather(tokens, "ctx", tiled=True)
    all_base = lax.all_gather(base_ids, "ctx", tiled=True)

    cot = cotangent.reshape(tok_rows, n_ctx, n_path, share)
    cot = lax.dynamic_index_in_dim(cot, path, 2, keepdims=False)
    cot = lax.all_to_all(cot.transpose(1, 0, 2), "ctx", 0, 0, tiled=True)
    upstream = cot.reshape(1, length, share).astype(F32)
    mine = lax.dynamic_slice_in_dim(embed, first, share, 1)
    gain = lax.dynamic_slice_in_dim(norm_gain, first, share, 0)
    taps = lax.dynamic_slice_in_dim(fir_taps, first, share, 2).astype(F32)
    filt = lax.dynamic_slice_in_dim(long_filter, path * share, share, 1)
    skip = lax.dynamic_slice_in_dim(skip_gain, path * share, share, 0)

    emb_tok = jnp.take(mine, all_tok, axis=0).astype(F32)
    emb_base = jnp.take(mine, all_base, axis=0).astype(F32)
    inputs = emb_base[None] + alphas * (emb_tok - emb_base)[None]
    normed = rounded(inputs * inv * gain)
    q_feat, k_feat, v_feat = (
        taps[f, 0] * normed + taps[f, 1] * shifted(normed, 1) + taps[f, 2] * shifted(normed, 2)
        for f in range(3)
    )
    filter_spec = spectrum(filt[None])
    conv = rounded(long_conv(rounded(k_feat * v_feat), filter_spec, skip, False))
    grad_z = rounded(long_conv(rounded(upstream * q_feat), filter_spec, skip, True))
    grads = (rounded(upstream * conv), rounded(grad_z * v_feat), rounded(grad_z * k_feat))
    by_tap = [sum(taps[f, tap] * grads[f] for f in range(3)) for tap in range(3)]
    scaled = gain * (by_tap[0] + shifted(by_tap[1], -1) + shifted(by_tap[2], -2))
    grad = jnp.sum(inv * scaled, 0).astype(BF16)
    along = jnp.sum(inputs * scaled, -1, keepdims=True) * inv**3 / width
    part = jnp.stack([jnp.sum(alphas * along, 0)[:, 0], jnp.sum((1.0 - alphas) * along, 0)[:, 0]])
    part = lax.psum(part, ("path", "ctx"))
    part = lax.dynamic_slice_in_dim(part, ctx * tok_rows, tok_rows, 1)

    back = lax.all_to_all(grad.reshape(n_ctx, tok_rows, share), "ctx", 0, 0, tiled=True)
    back = back.reshape(n_path, n_ctx // n_path, tok_rows, share)
    back = lax.all_to_all(back, "path", 0, 0, tiled=True).astype(F32)
    back = back.transpose(2, 1, 0, 3).reshape(tok_rows, own_width)
    own_tok = lax.dynamic_slice_in_dim(rows_tok, path * own_width, own_width, 1)
    own_base = lax.dynamic_slice_in_dim(rows_base, path * own_width, own_width, 1)
    grad = (back - own_tok * part[0][:, None] - own_base * part[1][:, None]) / points
    return (grad, (own_tok - own_base) * grad)


def body(tokens, sub_pos, sub_base, embed, *rest):
    n_path, n_ctx = lax.axis_size("path"), lax.axis_size("ctx")
    tok_rows = tokens.shape[0]
    share = embed.shape[1] // (n_path * n_ctx)
    tables = 4 * (tok_rows * n_ctx) ** 2
    fits = share == LANES and tok_rows == LANES and n_ctx == GROUP and tables <= TABLE_BYTES
    chosen = kernel_body if fits else plain_body
    return chosen(tokens, sub_pos, sub_base, embed, *rest)


def solution(mesh):
    return jax.shard_map(
        body,
        mesh=mesh,
        in_specs=(
            P("ctx"),
            P("ctx"),
            P("ctx"),
            P(),
            P(),
            P(),
            P(None, "ctx"),
            P("ctx"),
            P("ctx", None),
        ),
        out_specs=(P("ctx", "path"), P("ctx", "path")),
        check_vma=False,
    )
```

```python
import functools

import jax
import jax.numpy as jnp
import ml_dtypes
import numpy as np
from jax import lax
from jax.experimental import pallas as pl
from jax.experimental.pallas import tpu as pltpu
from jax.sharding import PartitionSpec as P

LANES = 128
GROUP = 8
FREQ_ROWS = 256
CHUNK = 32
EPS = 1e-06
CANCEL = 0.004
TABLE_BYTES = 4 * 2**20
F32 = jnp.float32
BF16 = jnp.bfloat16
precise = lax.Precision.HIGH


def angle_tables(length):
    outer_size = 64
    inner_size = length // outer_size
    outer_idx = jnp.arange(outer_size, dtype=jnp.int32)
    inner_idx = jnp.arange(inner_size, dtype=jnp.int32)
    outer_angle = (
        2.0 * jnp.pi / outer_size
        * (outer_idx[:, None] * outer_idx[None, :] % outer_size).astype(F32)
    )
    inner_angle = (
        2.0 * jnp.pi / inner_size
        * (inner_idx[:, None] * inner_idx[None, :] % inner_size).astype(F32)
    )
    twist_angle = (
        2.0 * jnp.pi / length
        * (outer_idx[:, None] * inner_idx[None, :] % length).astype(F32)
    )
    return (outer_angle, inner_angle, twist_angle)


def complex_table(angle, sign):
    cosine = jnp.cos(angle)
    sine = sign * jnp.sin(angle)
    return jnp.stack([jnp.stack([cosine, sine]), jnp.stack([-sine, cosine])])


def twisted(values, angle, sign):
    cosine = jnp.cos(angle)[None, :, :, None]
    sine = sign * jnp.sin(angle)[None, :, :, None]
    real_part = values[:, 0]
    imag_part = values[:, 1]
    return jnp.stack(
        [real_part * cosine - imag_part * sine, real_part * sine + imag_part * cosine], 1
    )


def spectrum(signal):
    batch, half, width = signal.shape
    length = 2 * half
    outer_angle, inner_angle, twist_angle = angle_tables(length)
    outer_size = outer_angle.shape[0]
    inner_size = inner_angle.shape[0]
    folded = signal.reshape(batch, outer_size // 2, inner_size, width)
    used = outer_angle[:, : outer_size // 2]
    outer_table = jnp.stack([jnp.cos(used), -jnp.sin(used)])
    first = jnp.einsum("rka,pabc->prkbc", outer_table, folded, precision=precise)
    turned = twisted(first, twist_angle, -1.0)
    return jnp.einsum(
        "prkbc,rsbm->pskmc", turned, complex_table(inner_angle, -1.0), precision=precise
    )


def inverse(spec):
    batch, parts, outer_size, inner_size, width = spec.shape
    length = outer_size * inner_size
    outer_angle, inner_angle, twist_angle = angle_tables(length)
    back = jnp.einsum("pskmc,stmb->ptkbc", spec, complex_table(inner_angle, 1.0), precision=precise)
    turned = twisted(back, twist_angle, 1.0)
    used = outer_angle[: outer_size // 2]
    outer_table = jnp.stack([jnp.cos(used), -jnp.sin(used)])
    result = jnp.einsum("rak,prkbc->pabc", outer_table, turned, precision=precise)
    return (result / length).reshape(batch, length // 2, width)


def long_conv(signal, filter_spec, skip_gain, adjoint):
    spec = spectrum(signal)
    sig_real = spec[:, 0]
    sig_imag = spec[:, 1]
    filt_real = filter_spec[:, 0]
    filt_imag = filter_spec[:, 1]
    if adjoint:
        prod_real = sig_real * filt_real + sig_imag * filt_imag
        prod_imag = sig_imag * filt_real - sig_real * filt_imag
    else:
        prod_real = sig_real * filt_real - sig_imag * filt_imag
        prod_imag = sig_real * filt_imag + sig_imag * filt_real
    return inverse(jnp.stack([prod_real, prod_imag], 1)) + skip_gain * signal


def rounded(value):
    return value.astype(BF16).astype(F32)


def shifted(values, step):
    zeros = jnp.zeros_like(values[:, : abs(step)])
    if step > 0:
        return jnp.concatenate([zeros, values[:, :-step]], 1)
    return jnp.concatenate([values[:, -step:], zeros], 1)


@functools.lru_cache(maxsize=None)
def dft_tables(length):
    half = length // 2
    freq = 4 * np.arange(half, dtype=np.int64) + 1
    place = np.arange(half, dtype=np.int64)
    tables = []
    for offset in (0, 1):
        turns = freq[:, None] * (2 * place + offset)[None, :] % (8 * half)
        angle = turns * (2.0 * np.pi / (8 * half))
        cosine = np.cos(angle).astype(ml_dtypes.bfloat16)
        sine = np.sin(angle).astype(ml_dtypes.bfloat16)
        tables.append((np.concatenate([cosine, sine], 0), np.concatenate([cosine.T, sine.T], 1)))
    return (tables[0][0], tables[1][0], tables[0][1], tables[1][1])


def transposed(rows):
    count = rows.shape[0]
    if count < LANES:
        rows = jnp.concatenate([rows, jnp.zeros((LANES - count, LANES), F32)], 0)
    return rows.T


def dot(left, right):
    return jnp.dot(left, right, preferred_element_type=F32)


def exact_dot(left, right, dims):
    return lax.dot_general(
        left, right, (dims, ((), ())), precision=lax.Precision.HIGHEST, preferred_element_type=F32
    )


def iota(dims, axis):
    return lax.broadcasted_iota(jnp.int32, dims, axis)


def even_first():
    row = iota((LANES, LANES), 0)
    half = LANES // 2
    source = jnp.where(row < half, 2 * row, 2 * (row - half) + 1)
    return (iota((LANES, LANES), 1) == source).astype(F32)


def hot(ids, vocab):
    lane = iota(ids.shape, 1).astype(F32)
    parts = [
        (ids == lane + float(column * LANES)).astype(F32).astype(BF16)
        for column in range(vocab // LANES)
    ]
    return jnp.concatenate(parts, 1)


def joined(block, kind):
    return 256.0 * block[2 * kind : 2 * kind + 1] + block[2 * kind + 1 : 2 * kind + 2]


def pack_kernel(
    tok_hbm, pos_hbm, put_hbm, cot_hbm, msg_ref, ids_ref, tok_ref, pos_ref, put_ref, cot_ref, sems
):
    dests, rows, share = msg_ref.shape
    tok_rows = cot_hbm.shape[0]
    n_path = cot_hbm.shape[1] // (dests * share)
    path = lax.axis_index("path")
    moves = [(tok_hbm, tok_ref), (pos_hbm, pos_ref), (put_hbm, put_ref)]
    for dest in range(dests):
        lanes = pl.ds(pl.multiple_of((dest * n_path + path) * share, LANES), share)
        moves.append((cot_hbm.at[:, lanes], cot_ref.at[:, pl.ds(dest * share, share)]))
    copies = [
        pltpu.make_async_copy(source, target, sems.at[index])
        for index, (source, target) in enumerate(moves)
    ]
    for copy in copies:
        copy.start()
    order = even_first().astype(BF16)
    for copy in copies[:3]:
        copy.wait()
    lists = []
    for ref in (tok_ref, pos_ref, put_ref):
        value = ref[...].astype(F32)
        if value.shape[1] < LANES:
            value = jnp.concatenate([value, jnp.zeros((1, LANES - value.shape[1]), F32)], 1)
        high = jnp.floor(value * (1.0 / 256.0))
        lists += [high, value - 256.0 * high]
    lists.append(jnp.zeros((rows - tok_rows - len(lists), LANES), F32))
    ids = jnp.concatenate(lists, 0)
    ids_ref[...] = ids
    turned = lax.dot_general(
        ids.astype(BF16), order, (((1,), (1,)), ((), ())), preferred_element_type=F32
    )
    ids = jnp.where(iota(ids.shape, 0) < 2, turned, ids).astype(BF16)
    for dest in range(dests):
        msg_ref[dest, tok_rows:, :] = ids
    for copy in copies[3:]:
        copy.wait()
    turned = dot(order, cot_ref[...]).astype(BF16)
    for dest in range(dests):
        msg_ref[dest, :tok_rows, :] = turned[:, dest * share : (dest + 1) * share]


def prepare_kernel(
    filt_hbm, even_hbm, odd_hbm, embed_hbm, after_ref,
    spec_ref, gram_ref,
    filt_ref, even_ref, odd_ref, embed_ref, sum_ref, sems,
):
    length, share = filt_ref.shape
    half = length // 2
    vocab, width = embed_ref.shape
    pieces = sems.shape[0] - 3
    wide = width // pieces
    path = lax.axis_index("path")
    lanes = pl.ds(pl.multiple_of(path * share, LANES), share)
    moves = [(filt_hbm.at[:, lanes], filt_ref), (even_hbm, even_ref), (odd_hbm, odd_ref)]
    for index in range(pieces):
        lanes = pl.ds(index * wide, wide)
        moves.append((embed_hbm.at[:, lanes], embed_ref.at[:, lanes]))
    copies = [
        pltpu.make_async_copy(source, target, sems.at[index])
        for index, (source, target) in enumerate(moves)
    ]
    for copy in copies:
        copy.start()

    copies[0].wait()
    parts = []
    for offset in range(2):
        value = filt_ref[pl.ds(offset, half, stride=2), :] * (1.0 / length)
        high = value.astype(BF16)
        parts.append(jnp.concatenate([high, (value - high.astype(F32)).astype(BF16)], 1))
    copies[1].wait()
    copies[2].wait()
    for index in range(half // FREQ_ROWS):
        found = []
        for table, part in ((even_ref, parts[0]), (odd_ref, parts[1])):
            for offset in (0, half):
                both = dot(table[pl.ds(offset + index * FREQ_ROWS, FREQ_ROWS), :], part)
                found.append(both[:, :share] + both[:, share:])
        rows = pl.ds(index * FREQ_ROWS, FREQ_ROWS)
        spec_ref[0, rows, :] = found[0] + found[2]
        spec_ref[1, rows, :] = -found[1] - found[3]
        spec_ref[2, rows, :] = found[0] - found[2]
        spec_ref[3, rows, :] = found[3] - found[1]

    for index in range(pieces):
        copies[3 + index].wait()
        part = embed_ref[:, index * wide : (index + 1) * wide]
        found = lax.dot_general(part, part, (((1,), (1,)), ((), ())), preferred_element_type=F32)
        if index == 0:
            sum_ref[...] = found
        else:
            sum_ref[...] += found
    first = (lax.axis_index("ctx") * lax.axis_size("path") + path) * share
    mine = embed_ref[:, pl.ds(pl.multiple_of(first, LANES), share)]
    same = iota((LANES, LANES), 0) == iota((LANES, LANES), 1)
    lane = iota((LANES, LANES), 1)
    below = 3 * vocab
    for block in range(vocab // LANES):
        rows = slice(block * LANES, (block + 1) * LANES)
        value = sum_ref[rows, :]
        norm = jnp.sum(jnp.where(same, value[:, rows], 0.0), 1, keepdims=True)
        inv = jnp.broadcast_to(lax.rsqrt(norm / width + EPS), (LANES, LANES))
        high = inv.astype(BF16).astype(F32)
        inv = jnp.where(lane < LANES // 2, high, inv - high).astype(BF16)
        side, start = block * LANES // (vocab // 2), block * LANES % (vocab // 2)
        into = slice(below + start, below + start + LANES)
        left = side * (share + LANES)
        gram_ref[into, left : left + share] = mine[rows]
        gram_ref[into, left + share : left + share + LANES] = inv
        for part in range(3):
            high = value.astype(BF16)
            gram_ref[part * vocab + block * LANES : part * vocab + (block + 1) * LANES, :] = high
            value = value - high.astype(F32)


def own_kernel(ids_ref, embed_hbm, grad_ref, own_ref, embed_ref, sem):
    vocab = embed_ref.shape[0]
    own_width = own_ref.shape[2]
    lanes = pl.ds(pl.multiple_of(lax.axis_index("path") * own_width, LANES), own_width)
    copy = pltpu.make_async_copy(embed_hbm.at[:, lanes], embed_ref, sem)
    copy.start()
    ids = ids_ref[...]
    columns = transposed(jnp.concatenate([joined(ids, kind) for kind in range(3)], 0))
    tok = jnp.broadcast_to(columns[:, 0:1], (LANES, LANES))
    place = jnp.broadcast_to(joined(ids, 1), (LANES, LANES))
    put = jnp.broadcast_to(joined(ids, 2), (LANES, LANES))
    first = lax.axis_index("ctx") * LANES
    subs = LANES // GROUP
    here = (place == (iota((LANES, LANES), 0) + first).astype(F32)) & (iota((LANES, LANES), 1) < subs)
    found = jnp.max(jnp.where(here, put, -1.0), 1, keepdims=True)
    base = jnp.where(found >= 0.0, found, tok)
    hots = jnp.concatenate([hot(tok, vocab), hot(base, vocab)], 0)
    copy.wait()
    both = dot(hots, embed_ref[...]).astype(BF16)
    own_ref[0] = both[:LANES]
    own_ref[1] = both[LANES:]


def transform(even_ref, odd_ref, signal_ref, spec_ref, prod_ref, points, adjoint):
    half = even_ref.shape[1]
    share = spec_ref.shape[2]
    for index in range(half // FREQ_ROWS):
        rows = pl.ds(index * FREQ_ROWS, FREQ_ROWS)
        after = pl.ds(half + index * FREQ_ROWS, FREQ_ROWS)
        even_real = dot(even_ref[rows, :], signal_ref[:half, :])
        even_imag = dot(even_ref[after, :], signal_ref[:half, :])
        odd_real = dot(odd_ref[rows, :], signal_ref[half:, :])
        odd_imag = dot(odd_ref[after, :], signal_ref[half:, :])
        filt = [spec_ref[part, rows, :] for part in range(4)]
        for point in range(points):
            lanes = slice(point * share, (point + 1) * share)
            prods = []
            for part, sign in ((0, 1.0), (2, -1.0)):
                real = even_real[:, lanes] + sign * odd_real[:, lanes]
                imag = even_imag[:, lanes] + sign * odd_imag[:, lanes]
                if adjoint:
                    prods.append(real * filt[part] - imag * filt[part + 1])
                    prods.append(real * filt[part + 1] + imag * filt[part])
                else:
                    prods.append(real * filt[part] + imag * filt[part + 1])
                    prods.append(imag * filt[part] - real * filt[part + 1])
            sums = (prods[0] + prods[2], prods[1] + prods[3], prods[0] - prods[2], prods[1] - prods[3])
            for part, value in enumerate(sums):
                into = pl.ds(part * half + index * FREQ_ROWS, FREQ_ROWS)
                prod_ref[into, lanes] = value.astype(BF16)


def inverse_rows(back_refs, prod_ref, rows):
    length = 2 * back_refs[0].shape[0]
    return [
        dot(ref[rows, :], prod_ref[offset : offset + length, :])
        for ref, offset in zip(back_refs, (0, length))
    ]


def ids_kernel(vocab, msg_ref, hot_ref, subs_ref, put_ref):
    length = hot_ref.shape[0]
    half = length // 2
    n_ctx = msg_ref.shape[0]
    block_half = LANES // 2
    per_block = LANES // GROUP
    subs = n_ctx * per_block
    blocks = [msg_ref[block, LANES:, :].astype(F32) for block in range(n_ctx)]
    toks = transposed(jnp.concatenate([joined(block, 0) for block in blocks], 0))
    spread = sum(
        blocks[block] if block == 0 else pltpu.roll(blocks[block], block * per_block, 1)
        for block in range(n_ctx)
    )
    place = joined(spread, 1)
    put = joined(spread, 2)
    back = jnp.floor(place * 0.5)
    place = back + (place - 2.0 * back) * half
    columns = transposed(jnp.concatenate([place, put], 0))
    for block in range(n_ctx):
        column = jnp.broadcast_to(toks[:, block : block + 1], (LANES, LANES))
        rows = hot(column, vocab)
        hot_ref[block * block_half : (block + 1) * block_half, :] = rows[:block_half]
        hot_ref[half + block * block_half : half + (block + 1) * block_half, :] = rows[block_half:]
    subs_ref[subs:, :] = hot(jnp.broadcast_to(columns[:, 1:2], (subs, LANES)), vocab)
    pick = jnp.concatenate(
        [
            (columns[:, 0:1] == (iota((subs, LANES), 1) + part * LANES).astype(F32)).astype(F32).astype(BF16)
            for part in range(length // LANES)
        ],
        1,
    )
    for index in range(length // LANES):
        row = (iota((LANES, subs), 0) + index * LANES).astype(F32)
        here = (row == place[:, :subs]).astype(F32).astype(BF16)
        put_ref[index * LANES : (index + 1) * LANES, :] = jnp.concatenate([here, here], 1)
    subs_ref[:subs, :] = dot(pick, hot_ref[...]).astype(BF16)


def feature_kernel(
    points, hot_ref, subs_hot_ref, put_ref, gram_ref, taps_ref, gain_ref, embed_hbm,
    signal_ref, q_ref, k_ref, v_ref, inv_ref, pair_ref,
    embed_ref, sums_ref, found_ref, look_ref, subs_ref, norm_ref, sem,
):
    length = signal_ref.shape[0]
    half = length // 2
    vocab, width = embed_hbm.shape
    share = pair_ref.shape[2]
    subs = subs_hot_ref.shape[0] // 2
    first = (lax.axis_index("ctx") * points + lax.axis_index("path")) * share
    first = pl.multiple_of(first, LANES)
    below = 3 * vocab
    table = jnp.concatenate(
        [gram_ref[below:, : share + LANES], gram_ref[below:, share + LANES :]], 0
    )

    alphas = [(point + 0.5) / points for point in range(points)]
    hots = subs_hot_ref[...]
    found = dot(jnp.concatenate([hots] * 3, 1), gram_ref[:below, :])
    hot_tok32, hot_base32 = hots[:subs].astype(F32), hots[subs:].astype(F32)
    tok_tok = jnp.sum(found[:subs] * hot_tok32, 1, keepdims=True)
    tok_base = jnp.sum(found[:subs] * hot_base32, 1, keepdims=True)
    base_base = jnp.sum(found[subs:] * hot_base32, 1, keepdims=True)
    cancels = jnp.zeros((subs, 1), F32)
    for point in range(points):
        alpha = alphas[point]
        terms = (1.0 - alpha) ** 2 * base_base + alpha**2 * tok_tok
        total = terms + 2.0 * alpha * (1.0 - alpha) * tok_base
        cancels = jnp.maximum(cancels, (total < CANCEL * terms).astype(F32))
        inv = lax.rsqrt(jnp.maximum(total, 0.0) / width + EPS)
        sums_ref[point] = jnp.broadcast_to(inv, (subs, LANES))

    @pl.when(jnp.max(cancels) > 0.5)
    def _():
        copy = pltpu.make_async_copy(embed_hbm, embed_ref, sem)
        copy.start()
        sums_ref[...] = jnp.zeros_like(sums_ref)
        copy.wait()
        wide = found_ref.shape[1]

        @pl.loop(0, width // wide)
        def _(step):
            lanes = pl.ds(pl.multiple_of(step * wide, wide), wide)
            found_ref[...] = dot(hots, embed_ref[:, lanes])
            for block in range(subs // GROUP):
                rows = slice(block * GROUP, (block + 1) * GROUP)
                sums = [sums_ref[point, rows, :] for point in range(points)]
                for column in range(wide // LANES):
                    cut = slice(column * LANES, (column + 1) * LANES)
                    base = found_ref[subs + block * GROUP : subs + (block + 1) * GROUP, cut]
                    diff = found_ref[rows, cut] - base
                    for point in range(points):
                        value = base + alphas[point] * diff
                        sums[point] = sums[point] + value * value
                for point in range(points):
                    sums_ref[point, rows, :] = sums[point]

        for point in range(points):
            mean = jnp.sum(sums_ref[point], 1, keepdims=True) / width
            sums_ref[point] = jnp.broadcast_to(lax.rsqrt(mean + EPS), (subs, LANES))

    high = [dot(hots[subs:], table[:, :share]), jnp.ones((subs, LANES), F32)]
    low = [jnp.zeros((subs, LANES), F32)] * 2
    for point in range(points):
        inv = sums_ref[point]
        high.append(inv.astype(BF16).astype(F32))
        low.append(inv - high[-1])
    held = jnp.concatenate([jnp.concatenate(high, 1), jnp.concatenate(low, 1)], 0).astype(BF16)
    for index in range(length // FREQ_ROWS):
        rows = pl.ds(index * FREQ_ROWS, FREQ_ROWS)
        look_ref[rows, :] = dot(hot_ref[rows, :], table)
        subs_ref[rows, :] = dot(put_ref[rows, :], held)

    cols = points * share
    norm_ref[:, :GROUP, :] = jnp.zeros((2, GROUP, cols), F32)
    gain = gain_ref[:, pl.ds(first, share)]
    taps = [taps_ref[f, :, pl.ds(first, share)].astype(F32) for f in range(3)]
    taps = [[taps[f][tap : tap + 1] for tap in range(3)] for f in range(3)]

    @pl.loop(0, half // CHUNK)
    def _(step):
        start = pl.multiple_of(step * CHUNK, CHUNK)
        sides = []
        for side in range(2):
            rows = pl.ds(pl.multiple_of(side * half + start, CHUNK), CHUNK)
            tok = look_ref[rows, :share]
            inv = look_ref[rows, share:]
            inv = inv + pltpu.roll(inv, LANES // 2, 1)
            chosen = subs_ref[rows, share : 2 * share] > 0.5
            base = jnp.where(chosen, subs_ref[rows, :share], tok)
            pair_ref[0, rows, :] = tok.astype(BF16)
            pair_ref[1, rows, :] = base.astype(BF16)
            sides.append((rows, base, tok - base, inv, chosen))
        for point in range(points):
            lanes = slice(point * share, (point + 1) * share)
            nows, backs = [], []
            for side, (rows, base, diff, inv_tok, chosen) in enumerate(sides):
                inv = jnp.where(
                    chosen, subs_ref[rows, (2 + point) * share : (3 + point) * share], inv_tok
                )
                inv_ref[rows, lanes] = inv
                now = rounded((base + alphas[point] * diff) * inv * gain)
                norm_ref[side, pl.ds(start + GROUP, CHUNK), lanes] = now
                window = norm_ref[side, pl.ds(start, CHUNK + GROUP), lanes]
                nows.append(now)
                backs.append(window[GROUP - 1 : GROUP - 1 + CHUNK])
            recent = ((nows[0], backs[1], backs[0]), (nows[1], nows[0], backs[1]))
            for side in range(2):
                rows = sides[side][0]
                feats = [sum(taps[f][tap] * recent[side][tap] for tap in range(3)) for f in range(3)]
                q_ref[rows, lanes] = feats[0]
                k_ref[rows, lanes] = feats[1]
                v_ref[rows, lanes] = feats[2]
                signal_ref[rows, lanes] = (feats[1] * feats[2]).astype(BF16)


def forward_kernel(
    points, signal_ref, skip_ref, even_ref, odd_ref, even_back_ref, odd_back_ref, spec_ref, conv_ref, prod_ref
):
    half = even_ref.shape[1]
    share = spec_ref.shape[2]
    transform(even_ref, odd_ref, signal_ref, spec_ref, prod_ref, points, False)
    skip = skip_ref[:, pl.ds(pl.multiple_of(lax.axis_index("path") * share, LANES), share)]
    skip = jnp.concatenate([skip] * points, 1)
    for index in range(half // FREQ_ROWS):
        found = inverse_rows((even_back_ref, odd_back_ref), prod_ref, pl.ds(index * FREQ_ROWS, FREQ_ROWS))
        for side in range(2):
            rows = pl.ds(side * half + index * FREQ_ROWS, FREQ_ROWS)
            conv_ref[rows, :] = (found[side] + skip * signal_ref[rows, :].astype(F32)).astype(BF16)


def backward_kernel(
    points, width, msg_ref, pair_ref, taps_ref, gain_ref, skip_ref,
    q_ref, k_ref, v_ref, inv_ref, conv_ref, even_ref, odd_ref, even_back_ref, odd_back_ref, spec_ref,
    grad_ref,
    signal_ref, prod_ref, tap0_ref, tap1_ref, tap2_ref,
):
    half = even_ref.shape[1]
    share = pair_ref.shape[2]
    n_ctx = msg_ref.shape[0]
    block_half = LANES // 2
    path = lax.axis_index("path")
    first = pl.multiple_of((lax.axis_index("ctx") * points + path) * share, LANES)

    @pl.loop(0, n_ctx)
    def _(block):
        for side in range(2):
            rows = pl.ds(pl.multiple_of(side * half + block * block_half, block_half), block_half)
            upstream = msg_ref[block, side * block_half : (side + 1) * block_half, :].astype(F32)
            for point in range(points):
                lanes = slice(point * share, (point + 1) * share)
                signal_ref[rows, lanes] = (upstream * q_ref[rows, lanes]).astype(BF16)

    transform(even_ref, odd_ref, signal_ref, spec_ref, prod_ref, points, True)
    skip = skip_ref[:, pl.ds(pl.multiple_of(path * share, LANES), share)]
    gain = gain_ref[:, pl.ds(first, share)]
    taps = [taps_ref[f, :, pl.ds(first, share)].astype(F32) for f in range(3)]
    taps_refs = (tap0_ref, tap1_ref, tap2_ref)
    for ref in taps_refs:
        ref[:, half:, :] = jnp.zeros((2, GROUP, points * share), F32)
    for index in range(half // FREQ_ROWS):
        found = inverse_rows((even_back_ref, odd_back_ref), prod_ref, pl.ds(index * FREQ_ROWS, FREQ_ROWS))
        for side in range(2):
            for part in range(FREQ_ROWS // CHUNK):
                inside = slice(part * CHUNK, (part + 1) * CHUNK)
                start = index * FREQ_ROWS + part * CHUNK
                rows = pl.ds(side * half + start, CHUNK)
                block = start // block_half
                sent = start % block_half + side * block_half
                upstream = msg_ref[block, sent : sent + CHUNK, :].astype(F32)
                for point in range(points):
                    lanes = slice(point * share, (point + 1) * share)
                    grad_z = found[side][inside, lanes] + skip * signal_ref[rows, lanes].astype(F32)
                    grads = (
                        upstream * conv_ref[rows, lanes].astype(F32),
                        grad_z * v_ref[rows, lanes],
                        grad_z * k_ref[rows, lanes],
                    )
                    for tap, ref in enumerate(taps_refs):
                        ref[side, pl.ds(start, CHUNK), lanes] = sum(
                            taps[f][tap : tap + 1] * grads[f] for f in range(3)
                        )

    alphas = [(point + 0.5) / points for point in range(points)]
    ones = jnp.ones((GROUP, share), F32)

    @pl.loop(0, n_ctx)
    def _(block):
        to_tok, to_base = [[], []], [[], []]
        for part in range(block_half // CHUNK):
            start = pl.multiple_of(block * block_half + part * CHUNK, CHUNK)
            here = pl.ds(start, CHUNK)
            ahead = pl.ds(start, CHUNK + GROUP)
            sides = []
            for side in range(2):
                rows = pl.ds(pl.multiple_of(side * half + start, CHUNK), CHUNK)
                base = pair_ref[1, rows, :].astype(F32)
                diff = pair_ref[0, rows, :].astype(F32) - base
                sides.append([rows, base, diff] + [jnp.zeros((CHUNK, share), F32)] * 3)
            for point in range(points):
                lanes = slice(point * share, (point + 1) * share)
                even1 = tap1_ref[0, ahead, lanes][1 : 1 + CHUNK]
                even2 = tap2_ref[0, ahead, lanes][1 : 1 + CHUNK]
                odd2 = tap2_ref[1, ahead, lanes][1 : 1 + CHUNK]
                sums = (
                    tap0_ref[0, here, lanes] + tap1_ref[1, here, lanes] + even2,
                    tap0_ref[1, here, lanes] + even1 + odd2,
                )
                for side in range(2):
                    rows, base, diff, total, sum_tok, sum_base = sides[side]
                    inv = inv_ref[rows, lanes]
                    along = inv * sums[side]
                    total = total + along
                    along = along * (base + alphas[point] * diff) * (inv * inv)
                    sum_tok = sum_tok + alphas[point] * along
                    sum_base = sum_base + along
                    sides[side][3:] = [total, sum_tok, sum_base]
            for side in range(2):
                sent = side * block_half + part * CHUNK
                grad_ref[block, sent : sent + CHUNK, :] = (gain * sides[side][3]).astype(BF16)
                to_tok[side].append(gain * sides[side][4])
                to_base[side].append(gain * (sides[side][5] - sides[side][4]))
        sent = []
        for sums in (to_tok, to_base):
            row = exact_dot(ones, jnp.concatenate(sums[0] + sums[1], 0), ((1,), (1,)))
            row = row[:1] / width
            high = row.astype(BF16).astype(F32)
            sent += [high, row - high]
        sent.append(jnp.zeros((grad_ref.shape[1] - LANES - len(sent), LANES), F32))
        grad_ref[block, LANES:, :] = jnp.concatenate(sent, 0).astype(BF16)


def partial_kernel(grad_ref, out_ref):
    dests, rows, _ = out_ref.shape
    n_ctx = grad_ref.shape[0]
    each = n_ctx // dests
    spare = sum(grad_ref[block, LANES:, :].astype(F32) for block in range(n_ctx))
    sums = [spare[0:1] + spare[1:2], spare[2:3] + spare[3:4]]
    sent = []
    for value in sums:
        high = value.astype(BF16).astype(F32)
        sent += [high, value - high]
    sent.append(jnp.zeros((rows - each * LANES - len(sent), LANES), F32))
    sent = jnp.concatenate(sent, 0).astype(BF16)
    for dest in range(dests):
        for piece in range(each):
            out_ref[dest, piece * LANES : (piece + 1) * LANES, :] = grad_ref[dest * each + piece, :LANES, :]
        out_ref[dest, each * LANES :, :] = sent


def finish_kernel(grad_ref, own_ref, path_ref, attr_ref):
    points, rows, share = grad_ref.shape
    pieces = rows // LANES
    spare = sum(grad_ref[path, pieces * LANES :, :].astype(F32) for path in range(points))
    sums = jnp.concatenate([spare[0:1] + spare[1:2], spare[2:3] + spare[3:4], spare[4:10]], 0)
    order = even_first()
    columns = transposed(exact_dot(sums, order, ((1,), (0,))))
    to_tok = columns[:, 0:1]
    to_base = columns[:, 1:2]
    order = order.T.astype(BF16)
    for piece in range(pieces):
        for path in range(points):
            lanes = slice((piece * points + path) * share, (piece * points + path + 1) * share)
            tok = own_ref[0, :, lanes].astype(F32)
            base = own_ref[1, :, lanes].astype(F32)
            grad = dot(order, grad_ref[path, piece * LANES : (piece + 1) * LANES, :])
            grad = (grad - tok * to_tok - base * to_base) / points
            path_ref[:, lanes] = grad
            attr_ref[:, lanes] = (tok - base) * grad


def any_spec():
    return pl.BlockSpec(memory_space=pl.ANY)


def vmem_spec():
    return pl.BlockSpec(memory_space=pltpu.VMEM)


def hbm_spec():
    return pl.BlockSpec(memory_space=pltpu.HBM)


def call(kernel, ins, outs, scratch, flops, moved, mebibytes):
    return pl.pallas_call(
        kernel,
        in_specs=ins,
        out_specs=[spec for spec, _ in outs],
        out_shape=[shape for _, shape in outs],
        scratch_shapes=scratch,
        compiler_params=pltpu.CompilerParams(vmem_limit_bytes=mebibytes * 2**20),
        cost_estimate=pl.CostEstimate(flops=flops, bytes_accessed=moved, transcendentals=0),
    )


def shape(dims, dtype):
    return jax.ShapeDtypeStruct(dims, dtype)


def kernel_body(tokens, sub_pos, sub_base, embed, norm_gain, fir_taps, long_filter, skip_gain, cotangent):
    n_path, n_ctx = lax.axis_size("path"), lax.axis_size("ctx")
    points = n_path
    tok_rows = tokens.shape[0]
    length = tok_rows * n_ctx
    vocab, width = embed.shape
    share = width // (n_path * n_ctx)
    subs = sub_pos.shape[0] * n_ctx
    own_width = width // n_path
    cols = points * share
    half = length // 2
    tables = dft_tables(length)
    dma = pltpu.SemaphoreType.DMA
    transform_flops = 2 * length * length
    spare = 16

    msg, ids = call(
        pack_kernel,
        [hbm_spec()] * 4,
        [
            (vmem_spec(), shape((n_ctx, tok_rows + spare, share), BF16)),
            (vmem_spec(), shape((spare, LANES), F32)),
        ],
        [
            pltpu.VMEM((1, tok_rows), jnp.int32),
            pltpu.VMEM((1, sub_pos.shape[0]), jnp.int32),
            pltpu.VMEM((1, sub_pos.shape[0]), jnp.int32),
            pltpu.VMEM((tok_rows, n_ctx * share), BF16),
            dma((n_ctx + 3,)),
        ],
        length * share,
        8 * length * share,
        60,
    )(
        tokens.reshape(1, tok_rows),
        sub_pos.reshape(1, -1),
        sub_base.reshape(1, -1),
        cotangent,
    )
    msg = lax.all_to_all(msg, "ctx", 0, 0, tiled=True)

    gain = norm_gain.reshape(1, width)
    skip = skip_gain.reshape(1, n_path * share)
    spec, gram = call(
        prepare_kernel,
        [hbm_spec()] * 4 + [any_spec()],
        [
            (vmem_spec(), shape((4, half, share), F32)),
            (vmem_spec(), shape((3 * vocab + vocab // 2, vocab), BF16)),
        ],
        [
            pltpu.VMEM((length, share), F32),
            pltpu.VMEM((length, half), BF16),
            pltpu.VMEM((length, half), BF16),
            pltpu.VMEM((vocab, width), BF16),
            pltpu.VMEM((vocab, vocab), F32),
            dma((7,)),
        ],
        2 * vocab * vocab * width,
        2 * vocab * width,
        58,
    )(long_filter, tables[0], tables[1], embed, ids)

    hots, subs_hots, put_hots = call(
        functools.partial(ids_kernel, vocab),
        [vmem_spec()],
        [
            (vmem_spec(), shape((length, vocab), BF16)),
            (vmem_spec(), shape((2 * subs, vocab), BF16)),
            (vmem_spec(), shape((length, 2 * subs), BF16)),
        ],
        [],
        2 * 10**9,
        4 * 10**6,
        8,
    )(msg)
    wide = 4 * LANES
    signal, q_feat, k_feat, v_feat, inv, pair = call(
        functools.partial(feature_kernel, points),
        [vmem_spec()] * 6 + [hbm_spec()],
        [(vmem_spec(), shape((length, cols), BF16))]
        + [(vmem_spec(), shape((length, cols), F32))] * 4
        + [(vmem_spec(), shape((2, length, share), BF16))],
        [
            pltpu.VMEM((vocab, width), BF16),
            pltpu.VMEM((points, subs, LANES), F32),
            pltpu.VMEM((2 * subs, wide), F32),
            pltpu.VMEM((length, 2 * share), F32),
            pltpu.VMEM((length, (2 + points) * share), F32),
            pltpu.VMEM((2, GROUP + half, cols), F32),
            dma,
        ],
        2 * length * vocab * 3 * share,
        2 * vocab * width + 16 * length * cols,
        42,
    )(hots, subs_hots, put_hots, gram, fir_taps, gain, embed)
    conv = call(
        functools.partial(forward_kernel, points),
        [vmem_spec()] * 7,
        [(vmem_spec(), shape((length, cols), BF16))],
        [pltpu.VMEM((2 * length, cols), BF16)],
        2 * transform_flops * cols,
        4 * length * length,
        12,
    )(signal, skip, *tables, spec)[0]

    grad = call(
        functools.partial(backward_kernel, points, width),
        [vmem_spec()] * 15,
        [(vmem_spec(), shape((n_ctx, tok_rows + spare, share), BF16))],
        [
            pltpu.VMEM((length, cols), BF16),
            pltpu.VMEM((2 * length, cols), BF16),
        ]
        + [pltpu.VMEM((2, half + GROUP, cols), F32)] * 3,
        2 * transform_flops * cols,
        4 * length * length + 16 * length * cols,
        18,
    )(msg, pair, fir_taps, gain, skip, q_feat, k_feat, v_feat, inv, conv, *tables, spec)[0]

    own = call(
        own_kernel,
        [vmem_spec(), hbm_spec(), any_spec()],
        [(vmem_spec(), shape((2, tok_rows, own_width), BF16))],
        [pltpu.VMEM((vocab, own_width), BF16), dma],
        4 * tok_rows * vocab * own_width,
        2 * vocab * own_width,
        58,
    )(ids, embed, grad)[0]
    grad = lax.all_to_all(grad, "ctx", 0, 0, tiled=True)
    each = n_ctx // n_path
    grad = call(
        partial_kernel,
        [vmem_spec()],
        [(vmem_spec(), shape((n_path, each * tok_rows + spare, share), BF16))],
        [],
        spare * LANES * n_ctx,
        4 * length * share,
        4,
    )(grad)[0]
    grad = lax.all_to_all(grad, "path", 0, 0, tiled=True)
    out = shape((tok_rows, own_width), F32)
    return tuple(
        call(
            finish_kernel,
            [vmem_spec()] * 2,
            [(vmem_spec(), out), (vmem_spec(), out)],
            [],
            8 * tok_rows * own_width,
            14 * tok_rows * own_width,
            8,
        )(grad, own)
    )


def plain_body(tokens, sub_pos, sub_base, embed, norm_gain, fir_taps, long_filter, skip_gain, cotangent):
    n_path, n_ctx = lax.axis_size("path"), lax.axis_size("ctx")
    path, ctx = lax.axis_index("path"), lax.axis_index("ctx")
    points = n_path
    tok_rows = tokens.shape[0]
    length = tok_rows * n_ctx
    width = embed.shape[1]
    share = width // (n_path * n_ctx)
    own_width = width // n_path
    first = (ctx * n_path + path) * share
    alphas = ((jnp.arange(points, dtype=jnp.int32)).astype(F32) + 0.5) / points
    alphas = alphas[:, None, None]

    local = jnp.arange(tok_rows, dtype=jnp.int32)[:, None] + ctx * tok_rows == sub_pos[None, :]
    put = jnp.sum(jnp.where(local, sub_base[None, :], 0), 1)
    base_ids = jnp.where(jnp.any(local, 1), put, tokens)
    rows_tok = jnp.take(embed, tokens, axis=0).astype(F32)
    rows_base = jnp.take(embed, base_ids, axis=0).astype(F32)
    rows_in = rows_base[None] + alphas * (rows_tok - rows_base)[None]
    inv = lax.rsqrt(jnp.mean(rows_in * rows_in, -1) + EPS)
    inv = lax.all_gather(inv, "ctx", axis=1, tiled=True)[:, :, None]
    all_tok = lax.all_gather(tokens, "ctx", tiled=True)
    all_base = lax.all_gather(base_ids, "ctx", tiled=True)

    cot = cotangent.reshape(tok_rows, n_ctx, n_path, share)
    cot = lax.dynamic_index_in_dim(cot, path, 2, keepdims=False)
    cot = lax.all_to_all(cot.transpose(1, 0, 2), "ctx", 0, 0, tiled=True)
    upstream = cot.reshape(1, length, share).astype(F32)
    mine = lax.dynamic_slice_in_dim(embed, first, share, 1)
    gain = lax.dynamic_slice_in_dim(norm_gain, first, share, 0)
    taps = lax.dynamic_slice_in_dim(fir_taps, first, share, 2).astype(F32)
    filt = lax.dynamic_slice_in_dim(long_filter, path * share, share, 1)
    skip = lax.dynamic_slice_in_dim(skip_gain, path * share, share, 0)

    emb_tok = jnp.take(mine, all_tok, axis=0).astype(F32)
    emb_base = jnp.take(mine, all_base, axis=0).astype(F32)
    inputs = emb_base[None] + alphas * (emb_tok - emb_base)[None]
    normed = rounded(inputs * inv * gain)
    q_feat, k_feat, v_feat = (
        taps[f, 0] * normed + taps[f, 1] * shifted(normed, 1) + taps[f, 2] * shifted(normed, 2)
        for f in range(3)
    )
    filter_spec = spectrum(filt[None])
    conv = rounded(long_conv(rounded(k_feat * v_feat), filter_spec, skip, False))
    grad_z = rounded(long_conv(rounded(upstream * q_feat), filter_spec, skip, True))
    grads = (rounded(upstream * conv), rounded(grad_z * v_feat), rounded(grad_z * k_feat))
    by_tap = [sum(taps[f, tap] * grads[f] for f in range(3)) for tap in range(3)]
    scaled = gain * (by_tap[0] + shifted(by_tap[1], -1) + shifted(by_tap[2], -2))
    grad = jnp.sum(inv * scaled, 0).astype(BF16)
    along = jnp.sum(inputs * scaled, -1, keepdims=True) * inv**3 / width
    part = jnp.stack([jnp.sum(alphas * along, 0)[:, 0], jnp.sum((1.0 - alphas) * along, 0)[:, 0]])
    part = lax.psum(part, ("path", "ctx"))
    part = lax.dynamic_slice_in_dim(part, ctx * tok_rows, tok_rows, 1)

    back = lax.all_to_all(grad.reshape(n_ctx, tok_rows, share), "ctx", 0, 0, tiled=True)
    back = back.reshape(n_path, n_ctx // n_path, tok_rows, share)
    back = lax.all_to_all(back, "path", 0, 0, tiled=True).astype(F32)
    back = back.transpose(2, 1, 0, 3).reshape(tok_rows, own_width)
    own_tok = lax.dynamic_slice_in_dim(rows_tok, path * own_width, own_width, 1)
    own_base = lax.dynamic_slice_in_dim(rows_base, path * own_width, own_width, 1)
    grad = (back - own_tok * part[0][:, None] - own_base * part[1][:, None]) / points
    return (grad, (own_tok - own_base) * grad)


def body(tokens, sub_pos, sub_base, embed, *rest):
    n_path, n_ctx = lax.axis_size("path"), lax.axis_size("ctx")
    tok_rows = tokens.shape[0]
    share = embed.shape[1] // (n_path * n_ctx)
    tables = 4 * (tok_rows * n_ctx) ** 2
    fits = share == LANES and tok_rows == LANES and n_ctx == GROUP and tables <= TABLE_BYTES
    chosen = kernel_body if fits else plain_body
    return chosen(tokens, sub_pos, sub_base, embed, *rest)


def solution(mesh):
    return jax.shard_map(
        body,
        mesh=mesh,
        in_specs=(
            P("ctx"),
            P("ctx"),
            P("ctx"),
            P(),
            P(),
            P(),
            P(None, "ctx"),
            P("ctx"),
            P("ctx", None),
        ),
        out_specs=(P("ctx", "path"), P("ctx", "path")),
        check_vma=False,
    )
```

```python
import functools

import jax
import jax.numpy as jnp
import ml_dtypes
import numpy as np
from jax import lax
from jax.experimental import pallas as pl
from jax.experimental.pallas import tpu as pltpu
from jax.sharding import PartitionSpec as P

LANES = 128
GROUP = 8
FREQ_ROWS = 256
CHUNK = 16
EPS = 1e-06
CANCEL = 0.004
TABLE_BYTES = 4 * 2**20
F32 = jnp.float32
BF16 = jnp.bfloat16
precise = lax.Precision.HIGH


def angle_tables(length):
    outer_size = 64
    inner_size = length // outer_size
    outer_idx = jnp.arange(outer_size, dtype=jnp.int32)
    inner_idx = jnp.arange(inner_size, dtype=jnp.int32)
    outer_angle = (
        2.0 * jnp.pi / outer_size
        * (outer_idx[:, None] * outer_idx[None, :] % outer_size).astype(F32)
    )
    inner_angle = (
        2.0 * jnp.pi / inner_size
        * (inner_idx[:, None] * inner_idx[None, :] % inner_size).astype(F32)
    )
    twist_angle = (
        2.0 * jnp.pi / length
        * (outer_idx[:, None] * inner_idx[None, :] % length).astype(F32)
    )
    return (outer_angle, inner_angle, twist_angle)


def complex_table(angle, sign):
    cosine = jnp.cos(angle)
    sine = sign * jnp.sin(angle)
    return jnp.stack([jnp.stack([cosine, sine]), jnp.stack([-sine, cosine])])


def twisted(values, angle, sign):
    cosine = jnp.cos(angle)[None, :, :, None]
    sine = sign * jnp.sin(angle)[None, :, :, None]
    real_part = values[:, 0]
    imag_part = values[:, 1]
    return jnp.stack(
        [real_part * cosine - imag_part * sine, real_part * sine + imag_part * cosine], 1
    )


def spectrum(signal):
    batch, half, width = signal.shape
    length = 2 * half
    outer_angle, inner_angle, twist_angle = angle_tables(length)
    outer_size = outer_angle.shape[0]
    inner_size = inner_angle.shape[0]
    folded = signal.reshape(batch, outer_size // 2, inner_size, width)
    used = outer_angle[:, : outer_size // 2]
    outer_table = jnp.stack([jnp.cos(used), -jnp.sin(used)])
    first = jnp.einsum("rka,pabc->prkbc", outer_table, folded, precision=precise)
    turned = twisted(first, twist_angle, -1.0)
    return jnp.einsum(
        "prkbc,rsbm->pskmc", turned, complex_table(inner_angle, -1.0), precision=precise
    )


def inverse(spec):
    batch, parts, outer_size, inner_size, width = spec.shape
    length = outer_size * inner_size
    outer_angle, inner_angle, twist_angle = angle_tables(length)
    back = jnp.einsum("pskmc,stmb->ptkbc", spec, complex_table(inner_angle, 1.0), precision=precise)
    turned = twisted(back, twist_angle, 1.0)
    used = outer_angle[: outer_size // 2]
    outer_table = jnp.stack([jnp.cos(used), -jnp.sin(used)])
    result = jnp.einsum("rak,prkbc->pabc", outer_table, turned, precision=precise)
    return (result / length).reshape(batch, length // 2, width)


def long_conv(signal, filter_spec, skip_gain, adjoint):
    spec = spectrum(signal)
    sig_real = spec[:, 0]
    sig_imag = spec[:, 1]
    filt_real = filter_spec[:, 0]
    filt_imag = filter_spec[:, 1]
    if adjoint:
        prod_real = sig_real * filt_real + sig_imag * filt_imag
        prod_imag = sig_imag * filt_real - sig_real * filt_imag
    else:
        prod_real = sig_real * filt_real - sig_imag * filt_imag
        prod_imag = sig_real * filt_imag + sig_imag * filt_real
    return inverse(jnp.stack([prod_real, prod_imag], 1)) + skip_gain * signal


def rounded(value):
    return value.astype(BF16).astype(F32)


def shifted(values, step):
    zeros = jnp.zeros_like(values[:, : abs(step)])
    if step > 0:
        return jnp.concatenate([zeros, values[:, :-step]], 1)
    return jnp.concatenate([values[:, -step:], zeros], 1)


@functools.lru_cache(maxsize=None)
def dft_tables(length):
    half = length // 2
    freq = 4 * np.arange(half, dtype=np.int64) + 1
    place = np.arange(half, dtype=np.int64)
    tables = []
    for offset in (0, 1):
        turns = freq[:, None] * (2 * place + offset)[None, :] % (8 * half)
        angle = turns * (2.0 * np.pi / (8 * half))
        cosine = np.cos(angle).astype(ml_dtypes.bfloat16)
        sine = np.sin(angle).astype(ml_dtypes.bfloat16)
        tables.append((np.concatenate([cosine, sine], 0), np.concatenate([cosine.T, sine.T], 1)))
    return (tables[0][0], tables[1][0], tables[0][1], tables[1][1])


def transposed(rows):
    count = rows.shape[0]
    if count < LANES:
        rows = jnp.concatenate([rows, jnp.zeros((LANES - count, LANES), F32)], 0)
    return rows.T


def dot(left, right):
    return jnp.dot(left, right, preferred_element_type=F32)


def exact_dot(left, right, dims):
    return lax.dot_general(
        left, right, (dims, ((), ())), precision=lax.Precision.HIGHEST, preferred_element_type=F32
    )


def iota(dims, axis):
    return lax.broadcasted_iota(jnp.int32, dims, axis)


def even_first():
    row = iota((LANES, LANES), 0)
    half = LANES // 2
    source = jnp.where(row < half, 2 * row, 2 * (row - half) + 1)
    return (iota((LANES, LANES), 1) == source).astype(F32)


def hot(ids, vocab):
    lane = iota(ids.shape, 1).astype(F32)
    parts = [
        (ids == lane + float(column * LANES)).astype(F32).astype(BF16)
        for column in range(vocab // LANES)
    ]
    return jnp.concatenate(parts, 1)


def joined(block, kind):
    return 256.0 * block[2 * kind : 2 * kind + 1] + block[2 * kind + 1 : 2 * kind + 2]


def pack_kernel(
    tok_hbm, pos_hbm, put_hbm, cot_hbm, msg_ref, ids_ref, tok_ref, pos_ref, put_ref, cot_ref, sems
):
    dests, rows, share = msg_ref.shape
    tok_rows = cot_hbm.shape[0]
    n_path = cot_hbm.shape[1] // (dests * share)
    path = lax.axis_index("path")
    moves = [(tok_hbm, tok_ref), (pos_hbm, pos_ref), (put_hbm, put_ref)]
    for dest in range(dests):
        lanes = pl.ds(pl.multiple_of((dest * n_path + path) * share, LANES), share)
        moves.append((cot_hbm.at[:, lanes], cot_ref.at[:, pl.ds(dest * share, share)]))
    copies = [
        pltpu.make_async_copy(source, target, sems.at[index])
        for index, (source, target) in enumerate(moves)
    ]
    for copy in copies:
        copy.start()
    order = even_first().astype(BF16)
    for copy in copies[:3]:
        copy.wait()
    lists = []
    for ref in (tok_ref, pos_ref, put_ref):
        value = ref[...].astype(F32)
        if value.shape[1] < LANES:
            value = jnp.concatenate([value, jnp.zeros((1, LANES - value.shape[1]), F32)], 1)
        high = jnp.floor(value * (1.0 / 256.0))
        lists += [high, value - 256.0 * high]
    lists.append(jnp.zeros((rows - tok_rows - len(lists), LANES), F32))
    ids = jnp.concatenate(lists, 0)
    ids_ref[...] = ids
    turned = lax.dot_general(
        ids.astype(BF16), order, (((1,), (1,)), ((), ())), preferred_element_type=F32
    )
    ids = jnp.where(iota(ids.shape, 0) < 2, turned, ids).astype(BF16)
    for dest in range(dests):
        msg_ref[dest, tok_rows:, :] = ids
    for copy in copies[3:]:
        copy.wait()
    turned = dot(order, cot_ref[...]).astype(BF16)
    for dest in range(dests):
        msg_ref[dest, :tok_rows, :] = turned[:, dest * share : (dest + 1) * share]


def prepare_kernel(
    filt_hbm, even_hbm, odd_hbm, embed_hbm, skip_ref, after_ref,
    spec_ref, gram_ref,
    filt_ref, even_ref, odd_ref, embed_ref, sum_ref, sems,
):
    length, share = filt_ref.shape
    half = length // 2
    vocab, width = embed_ref.shape
    pieces = sems.shape[0] - 3
    wide = width // pieces
    path = lax.axis_index("path")
    lanes = pl.ds(pl.multiple_of(path * share, LANES), share)
    moves = [(filt_hbm.at[:, lanes], filt_ref), (even_hbm, even_ref), (odd_hbm, odd_ref)]
    for index in range(pieces):
        lanes = pl.ds(index * wide, wide)
        moves.append((embed_hbm.at[:, lanes], embed_ref.at[:, lanes]))
    copies = [
        pltpu.make_async_copy(source, target, sems.at[index])
        for index, (source, target) in enumerate(moves)
    ]
    for copy in copies:
        copy.start()

    copies[0].wait()
    skip = skip_ref[:, pl.ds(pl.multiple_of(path * share, LANES), share)]
    filt_ref[0:1, :] = filt_ref[0:1, :] + skip
    parts = []
    for offset in range(2):
        value = filt_ref[pl.ds(offset, half, stride=2), :] * (1.0 / length)
        high = value.astype(BF16)
        parts.append(jnp.concatenate([high, (value - high.astype(F32)).astype(BF16)], 1))
    copies[1].wait()
    copies[2].wait()
    for index in range(half // FREQ_ROWS):
        found = []
        for table, part in ((even_ref, parts[0]), (odd_ref, parts[1])):
            for offset in (0, half):
                both = dot(table[pl.ds(offset + index * FREQ_ROWS, FREQ_ROWS), :], part)
                found.append(both[:, :share] + both[:, share:])
        rows = pl.ds(index * FREQ_ROWS, FREQ_ROWS)
        spec_ref[0, rows, :] = found[0] + found[2]
        spec_ref[1, rows, :] = -found[1] - found[3]
        spec_ref[2, rows, :] = found[0] - found[2]
        spec_ref[3, rows, :] = found[3] - found[1]

    for index in range(pieces):
        copies[3 + index].wait()
        part = embed_ref[:, index * wide : (index + 1) * wide]
        found = lax.dot_general(part, part, (((1,), (1,)), ((), ())), preferred_element_type=F32)
        if index == 0:
            sum_ref[...] = found
        else:
            sum_ref[...] += found
    first = (lax.axis_index("ctx") * lax.axis_size("path") + path) * share
    mine = embed_ref[:, pl.ds(pl.multiple_of(first, LANES), share)]
    same = iota((LANES, LANES), 0) == iota((LANES, LANES), 1)
    lane = iota((LANES, LANES), 1)
    below = 3 * vocab
    for block in range(vocab // LANES):
        rows = slice(block * LANES, (block + 1) * LANES)
        value = sum_ref[rows, :]
        norm = jnp.sum(jnp.where(same, value[:, rows], 0.0), 1, keepdims=True)
        inv = jnp.broadcast_to(lax.rsqrt(norm / width + EPS), (LANES, LANES))
        high = inv.astype(BF16).astype(F32)
        inv = jnp.where(lane < LANES // 2, high, inv - high).astype(BF16)
        side, start = block * LANES // (vocab // 2), block * LANES % (vocab // 2)
        into = slice(below + start, below + start + LANES)
        left = side * (share + LANES)
        gram_ref[into, left : left + share] = mine[rows]
        gram_ref[into, left + share : left + share + LANES] = inv
        for part in range(3):
            high = value.astype(BF16)
            gram_ref[part * vocab + block * LANES : part * vocab + (block + 1) * LANES, :] = high
            value = value - high.astype(F32)


def own_kernel(ids_ref, embed_hbm, grad_ref, own_ref, embed_ref, sem):
    vocab = embed_ref.shape[0]
    own_width = own_ref.shape[2]
    lanes = pl.ds(pl.multiple_of(lax.axis_index("path") * own_width, LANES), own_width)
    copy = pltpu.make_async_copy(embed_hbm.at[:, lanes], embed_ref, sem)
    copy.start()
    ids = ids_ref[...]
    columns = transposed(jnp.concatenate([joined(ids, kind) for kind in range(3)], 0))
    tok = jnp.broadcast_to(columns[:, 0:1], (LANES, LANES))
    place = jnp.broadcast_to(joined(ids, 1), (LANES, LANES))
    put = jnp.broadcast_to(joined(ids, 2), (LANES, LANES))
    first = lax.axis_index("ctx") * LANES
    subs = LANES // GROUP
    here = (place == (iota((LANES, LANES), 0) + first).astype(F32)) & (iota((LANES, LANES), 1) < subs)
    found = jnp.max(jnp.where(here, put, -1.0), 1, keepdims=True)
    base = jnp.where(found >= 0.0, found, tok)
    hots = jnp.concatenate([hot(tok, vocab), hot(base, vocab)], 0)
    copy.wait()
    both = dot(hots, embed_ref[...]).astype(BF16)
    own_ref[0] = both[:LANES]
    own_ref[1] = both[LANES:]


def transform(even_ref, odd_ref, signal_ref, spec_ref, prod_ref, points):
    half = even_ref.shape[1]
    share = spec_ref.shape[2]
    cols = points * share
    for index in range(half // FREQ_ROWS):
        rows = pl.ds(index * FREQ_ROWS, FREQ_ROWS)
        after = pl.ds(half + index * FREQ_ROWS, FREQ_ROWS)
        filt = [spec_ref[part, rows, :] for part in range(4)]
        for kind in range(2):
            signal = slice(kind * cols, (kind + 1) * cols)
            even_real = dot(even_ref[rows, :], signal_ref[:half, signal])
            even_imag = dot(even_ref[after, :], signal_ref[:half, signal])
            odd_real = dot(odd_ref[rows, :], signal_ref[half:, signal])
            odd_imag = dot(odd_ref[after, :], signal_ref[half:, signal])
            for point in range(points):
                lanes = slice(point * share, (point + 1) * share)
                prods = []
                for part, sign in ((0, 1.0), (2, -1.0)):
                    real = even_real[:, lanes] + sign * odd_real[:, lanes]
                    imag = even_imag[:, lanes] + sign * odd_imag[:, lanes]
                    if kind == 1:
                        prods.append(real * filt[part] - imag * filt[part + 1])
                        prods.append(real * filt[part + 1] + imag * filt[part])
                    else:
                        prods.append(real * filt[part] + imag * filt[part + 1])
                        prods.append(imag * filt[part] - real * filt[part + 1])
                sums = (
                    prods[0] + prods[2],
                    prods[1] + prods[3],
                    prods[0] - prods[2],
                    prods[1] - prods[3],
                )
                lanes = slice(kind * cols + point * share, kind * cols + (point + 1) * share)
                for part, value in enumerate(sums):
                    into = pl.ds(part * half + index * FREQ_ROWS, FREQ_ROWS)
                    prod_ref[into, lanes] = value.astype(BF16)


def ids_kernel(vocab, msg_ref, hot_ref, subs_ref, put_ref):
    length = hot_ref.shape[0]
    half = length // 2
    n_ctx = msg_ref.shape[0]
    block_half = LANES // 2
    per_block = LANES // GROUP
    subs = n_ctx * per_block
    blocks = [msg_ref[block, LANES:, :].astype(F32) for block in range(n_ctx)]
    toks = transposed(jnp.concatenate([joined(block, 0) for block in blocks], 0))
    spread = sum(
        blocks[block] if block == 0 else pltpu.roll(blocks[block], block * per_block, 1)
        for block in range(n_ctx)
    )
    place = joined(spread, 1)
    put = joined(spread, 2)
    back = jnp.floor(place * 0.5)
    place = back + (place - 2.0 * back) * half
    columns = transposed(jnp.concatenate([place, put], 0))
    for block in range(n_ctx):
        column = jnp.broadcast_to(toks[:, block : block + 1], (LANES, LANES))
        rows = hot(column, vocab)
        hot_ref[block * block_half : (block + 1) * block_half, :] = rows[:block_half]
        hot_ref[half + block * block_half : half + (block + 1) * block_half, :] = rows[block_half:]
    subs_ref[subs:, :] = hot(jnp.broadcast_to(columns[:, 1:2], (subs, LANES)), vocab)
    pick = jnp.concatenate(
        [
            (columns[:, 0:1] == (iota((subs, LANES), 1) + part * LANES).astype(F32)).astype(F32).astype(BF16)
            for part in range(length // LANES)
        ],
        1,
    )
    for index in range(length // LANES):
        row = (iota((LANES, subs), 0) + index * LANES).astype(F32)
        here = (row == place[:, :subs]).astype(F32).astype(BF16)
        put_ref[index * LANES : (index + 1) * LANES, :] = jnp.concatenate([here, here], 1)
    subs_ref[:subs, :] = dot(pick, hot_ref[...]).astype(BF16)


def feature_kernel(
    points, msg_ref, hot_ref, subs_hot_ref, put_ref, gram_ref, taps_ref, gain_ref, embed_hbm,
    signal_ref, k_ref, v_ref, inv_ref, pair_ref,
    embed_ref, sums_ref, found_ref, look_ref, subs_ref, last_ref, sem,
):
    length = signal_ref.shape[0]
    half = length // 2
    vocab, width = embed_hbm.shape
    share = pair_ref.shape[2]
    subs = subs_hot_ref.shape[0] // 2
    first = (lax.axis_index("ctx") * points + lax.axis_index("path")) * share
    first = pl.multiple_of(first, LANES)
    below = 3 * vocab
    table = jnp.concatenate(
        [gram_ref[below:, : share + LANES], gram_ref[below:, share + LANES :]], 0
    )

    alphas = [(point + 0.5) / points for point in range(points)]
    hots = subs_hot_ref[...]
    found = dot(jnp.concatenate([hots] * 3, 1), gram_ref[:below, :])
    hot_tok32, hot_base32 = hots[:subs].astype(F32), hots[subs:].astype(F32)
    tok_tok = jnp.sum(found[:subs] * hot_tok32, 1, keepdims=True)
    tok_base = jnp.sum(found[:subs] * hot_base32, 1, keepdims=True)
    base_base = jnp.sum(found[subs:] * hot_base32, 1, keepdims=True)
    cancels = jnp.zeros((subs, 1), F32)
    for point in range(points):
        alpha = alphas[point]
        terms = (1.0 - alpha) ** 2 * base_base + alpha**2 * tok_tok
        total = terms + 2.0 * alpha * (1.0 - alpha) * tok_base
        cancels = jnp.maximum(cancels, (total < CANCEL * terms).astype(F32))
        inv = lax.rsqrt(jnp.maximum(total, 0.0) / width + EPS)
        sums_ref[point] = jnp.broadcast_to(inv, (subs, LANES))

    @pl.when(jnp.max(cancels) > 0.5)
    def _():
        copy = pltpu.make_async_copy(embed_hbm, embed_ref, sem)
        copy.start()
        sums_ref[...] = jnp.zeros_like(sums_ref)
        copy.wait()
        wide = found_ref.shape[1]

        @pl.loop(0, width // wide)
        def _(step):
            lanes = pl.ds(pl.multiple_of(step * wide, wide), wide)
            found_ref[...] = dot(hots, embed_ref[:, lanes])
            for block in range(subs // GROUP):
                rows = slice(block * GROUP, (block + 1) * GROUP)
                sums = [sums_ref[point, rows, :] for point in range(points)]
                for column in range(wide // LANES):
                    cut = slice(column * LANES, (column + 1) * LANES)
                    base = found_ref[subs + block * GROUP : subs + (block + 1) * GROUP, cut]
                    diff = found_ref[rows, cut] - base
                    for point in range(points):
                        value = base + alphas[point] * diff
                        sums[point] = sums[point] + value * value
                for point in range(points):
                    sums_ref[point, rows, :] = sums[point]

        for point in range(points):
            mean = jnp.sum(sums_ref[point], 1, keepdims=True) / width
            sums_ref[point] = jnp.broadcast_to(lax.rsqrt(mean + EPS), (subs, LANES))

    high = [dot(hots[subs:], table[:, :share]), jnp.ones((subs, LANES), F32)]
    low = [jnp.zeros((subs, LANES), F32)] * 2
    for point in range(points):
        inv = sums_ref[point]
        high.append(inv.astype(BF16).astype(F32))
        low.append(inv - high[-1])
    held = jnp.concatenate([jnp.concatenate(high, 1), jnp.concatenate(low, 1)], 0).astype(BF16)
    for index in range(length // FREQ_ROWS):
        rows = pl.ds(index * FREQ_ROWS, FREQ_ROWS)
        look_ref[rows, :] = dot(hot_ref[rows, :], table)
        subs_ref[rows, :] = dot(put_ref[rows, :], held)

    cols = points * share
    block_half = LANES // 2
    last_ref[...] = jnp.zeros_like(last_ref)
    gain = gain_ref[:, pl.ds(first, share)]
    taps = [taps_ref[f, :, pl.ds(first, share)].astype(F32) for f in range(3)]
    taps = [[taps[f][tap : tap + 1] for tap in range(3)] for f in range(3)]

    @pl.loop(0, half // CHUNK)
    def _(step):
        start = pl.multiple_of(step * CHUNK, CHUNK)
        block = start // block_half
        sides = []
        for side in range(2):
            rows = pl.ds(pl.multiple_of(side * half + start, CHUNK), CHUNK)
            sent = pl.ds(pl.multiple_of(side * block_half + start - block * block_half, CHUNK), CHUNK)
            tok = look_ref[rows, :share]
            inv = look_ref[rows, share:]
            inv = inv + pltpu.roll(inv, LANES // 2, 1)
            chosen = subs_ref[rows, share : 2 * share] > 0.5
            base = jnp.where(chosen, subs_ref[rows, :share], tok)
            pair_ref[0, rows, :] = tok.astype(BF16)
            pair_ref[1, rows, :] = base.astype(BF16)
            sides.append((rows, base, tok - base, inv, chosen, msg_ref[block, sent, :].astype(F32)))
        for point in range(points):
            lanes = slice(point * share, (point + 1) * share)
            nows, backs = [], []
            for side, (rows, base, diff, inv_tok, chosen, _) in enumerate(sides):
                inv = jnp.where(
                    chosen, subs_ref[rows, (2 + point) * share : (3 + point) * share], inv_tok
                )
                inv_ref[rows, lanes] = inv
                now = rounded((base + alphas[point] * diff) * inv * gain)
                window = jnp.concatenate([last_ref[side, :, lanes], now], 0)
                last_ref[side, :, lanes] = now[CHUNK - GROUP :]
                nows.append(now)
                backs.append(window[GROUP - 1 : GROUP - 1 + CHUNK])
            recent = ((nows[0], backs[1], backs[0]), (nows[1], nows[0], backs[1]))
            for side in range(2):
                rows, upstream = sides[side][0], sides[side][5]
                feats = [sum(taps[f][tap] * recent[side][tap] for tap in range(3)) for f in range(3)]
                k_ref[rows, lanes] = feats[1]
                v_ref[rows, lanes] = feats[2]
                signal_ref[rows, lanes] = (feats[1] * feats[2]).astype(BF16)
                after = slice(cols + point * share, cols + (point + 1) * share)
                signal_ref[rows, after] = (upstream * feats[0]).astype(BF16)


def gradient_kernel(
    points, width, msg_ref, pair_ref, taps_ref, gain_ref,
    signal_ref, k_ref, v_ref, inv_ref, even_ref, odd_ref, even_back_ref, odd_back_ref, spec_ref,
    grad_ref,
    prod_ref, found_ref, sums_ref, next_ref,
):
    half = even_ref.shape[1]
    length = 2 * half
    share = pair_ref.shape[2]
    cols = points * share
    n_ctx = msg_ref.shape[0]
    block_half = LANES // 2
    first = (lax.axis_index("ctx") * points + lax.axis_index("path")) * share
    first = pl.multiple_of(first, LANES)
    gain = gain_ref[:, pl.ds(first, share)]
    taps = [taps_ref[f, :, pl.ds(first, share)].astype(F32) for f in range(3)]
    taps = [[taps[f][tap : tap + 1] for tap in range(3)] for f in range(3)]
    alphas = [(point + 0.5) / points for point in range(points)]

    transform(even_ref, odd_ref, signal_ref, spec_ref, prod_ref, points)
    next_ref[...] = jnp.zeros_like(next_ref)
    backs = ((even_back_ref, 0), (odd_back_ref, length))
    for index in reversed(range(half // FREQ_ROWS)):
        for side, (back_ref, offset) in enumerate(backs):
            table = back_ref[pl.ds(index * FREQ_ROWS, FREQ_ROWS), :]
            for kind in range(2):
                found_ref[2 * side + kind] = dot(
                    table, prod_ref[offset : offset + length, kind * cols : (kind + 1) * cols]
                )

        @pl.loop(0, FREQ_ROWS // CHUNK)
        def _(step):
            inside = pl.multiple_of(FREQ_ROWS - CHUNK - step * CHUNK, CHUNK)
            start = index * FREQ_ROWS + inside
            block = start // block_half
            here = pl.ds(inside, CHUNK)
            sides = []
            for side in range(2):
                rows = pl.ds(pl.multiple_of(side * half + start, CHUNK), CHUNK)
                sent = pl.ds(pl.multiple_of(side * block_half + start - block * block_half, CHUNK), CHUNK)
                base = pair_ref[1, rows, :].astype(F32)
                diff = pair_ref[0, rows, :].astype(F32) - base
                upstream = msg_ref[block, sent, :].astype(F32)
                sides.append([rows, sent, base, diff, upstream] + [jnp.zeros((CHUNK, share), F32)] * 3)
            for point in range(points):
                lanes = slice(point * share, (point + 1) * share)
                by_tap = []
                for side in range(2):
                    rows, upstream = sides[side][0], sides[side][4]
                    grad_z = found_ref[2 * side + 1, here, lanes]
                    grads = (
                        upstream * found_ref[2 * side, here, lanes],
                        grad_z * v_ref[rows, lanes],
                        grad_z * k_ref[rows, lanes],
                    )
                    by_tap.append([sum(taps[f][tap] * grads[f] for f in range(3)) for tap in range(3)])
                ahead = []
                for slot, value in enumerate((by_tap[0][1], by_tap[0][2], by_tap[1][2])):
                    window = jnp.concatenate([value, next_ref[slot, :, lanes]], 0)
                    next_ref[slot, :, lanes] = value[:GROUP]
                    ahead.append(window[1 : 1 + CHUNK])
                sums = (by_tap[0][0] + by_tap[1][1] + ahead[1], by_tap[1][0] + ahead[0] + ahead[2])
                for side in range(2):
                    rows, _, base, diff, _, total, sum_tok, sum_both = sides[side]
                    inv = inv_ref[rows, lanes]
                    along = inv * sums[side]
                    total = total + along
                    along = along * (base + alphas[point] * diff) * (inv * inv)
                    sum_tok = sum_tok + alphas[point] * along
                    sum_both = sum_both + along
                    sides[side][5:] = [total, sum_tok, sum_both]
            for side in range(2):
                _, sent, _, _, _, total, sum_tok, sum_both = sides[side]
                grad_ref[block, sent, :] = (gain * total).astype(BF16)
                sums_ref[0, block, sent, :] = gain * sum_tok
                sums_ref[1, block, sent, :] = gain * (sum_both - sum_tok)

    ones = jnp.ones((GROUP, share), F32)

    @pl.loop(0, n_ctx)
    def _(block):
        sent = []
        for kind in range(2):
            row = exact_dot(ones, sums_ref[kind, block], ((1,), (1,)))
            row = row[:1] / width
            high = row.astype(BF16).astype(F32)
            sent += [high, row - high]
        sent.append(jnp.zeros((grad_ref.shape[1] - LANES - len(sent), LANES), F32))
        grad_ref[block, LANES:, :] = jnp.concatenate(sent, 0).astype(BF16)


def partial_kernel(grad_ref, out_ref):
    dests, rows, _ = out_ref.shape
    n_ctx = grad_ref.shape[0]
    each = n_ctx // dests
    spare = sum(grad_ref[block, LANES:, :].astype(F32) for block in range(n_ctx))
    sums = [spare[0:1] + spare[1:2], spare[2:3] + spare[3:4]]
    sent = []
    for value in sums:
        high = value.astype(BF16).astype(F32)
        sent += [high, value - high]
    sent.append(jnp.zeros((rows - each * LANES - len(sent), LANES), F32))
    sent = jnp.concatenate(sent, 0).astype(BF16)
    for dest in range(dests):
        for piece in range(each):
            out_ref[dest, piece * LANES : (piece + 1) * LANES, :] = grad_ref[dest * each + piece, :LANES, :]
        out_ref[dest, each * LANES :, :] = sent


def finish_kernel(grad_ref, own_ref, path_ref, attr_ref):
    points, rows, share = grad_ref.shape
    pieces = rows // LANES
    spare = sum(grad_ref[path, pieces * LANES :, :].astype(F32) for path in range(points))
    sums = jnp.concatenate([spare[0:1] + spare[1:2], spare[2:3] + spare[3:4], spare[4:10]], 0)
    order = even_first()
    columns = transposed(exact_dot(sums, order, ((1,), (0,))))
    to_tok = columns[:, 0:1]
    to_base = columns[:, 1:2]
    order = order.T.astype(BF16)
    for piece in range(pieces):
        for path in range(points):
            lanes = slice((piece * points + path) * share, (piece * points + path + 1) * share)
            tok = own_ref[0, :, lanes].astype(F32)
            base = own_ref[1, :, lanes].astype(F32)
            grad = dot(order, grad_ref[path, piece * LANES : (piece + 1) * LANES, :])
            grad = (grad - tok * to_tok - base * to_base) / points
            path_ref[:, lanes] = grad
            attr_ref[:, lanes] = (tok - base) * grad


def any_spec():
    return pl.BlockSpec(memory_space=pl.ANY)


def vmem_spec():
    return pl.BlockSpec(memory_space=pltpu.VMEM)


def hbm_spec():
    return pl.BlockSpec(memory_space=pltpu.HBM)


def call(kernel, ins, outs, scratch, flops, moved, mebibytes):
    return pl.pallas_call(
        kernel,
        in_specs=ins,
        out_specs=[spec for spec, _ in outs],
        out_shape=[shape for _, shape in outs],
        scratch_shapes=scratch,
        compiler_params=pltpu.CompilerParams(vmem_limit_bytes=mebibytes * 2**20),
        cost_estimate=pl.CostEstimate(flops=flops, bytes_accessed=moved, transcendentals=0),
    )


def shape(dims, dtype):
    return jax.ShapeDtypeStruct(dims, dtype)


def kernel_body(tokens, sub_pos, sub_base, embed, norm_gain, fir_taps, long_filter, skip_gain, cotangent):
    n_path, n_ctx = lax.axis_size("path"), lax.axis_size("ctx")
    points = n_path
    tok_rows = tokens.shape[0]
    length = tok_rows * n_ctx
    vocab, width = embed.shape
    share = width // (n_path * n_ctx)
    subs = sub_pos.shape[0] * n_ctx
    own_width = width // n_path
    cols = points * share
    half = length // 2
    tables = dft_tables(length)
    dma = pltpu.SemaphoreType.DMA
    transform_flops = 2 * length * length
    spare = 16

    msg, ids = call(
        pack_kernel,
        [hbm_spec()] * 4,
        [
            (vmem_spec(), shape((n_ctx, tok_rows + spare, share), BF16)),
            (vmem_spec(), shape((spare, LANES), F32)),
        ],
        [
            pltpu.VMEM((1, tok_rows), jnp.int32),
            pltpu.VMEM((1, sub_pos.shape[0]), jnp.int32),
            pltpu.VMEM((1, sub_pos.shape[0]), jnp.int32),
            pltpu.VMEM((tok_rows, n_ctx * share), BF16),
            dma((n_ctx + 3,)),
        ],
        length * share,
        8 * length * share,
        60,
    )(
        tokens.reshape(1, tok_rows),
        sub_pos.reshape(1, -1),
        sub_base.reshape(1, -1),
        cotangent,
    )
    msg = lax.all_to_all(msg, "ctx", 0, 0, tiled=True)

    gain = norm_gain.reshape(1, width)
    skip = skip_gain.reshape(1, n_path * share)
    spec, gram = call(
        prepare_kernel,
        [hbm_spec()] * 4 + [vmem_spec(), any_spec()],
        [
            (vmem_spec(), shape((4, half, share), F32)),
            (vmem_spec(), shape((3 * vocab + vocab // 2, vocab), BF16)),
        ],
        [
            pltpu.VMEM((length, share), F32),
            pltpu.VMEM((length, half), BF16),
            pltpu.VMEM((length, half), BF16),
            pltpu.VMEM((vocab, width), BF16),
            pltpu.VMEM((vocab, vocab), F32),
            dma((7,)),
        ],
        2 * vocab * vocab * width,
        2 * vocab * width,
        58,
    )(long_filter, tables[0], tables[1], embed, skip, ids)

    hots, subs_hots, put_hots = call(
        functools.partial(ids_kernel, vocab),
        [vmem_spec()],
        [
            (vmem_spec(), shape((length, vocab), BF16)),
            (vmem_spec(), shape((2 * subs, vocab), BF16)),
            (vmem_spec(), shape((length, 2 * subs), BF16)),
        ],
        [],
        2 * 10**9,
        4 * 10**6,
        8,
    )(msg)
    wide = 4 * LANES
    signal, k_feat, v_feat, inv, pair = call(
        functools.partial(feature_kernel, points),
        [vmem_spec()] * 7 + [hbm_spec()],
        [(vmem_spec(), shape((length, 2 * cols), BF16))]
        + [(vmem_spec(), shape((length, cols), F32))] * 3
        + [(vmem_spec(), shape((2, length, share), BF16))],
        [
            pltpu.VMEM((vocab, width), BF16),
            pltpu.VMEM((points, subs, LANES), F32),
            pltpu.VMEM((2 * subs, wide), F32),
            pltpu.VMEM((length, 2 * share), F32),
            pltpu.VMEM((length, (2 + points) * share), F32),
            pltpu.VMEM((2, GROUP, cols), F32),
            dma,
        ],
        2 * length * vocab * 3 * share,
        2 * vocab * width + 16 * length * cols,
        42,
    )(msg, hots, subs_hots, put_hots, gram, fir_taps, gain, embed)

    grad = call(
        functools.partial(gradient_kernel, points, width),
        [vmem_spec()] * 13,
        [(vmem_spec(), shape((n_ctx, tok_rows + spare, share), BF16))],
        [
            pltpu.VMEM((2 * length, 2 * cols), BF16),
            pltpu.VMEM((4, FREQ_ROWS, cols), F32),
            pltpu.VMEM((2, n_ctx, tok_rows, share), F32),
            pltpu.VMEM((3, GROUP, cols), F32),
        ],
        4 * transform_flops * cols,
        4 * length * length + 16 * length * cols,
        20,
    )(msg, pair, fir_taps, gain, signal, k_feat, v_feat, inv, *tables, spec)[0]

    own = call(
        own_kernel,
        [vmem_spec(), hbm_spec(), any_spec()],
        [(vmem_spec(), shape((2, tok_rows, own_width), BF16))],
        [pltpu.VMEM((vocab, own_width), BF16), dma],
        4 * tok_rows * vocab * own_width,
        2 * vocab * own_width,
        60,
    )(ids, embed, grad)[0]
    grad = lax.all_to_all(grad, "ctx", 0, 0, tiled=True)
    each = n_ctx // n_path
    grad = call(
        partial_kernel,
        [vmem_spec()],
        [(vmem_spec(), shape((n_path, each * tok_rows + spare, share), BF16))],
        [],
        spare * LANES * n_ctx,
        4 * length * share,
        4,
    )(grad)[0]
    grad = lax.all_to_all(grad, "path", 0, 0, tiled=True)
    out = shape((tok_rows, own_width), F32)
    return tuple(
        call(
            finish_kernel,
            [vmem_spec()] * 2,
            [(vmem_spec(), out), (vmem_spec(), out)],
            [],
            8 * tok_rows * own_width,
            14 * tok_rows * own_width,
            8,
        )(grad, own)
    )


def plain_body(tokens, sub_pos, sub_base, embed, norm_gain, fir_taps, long_filter, skip_gain, cotangent):
    n_path, n_ctx = lax.axis_size("path"), lax.axis_size("ctx")
    path, ctx = lax.axis_index("path"), lax.axis_index("ctx")
    points = n_path
    tok_rows = tokens.shape[0]
    length = tok_rows * n_ctx
    width = embed.shape[1]
    share = width // (n_path * n_ctx)
    own_width = width // n_path
    first = (ctx * n_path + path) * share
    alphas = ((jnp.arange(points, dtype=jnp.int32)).astype(F32) + 0.5) / points
    alphas = alphas[:, None, None]

    local = jnp.arange(tok_rows, dtype=jnp.int32)[:, None] + ctx * tok_rows == sub_pos[None, :]
    put = jnp.sum(jnp.where(local, sub_base[None, :], 0), 1)
    base_ids = jnp.where(jnp.any(local, 1), put, tokens)
    rows_tok = jnp.take(embed, tokens, axis=0).astype(F32)
    rows_base = jnp.take(embed, base_ids, axis=0).astype(F32)
    rows_in = rows_base[None] + alphas * (rows_tok - rows_base)[None]
    inv = lax.rsqrt(jnp.mean(rows_in * rows_in, -1) + EPS)
    inv = lax.all_gather(inv, "ctx", axis=1, tiled=True)[:, :, None]
    all_tok = lax.all_gather(tokens, "ctx", tiled=True)
    all_base = lax.all_gather(base_ids, "ctx", tiled=True)

    cot = cotangent.reshape(tok_rows, n_ctx, n_path, share)
    cot = lax.dynamic_index_in_dim(cot, path, 2, keepdims=False)
    cot = lax.all_to_all(cot.transpose(1, 0, 2), "ctx", 0, 0, tiled=True)
    upstream = cot.reshape(1, length, share).astype(F32)
    mine = lax.dynamic_slice_in_dim(embed, first, share, 1)
    gain = lax.dynamic_slice_in_dim(norm_gain, first, share, 0)
    taps = lax.dynamic_slice_in_dim(fir_taps, first, share, 2).astype(F32)
    filt = lax.dynamic_slice_in_dim(long_filter, path * share, share, 1)
    skip = lax.dynamic_slice_in_dim(skip_gain, path * share, share, 0)

    emb_tok = jnp.take(mine, all_tok, axis=0).astype(F32)
    emb_base = jnp.take(mine, all_base, axis=0).astype(F32)
    inputs = emb_base[None] + alphas * (emb_tok - emb_base)[None]
    normed = rounded(inputs * inv * gain)
    q_feat, k_feat, v_feat = (
        taps[f, 0] * normed + taps[f, 1] * shifted(normed, 1) + taps[f, 2] * shifted(normed, 2)
        for f in range(3)
    )
    filter_spec = spectrum(filt[None])
    conv = rounded(long_conv(rounded(k_feat * v_feat), filter_spec, skip, False))
    grad_z = rounded(long_conv(rounded(upstream * q_feat), filter_spec, skip, True))
    grads = (rounded(upstream * conv), rounded(grad_z * v_feat), rounded(grad_z * k_feat))
    by_tap = [sum(taps[f, tap] * grads[f] for f in range(3)) for tap in range(3)]
    scaled = gain * (by_tap[0] + shifted(by_tap[1], -1) + shifted(by_tap[2], -2))
    grad = jnp.sum(inv * scaled, 0).astype(BF16)
    along = jnp.sum(inputs * scaled, -1, keepdims=True) * inv**3 / width
    part = jnp.stack([jnp.sum(alphas * along, 0)[:, 0], jnp.sum((1.0 - alphas) * along, 0)[:, 0]])
    part = lax.psum(part, ("path", "ctx"))
    part = lax.dynamic_slice_in_dim(part, ctx * tok_rows, tok_rows, 1)

    back = lax.all_to_all(grad.reshape(n_ctx, tok_rows, share), "ctx", 0, 0, tiled=True)
    back = back.reshape(n_path, n_ctx // n_path, tok_rows, share)
    back = lax.all_to_all(back, "path", 0, 0, tiled=True).astype(F32)
    back = back.transpose(2, 1, 0, 3).reshape(tok_rows, own_width)
    own_tok = lax.dynamic_slice_in_dim(rows_tok, path * own_width, own_width, 1)
    own_base = lax.dynamic_slice_in_dim(rows_base, path * own_width, own_width, 1)
    grad = (back - own_tok * part[0][:, None] - own_base * part[1][:, None]) / points
    return (grad, (own_tok - own_base) * grad)


def body(tokens, sub_pos, sub_base, embed, *rest):
    n_path, n_ctx = lax.axis_size("path"), lax.axis_size("ctx")
    tok_rows = tokens.shape[0]
    share = embed.shape[1] // (n_path * n_ctx)
    tables = 4 * (tok_rows * n_ctx) ** 2
    fits = share == LANES and tok_rows == LANES and n_ctx == GROUP and tables <= TABLE_BYTES
    chosen = kernel_body if fits else plain_body
    return chosen(tokens, sub_pos, sub_base, embed, *rest)


def solution(mesh):
    return jax.shard_map(
        body,
        mesh=mesh,
        in_specs=(
            P("ctx"),
            P("ctx"),
            P("ctx"),
            P(),
            P(),
            P(),
            P(None, "ctx"),
            P("ctx"),
            P("ctx", None),
        ),
        out_specs=(P("ctx", "path"), P("ctx", "path")),
        check_vma=False,
    )
```

```python
import functools

import jax
import jax.numpy as jnp
import ml_dtypes
import numpy as np
from jax import lax
from jax.experimental import pallas as pl
from jax.experimental.pallas import tpu as pltpu
from jax.sharding import PartitionSpec as P

LANES = 128
GROUP = 8
FREQ_ROWS = 256
CHUNK = 32
EPS = 1e-06
CANCEL = 0.004
TABLE_BYTES = 4 * 2**20
F32 = jnp.float32
BF16 = jnp.bfloat16
precise = lax.Precision.HIGH


def angle_tables(length):
    outer_size = 64
    inner_size = length // outer_size
    outer_idx = jnp.arange(outer_size, dtype=jnp.int32)
    inner_idx = jnp.arange(inner_size, dtype=jnp.int32)
    outer_angle = (
        2.0 * jnp.pi / outer_size
        * (outer_idx[:, None] * outer_idx[None, :] % outer_size).astype(F32)
    )
    inner_angle = (
        2.0 * jnp.pi / inner_size
        * (inner_idx[:, None] * inner_idx[None, :] % inner_size).astype(F32)
    )
    twist_angle = (
        2.0 * jnp.pi / length
        * (outer_idx[:, None] * inner_idx[None, :] % length).astype(F32)
    )
    return (outer_angle, inner_angle, twist_angle)


def complex_table(angle, sign):
    cosine = jnp.cos(angle)
    sine = sign * jnp.sin(angle)
    return jnp.stack([jnp.stack([cosine, sine]), jnp.stack([-sine, cosine])])


def twisted(values, angle, sign):
    cosine = jnp.cos(angle)[None, :, :, None]
    sine = sign * jnp.sin(angle)[None, :, :, None]
    real_part = values[:, 0]
    imag_part = values[:, 1]
    return jnp.stack(
        [real_part * cosine - imag_part * sine, real_part * sine + imag_part * cosine], 1
    )


def spectrum(signal):
    batch, half, width = signal.shape
    length = 2 * half
    outer_angle, inner_angle, twist_angle = angle_tables(length)
    outer_size = outer_angle.shape[0]
    inner_size = inner_angle.shape[0]
    folded = signal.reshape(batch, outer_size // 2, inner_size, width)
    used = outer_angle[:, : outer_size // 2]
    outer_table = jnp.stack([jnp.cos(used), -jnp.sin(used)])
    first = jnp.einsum("rka,pabc->prkbc", outer_table, folded, precision=precise)
    turned = twisted(first, twist_angle, -1.0)
    return jnp.einsum(
        "prkbc,rsbm->pskmc", turned, complex_table(inner_angle, -1.0), precision=precise
    )


def inverse(spec):
    batch, parts, outer_size, inner_size, width = spec.shape
    length = outer_size * inner_size
    outer_angle, inner_angle, twist_angle = angle_tables(length)
    back = jnp.einsum("pskmc,stmb->ptkbc", spec, complex_table(inner_angle, 1.0), precision=precise)
    turned = twisted(back, twist_angle, 1.0)
    used = outer_angle[: outer_size // 2]
    outer_table = jnp.stack([jnp.cos(used), -jnp.sin(used)])
    result = jnp.einsum("rak,prkbc->pabc", outer_table, turned, precision=precise)
    return (result / length).reshape(batch, length // 2, width)


def long_conv(signal, filter_spec, skip_gain, adjoint):
    spec = spectrum(signal)
    sig_real = spec[:, 0]
    sig_imag = spec[:, 1]
    filt_real = filter_spec[:, 0]
    filt_imag = filter_spec[:, 1]
    if adjoint:
        prod_real = sig_real * filt_real + sig_imag * filt_imag
        prod_imag = sig_imag * filt_real - sig_real * filt_imag
    else:
        prod_real = sig_real * filt_real - sig_imag * filt_imag
        prod_imag = sig_real * filt_imag + sig_imag * filt_real
    return inverse(jnp.stack([prod_real, prod_imag], 1)) + skip_gain * signal


def rounded(value):
    return value.astype(BF16).astype(F32)


def shifted(values, step):
    zeros = jnp.zeros_like(values[:, : abs(step)])
    if step > 0:
        return jnp.concatenate([zeros, values[:, :-step]], 1)
    return jnp.concatenate([values[:, -step:], zeros], 1)


@functools.lru_cache(maxsize=None)
def dft_tables(length):
    half = length // 2
    freq = 4 * np.arange(half, dtype=np.int64) + 1
    place = np.arange(half, dtype=np.int64)
    tables = []
    for offset in (0, 1):
        turns = freq[:, None] * (2 * place + offset)[None, :] % (8 * half)
        angle = turns * (2.0 * np.pi / (8 * half))
        cosine = np.cos(angle).astype(ml_dtypes.bfloat16)
        sine = np.sin(angle).astype(ml_dtypes.bfloat16)
        tables.append((np.concatenate([cosine, sine], 0), np.concatenate([cosine.T, sine.T], 1)))
    return (tables[0][0], tables[1][0], tables[0][1], tables[1][1])


def transposed(rows):
    count = rows.shape[0]
    if count < LANES:
        rows = jnp.concatenate([rows, jnp.zeros((LANES - count, LANES), F32)], 0)
    return rows.T


def dot(left, right):
    return jnp.dot(left, right, preferred_element_type=F32)


def exact_dot(left, right, dims):
    return lax.dot_general(
        left, right, (dims, ((), ())), precision=lax.Precision.HIGHEST, preferred_element_type=F32
    )


def iota(dims, axis):
    return lax.broadcasted_iota(jnp.int32, dims, axis)


def even_first():
    row = iota((LANES, LANES), 0)
    half = LANES // 2
    source = jnp.where(row < half, 2 * row, 2 * (row - half) + 1)
    return (iota((LANES, LANES), 1) == source).astype(F32)


def hot(ids, vocab):
    lane = iota(ids.shape, 1).astype(F32)
    parts = [
        (ids == lane + float(column * LANES)).astype(F32).astype(BF16)
        for column in range(vocab // LANES)
    ]
    return jnp.concatenate(parts, 1)


def joined(block, kind):
    return 256.0 * block[2 * kind : 2 * kind + 1] + block[2 * kind + 1 : 2 * kind + 2]


def pack_kernel(
    tok_hbm, pos_hbm, put_hbm, cot_hbm, msg_ref, ids_ref, tok_ref, pos_ref, put_ref, cot_ref, sems
):
    dests, rows, share = msg_ref.shape
    tok_rows = cot_hbm.shape[0]
    n_path = cot_hbm.shape[1] // (dests * share)
    path = lax.axis_index("path")
    moves = [(tok_hbm, tok_ref), (pos_hbm, pos_ref), (put_hbm, put_ref)]
    for dest in range(dests):
        lanes = pl.ds(pl.multiple_of((dest * n_path + path) * share, LANES), share)
        moves.append((cot_hbm.at[:, lanes], cot_ref.at[:, pl.ds(dest * share, share)]))
    copies = [
        pltpu.make_async_copy(source, target, sems.at[index])
        for index, (source, target) in enumerate(moves)
    ]
    for copy in copies:
        copy.start()
    order = even_first().astype(BF16)
    for copy in copies[:3]:
        copy.wait()
    lists = []
    for ref in (tok_ref, pos_ref, put_ref):
        value = ref[...].astype(F32)
        if value.shape[1] < LANES:
            value = jnp.concatenate([value, jnp.zeros((1, LANES - value.shape[1]), F32)], 1)
        high = jnp.floor(value * (1.0 / 256.0))
        lists += [high, value - 256.0 * high]
    lists.append(jnp.zeros((rows - tok_rows - len(lists), LANES), F32))
    ids = jnp.concatenate(lists, 0)
    ids_ref[...] = ids
    turned = lax.dot_general(
        ids.astype(BF16), order, (((1,), (1,)), ((), ())), preferred_element_type=F32
    )
    ids = jnp.where(iota(ids.shape, 0) < 2, turned, ids).astype(BF16)
    for dest in range(dests):
        msg_ref[dest, tok_rows:, :] = ids
    for copy in copies[3:]:
        copy.wait()
    turned = dot(order, cot_ref[...]).astype(BF16)
    for dest in range(dests):
        msg_ref[dest, :tok_rows, :] = turned[:, dest * share : (dest + 1) * share]


def prepare_kernel(
    filt_hbm, even_hbm, odd_hbm, embed_hbm, skip_hbm, after_ref,
    spec_hbm, gram_hbm,
    filt_ref, even_ref, odd_ref, embed_ref, skip_ref, sum_ref, spec_ref, gram_ref, sems, out_sems,
):
    length, share = filt_ref.shape
    half = length // 2
    vocab, width = embed_ref.shape
    pieces = sems.shape[0] - 4
    wide = width // pieces
    path = lax.axis_index("path")
    lanes = pl.ds(pl.multiple_of(path * share, LANES), share)
    moves = [
        (filt_hbm.at[:, lanes], filt_ref),
        (skip_hbm.at[:, lanes], skip_ref),
        (even_hbm, even_ref),
        (odd_hbm, odd_ref),
    ]
    for index in range(pieces):
        lanes = pl.ds(index * wide, wide)
        moves.append((embed_hbm.at[:, lanes], embed_ref.at[:, lanes]))
    copies = [
        pltpu.make_async_copy(source, target, sems.at[index])
        for index, (source, target) in enumerate(moves)
    ]
    for copy in copies:
        copy.start()

    copies[0].wait()
    copies[1].wait()
    filt_ref[0:1, :] = filt_ref[0:1, :] + skip_ref[...]
    parts = []
    for offset in range(2):
        value = filt_ref[pl.ds(offset, half, stride=2), :] * (1.0 / length)
        high = value.astype(BF16)
        parts.append(jnp.concatenate([high, (value - high.astype(F32)).astype(BF16)], 1))
    copies[2].wait()
    copies[3].wait()
    for index in range(half // FREQ_ROWS):
        found = []
        for table, part in ((even_ref, parts[0]), (odd_ref, parts[1])):
            for offset in (0, half):
                both = dot(table[pl.ds(offset + index * FREQ_ROWS, FREQ_ROWS), :], part)
                found.append(both[:, :share] + both[:, share:])
        rows = pl.ds(index * FREQ_ROWS, FREQ_ROWS)
        spec_ref[0, rows, :] = found[0] + found[2]
        spec_ref[1, rows, :] = -found[1] - found[3]
        spec_ref[2, rows, :] = found[0] - found[2]
        spec_ref[3, rows, :] = found[3] - found[1]
    outs = [pltpu.make_async_copy(spec_ref, spec_hbm, out_sems.at[0])]
    outs[0].start()

    for index in range(pieces):
        copies[4 + index].wait()
        part = embed_ref[:, index * wide : (index + 1) * wide]
        found = lax.dot_general(part, part, (((1,), (1,)), ((), ())), preferred_element_type=F32)
        if index == 0:
            sum_ref[...] = found
        else:
            sum_ref[...] += found
    first = (lax.axis_index("ctx") * lax.axis_size("path") + path) * share
    mine = embed_ref[:, pl.ds(pl.multiple_of(first, LANES), share)]
    same = iota((LANES, LANES), 0) == iota((LANES, LANES), 1)
    lane = iota((LANES, LANES), 1)
    below = 3 * vocab
    for block in range(vocab // LANES):
        rows = slice(block * LANES, (block + 1) * LANES)
        value = sum_ref[rows, :]
        norm = jnp.sum(jnp.where(same, value[:, rows], 0.0), 1, keepdims=True)
        inv = jnp.broadcast_to(lax.rsqrt(norm / width + EPS), (LANES, LANES))
        high = inv.astype(BF16).astype(F32)
        inv = jnp.where(lane < LANES // 2, high, inv - high).astype(BF16)
        side, start = block * LANES // (vocab // 2), block * LANES % (vocab // 2)
        into = slice(below + start, below + start + LANES)
        left = side * (share + LANES)
        gram_ref[into, left : left + share] = mine[rows]
        gram_ref[into, left + share : left + share + LANES] = inv
        for part in range(3):
            high = value.astype(BF16)
            into = slice(part * vocab + block * LANES, part * vocab + (block + 1) * LANES)
            gram_ref[into, :] = high
            value = value - high.astype(F32)
            into = pl.ds(part * vocab + block * LANES, LANES)
            sem = out_sems.at[1 + block * 3 + part]
            outs.append(pltpu.make_async_copy(gram_ref.at[into], gram_hbm.at[into], sem))
            outs[-1].start()
    into = pl.ds(below, vocab // 2)
    outs.append(pltpu.make_async_copy(gram_ref.at[into], gram_hbm.at[into], out_sems.at[out_sems.shape[0] - 1]))
    outs[-1].start()
    for copy in outs:
        copy.wait()


def own_kernel(ids_ref, embed_ref, grad_ref, own_ref):
    vocab = embed_ref.shape[0]
    own_width = own_ref.shape[2]
    lanes = pl.ds(pl.multiple_of(lax.axis_index("path") * own_width, LANES), own_width)
    ids = ids_ref[...]
    columns = transposed(jnp.concatenate([joined(ids, kind) for kind in range(3)], 0))
    tok = jnp.broadcast_to(columns[:, 0:1], (LANES, LANES))
    place = jnp.broadcast_to(joined(ids, 1), (LANES, LANES))
    put = jnp.broadcast_to(joined(ids, 2), (LANES, LANES))
    first = lax.axis_index("ctx") * LANES
    subs = LANES // GROUP
    here = (place == (iota((LANES, LANES), 0) + first).astype(F32)) & (iota((LANES, LANES), 1) < subs)
    found = jnp.max(jnp.where(here, put, -1.0), 1, keepdims=True)
    base = jnp.where(found >= 0.0, found, tok)
    hots = jnp.concatenate([hot(tok, vocab), hot(base, vocab)], 0)
    both = dot(hots, embed_ref[:, lanes]).astype(BF16)
    own_ref[0] = both[:LANES]
    own_ref[1] = both[LANES:]


def transform(even_ref, odd_ref, signal_ref, spec_ref, prod_ref, points):
    half = even_ref.shape[1]
    share = spec_ref.shape[2]
    cols = points * share
    for index in range(half // FREQ_ROWS):
        rows = pl.ds(index * FREQ_ROWS, FREQ_ROWS)
        after = pl.ds(half + index * FREQ_ROWS, FREQ_ROWS)
        filt = [spec_ref[part, rows, :] for part in range(4)]
        for kind in range(2):
            signal = slice(kind * cols, (kind + 1) * cols)
            even_real = dot(even_ref[rows, :], signal_ref[:half, signal])
            even_imag = dot(even_ref[after, :], signal_ref[:half, signal])
            odd_real = dot(odd_ref[rows, :], signal_ref[half:, signal])
            odd_imag = dot(odd_ref[after, :], signal_ref[half:, signal])
            for point in range(points):
                lanes = slice(point * share, (point + 1) * share)
                prods = []
                for part, sign in ((0, 1.0), (2, -1.0)):
                    real = even_real[:, lanes] + sign * odd_real[:, lanes]
                    imag = even_imag[:, lanes] + sign * odd_imag[:, lanes]
                    if kind == 1:
                        prods.append(real * filt[part] - imag * filt[part + 1])
                        prods.append(real * filt[part + 1] + imag * filt[part])
                    else:
                        prods.append(real * filt[part] + imag * filt[part + 1])
                        prods.append(imag * filt[part] - real * filt[part + 1])
                sums = (
                    prods[0] + prods[2],
                    prods[1] + prods[3],
                    prods[0] - prods[2],
                    prods[1] - prods[3],
                )
                lanes = slice(kind * cols + point * share, kind * cols + (point + 1) * share)
                for part, value in enumerate(sums):
                    into = pl.ds(part * half + index * FREQ_ROWS, FREQ_ROWS)
                    prod_ref[into, lanes] = value.astype(BF16)


def ids_kernel(vocab, msg_ref, hot_ref, subs_ref, put_ref):
    length = hot_ref.shape[0]
    half = length // 2
    n_ctx = msg_ref.shape[0]
    block_half = LANES // 2
    per_block = LANES // GROUP
    subs = n_ctx * per_block
    blocks = [msg_ref[block, LANES:, :].astype(F32) for block in range(n_ctx)]
    toks = transposed(jnp.concatenate([joined(block, 0) for block in blocks], 0))
    spread = sum(
        blocks[block] if block == 0 else pltpu.roll(blocks[block], block * per_block, 1)
        for block in range(n_ctx)
    )
    place = joined(spread, 1)
    put = joined(spread, 2)
    back = jnp.floor(place * 0.5)
    place = back + (place - 2.0 * back) * half
    columns = transposed(jnp.concatenate([place, put], 0))
    for block in range(n_ctx):
        column = jnp.broadcast_to(toks[:, block : block + 1], (LANES, LANES))
        rows = hot(column, vocab)
        hot_ref[block * block_half : (block + 1) * block_half, :] = rows[:block_half]
        hot_ref[half + block * block_half : half + (block + 1) * block_half, :] = rows[block_half:]
    subs_ref[subs:, :] = hot(jnp.broadcast_to(columns[:, 1:2], (subs, LANES)), vocab)
    pick = jnp.concatenate(
        [
            (columns[:, 0:1] == (iota((subs, LANES), 1) + part * LANES).astype(F32)).astype(F32).astype(BF16)
            for part in range(length // LANES)
        ],
        1,
    )
    for index in range(length // LANES):
        row = (iota((LANES, subs), 0) + index * LANES).astype(F32)
        here = (row == place[:, :subs]).astype(F32).astype(BF16)
        put_ref[index * LANES : (index + 1) * LANES, :] = jnp.concatenate([here, here], 1)
    subs_ref[:subs, :] = dot(pick, hot_ref[...]).astype(BF16)


def feature_kernel(
    points, msg_ref, hot_ref, subs_hot_ref, put_ref, gram_ref, taps_ref, gain_ref, embed_hbm,
    signal_ref, k_ref, v_ref, inv_ref, pair_ref,
    embed_ref, sums_ref, found_ref, look_ref, subs_ref, last_ref, sem,
):
    length = signal_ref.shape[0]
    half = length // 2
    vocab, width = embed_hbm.shape
    share = pair_ref.shape[2]
    subs = subs_hot_ref.shape[0] // 2
    first = (lax.axis_index("ctx") * points + lax.axis_index("path")) * share
    first = pl.multiple_of(first, LANES)
    below = 3 * vocab
    table = jnp.concatenate(
        [gram_ref[below:, : share + LANES], gram_ref[below:, share + LANES :]], 0
    )

    alphas = [(point + 0.5) / points for point in range(points)]
    hots = subs_hot_ref[...]
    found = dot(jnp.concatenate([hots] * 3, 1), gram_ref[:below, :])
    hot_tok32, hot_base32 = hots[:subs].astype(F32), hots[subs:].astype(F32)
    tok_tok = jnp.sum(found[:subs] * hot_tok32, 1, keepdims=True)
    tok_base = jnp.sum(found[:subs] * hot_base32, 1, keepdims=True)
    base_base = jnp.sum(found[subs:] * hot_base32, 1, keepdims=True)
    cancels = jnp.zeros((subs, 1), F32)
    for point in range(points):
        alpha = alphas[point]
        terms = (1.0 - alpha) ** 2 * base_base + alpha**2 * tok_tok
        total = terms + 2.0 * alpha * (1.0 - alpha) * tok_base
        cancels = jnp.maximum(cancels, (total < CANCEL * terms).astype(F32))
        inv = lax.rsqrt(jnp.maximum(total, 0.0) / width + EPS)
        sums_ref[point] = jnp.broadcast_to(inv, (subs, LANES))

    @pl.when(jnp.max(cancels) > 0.5)
    def _():
        sums_ref[...] = jnp.zeros_like(sums_ref)
        wide = found_ref.shape[1]

        @pl.loop(0, width // wide)
        def _(step):
            lanes = pl.ds(pl.multiple_of(step * wide, wide), wide)
            copy = pltpu.make_async_copy(embed_hbm.at[:, lanes], embed_ref, sem)
            copy.start()
            copy.wait()
            found_ref[...] = dot(hots, embed_ref[...])
            for block in range(subs // GROUP):
                rows = slice(block * GROUP, (block + 1) * GROUP)
                sums = [sums_ref[point, rows, :] for point in range(points)]
                for column in range(wide // LANES):
                    cut = slice(column * LANES, (column + 1) * LANES)
                    base = found_ref[subs + block * GROUP : subs + (block + 1) * GROUP, cut]
                    diff = found_ref[rows, cut] - base
                    for point in range(points):
                        value = base + alphas[point] * diff
                        sums[point] = sums[point] + value * value
                for point in range(points):
                    sums_ref[point, rows, :] = sums[point]

        for point in range(points):
            mean = jnp.sum(sums_ref[point], 1, keepdims=True) / width
            sums_ref[point] = jnp.broadcast_to(lax.rsqrt(mean + EPS), (subs, LANES))

    high = [dot(hots[subs:], table[:, :share]), jnp.ones((subs, LANES), F32)]
    low = [jnp.zeros((subs, LANES), F32)] * 2
    for point in range(points):
        inv = sums_ref[point]
        high.append(inv.astype(BF16).astype(F32))
        low.append(inv - high[-1])
    held = jnp.concatenate([jnp.concatenate(high, 1), jnp.concatenate(low, 1)], 0).astype(BF16)
    for index in range(length // FREQ_ROWS):
        rows = pl.ds(index * FREQ_ROWS, FREQ_ROWS)
        look_ref[rows, :] = dot(hot_ref[rows, :], table)
        subs_ref[rows, :] = dot(put_ref[rows, :], held)

    cols = points * share
    block_half = LANES // 2
    last_ref[...] = jnp.zeros_like(last_ref)
    gain = gain_ref[:, pl.ds(first, share)]
    taps = [taps_ref[f, :, pl.ds(first, share)].astype(F32) for f in range(3)]
    taps = [[taps[f][tap : tap + 1] for tap in range(3)] for f in range(3)]

    @pl.loop(0, half // CHUNK, unroll=2)
    def _(step):
        start = pl.multiple_of(step * CHUNK, CHUNK)
        block = start // block_half
        sides = []
        for side in range(2):
            rows = pl.ds(pl.multiple_of(side * half + start, CHUNK), CHUNK)
            sent = pl.ds(pl.multiple_of(side * block_half + start - block * block_half, CHUNK), CHUNK)
            tok = look_ref[rows, :share]
            inv = look_ref[rows, share:]
            inv = inv + pltpu.roll(inv, LANES // 2, 1)
            chosen = subs_ref[rows, share : 2 * share] > 0.5
            base = jnp.where(chosen, subs_ref[rows, :share], tok)
            pair_ref[0, rows, :] = tok.astype(BF16)
            pair_ref[1, rows, :] = base.astype(BF16)
            sides.append((rows, base, tok - base, inv, chosen, msg_ref[block, sent, :].astype(F32)))
        for point in range(points):
            lanes = slice(point * share, (point + 1) * share)
            nows, backs = [], []
            for side, (rows, base, diff, inv_tok, chosen, _) in enumerate(sides):
                inv = jnp.where(
                    chosen, subs_ref[rows, (2 + point) * share : (3 + point) * share], inv_tok
                )
                inv_ref[rows, lanes] = inv
                now = rounded((base + alphas[point] * diff) * inv * gain)
                window = jnp.concatenate([last_ref[side, :, lanes], now], 0)
                last_ref[side, :, lanes] = now[CHUNK - GROUP :]
                nows.append(now)
                backs.append(window[GROUP - 1 : GROUP - 1 + CHUNK])
            recent = ((nows[0], backs[1], backs[0]), (nows[1], nows[0], backs[1]))
            for side in range(2):
                rows, upstream = sides[side][0], sides[side][5]
                feats = [sum(taps[f][tap] * recent[side][tap] for tap in range(3)) for f in range(3)]
                k_ref[rows, lanes] = feats[1]
                v_ref[rows, lanes] = feats[2]
                signal_ref[rows, lanes] = (feats[1] * feats[2]).astype(BF16)
                after = slice(cols + point * share, cols + (point + 1) * share)
                signal_ref[rows, after] = (upstream * feats[0]).astype(BF16)


def gradient_kernel(
    points, width, msg_ref, pair_ref, taps_ref, gain_ref,
    signal_ref, k_ref, v_ref, inv_ref, even_ref, odd_ref, even_back_ref, odd_back_ref, spec_ref,
    grad_ref,
    prod_ref, sums_ref,
):
    half = even_ref.shape[1]
    length = 2 * half
    share = pair_ref.shape[2]
    cols = points * share
    n_ctx = msg_ref.shape[0]
    block_half = LANES // 2
    first = (lax.axis_index("ctx") * points + lax.axis_index("path")) * share
    first = pl.multiple_of(first, LANES)
    gain = gain_ref[:, pl.ds(first, share)]
    taps = [taps_ref[f, :, pl.ds(first, share)].astype(F32) for f in range(3)]
    taps = [[taps[f][tap : tap + 1] for tap in range(3)] for f in range(3)]
    alphas = [(point + 0.5) / points for point in range(points)]

    transform(even_ref, odd_ref, signal_ref, spec_ref, prod_ref, points)
    carried = [[jnp.zeros((GROUP, share), F32)] * points for _ in range(3)]
    for index in reversed(range(half // FREQ_ROWS)):
        found = []
        for back_ref, offset in ((even_back_ref, 0), (odd_back_ref, length)):
            table = back_ref[pl.ds(index * FREQ_ROWS, FREQ_ROWS), :]
            for kind in range(2):
                prod = prod_ref[offset : offset + length, kind * cols : (kind + 1) * cols]
                found.append(dot(table, prod))
        for part in reversed(range(FREQ_ROWS // CHUNK)):
            start = index * FREQ_ROWS + part * CHUNK
            block = start // block_half
            here = slice(part * CHUNK, (part + 1) * CHUNK)
            sides = []
            for side in range(2):
                rows = pl.ds(side * half + start, CHUNK)
                sent = pl.ds(side * block_half + start % block_half, CHUNK)
                base = pair_ref[1, rows, :].astype(F32)
                diff = pair_ref[0, rows, :].astype(F32) - base
                upstream = msg_ref[block, sent, :].astype(F32)
                sides.append([rows, sent, base, diff, upstream] + [jnp.zeros((CHUNK, share), F32)] * 3)
            for point in range(points):
                lanes = slice(point * share, (point + 1) * share)
                by_tap = []
                for side in range(2):
                    rows, upstream = sides[side][0], sides[side][4]
                    grad_z = found[2 * side + 1][here, lanes]
                    grads = (
                        upstream * found[2 * side][here, lanes],
                        grad_z * v_ref[rows, lanes],
                        grad_z * k_ref[rows, lanes],
                    )
                    by_tap.append([sum(taps[f][tap] * grads[f] for f in range(3)) for tap in range(3)])
                ahead = []
                for slot, value in enumerate((by_tap[0][1], by_tap[0][2], by_tap[1][2])):
                    window = jnp.concatenate([value, carried[slot][point]], 0)
                    carried[slot][point] = value[:GROUP]
                    ahead.append(window[1 : 1 + CHUNK])
                sums = (by_tap[0][0] + by_tap[1][1] + ahead[1], by_tap[1][0] + ahead[0] + ahead[2])
                for side in range(2):
                    rows, _, base, diff, _, total, sum_tok, sum_both = sides[side]
                    inv = inv_ref[rows, lanes]
                    along = inv * sums[side]
                    total = total + along
                    along = along * (base + alphas[point] * diff) * (inv * inv)
                    sum_tok = sum_tok + alphas[point] * along
                    sum_both = sum_both + along
                    sides[side][5:] = [total, sum_tok, sum_both]
            for side in range(2):
                _, sent, _, _, _, total, sum_tok, sum_both = sides[side]
                grad_ref[block, sent, :] = (gain * total).astype(BF16)
                for kind, value in enumerate((gain * sum_tok, gain * (sum_both - sum_tok))):
                    high = value.astype(BF16)
                    into = pl.ds((kind * n_ctx + block) * LANES + side * block_half + start % block_half, CHUNK)
                    sums_ref[into, :share] = high
                    sums_ref[into, share:] = (value - high.astype(F32)).astype(BF16)

    ones = jnp.ones((GROUP, 2 * share), BF16)
    row = lax.dot_general(ones, sums_ref[...], (((1,), (1,)), ((), ())), preferred_element_type=F32)
    row = row[:1] / width
    high = row.astype(BF16).astype(F32)
    for block in range(n_ctx):
        sent = []
        for kind in range(2):
            lanes = slice((kind * n_ctx + block) * LANES, (kind * n_ctx + block + 1) * LANES)
            sent += [high[:, lanes], row[:, lanes] - high[:, lanes]]
        sent.append(jnp.zeros((grad_ref.shape[1] - LANES - len(sent), LANES), F32))
        grad_ref[block, LANES:, :] = jnp.concatenate(sent, 0).astype(BF16)


def partial_kernel(grad_ref, out_ref):
    dests, rows, _ = out_ref.shape
    n_ctx = grad_ref.shape[0]
    each = n_ctx // dests
    spare = sum(grad_ref[block, LANES:, :].astype(F32) for block in range(n_ctx))
    sums = [spare[0:1] + spare[1:2], spare[2:3] + spare[3:4]]
    sent = []
    for value in sums:
        high = value.astype(BF16).astype(F32)
        sent += [high, value - high]
    sent.append(jnp.zeros((rows - each * LANES - len(sent), LANES), F32))
    sent = jnp.concatenate(sent, 0).astype(BF16)
    for dest in range(dests):
        for piece in range(each):
            out_ref[dest, piece * LANES : (piece + 1) * LANES, :] = grad_ref[dest * each + piece, :LANES, :]
        out_ref[dest, each * LANES :, :] = sent


def finish_kernel(grad_ref, own_ref, path_ref, attr_ref):
    points, rows, share = grad_ref.shape
    pieces = rows // LANES
    spare = sum(grad_ref[path, pieces * LANES :, :].astype(F32) for path in range(points))
    sums = jnp.concatenate([spare[0:1] + spare[1:2], spare[2:3] + spare[3:4], spare[4:10]], 0)
    order = even_first()
    columns = transposed(exact_dot(sums, order, ((1,), (0,))))
    to_tok = columns[:, 0:1]
    to_base = columns[:, 1:2]
    order = order.T.astype(BF16)
    for piece in range(pieces):
        for path in range(points):
            lanes = slice((piece * points + path) * share, (piece * points + path + 1) * share)
            tok = own_ref[0, :, lanes].astype(F32)
            base = own_ref[1, :, lanes].astype(F32)
            grad = dot(order, grad_ref[path, piece * LANES : (piece + 1) * LANES, :])
            grad = (grad - tok * to_tok - base * to_base) / points
            path_ref[:, lanes] = grad
            attr_ref[:, lanes] = (tok - base) * grad


def any_spec():
    return pl.BlockSpec(memory_space=pl.ANY)


def vmem_spec():
    return pl.BlockSpec(memory_space=pltpu.VMEM)


def hbm_spec():
    return pl.BlockSpec(memory_space=pltpu.HBM)


def call(kernel, ins, outs, scratch, flops, moved, mebibytes):
    return pl.pallas_call(
        kernel,
        in_specs=ins,
        out_specs=[spec for spec, _ in outs],
        out_shape=[shape for _, shape in outs],
        scratch_shapes=scratch,
        compiler_params=pltpu.CompilerParams(vmem_limit_bytes=mebibytes * 2**20),
        cost_estimate=pl.CostEstimate(flops=flops, bytes_accessed=moved, transcendentals=0),
    )


def shape(dims, dtype):
    return jax.ShapeDtypeStruct(dims, dtype)


def kernel_body(tokens, sub_pos, sub_base, embed, norm_gain, fir_taps, long_filter, skip_gain, cotangent):
    n_path, n_ctx = lax.axis_size("path"), lax.axis_size("ctx")
    points = n_path
    tok_rows = tokens.shape[0]
    length = tok_rows * n_ctx
    vocab, width = embed.shape
    share = width // (n_path * n_ctx)
    subs = sub_pos.shape[0] * n_ctx
    own_width = width // n_path
    cols = points * share
    half = length // 2
    tables = dft_tables(length)
    dma = pltpu.SemaphoreType.DMA
    transform_flops = 2 * length * length
    spare = 16

    msg, ids = call(
        pack_kernel,
        [hbm_spec()] * 4,
        [
            (vmem_spec(), shape((n_ctx, tok_rows + spare, share), BF16)),
            (vmem_spec(), shape((spare, LANES), F32)),
        ],
        [
            pltpu.VMEM((1, tok_rows), jnp.int32),
            pltpu.VMEM((1, sub_pos.shape[0]), jnp.int32),
            pltpu.VMEM((1, sub_pos.shape[0]), jnp.int32),
            pltpu.VMEM((tok_rows, n_ctx * share), BF16),
            dma((n_ctx + 3,)),
        ],
        length * share,
        8 * length * share,
        60,
    )(
        tokens.reshape(1, tok_rows),
        sub_pos.reshape(1, -1),
        sub_base.reshape(1, -1),
        cotangent,
    )
    msg = lax.all_to_all(msg, "ctx", 0, 0, tiled=True)

    gain = norm_gain.reshape(1, width)
    skip = skip_gain.reshape(1, n_path * share)
    spec, gram = call(
        prepare_kernel,
        [hbm_spec()] * 5 + [any_spec()],
        [
            (any_spec(), shape((4, half, share), F32)),
            (any_spec(), shape((3 * vocab + vocab // 2, vocab), BF16)),
        ],
        [
            pltpu.VMEM((length, share), F32),
            pltpu.VMEM((length, half), BF16),
            pltpu.VMEM((length, half), BF16),
            pltpu.VMEM((vocab, width), BF16),
            pltpu.VMEM((1, share), F32),
            pltpu.VMEM((vocab, vocab), F32),
            pltpu.VMEM((4, half, share), F32),
            pltpu.VMEM((3 * vocab + vocab // 2, vocab), BF16),
            dma((8,)),
            dma((3 * vocab // LANES + 2,)),
        ],
        2 * vocab * vocab * width,
        2 * vocab * width,
        58,
    )(long_filter, tables[0], tables[1], embed, skip, ids)

    hots, subs_hots, put_hots = call(
        functools.partial(ids_kernel, vocab),
        [vmem_spec()],
        [
            (vmem_spec(), shape((length, vocab), BF16)),
            (vmem_spec(), shape((2 * subs, vocab), BF16)),
            (vmem_spec(), shape((length, 2 * subs), BF16)),
        ],
        [],
        2 * 10**9,
        4 * 10**6,
        8,
    )(msg)
    wide = 4 * LANES
    signal, k_feat, v_feat, inv, pair = call(
        functools.partial(feature_kernel, points),
        [vmem_spec()] * 7 + [hbm_spec()],
        [(vmem_spec(), shape((length, 2 * cols), BF16))]
        + [(vmem_spec(), shape((length, cols), F32))] * 3
        + [(vmem_spec(), shape((2, length, share), BF16))],
        [
            pltpu.VMEM((vocab, wide), BF16),
            pltpu.VMEM((points, subs, LANES), F32),
            pltpu.VMEM((2 * subs, wide), F32),
            pltpu.VMEM((length, 2 * share), F32),
            pltpu.VMEM((length, (2 + points) * share), F32),
            pltpu.VMEM((2, GROUP, cols), F32),
            dma,
        ],
        2 * length * vocab * 3 * share,
        2 * vocab * width + 16 * length * cols,
        39,
    )(msg, hots, subs_hots, put_hots, gram, fir_taps, gain, embed)

    grad = call(
        functools.partial(gradient_kernel, points, width),
        [vmem_spec()] * 13,
        [(vmem_spec(), shape((n_ctx, tok_rows + spare, share), BF16))],
        [
            pltpu.VMEM((2 * length, 2 * cols), BF16),
            pltpu.VMEM((2 * length, 2 * share), BF16),
        ],
        4 * transform_flops * cols,
        4 * length * length + 16 * length * cols,
        24,
    )(msg, pair, fir_taps, gain, signal, k_feat, v_feat, inv, *tables, spec)[0]

    own = call(
        own_kernel,
        [vmem_spec(), vmem_spec(), any_spec()],
        [(vmem_spec(), shape((2, tok_rows, own_width), BF16))],
        [],
        4 * tok_rows * vocab * own_width,
        2 * vocab * own_width,
        10,
    )(ids, embed, grad)[0]
    grad = lax.all_to_all(grad, "ctx", 0, 0, tiled=True)
    each = n_ctx // n_path
    grad = call(
        partial_kernel,
        [vmem_spec()],
        [(vmem_spec(), shape((n_path, each * tok_rows + spare, share), BF16))],
        [],
        spare * LANES * n_ctx,
        4 * length * share,
        4,
    )(grad)[0]
    grad = lax.all_to_all(grad, "path", 0, 0, tiled=True)
    out = shape((tok_rows, own_width), F32)
    return tuple(
        call(
            finish_kernel,
            [vmem_spec()] * 2,
            [(vmem_spec(), out), (vmem_spec(), out)],
            [],
            8 * tok_rows * own_width,
            14 * tok_rows * own_width,
            8,
        )(grad, own)
    )


def plain_body(tokens, sub_pos, sub_base, embed, norm_gain, fir_taps, long_filter, skip_gain, cotangent):
    n_path, n_ctx = lax.axis_size("path"), lax.axis_size("ctx")
    path, ctx = lax.axis_index("path"), lax.axis_index("ctx")
    points = n_path
    tok_rows = tokens.shape[0]
    length = tok_rows * n_ctx
    width = embed.shape[1]
    share = width // (n_path * n_ctx)
    own_width = width // n_path
    first = (ctx * n_path + path) * share
    alphas = ((jnp.arange(points, dtype=jnp.int32)).astype(F32) + 0.5) / points
    alphas = alphas[:, None, None]

    local = jnp.arange(tok_rows, dtype=jnp.int32)[:, None] + ctx * tok_rows == sub_pos[None, :]
    put = jnp.sum(jnp.where(local, sub_base[None, :], 0), 1)
    base_ids = jnp.where(jnp.any(local, 1), put, tokens)
    rows_tok = jnp.take(embed, tokens, axis=0).astype(F32)
    rows_base = jnp.take(embed, base_ids, axis=0).astype(F32)
    rows_in = rows_base[None] + alphas * (rows_tok - rows_base)[None]
    inv = lax.rsqrt(jnp.mean(rows_in * rows_in, -1) + EPS)
    inv = lax.all_gather(inv, "ctx", axis=1, tiled=True)[:, :, None]
    all_tok = lax.all_gather(tokens, "ctx", tiled=True)
    all_base = lax.all_gather(base_ids, "ctx", tiled=True)

    cot = cotangent.reshape(tok_rows, n_ctx, n_path, share)
    cot = lax.dynamic_index_in_dim(cot, path, 2, keepdims=False)
    cot = lax.all_to_all(cot.transpose(1, 0, 2), "ctx", 0, 0, tiled=True)
    upstream = cot.reshape(1, length, share).astype(F32)
    mine = lax.dynamic_slice_in_dim(embed, first, share, 1)
    gain = lax.dynamic_slice_in_dim(norm_gain, first, share, 0)
    taps = lax.dynamic_slice_in_dim(fir_taps, first, share, 2).astype(F32)
    filt = lax.dynamic_slice_in_dim(long_filter, path * share, share, 1)
    skip = lax.dynamic_slice_in_dim(skip_gain, path * share, share, 0)

    emb_tok = jnp.take(mine, all_tok, axis=0).astype(F32)
    emb_base = jnp.take(mine, all_base, axis=0).astype(F32)
    inputs = emb_base[None] + alphas * (emb_tok - emb_base)[None]
    normed = rounded(inputs * inv * gain)
    q_feat, k_feat, v_feat = (
        taps[f, 0] * normed + taps[f, 1] * shifted(normed, 1) + taps[f, 2] * shifted(normed, 2)
        for f in range(3)
    )
    filter_spec = spectrum(filt[None])
    conv = rounded(long_conv(rounded(k_feat * v_feat), filter_spec, skip, False))
    grad_z = rounded(long_conv(rounded(upstream * q_feat), filter_spec, skip, True))
    grads = (rounded(upstream * conv), rounded(grad_z * v_feat), rounded(grad_z * k_feat))
    by_tap = [sum(taps[f, tap] * grads[f] for f in range(3)) for tap in range(3)]
    scaled = gain * (by_tap[0] + shifted(by_tap[1], -1) + shifted(by_tap[2], -2))
    grad = jnp.sum(inv * scaled, 0).astype(BF16)
    along = jnp.sum(inputs * scaled, -1, keepdims=True) * inv**3 / width
    part = jnp.stack([jnp.sum(alphas * along, 0)[:, 0], jnp.sum((1.0 - alphas) * along, 0)[:, 0]])
    part = lax.psum(part, ("path", "ctx"))
    part = lax.dynamic_slice_in_dim(part, ctx * tok_rows, tok_rows, 1)

    back = lax.all_to_all(grad.reshape(n_ctx, tok_rows, share), "ctx", 0, 0, tiled=True)
    back = back.reshape(n_path, n_ctx // n_path, tok_rows, share)
    back = lax.all_to_all(back, "path", 0, 0, tiled=True).astype(F32)
    back = back.transpose(2, 1, 0, 3).reshape(tok_rows, own_width)
    own_tok = lax.dynamic_slice_in_dim(rows_tok, path * own_width, own_width, 1)
    own_base = lax.dynamic_slice_in_dim(rows_base, path * own_width, own_width, 1)
    grad = (back - own_tok * part[0][:, None] - own_base * part[1][:, None]) / points
    return (grad, (own_tok - own_base) * grad)


def body(tokens, sub_pos, sub_base, embed, *rest):
    n_path, n_ctx = lax.axis_size("path"), lax.axis_size("ctx")
    tok_rows = tokens.shape[0]
    share = embed.shape[1] // (n_path * n_ctx)
    tables = 4 * (tok_rows * n_ctx) ** 2
    fits = share == LANES and tok_rows == LANES and n_ctx == GROUP and tables <= TABLE_BYTES
    chosen = kernel_body if fits else plain_body
    return chosen(tokens, sub_pos, sub_base, embed, *rest)


def solution(mesh):
    return jax.shard_map(
        body,
        mesh=mesh,
        in_specs=(
            P("ctx"),
            P("ctx"),
            P("ctx"),
            P(),
            P(),
            P(),
            P(None, "ctx"),
            P("ctx"),
            P("ctx", None),
        ),
        out_specs=(P("ctx", "path"), P("ctx", "path")),
        check_vma=False,
    )
```

```python
import functools

import jax
import jax.numpy as jnp
import ml_dtypes
import numpy as np
from jax import lax
from jax.experimental import pallas as pl
from jax.experimental.pallas import tpu as pltpu
from jax.sharding import PartitionSpec as P

LANES = 128
GROUP = 8
FREQ_ROWS = 512
LOOK_ROWS = 256
CHUNK = 32
EPS = 1e-06
CANCEL = 0.004
TABLE_BYTES = 4 * 2**20
F32 = jnp.float32
BF16 = jnp.bfloat16
precise = lax.Precision.HIGH


def angle_tables(length):
    outer_size = 64
    inner_size = length // outer_size
    outer_idx = jnp.arange(outer_size, dtype=jnp.int32)
    inner_idx = jnp.arange(inner_size, dtype=jnp.int32)
    outer_angle = (
        2.0 * jnp.pi / outer_size
        * (outer_idx[:, None] * outer_idx[None, :] % outer_size).astype(F32)
    )
    inner_angle = (
        2.0 * jnp.pi / inner_size
        * (inner_idx[:, None] * inner_idx[None, :] % inner_size).astype(F32)
    )
    twist_angle = (
        2.0 * jnp.pi / length
        * (outer_idx[:, None] * inner_idx[None, :] % length).astype(F32)
    )
    return (outer_angle, inner_angle, twist_angle)


def complex_table(angle, sign):
    cosine = jnp.cos(angle)
    sine = sign * jnp.sin(angle)
    return jnp.stack([jnp.stack([cosine, sine]), jnp.stack([-sine, cosine])])


def twisted(values, angle, sign):
    cosine = jnp.cos(angle)[None, :, :, None]
    sine = sign * jnp.sin(angle)[None, :, :, None]
    real_part = values[:, 0]
    imag_part = values[:, 1]
    return jnp.stack(
        [real_part * cosine - imag_part * sine, real_part * sine + imag_part * cosine], 1
    )


def spectrum(signal):
    batch, half, width = signal.shape
    length = 2 * half
    outer_angle, inner_angle, twist_angle = angle_tables(length)
    outer_size = outer_angle.shape[0]
    inner_size = inner_angle.shape[0]
    folded = signal.reshape(batch, outer_size // 2, inner_size, width)
    used = outer_angle[:, : outer_size // 2]
    outer_table = jnp.stack([jnp.cos(used), -jnp.sin(used)])
    first = jnp.einsum("rka,pabc->prkbc", outer_table, folded, precision=precise)
    turned = twisted(first, twist_angle, -1.0)
    return jnp.einsum(
        "prkbc,rsbm->pskmc", turned, complex_table(inner_angle, -1.0), precision=precise
    )


def inverse(spec):
    batch, parts, outer_size, inner_size, width = spec.shape
    length = outer_size * inner_size
    outer_angle, inner_angle, twist_angle = angle_tables(length)
    back = jnp.einsum("pskmc,stmb->ptkbc", spec, complex_table(inner_angle, 1.0), precision=precise)
    turned = twisted(back, twist_angle, 1.0)
    used = outer_angle[: outer_size // 2]
    outer_table = jnp.stack([jnp.cos(used), -jnp.sin(used)])
    result = jnp.einsum("rak,prkbc->pabc", outer_table, turned, precision=precise)
    return (result / length).reshape(batch, length // 2, width)


def long_conv(signal, filter_spec, skip_gain, adjoint):
    spec = spectrum(signal)
    sig_real = spec[:, 0]
    sig_imag = spec[:, 1]
    filt_real = filter_spec[:, 0]
    filt_imag = filter_spec[:, 1]
    if adjoint:
        prod_real = sig_real * filt_real + sig_imag * filt_imag
        prod_imag = sig_imag * filt_real - sig_real * filt_imag
    else:
        prod_real = sig_real * filt_real - sig_imag * filt_imag
        prod_imag = sig_real * filt_imag + sig_imag * filt_real
    return inverse(jnp.stack([prod_real, prod_imag], 1)) + skip_gain * signal


def rounded(value):
    return value.astype(BF16).astype(F32)


def shifted(values, step):
    zeros = jnp.zeros_like(values[:, : abs(step)])
    if step > 0:
        return jnp.concatenate([zeros, values[:, :-step]], 1)
    return jnp.concatenate([values[:, -step:], zeros], 1)


@functools.lru_cache(maxsize=None)
def dft_tables(length):
    half = length // 2
    freq = 4 * np.arange(half, dtype=np.int64) + 1
    place = np.arange(half, dtype=np.int64)
    tables = []
    for offset in (0, 1):
        turns = freq[:, None] * (2 * place + offset)[None, :] % (8 * half)
        angle = turns * (2.0 * np.pi / (8 * half))
        cosine = np.cos(angle).astype(ml_dtypes.bfloat16)
        sine = np.sin(angle).astype(ml_dtypes.bfloat16)
        tables.append((np.concatenate([cosine, sine], 0), np.concatenate([cosine.T, sine.T], 1)))
    return (tables[0][0], tables[1][0], tables[0][1], tables[1][1])


def transposed(rows):
    count = rows.shape[0]
    if count < LANES:
        rows = jnp.concatenate([rows, jnp.zeros((LANES - count, LANES), F32)], 0)
    return rows.T


def dot(left, right):
    return jnp.dot(left, right, preferred_element_type=F32)


def exact_dot(left, right, dims):
    return lax.dot_general(
        left, right, (dims, ((), ())), precision=lax.Precision.HIGHEST, preferred_element_type=F32
    )


def iota(dims, axis):
    return lax.broadcasted_iota(jnp.int32, dims, axis)


def even_first():
    row = iota((LANES, LANES), 0)
    half = LANES // 2
    source = jnp.where(row < half, 2 * row, 2 * (row - half) + 1)
    return (iota((LANES, LANES), 1) == source).astype(F32)


def hot(ids, vocab):
    lane = iota(ids.shape, 1).astype(F32)
    parts = [
        (ids == lane + float(column * LANES)).astype(F32).astype(BF16)
        for column in range(vocab // LANES)
    ]
    return jnp.concatenate(parts, 1)


def joined(block, kind):
    return 256.0 * block[2 * kind : 2 * kind + 1] + block[2 * kind + 1 : 2 * kind + 2]


def pack_kernel(
    tok_hbm, pos_hbm, put_hbm, cot_hbm, msg_ref, ids_ref, tok_ref, pos_ref, put_ref, cot_ref, sems
):
    dests, rows, share = msg_ref.shape
    tok_rows = cot_hbm.shape[0]
    n_path = cot_hbm.shape[1] // (dests * share)
    path = lax.axis_index("path")
    moves = [(tok_hbm, tok_ref), (pos_hbm, pos_ref), (put_hbm, put_ref)]
    for dest in range(dests):
        lanes = pl.ds(pl.multiple_of((dest * n_path + path) * share, LANES), share)
        moves.append((cot_hbm.at[:, lanes], cot_ref.at[:, pl.ds(dest * share, share)]))
    copies = [
        pltpu.make_async_copy(source, target, sems.at[index])
        for index, (source, target) in enumerate(moves)
    ]
    for copy in copies:
        copy.start()
    order = even_first().astype(BF16)
    for copy in copies[:3]:
        copy.wait()
    lists = []
    for ref in (tok_ref, pos_ref, put_ref):
        value = ref[...].astype(F32)
        if value.shape[1] < LANES:
            value = jnp.concatenate([value, jnp.zeros((1, LANES - value.shape[1]), F32)], 1)
        high = jnp.floor(value * (1.0 / 256.0))
        lists += [high, value - 256.0 * high]
    lists.append(jnp.zeros((rows - tok_rows - len(lists), LANES), F32))
    ids = jnp.concatenate(lists, 0)
    ids_ref[...] = ids
    turned = lax.dot_general(
        ids.astype(BF16), order, (((1,), (1,)), ((), ())), preferred_element_type=F32
    )
    ids = jnp.where(iota(ids.shape, 0) < 2, turned, ids).astype(BF16)
    for dest in range(dests):
        msg_ref[dest, tok_rows:, :] = ids
    for copy in copies[3:]:
        copy.wait()
    turned = dot(order, cot_ref[...]).astype(BF16)
    for dest in range(dests):
        msg_ref[dest, :tok_rows, :] = turned[:, dest * share : (dest + 1) * share]


def prepare_kernel(
    filt_hbm, even_hbm, odd_hbm, embed_hbm, skip_hbm, after_ref,
    spec_hbm, gram_hbm,
    filt_ref, even_ref, odd_ref, embed_ref, skip_ref, sum_ref, spec_ref, gram_ref, sems, out_sems,
):
    length, share = filt_ref.shape
    half = length // 2
    vocab, width = embed_ref.shape
    pieces = sems.shape[0] - 4
    wide = width // pieces
    path = lax.axis_index("path")
    lanes = pl.ds(pl.multiple_of(path * share, LANES), share)
    moves = [
        (filt_hbm.at[:, lanes], filt_ref),
        (skip_hbm.at[:, lanes], skip_ref),
        (even_hbm, even_ref),
        (odd_hbm, odd_ref),
    ]
    for index in range(pieces):
        lanes = pl.ds(index * wide, wide)
        moves.append((embed_hbm.at[:, lanes], embed_ref.at[:, lanes]))
    copies = [
        pltpu.make_async_copy(source, target, sems.at[index])
        for index, (source, target) in enumerate(moves)
    ]
    for copy in copies:
        copy.start()

    copies[0].wait()
    copies[1].wait()
    filt_ref[0:1, :] = filt_ref[0:1, :] + skip_ref[...]
    parts = []
    for offset in range(2):
        value = filt_ref[pl.ds(offset, half, stride=2), :] * (1.0 / length)
        high = value.astype(BF16)
        parts.append(jnp.concatenate([high, (value - high.astype(F32)).astype(BF16)], 1))
    copies[2].wait()
    copies[3].wait()
    for index in range(half // FREQ_ROWS):
        found = []
        for table, part in ((even_ref, parts[0]), (odd_ref, parts[1])):
            for offset in (0, half):
                both = dot(table[pl.ds(offset + index * FREQ_ROWS, FREQ_ROWS), :], part)
                found.append(both[:, :share] + both[:, share:])
        rows = pl.ds(index * FREQ_ROWS, FREQ_ROWS)
        spec_ref[0, rows, :] = found[0] + found[2]
        spec_ref[1, rows, :] = -found[1] - found[3]
        spec_ref[2, rows, :] = found[0] - found[2]
        spec_ref[3, rows, :] = found[3] - found[1]
    outs = [pltpu.make_async_copy(spec_ref, spec_hbm, out_sems.at[0])]
    outs[0].start()

    for index in range(pieces):
        copies[4 + index].wait()
        part = embed_ref[:, index * wide : (index + 1) * wide]
        found = lax.dot_general(part, part, (((1,), (1,)), ((), ())), preferred_element_type=F32)
        if index == 0:
            sum_ref[...] = found
        else:
            sum_ref[...] += found
    first = (lax.axis_index("ctx") * lax.axis_size("path") + path) * share
    mine = embed_ref[:, pl.ds(pl.multiple_of(first, LANES), share)]
    same = iota((LANES, LANES), 0) == iota((LANES, LANES), 1)
    lane = iota((LANES, LANES), 1)
    below = 3 * vocab
    for block in range(vocab // LANES):
        rows = slice(block * LANES, (block + 1) * LANES)
        value = sum_ref[rows, :]
        norm = jnp.sum(jnp.where(same, value[:, rows], 0.0), 1, keepdims=True)
        inv = jnp.broadcast_to(lax.rsqrt(norm / width + EPS), (LANES, LANES))
        high = inv.astype(BF16).astype(F32)
        inv = jnp.where(lane < LANES // 2, high, inv - high).astype(BF16)
        side, start = block * LANES // (vocab // 2), block * LANES % (vocab // 2)
        into = slice(below + start, below + start + LANES)
        left = side * (share + LANES)
        gram_ref[into, left : left + share] = mine[rows]
        gram_ref[into, left + share : left + share + LANES] = inv
        for part in range(3):
            high = value.astype(BF16)
            into = slice(part * vocab + block * LANES, part * vocab + (block + 1) * LANES)
            gram_ref[into, :] = high
            value = value - high.astype(F32)
            into = pl.ds(part * vocab + block * LANES, LANES)
            sem = out_sems.at[1 + block * 3 + part]
            outs.append(pltpu.make_async_copy(gram_ref.at[into], gram_hbm.at[into], sem))
            outs[-1].start()
    into = pl.ds(below, vocab // 2)
    outs.append(pltpu.make_async_copy(gram_ref.at[into], gram_hbm.at[into], out_sems.at[out_sems.shape[0] - 1]))
    outs[-1].start()
    for copy in outs:
        copy.wait()


def own_kernel(ids_ref, embed_ref, grad_ref, own_ref):
    vocab = embed_ref.shape[0]
    own_width = own_ref.shape[2]
    lanes = pl.ds(pl.multiple_of(lax.axis_index("path") * own_width, LANES), own_width)
    ids = ids_ref[...]
    columns = transposed(jnp.concatenate([joined(ids, kind) for kind in range(3)], 0))
    tok = jnp.broadcast_to(columns[:, 0:1], (LANES, LANES))
    place = jnp.broadcast_to(joined(ids, 1), (LANES, LANES))
    put = jnp.broadcast_to(joined(ids, 2), (LANES, LANES))
    first = lax.axis_index("ctx") * LANES
    subs = LANES // GROUP
    here = (place == (iota((LANES, LANES), 0) + first).astype(F32)) & (iota((LANES, LANES), 1) < subs)
    found = jnp.max(jnp.where(here, put, -1.0), 1, keepdims=True)
    base = jnp.where(found >= 0.0, found, tok)
    hots = jnp.concatenate([hot(tok, vocab), hot(base, vocab)], 0)
    both = dot(hots, embed_ref[:, lanes]).astype(BF16)
    own_ref[0] = both[:LANES]
    own_ref[1] = both[LANES:]


def transform(even_ref, odd_ref, signal_ref, spec_ref, prod_ref, points):
    half = even_ref.shape[1]
    share = spec_ref.shape[2]
    cols = points * share
    for kind in range(2):
        signal = slice(kind * cols, (kind + 1) * cols)
        even = dot(even_ref[...], signal_ref[:half, signal])
        odd = dot(odd_ref[...], signal_ref[half:, signal])
        for start in range(0, half, CHUNK):
            real_rows = slice(start, start + CHUNK)
            imag_rows = slice(half + start, half + start + CHUNK)
            filt = [spec_ref[part, real_rows, :] for part in range(4)]
            for point in range(points):
                lanes = slice(point * share, (point + 1) * share)
                prods = []
                for part, sign in ((0, 1.0), (2, -1.0)):
                    real = even[real_rows, lanes] + sign * odd[real_rows, lanes]
                    imag = even[imag_rows, lanes] + sign * odd[imag_rows, lanes]
                    if kind == 1:
                        prods.append(real * filt[part] - imag * filt[part + 1])
                        prods.append(real * filt[part + 1] + imag * filt[part])
                    else:
                        prods.append(real * filt[part] + imag * filt[part + 1])
                        prods.append(imag * filt[part] - real * filt[part + 1])
                sums = (
                    prods[0] + prods[2],
                    prods[1] + prods[3],
                    prods[0] - prods[2],
                    prods[1] - prods[3],
                )
                lanes = slice(kind * cols + point * share, kind * cols + (point + 1) * share)
                for part, value in enumerate(sums):
                    prod_ref[part * half + start : part * half + start + CHUNK, lanes] = value.astype(BF16)


def ids_kernel(vocab, msg_ref, hot_ref, subs_ref, put_ref):
    length = hot_ref.shape[0]
    half = length // 2
    n_ctx = msg_ref.shape[0]
    block_half = LANES // 2
    per_block = LANES // GROUP
    subs = n_ctx * per_block
    blocks = [msg_ref[block, LANES:, :].astype(F32) for block in range(n_ctx)]
    toks = transposed(jnp.concatenate([joined(block, 0) for block in blocks], 0))
    spread = sum(
        blocks[block] if block == 0 else pltpu.roll(blocks[block], block * per_block, 1)
        for block in range(n_ctx)
    )
    place = joined(spread, 1)
    put = joined(spread, 2)
    back = jnp.floor(place * 0.5)
    place = back + (place - 2.0 * back) * half
    columns = transposed(jnp.concatenate([place, put], 0))
    for block in range(n_ctx):
        column = jnp.broadcast_to(toks[:, block : block + 1], (LANES, LANES))
        rows = hot(column, vocab)
        hot_ref[block * block_half : (block + 1) * block_half, :] = rows[:block_half]
        hot_ref[half + block * block_half : half + (block + 1) * block_half, :] = rows[block_half:]
    subs_ref[subs:, :] = hot(jnp.broadcast_to(columns[:, 1:2], (subs, LANES)), vocab)
    pick = jnp.concatenate(
        [
            (columns[:, 0:1] == (iota((subs, LANES), 1) + part * LANES).astype(F32)).astype(F32).astype(BF16)
            for part in range(length // LANES)
        ],
        1,
    )
    for index in range(length // LANES):
        row = (iota((LANES, subs), 0) + index * LANES).astype(F32)
        here = (row == place[:, :subs]).astype(F32).astype(BF16)
        put_ref[index * LANES : (index + 1) * LANES, :] = jnp.concatenate([here, here], 1)
    subs_ref[:subs, :] = dot(pick, hot_ref[...]).astype(BF16)


def feature_kernel(
    points, msg_ref, hot_ref, subs_hot_ref, put_ref, gram_ref, taps_ref, gain_ref, embed_hbm,
    signal_ref, k_ref, v_ref, inv_ref, pair_ref,
    embed_ref, sums_ref, found_ref, look_ref, subs_ref, sem,
):
    length = signal_ref.shape[0]
    half = length // 2
    vocab, width = embed_hbm.shape
    share = pair_ref.shape[2]
    subs = subs_hot_ref.shape[0] // 2
    first = (lax.axis_index("ctx") * points + lax.axis_index("path")) * share
    first = pl.multiple_of(first, LANES)
    below = 3 * vocab
    table = jnp.concatenate(
        [gram_ref[below:, : share + LANES], gram_ref[below:, share + LANES :]], 0
    )

    alphas = [(point + 0.5) / points for point in range(points)]
    hots = subs_hot_ref[...]
    found = dot(jnp.concatenate([hots] * 3, 1), gram_ref[:below, :])
    hot_tok32, hot_base32 = hots[:subs].astype(F32), hots[subs:].astype(F32)
    tok_tok = jnp.sum(found[:subs] * hot_tok32, 1, keepdims=True)
    tok_base = jnp.sum(found[:subs] * hot_base32, 1, keepdims=True)
    base_base = jnp.sum(found[subs:] * hot_base32, 1, keepdims=True)
    cancels = jnp.zeros((subs, 1), F32)
    for point in range(points):
        alpha = alphas[point]
        terms = (1.0 - alpha) ** 2 * base_base + alpha**2 * tok_tok
        total = terms + 2.0 * alpha * (1.0 - alpha) * tok_base
        cancels = jnp.maximum(cancels, (total < CANCEL * terms).astype(F32))
        inv = lax.rsqrt(jnp.maximum(total, 0.0) / width + EPS)
        sums_ref[point] = jnp.broadcast_to(inv, (subs, LANES))

    @pl.when(jnp.max(cancels) > 0.5)
    def _():
        sums_ref[...] = jnp.zeros_like(sums_ref)
        wide = found_ref.shape[1]

        @pl.loop(0, width // wide)
        def _(step):
            lanes = pl.ds(pl.multiple_of(step * wide, wide), wide)
            copy = pltpu.make_async_copy(embed_hbm.at[:, lanes], embed_ref, sem)
            copy.start()
            copy.wait()
            found_ref[...] = dot(hots, embed_ref[...])
            for block in range(subs // GROUP):
                rows = slice(block * GROUP, (block + 1) * GROUP)
                sums = [sums_ref[point, rows, :] for point in range(points)]
                for column in range(wide // LANES):
                    cut = slice(column * LANES, (column + 1) * LANES)
                    base = found_ref[subs + block * GROUP : subs + (block + 1) * GROUP, cut]
                    diff = found_ref[rows, cut] - base
                    for point in range(points):
                        value = base + alphas[point] * diff
                        sums[point] = sums[point] + value * value
                for point in range(points):
                    sums_ref[point, rows, :] = sums[point]

        for point in range(points):
            mean = jnp.sum(sums_ref[point], 1, keepdims=True) / width
            sums_ref[point] = jnp.broadcast_to(lax.rsqrt(mean + EPS), (subs, LANES))

    high = [dot(hots[subs:], table[:, :share]), jnp.ones((subs, LANES), F32)]
    low = [jnp.zeros((subs, LANES), F32)] * 2
    for point in range(points):
        inv = sums_ref[point]
        high.append(inv.astype(BF16).astype(F32))
        low.append(inv - high[-1])
    held = jnp.concatenate([jnp.concatenate(high, 1), jnp.concatenate(low, 1)], 0).astype(BF16)
    for index in range(length // LOOK_ROWS):
        rows = pl.ds(index * LOOK_ROWS, LOOK_ROWS)
        look_ref[rows, :] = dot(hot_ref[rows, :], table)
        subs_ref[rows, :] = dot(put_ref[rows, :], held)

    cols = points * share
    block_half = LANES // 2
    last = [[jnp.zeros((GROUP, share), F32)] * points for _ in range(2)]
    gain = gain_ref[:, pl.ds(first, share)]
    taps = [taps_ref[f, :, pl.ds(first, share)].astype(F32) for f in range(3)]
    taps = [[taps[f][tap : tap + 1] for tap in range(3)] for f in range(3)]

    for start in range(0, half, CHUNK):
        block = start // block_half
        sides = []
        for side in range(2):
            rows = pl.ds(side * half + start, CHUNK)
            sent = pl.ds(side * block_half + start % block_half, CHUNK)
            tok = look_ref[rows, :share]
            inv = look_ref[rows, share:]
            inv = inv + pltpu.roll(inv, LANES // 2, 1)
            chosen = subs_ref[rows, share : 2 * share] > 0.5
            base = jnp.where(chosen, subs_ref[rows, :share], tok)
            pair_ref[0, rows, :] = tok.astype(BF16)
            pair_ref[1, rows, :] = base.astype(BF16)
            sides.append((rows, base, tok - base, inv, chosen, msg_ref[block, sent, :].astype(F32)))
        for point in range(points):
            lanes = slice(point * share, (point + 1) * share)
            nows, backs = [], []
            for side, (rows, base, diff, inv_tok, chosen, _) in enumerate(sides):
                inv = jnp.where(
                    chosen, subs_ref[rows, (2 + point) * share : (3 + point) * share], inv_tok
                )
                inv_ref[rows, lanes] = inv
                now = rounded((base + alphas[point] * diff) * inv * gain)
                window = jnp.concatenate([last[side][point], now], 0)
                last[side][point] = now[CHUNK - GROUP :]
                nows.append(now)
                backs.append(window[GROUP - 1 : GROUP - 1 + CHUNK])
            recent = ((nows[0], backs[1], backs[0]), (nows[1], nows[0], backs[1]))
            for side in range(2):
                rows, upstream = sides[side][0], sides[side][5]
                feats = [sum(taps[f][tap] * recent[side][tap] for tap in range(3)) for f in range(3)]
                k_ref[rows, lanes] = feats[1]
                v_ref[rows, lanes] = feats[2]
                signal_ref[rows, lanes] = (feats[1] * feats[2]).astype(BF16)
                after = slice(cols + point * share, cols + (point + 1) * share)
                signal_ref[rows, after] = (upstream * feats[0]).astype(BF16)


def gradient_kernel(
    points, width, msg_ref, pair_ref, taps_ref, gain_ref,
    signal_ref, k_ref, v_ref, inv_ref, even_ref, odd_ref, even_back_ref, odd_back_ref, spec_ref,
    grad_ref,
    prod_ref, sums_ref,
):
    half = even_ref.shape[1]
    length = 2 * half
    share = pair_ref.shape[2]
    cols = points * share
    n_ctx = msg_ref.shape[0]
    block_half = LANES // 2
    first = (lax.axis_index("ctx") * points + lax.axis_index("path")) * share
    first = pl.multiple_of(first, LANES)
    gain = gain_ref[:, pl.ds(first, share)]
    taps = [taps_ref[f, :, pl.ds(first, share)].astype(F32) for f in range(3)]
    taps = [[taps[f][tap : tap + 1] for tap in range(3)] for f in range(3)]
    alphas = [(point + 0.5) / points for point in range(points)]

    transform(even_ref, odd_ref, signal_ref, spec_ref, prod_ref, points)
    carried = [[jnp.zeros((GROUP, share), F32)] * points for _ in range(3)]
    for index in reversed(range(half // FREQ_ROWS)):
        found = []
        for back_ref, offset in ((even_back_ref, 0), (odd_back_ref, length)):
            table = back_ref[pl.ds(index * FREQ_ROWS, FREQ_ROWS), :]
            for kind in range(2):
                prod = prod_ref[offset : offset + length, kind * cols : (kind + 1) * cols]
                found.append(dot(table, prod))
        for part in reversed(range(FREQ_ROWS // CHUNK)):
            start = index * FREQ_ROWS + part * CHUNK
            block = start // block_half
            here = slice(part * CHUNK, (part + 1) * CHUNK)
            sides = []
            for side in range(2):
                rows = pl.ds(side * half + start, CHUNK)
                sent = pl.ds(side * block_half + start % block_half, CHUNK)
                base = pair_ref[1, rows, :].astype(F32)
                diff = pair_ref[0, rows, :].astype(F32) - base
                upstream = msg_ref[block, sent, :].astype(F32)
                sides.append([rows, sent, base, diff, upstream] + [jnp.zeros((CHUNK, share), F32)] * 3)
            for point in range(points):
                lanes = slice(point * share, (point + 1) * share)
                by_tap = []
                for side in range(2):
                    rows, upstream = sides[side][0], sides[side][4]
                    grad_z = found[2 * side + 1][here, lanes]
                    grads = (
                        upstream * found[2 * side][here, lanes],
                        grad_z * v_ref[rows, lanes],
                        grad_z * k_ref[rows, lanes],
                    )
                    by_tap.append([sum(taps[f][tap] * grads[f] for f in range(3)) for tap in range(3)])
                ahead = []
                for slot, value in enumerate((by_tap[0][1], by_tap[0][2], by_tap[1][2])):
                    window = jnp.concatenate([value, carried[slot][point]], 0)
                    carried[slot][point] = value[:GROUP]
                    ahead.append(window[1 : 1 + CHUNK])
                sums = (by_tap[0][0] + by_tap[1][1] + ahead[1], by_tap[1][0] + ahead[0] + ahead[2])
                for side in range(2):
                    rows, _, base, diff, _, total, sum_tok, sum_both = sides[side]
                    inv = inv_ref[rows, lanes]
                    along = inv * sums[side]
                    total = total + along
                    along = along * (base + alphas[point] * diff) * (inv * inv)
                    sum_tok = sum_tok + alphas[point] * along
                    sum_both = sum_both + along
                    sides[side][5:] = [total, sum_tok, sum_both]
            for side in range(2):
                _, sent, _, _, _, total, sum_tok, sum_both = sides[side]
                grad_ref[block, sent, :] = (gain * total).astype(BF16)
                for kind, value in enumerate((gain * sum_tok, gain * (sum_both - sum_tok))):
                    high = value.astype(BF16)
                    into = pl.ds((kind * n_ctx + block) * LANES + side * block_half + start % block_half, CHUNK)
                    sums_ref[into, :share] = high
                    sums_ref[into, share:] = (value - high.astype(F32)).astype(BF16)

    ones = jnp.ones((GROUP, 2 * share), BF16)
    row = lax.dot_general(ones, sums_ref[...], (((1,), (1,)), ((), ())), preferred_element_type=F32)
    row = row[:1] / width
    high = row.astype(BF16).astype(F32)
    for block in range(n_ctx):
        sent = []
        for kind in range(2):
            lanes = slice((kind * n_ctx + block) * LANES, (kind * n_ctx + block + 1) * LANES)
            sent += [high[:, lanes], row[:, lanes] - high[:, lanes]]
        sent.append(jnp.zeros((grad_ref.shape[1] - LANES - len(sent), LANES), F32))
        grad_ref[block, LANES:, :] = jnp.concatenate(sent, 0).astype(BF16)


def partial_kernel(grad_ref, *out_refs):
    rows, _ = out_refs[0].shape
    n_ctx = grad_ref.shape[0]
    each = n_ctx // len(out_refs)
    spare = sum(grad_ref[block, LANES:, :].astype(F32) for block in range(n_ctx))
    sums = [spare[0:1] + spare[1:2], spare[2:3] + spare[3:4]]
    sent = []
    for value in sums:
        high = value.astype(BF16).astype(F32)
        sent += [high, value - high]
    sent.append(jnp.zeros((rows - each * LANES - len(sent), LANES), F32))
    sent = jnp.concatenate(sent, 0).astype(BF16)
    path = lax.axis_index("path")
    for step, ref in enumerate(out_refs):
        dest = path ^ step
        for piece in range(each):
            ref[piece * LANES : (piece + 1) * LANES, :] = grad_ref[dest * each + piece, :LANES, :]
        ref[each * LANES :, :] = sent


def finish_kernel(own_ref, *refs):
    grad_refs, (path_ref, attr_ref) = refs[:-2], refs[-2:]
    points = len(grad_refs)
    rows, share = grad_refs[0].shape
    pieces = rows // LANES
    spare = sum(ref[pieces * LANES :, :].astype(F32) for ref in grad_refs)
    sums = jnp.concatenate([spare[0:1] + spare[1:2], spare[2:3] + spare[3:4], spare[4:10]], 0)
    order = even_first()
    columns = transposed(exact_dot(sums, order, ((1,), (0,))))
    to_tok = columns[:, 0:1]
    to_base = columns[:, 1:2]
    order = order.T.astype(BF16)
    path = lax.axis_index("path")
    for step, ref in enumerate(grad_refs):
        for piece in range(pieces):
            first = (piece * points + (path ^ step)) * share
            lanes = pl.ds(pl.multiple_of(first, LANES), share)
            tok = own_ref[0, :, lanes].astype(F32)
            base = own_ref[1, :, lanes].astype(F32)
            grad = dot(order, ref[piece * LANES : (piece + 1) * LANES, :])
            grad = (grad - tok * to_tok - base * to_base) / points
            path_ref[:, lanes] = grad
            attr_ref[:, lanes] = (tok - base) * grad


def any_spec():
    return pl.BlockSpec(memory_space=pl.ANY)


def vmem_spec():
    return pl.BlockSpec(memory_space=pltpu.VMEM)


def hbm_spec():
    return pl.BlockSpec(memory_space=pltpu.HBM)


def call(kernel, ins, outs, scratch, flops, moved, mebibytes):
    return pl.pallas_call(
        kernel,
        in_specs=ins,
        out_specs=[spec for spec, _ in outs],
        out_shape=[shape for _, shape in outs],
        scratch_shapes=scratch,
        compiler_params=pltpu.CompilerParams(vmem_limit_bytes=mebibytes * 2**20),
        cost_estimate=pl.CostEstimate(flops=flops, bytes_accessed=moved, transcendentals=0),
    )


def shape(dims, dtype):
    return jax.ShapeDtypeStruct(dims, dtype)


def kernel_body(tokens, sub_pos, sub_base, embed, norm_gain, fir_taps, long_filter, skip_gain, cotangent):
    n_path, n_ctx = lax.axis_size("path"), lax.axis_size("ctx")
    points = n_path
    tok_rows = tokens.shape[0]
    length = tok_rows * n_ctx
    vocab, width = embed.shape
    share = width // (n_path * n_ctx)
    subs = sub_pos.shape[0] * n_ctx
    own_width = width // n_path
    cols = points * share
    half = length // 2
    tables = dft_tables(length)
    dma = pltpu.SemaphoreType.DMA
    transform_flops = 2 * length * length
    spare = 16

    msg, ids = call(
        pack_kernel,
        [hbm_spec()] * 4,
        [
            (vmem_spec(), shape((n_ctx, tok_rows + spare, share), BF16)),
            (vmem_spec(), shape((spare, LANES), F32)),
        ],
        [
            pltpu.VMEM((1, tok_rows), jnp.int32),
            pltpu.VMEM((1, sub_pos.shape[0]), jnp.int32),
            pltpu.VMEM((1, sub_pos.shape[0]), jnp.int32),
            pltpu.VMEM((tok_rows, n_ctx * share), BF16),
            dma((n_ctx + 3,)),
        ],
        length * share,
        8 * length * share,
        60,
    )(
        tokens.reshape(1, tok_rows),
        sub_pos.reshape(1, -1),
        sub_base.reshape(1, -1),
        cotangent,
    )
    msg = lax.all_to_all(msg, "ctx", 0, 0, tiled=True)

    gain = norm_gain.reshape(1, width)
    skip = skip_gain.reshape(1, n_path * share)
    spec, gram = call(
        prepare_kernel,
        [hbm_spec()] * 5 + [any_spec()],
        [
            (any_spec(), shape((4, half, share), F32)),
            (any_spec(), shape((3 * vocab + vocab // 2, vocab), BF16)),
        ],
        [
            pltpu.VMEM((length, share), F32),
            pltpu.VMEM((length, half), BF16),
            pltpu.VMEM((length, half), BF16),
            pltpu.VMEM((vocab, width), BF16),
            pltpu.VMEM((1, share), F32),
            pltpu.VMEM((vocab, vocab), F32),
            pltpu.VMEM((4, half, share), F32),
            pltpu.VMEM((3 * vocab + vocab // 2, vocab), BF16),
            dma((8,)),
            dma((3 * vocab // LANES + 2,)),
        ],
        2 * vocab * vocab * width,
        2 * vocab * width,
        58,
    )(long_filter, tables[0], tables[1], embed, skip, ids)

    hots, subs_hots, put_hots = call(
        functools.partial(ids_kernel, vocab),
        [vmem_spec()],
        [
            (vmem_spec(), shape((length, vocab), BF16)),
            (vmem_spec(), shape((2 * subs, vocab), BF16)),
            (vmem_spec(), shape((length, 2 * subs), BF16)),
        ],
        [],
        2 * 10**9,
        4 * 10**6,
        8,
    )(msg)
    wide = 4 * LANES
    signal, k_feat, v_feat, inv, pair = call(
        functools.partial(feature_kernel, points),
        [vmem_spec()] * 7 + [hbm_spec()],
        [(vmem_spec(), shape((length, 2 * cols), BF16))]
        + [(vmem_spec(), shape((length, cols), F32))] * 3
        + [(vmem_spec(), shape((2, length, share), BF16))],
        [
            pltpu.VMEM((vocab, wide), BF16),
            pltpu.VMEM((points, subs, LANES), F32),
            pltpu.VMEM((2 * subs, wide), F32),
            pltpu.VMEM((length, 2 * share), F32),
            pltpu.VMEM((length, (2 + points) * share), F32),
            dma,
        ],
        2 * length * vocab * 3 * share,
        2 * vocab * width + 16 * length * cols,
        39,
    )(msg, hots, subs_hots, put_hots, gram, fir_taps, gain, embed)

    grad = call(
        functools.partial(gradient_kernel, points, width),
        [vmem_spec()] * 13,
        [(vmem_spec(), shape((n_ctx, tok_rows + spare, share), BF16))],
        [
            pltpu.VMEM((2 * length, 2 * cols), BF16),
            pltpu.VMEM((2 * length, 2 * share), BF16),
        ],
        4 * transform_flops * cols,
        4 * length * length + 16 * length * cols,
        32,
    )(msg, pair, fir_taps, gain, signal, k_feat, v_feat, inv, *tables, spec)[0]

    own = call(
        own_kernel,
        [vmem_spec(), vmem_spec(), any_spec()],
        [(vmem_spec(), shape((2, tok_rows, own_width), BF16))],
        [],
        4 * tok_rows * vocab * own_width,
        2 * vocab * own_width,
        10,
    )(ids, embed, grad)[0]
    grad = lax.all_to_all(grad, "ctx", 0, 0, tiled=True)
    each = n_ctx // n_path
    parts = call(
        partial_kernel,
        [vmem_spec()],
        [(vmem_spec(), shape((each * tok_rows + spare, share), BF16))] * n_path,
        [],
        spare * LANES * n_ctx,
        4 * length * share,
        4,
    )(grad)
    parts = [
        part if step == 0 else lax.ppermute(part, "path", [(p, p ^ step) for p in range(n_path)])
        for step, part in enumerate(parts)
    ]
    out = shape((tok_rows, own_width), F32)
    return tuple(
        call(
            finish_kernel,
            [vmem_spec()] * (1 + n_path),
            [(vmem_spec(), out), (vmem_spec(), out)],
            [],
            8 * tok_rows * own_width,
            14 * tok_rows * own_width,
            8,
        )(own, *parts)
    )


def plain_body(tokens, sub_pos, sub_base, embed, norm_gain, fir_taps, long_filter, skip_gain, cotangent):
    n_path, n_ctx = lax.axis_size("path"), lax.axis_size("ctx")
    path, ctx = lax.axis_index("path"), lax.axis_index("ctx")
    points = n_path
    tok_rows = tokens.shape[0]
    length = tok_rows * n_ctx
    width = embed.shape[1]
    share = width // (n_path * n_ctx)
    own_width = width // n_path
    first = (ctx * n_path + path) * share
    alphas = ((jnp.arange(points, dtype=jnp.int32)).astype(F32) + 0.5) / points
    alphas = alphas[:, None, None]

    local = jnp.arange(tok_rows, dtype=jnp.int32)[:, None] + ctx * tok_rows == sub_pos[None, :]
    put = jnp.sum(jnp.where(local, sub_base[None, :], 0), 1)
    base_ids = jnp.where(jnp.any(local, 1), put, tokens)
    rows_tok = jnp.take(embed, tokens, axis=0).astype(F32)
    rows_base = jnp.take(embed, base_ids, axis=0).astype(F32)
    rows_in = rows_base[None] + alphas * (rows_tok - rows_base)[None]
    inv = lax.rsqrt(jnp.mean(rows_in * rows_in, -1) + EPS)
    inv = lax.all_gather(inv, "ctx", axis=1, tiled=True)[:, :, None]
    all_tok = lax.all_gather(tokens, "ctx", tiled=True)
    all_base = lax.all_gather(base_ids, "ctx", tiled=True)

    cot = cotangent.reshape(tok_rows, n_ctx, n_path, share)
    cot = lax.dynamic_index_in_dim(cot, path, 2, keepdims=False)
    cot = lax.all_to_all(cot.transpose(1, 0, 2), "ctx", 0, 0, tiled=True)
    upstream = cot.reshape(1, length, share).astype(F32)
    mine = lax.dynamic_slice_in_dim(embed, first, share, 1)
    gain = lax.dynamic_slice_in_dim(norm_gain, first, share, 0)
    taps = lax.dynamic_slice_in_dim(fir_taps, first, share, 2).astype(F32)
    filt = lax.dynamic_slice_in_dim(long_filter, path * share, share, 1)
    skip = lax.dynamic_slice_in_dim(skip_gain, path * share, share, 0)

    emb_tok = jnp.take(mine, all_tok, axis=0).astype(F32)
    emb_base = jnp.take(mine, all_base, axis=0).astype(F32)
    inputs = emb_base[None] + alphas * (emb_tok - emb_base)[None]
    normed = rounded(inputs * inv * gain)
    q_feat, k_feat, v_feat = (
        taps[f, 0] * normed + taps[f, 1] * shifted(normed, 1) + taps[f, 2] * shifted(normed, 2)
        for f in range(3)
    )
    filter_spec = spectrum(filt[None])
    conv = rounded(long_conv(rounded(k_feat * v_feat), filter_spec, skip, False))
    grad_z = rounded(long_conv(rounded(upstream * q_feat), filter_spec, skip, True))
    grads = (rounded(upstream * conv), rounded(grad_z * v_feat), rounded(grad_z * k_feat))
    by_tap = [sum(taps[f, tap] * grads[f] for f in range(3)) for tap in range(3)]
    scaled = gain * (by_tap[0] + shifted(by_tap[1], -1) + shifted(by_tap[2], -2))
    grad = jnp.sum(inv * scaled, 0).astype(BF16)
    along = jnp.sum(inputs * scaled, -1, keepdims=True) * inv**3 / width
    part = jnp.stack([jnp.sum(alphas * along, 0)[:, 0], jnp.sum((1.0 - alphas) * along, 0)[:, 0]])
    part = lax.psum(part, ("path", "ctx"))
    part = lax.dynamic_slice_in_dim(part, ctx * tok_rows, tok_rows, 1)

    back = lax.all_to_all(grad.reshape(n_ctx, tok_rows, share), "ctx", 0, 0, tiled=True)
    back = back.reshape(n_path, n_ctx // n_path, tok_rows, share)
    back = lax.all_to_all(back, "path", 0, 0, tiled=True).astype(F32)
    back = back.transpose(2, 1, 0, 3).reshape(tok_rows, own_width)
    own_tok = lax.dynamic_slice_in_dim(rows_tok, path * own_width, own_width, 1)
    own_base = lax.dynamic_slice_in_dim(rows_base, path * own_width, own_width, 1)
    grad = (back - own_tok * part[0][:, None] - own_base * part[1][:, None]) / points
    return (grad, (own_tok - own_base) * grad)


def body(tokens, sub_pos, sub_base, embed, *rest):
    n_path, n_ctx = lax.axis_size("path"), lax.axis_size("ctx")
    tok_rows = tokens.shape[0]
    share = embed.shape[1] // (n_path * n_ctx)
    tables = 4 * (tok_rows * n_ctx) ** 2
    fits = share == LANES and tok_rows == LANES and n_ctx == GROUP and tables <= TABLE_BYTES
    fits = fits and n_ctx % n_path == 0 and n_path & (n_path - 1) == 0
    chosen = kernel_body if fits else plain_body
    return chosen(tokens, sub_pos, sub_base, embed, *rest)


def solution(mesh):
    return jax.shard_map(
        body,
        mesh=mesh,
        in_specs=(
            P("ctx"),
            P("ctx"),
            P("ctx"),
            P(),
            P(),
            P(),
            P(None, "ctx"),
            P("ctx"),
            P("ctx", None),
        ),
        out_specs=(P("ctx", "path"), P("ctx", "path")),
        check_vma=False,
    )
```

```python
import functools

import jax
import jax.numpy as jnp
import ml_dtypes
import numpy as np
from jax import lax
from jax.experimental import pallas as pl
from jax.experimental.pallas import tpu as pltpu
from jax.sharding import PartitionSpec as P

LANES = 128
GROUP = 8
FREQ_ROWS = 512
LOOK_ROWS = 256
CHUNK = 32
EPS = 1e-06
CANCEL = 0.004
TABLE_BYTES = 4 * 2**20
F32 = jnp.float32
BF16 = jnp.bfloat16
precise = lax.Precision.HIGH


def angle_tables(length):
    outer_size = 64
    inner_size = length // outer_size
    outer_idx = jnp.arange(outer_size, dtype=jnp.int32)
    inner_idx = jnp.arange(inner_size, dtype=jnp.int32)
    outer_angle = (
        2.0 * jnp.pi / outer_size
        * (outer_idx[:, None] * outer_idx[None, :] % outer_size).astype(F32)
    )
    inner_angle = (
        2.0 * jnp.pi / inner_size
        * (inner_idx[:, None] * inner_idx[None, :] % inner_size).astype(F32)
    )
    twist_angle = (
        2.0 * jnp.pi / length
        * (outer_idx[:, None] * inner_idx[None, :] % length).astype(F32)
    )
    return (outer_angle, inner_angle, twist_angle)


def complex_table(angle, sign):
    cosine = jnp.cos(angle)
    sine = sign * jnp.sin(angle)
    return jnp.stack([jnp.stack([cosine, sine]), jnp.stack([-sine, cosine])])


def twisted(values, angle, sign):
    cosine = jnp.cos(angle)[None, :, :, None]
    sine = sign * jnp.sin(angle)[None, :, :, None]
    real_part = values[:, 0]
    imag_part = values[:, 1]
    return jnp.stack(
        [real_part * cosine - imag_part * sine, real_part * sine + imag_part * cosine], 1
    )


def spectrum(signal):
    batch, half, width = signal.shape
    length = 2 * half
    outer_angle, inner_angle, twist_angle = angle_tables(length)
    outer_size = outer_angle.shape[0]
    inner_size = inner_angle.shape[0]
    folded = signal.reshape(batch, outer_size // 2, inner_size, width)
    used = outer_angle[:, : outer_size // 2]
    outer_table = jnp.stack([jnp.cos(used), -jnp.sin(used)])
    first = jnp.einsum("rka,pabc->prkbc", outer_table, folded, precision=precise)
    turned = twisted(first, twist_angle, -1.0)
    return jnp.einsum(
        "prkbc,rsbm->pskmc", turned, complex_table(inner_angle, -1.0), precision=precise
    )


def inverse(spec):
    batch, parts, outer_size, inner_size, width = spec.shape
    length = outer_size * inner_size
    outer_angle, inner_angle, twist_angle = angle_tables(length)
    back = jnp.einsum("pskmc,stmb->ptkbc", spec, complex_table(inner_angle, 1.0), precision=precise)
    turned = twisted(back, twist_angle, 1.0)
    used = outer_angle[: outer_size // 2]
    outer_table = jnp.stack([jnp.cos(used), -jnp.sin(used)])
    result = jnp.einsum("rak,prkbc->pabc", outer_table, turned, precision=precise)
    return (result / length).reshape(batch, length // 2, width)


def long_conv(signal, filter_spec, skip_gain, adjoint):
    spec = spectrum(signal)
    sig_real = spec[:, 0]
    sig_imag = spec[:, 1]
    filt_real = filter_spec[:, 0]
    filt_imag = filter_spec[:, 1]
    if adjoint:
        prod_real = sig_real * filt_real + sig_imag * filt_imag
        prod_imag = sig_imag * filt_real - sig_real * filt_imag
    else:
        prod_real = sig_real * filt_real - sig_imag * filt_imag
        prod_imag = sig_real * filt_imag + sig_imag * filt_real
    return inverse(jnp.stack([prod_real, prod_imag], 1)) + skip_gain * signal


def rounded(value):
    return value.astype(BF16).astype(F32)


def shifted(values, step):
    zeros = jnp.zeros_like(values[:, : abs(step)])
    if step > 0:
        return jnp.concatenate([zeros, values[:, :-step]], 1)
    return jnp.concatenate([values[:, -step:], zeros], 1)


@functools.lru_cache(maxsize=None)
def dft_tables(length):
    half = length // 2
    freq = 4 * np.arange(half, dtype=np.int64) + 1
    place = np.arange(half, dtype=np.int64)
    tables = []
    for offset in (0, 1):
        turns = freq[:, None] * (2 * place + offset)[None, :] % (8 * half)
        angle = turns * (2.0 * np.pi / (8 * half))
        cosine = np.cos(angle).astype(ml_dtypes.bfloat16)
        sine = np.sin(angle).astype(ml_dtypes.bfloat16)
        tables.append((np.concatenate([cosine, sine], 0), np.concatenate([cosine.T, sine.T], 1)))
    return (tables[0][0], tables[1][0], tables[0][1], tables[1][1])


def transposed(rows):
    count = rows.shape[0]
    if count < LANES:
        rows = jnp.concatenate([rows, jnp.zeros((LANES - count, LANES), F32)], 0)
    return rows.T


def dot(left, right):
    return jnp.dot(left, right, preferred_element_type=F32)


def exact_dot(left, right, dims):
    return lax.dot_general(
        left, right, (dims, ((), ())), precision=lax.Precision.HIGHEST, preferred_element_type=F32
    )


def iota(dims, axis):
    return lax.broadcasted_iota(jnp.int32, dims, axis)


def even_first():
    row = iota((LANES, LANES), 0)
    half = LANES // 2
    source = jnp.where(row < half, 2 * row, 2 * (row - half) + 1)
    return (iota((LANES, LANES), 1) == source).astype(F32)


def hot(ids, vocab):
    lane = iota(ids.shape, 1).astype(F32)
    parts = [
        (ids == lane + float(column * LANES)).astype(F32).astype(BF16)
        for column in range(vocab // LANES)
    ]
    return jnp.concatenate(parts, 1)


def joined(block, kind):
    return 256.0 * block[2 * kind : 2 * kind + 1] + block[2 * kind + 1 : 2 * kind + 2]


def pack_kernel(dests, tok_hbm, pos_hbm, put_hbm, cot_hbm, *refs):
    msg_refs, (ids_ref, tok_ref, pos_ref, put_ref, cot_ref, sems) = refs[:dests], refs[dests:]
    rows, share = msg_refs[0].shape
    tok_rows = cot_hbm.shape[0]
    n_path = cot_hbm.shape[1] // (dests * share)
    path, ctx = lax.axis_index("path"), lax.axis_index("ctx")
    moves = [(tok_hbm, tok_ref), (pos_hbm, pos_ref), (put_hbm, put_ref)]
    for step in range(dests):
        lanes = pl.ds(pl.multiple_of(((ctx ^ step) * n_path + path) * share, LANES), share)
        moves.append((cot_hbm.at[:, lanes], cot_ref.at[:, pl.ds(step * share, share)]))
    copies = [
        pltpu.make_async_copy(source, target, sems.at[index])
        for index, (source, target) in enumerate(moves)
    ]
    for copy in copies:
        copy.start()
    order = even_first().astype(BF16)
    for copy in copies[:3]:
        copy.wait()
    lists = []
    for ref in (tok_ref, pos_ref, put_ref):
        value = ref[...].astype(F32)
        if value.shape[1] < LANES:
            value = jnp.concatenate([value, jnp.zeros((1, LANES - value.shape[1]), F32)], 1)
        high = jnp.floor(value * (1.0 / 256.0))
        lists += [high, value - 256.0 * high]
    lists.append(jnp.zeros((rows - tok_rows - len(lists), LANES), F32))
    ids = jnp.concatenate(lists, 0)
    ids_ref[...] = ids
    turned = lax.dot_general(
        ids.astype(BF16), order, (((1,), (1,)), ((), ())), preferred_element_type=F32
    )
    ids = jnp.where(iota(ids.shape, 0) < 2, turned, ids).astype(BF16)
    for ref in msg_refs:
        ref[tok_rows:, :] = ids
    for copy in copies[3:]:
        copy.wait()
    turned = dot(order, cot_ref[...]).astype(BF16)
    for step, ref in enumerate(msg_refs):
        ref[:tok_rows, :] = turned[:, step * share : (step + 1) * share]


def prepare_kernel(
    filt_hbm, even_hbm, odd_hbm, embed_hbm, skip_hbm, after_ref,
    spec_hbm, gram_hbm,
    filt_ref, even_ref, odd_ref, embed_ref, skip_ref, sum_ref, spec_ref, gram_ref, sems, out_sems,
):
    length, share = filt_ref.shape
    half = length // 2
    vocab, width = embed_ref.shape
    pieces = sems.shape[0] - 4
    wide = width // pieces
    path = lax.axis_index("path")
    lanes = pl.ds(pl.multiple_of(path * share, LANES), share)
    moves = [
        (filt_hbm.at[:, lanes], filt_ref),
        (skip_hbm.at[:, lanes], skip_ref),
        (even_hbm, even_ref),
        (odd_hbm, odd_ref),
    ]
    for index in range(pieces):
        lanes = pl.ds(index * wide, wide)
        moves.append((embed_hbm.at[:, lanes], embed_ref.at[:, lanes]))
    copies = [
        pltpu.make_async_copy(source, target, sems.at[index])
        for index, (source, target) in enumerate(moves)
    ]
    for copy in copies:
        copy.start()

    copies[0].wait()
    copies[1].wait()
    filt_ref[0:1, :] = filt_ref[0:1, :] + skip_ref[...]
    parts = []
    for offset in range(2):
        value = filt_ref[pl.ds(offset, half, stride=2), :] * (1.0 / length)
        high = value.astype(BF16)
        parts.append(jnp.concatenate([high, (value - high.astype(F32)).astype(BF16)], 1))
    copies[2].wait()
    copies[3].wait()
    for index in range(half // FREQ_ROWS):
        found = []
        for table, part in ((even_ref, parts[0]), (odd_ref, parts[1])):
            for offset in (0, half):
                both = dot(table[pl.ds(offset + index * FREQ_ROWS, FREQ_ROWS), :], part)
                found.append(both[:, :share] + both[:, share:])
        rows = pl.ds(index * FREQ_ROWS, FREQ_ROWS)
        spec_ref[0, rows, :] = found[0] + found[2]
        spec_ref[1, rows, :] = -found[1] - found[3]
        spec_ref[2, rows, :] = found[0] - found[2]
        spec_ref[3, rows, :] = found[3] - found[1]
    outs = [pltpu.make_async_copy(spec_ref, spec_hbm, out_sems.at[0])]
    outs[0].start()

    for index in range(pieces):
        copies[4 + index].wait()
        part = embed_ref[:, index * wide : (index + 1) * wide]
        found = lax.dot_general(part, part, (((1,), (1,)), ((), ())), preferred_element_type=F32)
        if index == 0:
            sum_ref[...] = found
        else:
            sum_ref[...] += found
    first = (lax.axis_index("ctx") * lax.axis_size("path") + path) * share
    mine = embed_ref[:, pl.ds(pl.multiple_of(first, LANES), share)]
    same = iota((LANES, LANES), 0) == iota((LANES, LANES), 1)
    lane = iota((LANES, LANES), 1)
    below = 3 * vocab
    for block in range(vocab // LANES):
        rows = slice(block * LANES, (block + 1) * LANES)
        value = sum_ref[rows, :]
        norm = jnp.sum(jnp.where(same, value[:, rows], 0.0), 1, keepdims=True)
        inv = jnp.broadcast_to(lax.rsqrt(norm / width + EPS), (LANES, LANES))
        high = inv.astype(BF16).astype(F32)
        inv = jnp.where(lane < LANES // 2, high, inv - high).astype(BF16)
        side, start = block * LANES // (vocab // 2), block * LANES % (vocab // 2)
        into = slice(below + start, below + start + LANES)
        left = side * (share + LANES)
        gram_ref[into, left : left + share] = mine[rows]
        gram_ref[into, left + share : left + share + LANES] = inv
        for part in range(3):
            high = value.astype(BF16)
            into = slice(part * vocab + block * LANES, part * vocab + (block + 1) * LANES)
            gram_ref[into, :] = high
            value = value - high.astype(F32)
            into = pl.ds(part * vocab + block * LANES, LANES)
            sem = out_sems.at[1 + block * 3 + part]
            outs.append(pltpu.make_async_copy(gram_ref.at[into], gram_hbm.at[into], sem))
            outs[-1].start()
    into = pl.ds(below, vocab // 2)
    outs.append(pltpu.make_async_copy(gram_ref.at[into], gram_hbm.at[into], out_sems.at[out_sems.shape[0] - 1]))
    outs[-1].start()
    for copy in outs:
        copy.wait()


def own_kernel(ids_ref, embed_ref, grad_ref, own_ref):
    vocab = embed_ref.shape[0]
    own_width = own_ref.shape[2]
    lanes = pl.ds(pl.multiple_of(lax.axis_index("path") * own_width, LANES), own_width)
    ids = ids_ref[...]
    columns = transposed(jnp.concatenate([joined(ids, kind) for kind in range(3)], 0))
    tok = jnp.broadcast_to(columns[:, 0:1], (LANES, LANES))
    place = jnp.broadcast_to(joined(ids, 1), (LANES, LANES))
    put = jnp.broadcast_to(joined(ids, 2), (LANES, LANES))
    first = lax.axis_index("ctx") * LANES
    subs = LANES // GROUP
    here = (place == (iota((LANES, LANES), 0) + first).astype(F32)) & (iota((LANES, LANES), 1) < subs)
    found = jnp.max(jnp.where(here, put, -1.0), 1, keepdims=True)
    base = jnp.where(found >= 0.0, found, tok)
    hots = jnp.concatenate([hot(tok, vocab), hot(base, vocab)], 0)
    both = dot(hots, embed_ref[:, lanes]).astype(BF16)
    own_ref[0] = both[:LANES]
    own_ref[1] = both[LANES:]


def transform(even_ref, odd_ref, signal_ref, spec_ref, prod_ref, points):
    half = even_ref.shape[1]
    share = spec_ref.shape[2]
    cols = points * share
    for kind in range(2):
        signal = slice(kind * cols, (kind + 1) * cols)
        even = dot(even_ref[...], signal_ref[:half, signal])
        odd = dot(odd_ref[...], signal_ref[half:, signal])
        for start in range(0, half, CHUNK):
            real_rows = slice(start, start + CHUNK)
            imag_rows = slice(half + start, half + start + CHUNK)
            filt = [spec_ref[part, real_rows, :] for part in range(4)]
            for point in range(points):
                lanes = slice(point * share, (point + 1) * share)
                prods = []
                for part, sign in ((0, 1.0), (2, -1.0)):
                    real = even[real_rows, lanes] + sign * odd[real_rows, lanes]
                    imag = even[imag_rows, lanes] + sign * odd[imag_rows, lanes]
                    if kind == 1:
                        prods.append(real * filt[part] - imag * filt[part + 1])
                        prods.append(real * filt[part + 1] + imag * filt[part])
                    else:
                        prods.append(real * filt[part] + imag * filt[part + 1])
                        prods.append(imag * filt[part] - real * filt[part + 1])
                sums = (
                    prods[0] + prods[2],
                    prods[1] + prods[3],
                    prods[0] - prods[2],
                    prods[1] - prods[3],
                )
                lanes = slice(kind * cols + point * share, kind * cols + (point + 1) * share)
                for part, value in enumerate(sums):
                    prod_ref[part * half + start : part * half + start + CHUNK, lanes] = value.astype(BF16)


def ids_kernel(vocab, *refs):
    sent_refs, (msg_ref, hot_ref, subs_ref, put_ref) = refs[:-4], refs[-4:]
    length = hot_ref.shape[0]
    half = length // 2
    n_ctx = msg_ref.shape[0]
    for step, ref in enumerate(sent_refs):
        msg_ref[lax.axis_index("ctx") ^ step] = ref[...]
    block_half = LANES // 2
    per_block = LANES // GROUP
    subs = n_ctx * per_block
    blocks = [msg_ref[block, LANES:, :].astype(F32) for block in range(n_ctx)]
    toks = transposed(jnp.concatenate([joined(block, 0) for block in blocks], 0))
    spread = sum(
        blocks[block] if block == 0 else pltpu.roll(blocks[block], block * per_block, 1)
        for block in range(n_ctx)
    )
    place = joined(spread, 1)
    put = joined(spread, 2)
    back = jnp.floor(place * 0.5)
    place = back + (place - 2.0 * back) * half
    columns = transposed(jnp.concatenate([place, put], 0))
    for block in range(n_ctx):
        column = jnp.broadcast_to(toks[:, block : block + 1], (LANES, LANES))
        rows = hot(column, vocab)
        hot_ref[block * block_half : (block + 1) * block_half, :] = rows[:block_half]
        hot_ref[half + block * block_half : half + (block + 1) * block_half, :] = rows[block_half:]
    subs_ref[subs:, :] = hot(jnp.broadcast_to(columns[:, 1:2], (subs, LANES)), vocab)
    pick = jnp.concatenate(
        [
            (columns[:, 0:1] == (iota((subs, LANES), 1) + part * LANES).astype(F32)).astype(F32).astype(BF16)
            for part in range(length // LANES)
        ],
        1,
    )
    for index in range(length // LANES):
        row = (iota((LANES, subs), 0) + index * LANES).astype(F32)
        here = (row == place[:, :subs]).astype(F32).astype(BF16)
        put_ref[index * LANES : (index + 1) * LANES, :] = jnp.concatenate([here, here], 1)
    subs_ref[:subs, :] = dot(pick, hot_ref[...]).astype(BF16)


def feature_kernel(
    points, msg_ref, hot_ref, subs_hot_ref, put_ref, gram_ref, taps_ref, gain_ref, embed_hbm,
    signal_ref, k_ref, v_ref, inv_ref, pair_ref,
    embed_ref, sums_ref, found_ref, look_ref, subs_ref, sem,
):
    length = signal_ref.shape[0]
    half = length // 2
    vocab, width = embed_hbm.shape
    share = pair_ref.shape[2]
    subs = subs_hot_ref.shape[0] // 2
    first = (lax.axis_index("ctx") * points + lax.axis_index("path")) * share
    first = pl.multiple_of(first, LANES)
    below = 3 * vocab
    table = jnp.concatenate(
        [gram_ref[below:, : share + LANES], gram_ref[below:, share + LANES :]], 0
    )

    alphas = [(point + 0.5) / points for point in range(points)]
    hots = subs_hot_ref[...]
    found = dot(jnp.concatenate([hots] * 3, 1), gram_ref[:below, :])
    hot_tok32, hot_base32 = hots[:subs].astype(F32), hots[subs:].astype(F32)
    tok_tok = jnp.sum(found[:subs] * hot_tok32, 1, keepdims=True)
    tok_base = jnp.sum(found[:subs] * hot_base32, 1, keepdims=True)
    base_base = jnp.sum(found[subs:] * hot_base32, 1, keepdims=True)
    cancels = jnp.zeros((subs, 1), F32)
    for point in range(points):
        alpha = alphas[point]
        terms = (1.0 - alpha) ** 2 * base_base + alpha**2 * tok_tok
        total = terms + 2.0 * alpha * (1.0 - alpha) * tok_base
        cancels = jnp.maximum(cancels, (total < CANCEL * terms).astype(F32))
        inv = lax.rsqrt(jnp.maximum(total, 0.0) / width + EPS)
        sums_ref[point] = jnp.broadcast_to(inv, (subs, LANES))

    @pl.when(jnp.max(cancels) > 0.5)
    def _():
        sums_ref[...] = jnp.zeros_like(sums_ref)
        wide = found_ref.shape[1]

        @pl.loop(0, width // wide)
        def _(step):
            lanes = pl.ds(pl.multiple_of(step * wide, wide), wide)
            copy = pltpu.make_async_copy(embed_hbm.at[:, lanes], embed_ref, sem)
            copy.start()
            copy.wait()
            found_ref[...] = dot(hots, embed_ref[...])
            for block in range(subs // GROUP):
                rows = slice(block * GROUP, (block + 1) * GROUP)
                sums = [sums_ref[point, rows, :] for point in range(points)]
                for column in range(wide // LANES):
                    cut = slice(column * LANES, (column + 1) * LANES)
                    base = found_ref[subs + block * GROUP : subs + (block + 1) * GROUP, cut]
                    diff = found_ref[rows, cut] - base
                    for point in range(points):
                        value = base + alphas[point] * diff
                        sums[point] = sums[point] + value * value
                for point in range(points):
                    sums_ref[point, rows, :] = sums[point]

        for point in range(points):
            mean = jnp.sum(sums_ref[point], 1, keepdims=True) / width
            sums_ref[point] = jnp.broadcast_to(lax.rsqrt(mean + EPS), (subs, LANES))

    high = [dot(hots[subs:], table[:, :share]), jnp.ones((subs, LANES), F32)]
    low = [jnp.zeros((subs, LANES), F32)] * 2
    for point in range(points):
        inv = sums_ref[point]
        high.append(inv.astype(BF16).astype(F32))
        low.append(inv - high[-1])
    held = jnp.concatenate([jnp.concatenate(high, 1), jnp.concatenate(low, 1)], 0).astype(BF16)
    for index in range(length // LOOK_ROWS):
        rows = pl.ds(index * LOOK_ROWS, LOOK_ROWS)
        look_ref[rows, :] = dot(hot_ref[rows, :], table)
        subs_ref[rows, :] = dot(put_ref[rows, :], held)

    cols = points * share
    block_half = LANES // 2
    last = [[jnp.zeros((GROUP, share), F32)] * points for _ in range(2)]
    gain = gain_ref[:, pl.ds(first, share)]
    taps = [taps_ref[f, :, pl.ds(first, share)].astype(F32) for f in range(3)]
    taps = [[taps[f][tap : tap + 1] for tap in range(3)] for f in range(3)]

    for start in range(0, half, CHUNK):
        block = start // block_half
        sides = []
        for side in range(2):
            rows = pl.ds(side * half + start, CHUNK)
            sent = pl.ds(side * block_half + start % block_half, CHUNK)
            tok = look_ref[rows, :share]
            inv = look_ref[rows, share:]
            inv = inv + pltpu.roll(inv, LANES // 2, 1)
            chosen = subs_ref[rows, share : 2 * share] > 0.5
            base = jnp.where(chosen, subs_ref[rows, :share], tok)
            pair_ref[0, rows, :] = tok.astype(BF16)
            pair_ref[1, rows, :] = base.astype(BF16)
            sides.append((rows, base, tok - base, inv, chosen, msg_ref[block, sent, :].astype(F32)))
        for point in range(points):
            lanes = slice(point * share, (point + 1) * share)
            nows, backs = [], []
            for side, (rows, base, diff, inv_tok, chosen, _) in enumerate(sides):
                inv = jnp.where(
                    chosen, subs_ref[rows, (2 + point) * share : (3 + point) * share], inv_tok
                )
                inv_ref[rows, lanes] = inv
                now = rounded((base + alphas[point] * diff) * inv * gain)
                window = jnp.concatenate([last[side][point], now], 0)
                last[side][point] = now[CHUNK - GROUP :]
                nows.append(now)
                backs.append(window[GROUP - 1 : GROUP - 1 + CHUNK])
            recent = ((nows[0], backs[1], backs[0]), (nows[1], nows[0], backs[1]))
            for side in range(2):
                rows, upstream = sides[side][0], sides[side][5]
                feats = [sum(taps[f][tap] * recent[side][tap] for tap in range(3)) for f in range(3)]
                k_ref[rows, lanes] = feats[1]
                v_ref[rows, lanes] = feats[2]
                signal_ref[rows, lanes] = (feats[1] * feats[2]).astype(BF16)
                after = slice(cols + point * share, cols + (point + 1) * share)
                signal_ref[rows, after] = (upstream * feats[0]).astype(BF16)


def gradient_kernel(
    points, width, msg_ref, pair_ref, taps_ref, gain_ref,
    signal_ref, k_ref, v_ref, inv_ref, even_ref, odd_ref, even_back_ref, odd_back_ref, spec_ref,
    *refs,
):
    out_refs, (grad_ref, prod_ref, sums_ref) = refs[:-3], refs[-3:]
    half = even_ref.shape[1]
    length = 2 * half
    share = pair_ref.shape[2]
    cols = points * share
    n_ctx = msg_ref.shape[0]
    block_half = LANES // 2
    first = (lax.axis_index("ctx") * points + lax.axis_index("path")) * share
    first = pl.multiple_of(first, LANES)
    gain = gain_ref[:, pl.ds(first, share)]
    taps = [taps_ref[f, :, pl.ds(first, share)].astype(F32) for f in range(3)]
    taps = [[taps[f][tap : tap + 1] for tap in range(3)] for f in range(3)]
    alphas = [(point + 0.5) / points for point in range(points)]

    transform(even_ref, odd_ref, signal_ref, spec_ref, prod_ref, points)
    carried = [[jnp.zeros((GROUP, share), F32)] * points for _ in range(3)]
    for index in reversed(range(half // FREQ_ROWS)):
        found = []
        for back_ref, offset in ((even_back_ref, 0), (odd_back_ref, length)):
            table = back_ref[pl.ds(index * FREQ_ROWS, FREQ_ROWS), :]
            for kind in range(2):
                prod = prod_ref[offset : offset + length, kind * cols : (kind + 1) * cols]
                found.append(dot(table, prod))
        for part in reversed(range(FREQ_ROWS // CHUNK)):
            start = index * FREQ_ROWS + part * CHUNK
            block = start // block_half
            here = slice(part * CHUNK, (part + 1) * CHUNK)
            sides = []
            for side in range(2):
                rows = pl.ds(side * half + start, CHUNK)
                sent = pl.ds(side * block_half + start % block_half, CHUNK)
                base = pair_ref[1, rows, :].astype(F32)
                diff = pair_ref[0, rows, :].astype(F32) - base
                upstream = msg_ref[block, sent, :].astype(F32)
                sides.append([rows, sent, base, diff, upstream] + [jnp.zeros((CHUNK, share), F32)] * 3)
            for point in range(points):
                lanes = slice(point * share, (point + 1) * share)
                by_tap = []
                for side in range(2):
                    rows, upstream = sides[side][0], sides[side][4]
                    grad_z = found[2 * side + 1][here, lanes]
                    grads = (
                        upstream * found[2 * side][here, lanes],
                        grad_z * v_ref[rows, lanes],
                        grad_z * k_ref[rows, lanes],
                    )
                    by_tap.append([sum(taps[f][tap] * grads[f] for f in range(3)) for tap in range(3)])
                ahead = []
                for slot, value in enumerate((by_tap[0][1], by_tap[0][2], by_tap[1][2])):
                    window = jnp.concatenate([value, carried[slot][point]], 0)
                    carried[slot][point] = value[:GROUP]
                    ahead.append(window[1 : 1 + CHUNK])
                sums = (by_tap[0][0] + by_tap[1][1] + ahead[1], by_tap[1][0] + ahead[0] + ahead[2])
                for side in range(2):
                    rows, _, base, diff, _, total, sum_tok, sum_both = sides[side]
                    inv = inv_ref[rows, lanes]
                    along = inv * sums[side]
                    total = total + along
                    along = along * (base + alphas[point] * diff) * (inv * inv)
                    sum_tok = sum_tok + alphas[point] * along
                    sum_both = sum_both + along
                    sides[side][5:] = [total, sum_tok, sum_both]
            for side in range(2):
                _, sent, _, _, _, total, sum_tok, sum_both = sides[side]
                grad_ref[block, sent, :] = (gain * total).astype(BF16)
                for kind, value in enumerate((gain * sum_tok, gain * (sum_both - sum_tok))):
                    high = value.astype(BF16)
                    into = pl.ds((kind * n_ctx + block) * LANES + side * block_half + start % block_half, CHUNK)
                    sums_ref[into, :share] = high
                    sums_ref[into, share:] = (value - high.astype(F32)).astype(BF16)

    ones = jnp.ones((GROUP, 2 * share), BF16)
    row = lax.dot_general(ones, sums_ref[...], (((1,), (1,)), ((), ())), preferred_element_type=F32)
    row = row[:1] / width
    high = row.astype(BF16).astype(F32)
    for block in range(n_ctx):
        sent = []
        for kind in range(2):
            lanes = slice((kind * n_ctx + block) * LANES, (kind * n_ctx + block + 1) * LANES)
            sent += [high[:, lanes], row[:, lanes] - high[:, lanes]]
        sent.append(jnp.zeros((grad_ref.shape[1] - LANES - len(sent), LANES), F32))
        grad_ref[block, LANES:, :] = jnp.concatenate(sent, 0).astype(BF16)
    for step, ref in enumerate(out_refs):
        ref[...] = grad_ref[lax.axis_index("ctx") ^ step]


def partial_kernel(n_ctx, *refs):
    sent_refs, out_refs, grad_ref = refs[:n_ctx], refs[n_ctx:-1], refs[-1]
    rows, _ = out_refs[0].shape
    for step, ref in enumerate(sent_refs):
        grad_ref[lax.axis_index("ctx") ^ step] = ref[...]
    each = n_ctx // len(out_refs)
    spare = sum(grad_ref[block, LANES:, :].astype(F32) for block in range(n_ctx))
    sums = [spare[0:1] + spare[1:2], spare[2:3] + spare[3:4]]
    sent = []
    for value in sums:
        high = value.astype(BF16).astype(F32)
        sent += [high, value - high]
    sent.append(jnp.zeros((rows - each * LANES - len(sent), LANES), F32))
    sent = jnp.concatenate(sent, 0).astype(BF16)
    path = lax.axis_index("path")
    for step, ref in enumerate(out_refs):
        dest = path ^ step
        for piece in range(each):
            ref[piece * LANES : (piece + 1) * LANES, :] = grad_ref[dest * each + piece, :LANES, :]
        ref[each * LANES :, :] = sent


def finish_kernel(own_ref, *refs):
    grad_refs, (path_ref, attr_ref) = refs[:-2], refs[-2:]
    points = len(grad_refs)
    rows, share = grad_refs[0].shape
    pieces = rows // LANES
    spare = sum(ref[pieces * LANES :, :].astype(F32) for ref in grad_refs)
    sums = jnp.concatenate([spare[0:1] + spare[1:2], spare[2:3] + spare[3:4], spare[4:10]], 0)
    order = even_first()
    columns = transposed(exact_dot(sums, order, ((1,), (0,))))
    to_tok = columns[:, 0:1]
    to_base = columns[:, 1:2]
    order = order.T.astype(BF16)
    path = lax.axis_index("path")
    for step, ref in enumerate(grad_refs):
        for piece in range(pieces):
            first = (piece * points + (path ^ step)) * share
            lanes = pl.ds(pl.multiple_of(first, LANES), share)
            tok = own_ref[0, :, lanes].astype(F32)
            base = own_ref[1, :, lanes].astype(F32)
            grad = dot(order, ref[piece * LANES : (piece + 1) * LANES, :])
            grad = (grad - tok * to_tok - base * to_base) / points
            path_ref[:, lanes] = grad
            attr_ref[:, lanes] = (tok - base) * grad


def any_spec():
    return pl.BlockSpec(memory_space=pl.ANY)


def vmem_spec():
    return pl.BlockSpec(memory_space=pltpu.VMEM)


def hbm_spec():
    return pl.BlockSpec(memory_space=pltpu.HBM)


def call(kernel, ins, outs, scratch, flops, moved, mebibytes):
    return pl.pallas_call(
        kernel,
        in_specs=ins,
        out_specs=[spec for spec, _ in outs],
        out_shape=[shape for _, shape in outs],
        scratch_shapes=scratch,
        compiler_params=pltpu.CompilerParams(vmem_limit_bytes=mebibytes * 2**20),
        cost_estimate=pl.CostEstimate(flops=flops, bytes_accessed=moved, transcendentals=0),
    )


def shape(dims, dtype):
    return jax.ShapeDtypeStruct(dims, dtype)


def kernel_body(tokens, sub_pos, sub_base, embed, norm_gain, fir_taps, long_filter, skip_gain, cotangent):
    n_path, n_ctx = lax.axis_size("path"), lax.axis_size("ctx")
    points = n_path
    tok_rows = tokens.shape[0]
    length = tok_rows * n_ctx
    vocab, width = embed.shape
    share = width // (n_path * n_ctx)
    subs = sub_pos.shape[0] * n_ctx
    own_width = width // n_path
    cols = points * share
    half = length // 2
    tables = dft_tables(length)
    dma = pltpu.SemaphoreType.DMA
    transform_flops = 2 * length * length
    spare = 16

    def swapped(parts, axis):
        size = len(parts)
        return [
            part if step == 0 else lax.ppermute(part, axis, [(i, i ^ step) for i in range(size)])
            for step, part in enumerate(parts)
        ]

    *msgs, ids = call(
        functools.partial(pack_kernel, n_ctx),
        [hbm_spec()] * 4,
        [(vmem_spec(), shape((tok_rows + spare, share), BF16))] * n_ctx
        + [(vmem_spec(), shape((spare, LANES), F32))],
        [
            pltpu.VMEM((1, tok_rows), jnp.int32),
            pltpu.VMEM((1, sub_pos.shape[0]), jnp.int32),
            pltpu.VMEM((1, sub_pos.shape[0]), jnp.int32),
            pltpu.VMEM((tok_rows, n_ctx * share), BF16),
            dma((n_ctx + 3,)),
        ],
        length * share,
        8 * length * share,
        60,
    )(
        tokens.reshape(1, tok_rows),
        sub_pos.reshape(1, -1),
        sub_base.reshape(1, -1),
        cotangent,
    )
    msgs = swapped(msgs, "ctx")

    gain = norm_gain.reshape(1, width)
    skip = skip_gain.reshape(1, n_path * share)
    spec, gram = call(
        prepare_kernel,
        [hbm_spec()] * 5 + [any_spec()],
        [
            (any_spec(), shape((4, half, share), F32)),
            (any_spec(), shape((3 * vocab + vocab // 2, vocab), BF16)),
        ],
        [
            pltpu.VMEM((length, share), F32),
            pltpu.VMEM((length, half), BF16),
            pltpu.VMEM((length, half), BF16),
            pltpu.VMEM((vocab, width), BF16),
            pltpu.VMEM((1, share), F32),
            pltpu.VMEM((vocab, vocab), F32),
            pltpu.VMEM((4, half, share), F32),
            pltpu.VMEM((3 * vocab + vocab // 2, vocab), BF16),
            dma((8,)),
            dma((3 * vocab // LANES + 2,)),
        ],
        2 * vocab * vocab * width,
        2 * vocab * width,
        58,
    )(long_filter, tables[0], tables[1], embed, skip, ids)

    msg, hots, subs_hots, put_hots = call(
        functools.partial(ids_kernel, vocab),
        [vmem_spec()] * n_ctx,
        [
            (vmem_spec(), shape((n_ctx, tok_rows + spare, share), BF16)),
            (vmem_spec(), shape((length, vocab), BF16)),
            (vmem_spec(), shape((2 * subs, vocab), BF16)),
            (vmem_spec(), shape((length, 2 * subs), BF16)),
        ],
        [],
        2 * 10**9,
        4 * 10**6,
        8,
    )(*msgs)
    wide = 4 * LANES
    signal, k_feat, v_feat, inv, pair = call(
        functools.partial(feature_kernel, points),
        [vmem_spec()] * 7 + [hbm_spec()],
        [(vmem_spec(), shape((length, 2 * cols), BF16))]
        + [(vmem_spec(), shape((length, cols), F32))] * 3
        + [(vmem_spec(), shape((2, length, share), BF16))],
        [
            pltpu.VMEM((vocab, wide), BF16),
            pltpu.VMEM((points, subs, LANES), F32),
            pltpu.VMEM((2 * subs, wide), F32),
            pltpu.VMEM((length, 2 * share), F32),
            pltpu.VMEM((length, (2 + points) * share), F32),
            dma,
        ],
        2 * length * vocab * 3 * share,
        2 * vocab * width + 16 * length * cols,
        39,
    )(msg, hots, subs_hots, put_hots, gram, fir_taps, gain, embed)

    grads = call(
        functools.partial(gradient_kernel, points, width),
        [vmem_spec()] * 13,
        [(vmem_spec(), shape((tok_rows + spare, share), BF16))] * n_ctx,
        [
            pltpu.VMEM((n_ctx, tok_rows + spare, share), BF16),
            pltpu.VMEM((2 * length, 2 * cols), BF16),
            pltpu.VMEM((2 * length, 2 * share), BF16),
        ],
        4 * transform_flops * cols,
        4 * length * length + 16 * length * cols,
        32,
    )(msg, pair, fir_taps, gain, signal, k_feat, v_feat, inv, *tables, spec)

    own = call(
        own_kernel,
        [vmem_spec(), vmem_spec(), any_spec()],
        [(vmem_spec(), shape((2, tok_rows, own_width), BF16))],
        [],
        4 * tok_rows * vocab * own_width,
        2 * vocab * own_width,
        10,
    )(ids, embed, grads[0])[0]
    grads = swapped(grads, "ctx")
    each = n_ctx // n_path
    parts = call(
        functools.partial(partial_kernel, n_ctx),
        [vmem_spec()] * n_ctx,
        [(vmem_spec(), shape((each * tok_rows + spare, share), BF16))] * n_path,
        [pltpu.VMEM((n_ctx, tok_rows + spare, share), BF16)],
        spare * LANES * n_ctx,
        4 * length * share,
        4,
    )(*grads)
    parts = swapped(parts, "path")
    out = shape((tok_rows, own_width), F32)
    return tuple(
        call(
            finish_kernel,
            [vmem_spec()] * (1 + n_path),
            [(vmem_spec(), out), (vmem_spec(), out)],
            [],
            8 * tok_rows * own_width,
            14 * tok_rows * own_width,
            8,
        )(own, *parts)
    )


def plain_body(tokens, sub_pos, sub_base, embed, norm_gain, fir_taps, long_filter, skip_gain, cotangent):
    n_path, n_ctx = lax.axis_size("path"), lax.axis_size("ctx")
    path, ctx = lax.axis_index("path"), lax.axis_index("ctx")
    points = n_path
    tok_rows = tokens.shape[0]
    length = tok_rows * n_ctx
    width = embed.shape[1]
    share = width // (n_path * n_ctx)
    own_width = width // n_path
    first = (ctx * n_path + path) * share
    alphas = ((jnp.arange(points, dtype=jnp.int32)).astype(F32) + 0.5) / points
    alphas = alphas[:, None, None]

    local = jnp.arange(tok_rows, dtype=jnp.int32)[:, None] + ctx * tok_rows == sub_pos[None, :]
    put = jnp.sum(jnp.where(local, sub_base[None, :], 0), 1)
    base_ids = jnp.where(jnp.any(local, 1), put, tokens)
    rows_tok = jnp.take(embed, tokens, axis=0).astype(F32)
    rows_base = jnp.take(embed, base_ids, axis=0).astype(F32)
    rows_in = rows_base[None] + alphas * (rows_tok - rows_base)[None]
    inv = lax.rsqrt(jnp.mean(rows_in * rows_in, -1) + EPS)
    inv = lax.all_gather(inv, "ctx", axis=1, tiled=True)[:, :, None]
    all_tok = lax.all_gather(tokens, "ctx", tiled=True)
    all_base = lax.all_gather(base_ids, "ctx", tiled=True)

    cot = cotangent.reshape(tok_rows, n_ctx, n_path, share)
    cot = lax.dynamic_index_in_dim(cot, path, 2, keepdims=False)
    cot = lax.all_to_all(cot.transpose(1, 0, 2), "ctx", 0, 0, tiled=True)
    upstream = cot.reshape(1, length, share).astype(F32)
    mine = lax.dynamic_slice_in_dim(embed, first, share, 1)
    gain = lax.dynamic_slice_in_dim(norm_gain, first, share, 0)
    taps = lax.dynamic_slice_in_dim(fir_taps, first, share, 2).astype(F32)
    filt = lax.dynamic_slice_in_dim(long_filter, path * share, share, 1)
    skip = lax.dynamic_slice_in_dim(skip_gain, path * share, share, 0)

    emb_tok = jnp.take(mine, all_tok, axis=0).astype(F32)
    emb_base = jnp.take(mine, all_base, axis=0).astype(F32)
    inputs = emb_base[None] + alphas * (emb_tok - emb_base)[None]
    normed = rounded(inputs * inv * gain)
    q_feat, k_feat, v_feat = (
        taps[f, 0] * normed + taps[f, 1] * shifted(normed, 1) + taps[f, 2] * shifted(normed, 2)
        for f in range(3)
    )
    filter_spec = spectrum(filt[None])
    conv = rounded(long_conv(rounded(k_feat * v_feat), filter_spec, skip, False))
    grad_z = rounded(long_conv(rounded(upstream * q_feat), filter_spec, skip, True))
    grads = (rounded(upstream * conv), rounded(grad_z * v_feat), rounded(grad_z * k_feat))
    by_tap = [sum(taps[f, tap] * grads[f] for f in range(3)) for tap in range(3)]
    scaled = gain * (by_tap[0] + shifted(by_tap[1], -1) + shifted(by_tap[2], -2))
    grad = jnp.sum(inv * scaled, 0).astype(BF16)
    along = jnp.sum(inputs * scaled, -1, keepdims=True) * inv**3 / width
    part = jnp.stack([jnp.sum(alphas * along, 0)[:, 0], jnp.sum((1.0 - alphas) * along, 0)[:, 0]])
    part = lax.psum(part, ("path", "ctx"))
    part = lax.dynamic_slice_in_dim(part, ctx * tok_rows, tok_rows, 1)

    back = lax.all_to_all(grad.reshape(n_ctx, tok_rows, share), "ctx", 0, 0, tiled=True)
    back = back.reshape(n_path, n_ctx // n_path, tok_rows, share)
    back = lax.all_to_all(back, "path", 0, 0, tiled=True).astype(F32)
    back = back.transpose(2, 1, 0, 3).reshape(tok_rows, own_width)
    own_tok = lax.dynamic_slice_in_dim(rows_tok, path * own_width, own_width, 1)
    own_base = lax.dynamic_slice_in_dim(rows_base, path * own_width, own_width, 1)
    grad = (back - own_tok * part[0][:, None] - own_base * part[1][:, None]) / points
    return (grad, (own_tok - own_base) * grad)


def body(tokens, sub_pos, sub_base, embed, *rest):
    n_path, n_ctx = lax.axis_size("path"), lax.axis_size("ctx")
    tok_rows = tokens.shape[0]
    share = embed.shape[1] // (n_path * n_ctx)
    tables = 4 * (tok_rows * n_ctx) ** 2
    fits = share == LANES and tok_rows == LANES and n_ctx == GROUP and tables <= TABLE_BYTES
    fits = fits and n_ctx % n_path == 0 and n_path & (n_path - 1) == 0
    chosen = kernel_body if fits else plain_body
    return chosen(tokens, sub_pos, sub_base, embed, *rest)


def solution(mesh):
    return jax.shard_map(
        body,
        mesh=mesh,
        in_specs=(
            P("ctx"),
            P("ctx"),
            P("ctx"),
            P(),
            P(),
            P(),
            P(None, "ctx"),
            P("ctx"),
            P("ctx", None),
        ),
        out_specs=(P("ctx", "path"), P("ctx", "path")),
        check_vma=False,
    )
```

```python
import functools

import jax
import jax.numpy as jnp
import ml_dtypes
import numpy as np
from jax import lax
from jax.experimental import pallas as pl
from jax.experimental.pallas import tpu as pltpu
from jax.sharding import PartitionSpec as P

LANES = 128
GROUP = 8
FREQ_ROWS = 256
LOOK_ROWS = 256
CHUNK = 32
EPS = 1e-06
CANCEL = 0.004
TABLE_BYTES = 4 * 2**20
F32 = jnp.float32
BF16 = jnp.bfloat16
precise = lax.Precision.HIGH


def angle_tables(length):
    outer_size = 64
    inner_size = length // outer_size
    outer_idx = jnp.arange(outer_size, dtype=jnp.int32)
    inner_idx = jnp.arange(inner_size, dtype=jnp.int32)
    outer_angle = (
        2.0 * jnp.pi / outer_size
        * (outer_idx[:, None] * outer_idx[None, :] % outer_size).astype(F32)
    )
    inner_angle = (
        2.0 * jnp.pi / inner_size
        * (inner_idx[:, None] * inner_idx[None, :] % inner_size).astype(F32)
    )
    twist_angle = (
        2.0 * jnp.pi / length
        * (outer_idx[:, None] * inner_idx[None, :] % length).astype(F32)
    )
    return (outer_angle, inner_angle, twist_angle)


def complex_table(angle, sign):
    cosine = jnp.cos(angle)
    sine = sign * jnp.sin(angle)
    return jnp.stack([jnp.stack([cosine, sine]), jnp.stack([-sine, cosine])])


def twisted(values, angle, sign):
    cosine = jnp.cos(angle)[None, :, :, None]
    sine = sign * jnp.sin(angle)[None, :, :, None]
    real_part = values[:, 0]
    imag_part = values[:, 1]
    return jnp.stack(
        [real_part * cosine - imag_part * sine, real_part * sine + imag_part * cosine], 1
    )


def spectrum(signal):
    batch, half, width = signal.shape
    length = 2 * half
    outer_angle, inner_angle, twist_angle = angle_tables(length)
    outer_size = outer_angle.shape[0]
    inner_size = inner_angle.shape[0]
    folded = signal.reshape(batch, outer_size // 2, inner_size, width)
    used = outer_angle[:, : outer_size // 2]
    outer_table = jnp.stack([jnp.cos(used), -jnp.sin(used)])
    first = jnp.einsum("rka,pabc->prkbc", outer_table, folded, precision=precise)
    turned = twisted(first, twist_angle, -1.0)
    return jnp.einsum(
        "prkbc,rsbm->pskmc", turned, complex_table(inner_angle, -1.0), precision=precise
    )


def inverse(spec):
    batch, parts, outer_size, inner_size, width = spec.shape
    length = outer_size * inner_size
    outer_angle, inner_angle, twist_angle = angle_tables(length)
    back = jnp.einsum("pskmc,stmb->ptkbc", spec, complex_table(inner_angle, 1.0), precision=precise)
    turned = twisted(back, twist_angle, 1.0)
    used = outer_angle[: outer_size // 2]
    outer_table = jnp.stack([jnp.cos(used), -jnp.sin(used)])
    result = jnp.einsum("rak,prkbc->pabc", outer_table, turned, precision=precise)
    return (result / length).reshape(batch, length // 2, width)


def long_conv(signal, filter_spec, skip_gain, adjoint):
    spec = spectrum(signal)
    sig_real = spec[:, 0]
    sig_imag = spec[:, 1]
    filt_real = filter_spec[:, 0]
    filt_imag = filter_spec[:, 1]
    if adjoint:
        prod_real = sig_real * filt_real + sig_imag * filt_imag
        prod_imag = sig_imag * filt_real - sig_real * filt_imag
    else:
        prod_real = sig_real * filt_real - sig_imag * filt_imag
        prod_imag = sig_real * filt_imag + sig_imag * filt_real
    return inverse(jnp.stack([prod_real, prod_imag], 1)) + skip_gain * signal


def rounded(value):
    return value.astype(BF16).astype(F32)


def shifted(values, step):
    zeros = jnp.zeros_like(values[:, : abs(step)])
    if step > 0:
        return jnp.concatenate([zeros, values[:, :-step]], 1)
    return jnp.concatenate([values[:, -step:], zeros], 1)


@functools.lru_cache(maxsize=None)
def dft_tables(length):
    half = length // 2
    freq = 4 * np.arange(half, dtype=np.int64) + 1
    place = np.arange(half, dtype=np.int64)
    tables = []
    for offset in (0, 1):
        turns = freq[:, None] * (2 * place + offset)[None, :] % (8 * half)
        angle = turns * (2.0 * np.pi / (8 * half))
        cosine = np.cos(angle).astype(ml_dtypes.bfloat16)
        sine = np.sin(angle).astype(ml_dtypes.bfloat16)
        tables.append((np.concatenate([cosine, sine], 0), np.concatenate([cosine.T, sine.T], 1)))
    return (tables[0][0], tables[1][0], tables[0][1], tables[1][1])


def transposed(rows):
    count = rows.shape[0]
    if count < LANES:
        rows = jnp.concatenate([rows, jnp.zeros((LANES - count, LANES), F32)], 0)
    return rows.T


def dot(left, right):
    return jnp.dot(left, right, preferred_element_type=F32)


def exact_dot(left, right, dims):
    return lax.dot_general(
        left, right, (dims, ((), ())), precision=lax.Precision.HIGHEST, preferred_element_type=F32
    )


def iota(dims, axis):
    return lax.broadcasted_iota(jnp.int32, dims, axis)


def even_first():
    row = iota((LANES, LANES), 0)
    half = LANES // 2
    source = jnp.where(row < half, 2 * row, 2 * (row - half) + 1)
    return (iota((LANES, LANES), 1) == source).astype(F32)


def hot(ids, vocab):
    lane = iota(ids.shape, 1).astype(F32)
    parts = [
        (ids == lane + float(column * LANES)).astype(F32).astype(BF16)
        for column in range(vocab // LANES)
    ]
    return jnp.concatenate(parts, 1)


def joined(block, kind):
    return 256.0 * block[2 * kind : 2 * kind + 1] + block[2 * kind + 1 : 2 * kind + 2]


def pack_kernel(
    tok_hbm, pos_hbm, put_hbm, cot_hbm, msg_ref, ids_ref, tok_ref, pos_ref, put_ref, cot_ref, sems
):
    dests, rows, share = msg_ref.shape
    tok_rows = cot_hbm.shape[0]
    n_path = cot_hbm.shape[1] // (dests * share)
    path = lax.axis_index("path")
    moves = [(tok_hbm, tok_ref), (pos_hbm, pos_ref), (put_hbm, put_ref)]
    for dest in range(dests):
        lanes = pl.ds(pl.multiple_of((dest * n_path + path) * share, LANES), share)
        moves.append((cot_hbm.at[:, lanes], cot_ref.at[:, pl.ds(dest * share, share)]))
    copies = [
        pltpu.make_async_copy(source, target, sems.at[index])
        for index, (source, target) in enumerate(moves)
    ]
    for copy in copies:
        copy.start()
    order = even_first().astype(BF16)
    for copy in copies[:3]:
        copy.wait()
    lists = []
    for ref in (tok_ref, pos_ref, put_ref):
        value = ref[...].astype(F32)
        if value.shape[1] < LANES:
            value = jnp.concatenate([value, jnp.zeros((1, LANES - value.shape[1]), F32)], 1)
        high = jnp.floor(value * (1.0 / 256.0))
        lists += [high, value - 256.0 * high]
    lists.append(jnp.zeros((rows - tok_rows - len(lists), LANES), F32))
    ids = jnp.concatenate(lists, 0)
    ids_ref[...] = ids
    turned = lax.dot_general(
        ids.astype(BF16), order, (((1,), (1,)), ((), ())), preferred_element_type=F32
    )
    ids = jnp.where(iota(ids.shape, 0) < 2, turned, ids).astype(BF16)
    for dest in range(dests):
        msg_ref[dest, tok_rows:, :] = ids
    for copy in copies[3:]:
        copy.wait()
    turned = dot(order, cot_ref[...]).astype(BF16)
    for dest in range(dests):
        msg_ref[dest, :tok_rows, :] = turned[:, dest * share : (dest + 1) * share]


def prepare_kernel(
    filt_hbm, even_hbm, odd_hbm, embed_hbm, skip_hbm, after_ref,
    spec_hbm, gram_hbm,
    filt_ref, even_ref, odd_ref, embed_ref, skip_ref, sum_ref, spec_ref, gram_ref, sems, out_sems,
):
    length, share = filt_ref.shape
    half = length // 2
    vocab, width = embed_ref.shape
    pieces = sems.shape[0] - 4
    wide = width // pieces
    path = lax.axis_index("path")
    lanes = pl.ds(pl.multiple_of(path * share, LANES), share)
    moves = [
        (filt_hbm.at[:, lanes], filt_ref),
        (skip_hbm.at[:, lanes], skip_ref),
        (even_hbm, even_ref),
        (odd_hbm, odd_ref),
    ]
    for index in range(pieces):
        lanes = pl.ds(index * wide, wide)
        moves.append((embed_hbm.at[:, lanes], embed_ref.at[:, lanes]))
    copies = [
        pltpu.make_async_copy(source, target, sems.at[index])
        for index, (source, target) in enumerate(moves)
    ]
    for copy in copies:
        copy.start()

    copies[0].wait()
    copies[1].wait()
    filt_ref[0:1, :] = filt_ref[0:1, :] + skip_ref[...]
    parts = []
    for offset in range(2):
        value = filt_ref[pl.ds(offset, half, stride=2), :] * (1.0 / length)
        high = value.astype(BF16)
        parts.append(jnp.concatenate([high, (value - high.astype(F32)).astype(BF16)], 1))
    copies[2].wait()
    copies[3].wait()
    for index in range(half // FREQ_ROWS):
        found = []
        for table, part in ((even_ref, parts[0]), (odd_ref, parts[1])):
            for offset in (0, half):
                both = dot(table[pl.ds(offset + index * FREQ_ROWS, FREQ_ROWS), :], part)
                found.append(both[:, :share] + both[:, share:])
        rows = pl.ds(index * FREQ_ROWS, FREQ_ROWS)
        spec_ref[0, rows, :] = found[0] + found[2]
        spec_ref[1, rows, :] = -found[1] - found[3]
        spec_ref[2, rows, :] = found[0] - found[2]
        spec_ref[3, rows, :] = found[3] - found[1]
    outs = [pltpu.make_async_copy(spec_ref, spec_hbm, out_sems.at[0])]
    outs[0].start()

    sum_ref[vocab // 2 :, : vocab // 2] = jnp.zeros((vocab // 2, vocab // 2), F32)
    for index in range(pieces):
        copies[4 + index].wait()
        part = embed_ref[:, index * wide : (index + 1) * wide]
        for rows, lanes in ((slice(0, vocab // 2), slice(0, vocab)), (slice(vocab // 2, vocab),) * 2):
            found = lax.dot_general(
                part[rows], part[lanes], (((1,), (1,)), ((), ())), preferred_element_type=F32
            )
            if index == 0:
                sum_ref[rows, lanes] = found
            else:
                sum_ref[rows, lanes] += found
    first = (lax.axis_index("ctx") * lax.axis_size("path") + path) * share
    mine = embed_ref[:, pl.ds(pl.multiple_of(first, LANES), share)]
    same = iota((LANES, LANES), 0) == iota((LANES, LANES), 1)
    lane = iota((LANES, LANES), 1)
    below = 3 * vocab
    for block in range(vocab // LANES):
        rows = slice(block * LANES, (block + 1) * LANES)
        value = sum_ref[rows, :]
        norm = jnp.sum(jnp.where(same, value[:, rows], 0.0), 1, keepdims=True)
        inv = jnp.broadcast_to(lax.rsqrt(norm / width + EPS), (LANES, LANES))
        high = inv.astype(BF16).astype(F32)
        inv = jnp.where(lane < LANES // 2, high, inv - high).astype(BF16)
        side, start = block * LANES // (vocab // 2), block * LANES % (vocab // 2)
        into = slice(below + start, below + start + LANES)
        left = side * (share + LANES)
        gram_ref[into, left : left + share] = mine[rows]
        gram_ref[into, left + share : left + share + LANES] = inv
        for part in range(3):
            high = value.astype(BF16)
            into = slice(part * vocab + block * LANES, part * vocab + (block + 1) * LANES)
            gram_ref[into, :] = high
            value = value - high.astype(F32)
            into = pl.ds(part * vocab + block * LANES, LANES)
            sem = out_sems.at[1 + block * 3 + part]
            outs.append(pltpu.make_async_copy(gram_ref.at[into], gram_hbm.at[into], sem))
            outs[-1].start()
    into = pl.ds(below, vocab // 2)
    outs.append(pltpu.make_async_copy(gram_ref.at[into], gram_hbm.at[into], out_sems.at[out_sems.shape[0] - 1]))
    outs[-1].start()
    for copy in outs:
        copy.wait()


def own_kernel(ids_ref, embed_ref, grad_ref, own_ref):
    vocab = embed_ref.shape[0]
    own_width = own_ref.shape[2]
    lanes = pl.ds(pl.multiple_of(lax.axis_index("path") * own_width, LANES), own_width)
    ids = ids_ref[...]
    columns = transposed(jnp.concatenate([joined(ids, kind) for kind in range(3)], 0))
    tok = jnp.broadcast_to(columns[:, 0:1], (LANES, LANES))
    place = jnp.broadcast_to(joined(ids, 1), (LANES, LANES))
    put = jnp.broadcast_to(joined(ids, 2), (LANES, LANES))
    first = lax.axis_index("ctx") * LANES
    subs = LANES // GROUP
    here = (place == (iota((LANES, LANES), 0) + first).astype(F32)) & (iota((LANES, LANES), 1) < subs)
    found = jnp.max(jnp.where(here, put, -1.0), 1, keepdims=True)
    base = jnp.where(found >= 0.0, found, tok)
    hots = jnp.concatenate([hot(tok, vocab), hot(base, vocab)], 0)
    both = dot(hots, embed_ref[:, lanes]).astype(BF16)
    own_ref[0] = both[:LANES]
    own_ref[1] = both[LANES:]


def forward_rows(tables, signal_ref, signal, index):
    half = tables[0].shape[1]
    found = []
    for side, table in enumerate(tables):
        for offset in (0, half):
            rows = pl.ds(offset + index * FREQ_ROWS, FREQ_ROWS)
            found.append(dot(table[rows, :], signal_ref[side * half : (side + 1) * half, signal]))
    return found


def multiply_rows(found, spec_ref, prod_ref, points, kind, index):
    _, half, share = spec_ref.shape
    for inside in range(0, FREQ_ROWS, CHUNK):
        here = slice(inside, inside + CHUNK)
        start = index * FREQ_ROWS + inside
        filt = [spec_ref[part, start : start + CHUNK, :] for part in range(4)]
        for point in range(points):
            lanes = slice(point * share, (point + 1) * share)
            prods = []
            for part in (0, 2):
                if part == 0:
                    real = found[0][here, lanes] + found[2][here, lanes]
                    imag = found[1][here, lanes] + found[3][here, lanes]
                else:
                    real = found[0][here, lanes] - found[2][here, lanes]
                    imag = found[1][here, lanes] - found[3][here, lanes]
                if kind == 1:
                    prods.append(real * filt[part] - imag * filt[part + 1])
                    prods.append(real * filt[part + 1] + imag * filt[part])
                else:
                    prods.append(real * filt[part] + imag * filt[part + 1])
                    prods.append(imag * filt[part] - real * filt[part + 1])
            sums = (prods[0] + prods[2], prods[1] + prods[3], prods[0] - prods[2], prods[1] - prods[3])
            lanes = slice((kind * points + point) * share, (kind * points + point + 1) * share)
            for part, value in enumerate(sums):
                prod_ref[part * half + start : part * half + start + CHUNK, lanes] = value.astype(BF16)


def ids_kernel(vocab, msg_ref, hot_ref, subs_ref, put_ref):
    length = hot_ref.shape[0]
    half = length // 2
    n_ctx = msg_ref.shape[0]
    block_half = LANES // 2
    per_block = LANES // GROUP
    subs = n_ctx * per_block
    blocks = [msg_ref[block, LANES:, :].astype(F32) for block in range(n_ctx)]
    toks = transposed(jnp.concatenate([joined(block, 0) for block in blocks], 0))
    spread = sum(
        blocks[block] if block == 0 else pltpu.roll(blocks[block], block * per_block, 1)
        for block in range(n_ctx)
    )
    place = joined(spread, 1)
    put = joined(spread, 2)
    back = jnp.floor(place * 0.5)
    place = back + (place - 2.0 * back) * half
    columns = transposed(jnp.concatenate([place, put], 0))
    for block in range(n_ctx):
        column = jnp.broadcast_to(toks[:, block : block + 1], (LANES, LANES))
        rows = hot(column, vocab)
        hot_ref[block * block_half : (block + 1) * block_half, :] = rows[:block_half]
        hot_ref[half + block * block_half : half + (block + 1) * block_half, :] = rows[block_half:]
    subs_ref[subs:, :] = hot(jnp.broadcast_to(columns[:, 1:2], (subs, LANES)), vocab)
    pick = jnp.concatenate(
        [
            (columns[:, 0:1] == (iota((subs, LANES), 1) + part * LANES).astype(F32)).astype(F32).astype(BF16)
            for part in range(length // LANES)
        ],
        1,
    )
    for index in range(length // LANES):
        row = (iota((LANES, subs), 0) + index * LANES).astype(F32)
        here = (row == place[:, :subs]).astype(F32).astype(BF16)
        put_ref[index * LANES : (index + 1) * LANES, :] = jnp.concatenate([here, here], 1)
    subs_ref[:subs, :] = dot(pick, hot_ref[...]).astype(BF16)


def feature_kernel(
    points, msg_ref, hot_ref, subs_hot_ref, put_ref, gram_ref, taps_ref, gain_ref, embed_hbm,
    signal_ref, k_ref, v_ref, inv_ref, pair_ref,
    embed_ref, sums_ref, found_ref, look_ref, subs_ref, sem,
):
    length = signal_ref.shape[0]
    half = length // 2
    vocab, width = embed_hbm.shape
    share = pair_ref.shape[2]
    subs = subs_hot_ref.shape[0] // 2
    first = (lax.axis_index("ctx") * points + lax.axis_index("path")) * share
    first = pl.multiple_of(first, LANES)
    below = 3 * vocab
    table = jnp.concatenate(
        [gram_ref[below:, : share + LANES], gram_ref[below:, share + LANES :]], 0
    )

    for index in range(length // LOOK_ROWS):
        rows = pl.ds(index * LOOK_ROWS, LOOK_ROWS)
        look_ref[rows, :] = dot(hot_ref[rows, :], table)

    alphas = [(point + 0.5) / points for point in range(points)]
    hots = subs_hot_ref[...]
    found = dot(jnp.concatenate([hots] * 3, 1), gram_ref[:below, :])
    hot_tok32, hot_base32 = hots[:subs].astype(F32), hots[subs:].astype(F32)
    tok_tok = jnp.sum(found[:subs] * hot_tok32, 1, keepdims=True)
    tok_base = jnp.sum(found[:subs] * hot_base32, 1, keepdims=True)
    base_tok = jnp.sum(found[subs:] * hot_tok32, 1, keepdims=True)
    tok_base = jnp.where(tok_base == 0.0, base_tok, tok_base)
    base_base = jnp.sum(found[subs:] * hot_base32, 1, keepdims=True)
    cancels = jnp.zeros((subs, 1), F32)
    for point in range(points):
        alpha = alphas[point]
        terms = (1.0 - alpha) ** 2 * base_base + alpha**2 * tok_tok
        total = terms + 2.0 * alpha * (1.0 - alpha) * tok_base
        cancels = jnp.maximum(cancels, (total < CANCEL * terms).astype(F32))
        inv = lax.rsqrt(jnp.maximum(total, 0.0) / width + EPS)
        sums_ref[point] = jnp.broadcast_to(inv, (subs, LANES))

    @pl.when(jnp.max(cancels) > 0.5)
    def _():
        sums_ref[...] = jnp.zeros_like(sums_ref)
        wide = found_ref.shape[1]

        @pl.loop(0, width // wide)
        def _(step):
            lanes = pl.ds(pl.multiple_of(step * wide, wide), wide)
            copy = pltpu.make_async_copy(embed_hbm.at[:, lanes], embed_ref, sem)
            copy.start()
            copy.wait()
            found_ref[...] = dot(hots, embed_ref[...])
            for block in range(subs // GROUP):
                rows = slice(block * GROUP, (block + 1) * GROUP)
                sums = [sums_ref[point, rows, :] for point in range(points)]
                for column in range(wide // LANES):
                    cut = slice(column * LANES, (column + 1) * LANES)
                    base = found_ref[subs + block * GROUP : subs + (block + 1) * GROUP, cut]
                    diff = found_ref[rows, cut] - base
                    for point in range(points):
                        value = base + alphas[point] * diff
                        sums[point] = sums[point] + value * value
                for point in range(points):
                    sums_ref[point, rows, :] = sums[point]

        for point in range(points):
            mean = jnp.sum(sums_ref[point], 1, keepdims=True) / width
            sums_ref[point] = jnp.broadcast_to(lax.rsqrt(mean + EPS), (subs, LANES))

    high = [dot(hots[subs:], table[:, :share]), jnp.ones((subs, LANES), F32)]
    low = [jnp.zeros((subs, LANES), F32)] * 2
    for point in range(points):
        inv = sums_ref[point]
        high.append(inv.astype(BF16).astype(F32))
        low.append(inv - high[-1])
    held = jnp.concatenate([jnp.concatenate(high, 1), jnp.concatenate(low, 1)], 0).astype(BF16)
    for index in range(length // LOOK_ROWS):
        rows = pl.ds(index * LOOK_ROWS, LOOK_ROWS)
        subs_ref[rows, :] = dot(put_ref[rows, :], held)

    cols = points * share
    block_half = LANES // 2
    last = [[jnp.zeros((GROUP, share), F32)] * points for _ in range(2)]
    gain = gain_ref[:, pl.ds(first, share)]
    taps = [taps_ref[f, :, pl.ds(first, share)].astype(F32) for f in range(3)]
    taps = [[taps[f][tap : tap + 1] for tap in range(3)] for f in range(3)]

    for start in range(0, half, CHUNK):
        block = start // block_half
        sides = []
        for side in range(2):
            rows = pl.ds(side * half + start, CHUNK)
            sent = pl.ds(side * block_half + start % block_half, CHUNK)
            tok = look_ref[rows, :share]
            inv = look_ref[rows, share:]
            inv = inv + pltpu.roll(inv, LANES // 2, 1)
            chosen = subs_ref[rows, share : 2 * share] > 0.5
            base = jnp.where(chosen, subs_ref[rows, :share], tok)
            pair_ref[0, rows, :] = tok.astype(BF16)
            pair_ref[1, rows, :] = base.astype(BF16)
            sides.append((rows, base, tok - base, inv, chosen, msg_ref[block, sent, :].astype(F32)))
        for point in range(points):
            lanes = slice(point * share, (point + 1) * share)
            nows, backs = [], []
            for side, (rows, base, diff, inv_tok, chosen, _) in enumerate(sides):
                inv = jnp.where(
                    chosen, subs_ref[rows, (2 + point) * share : (3 + point) * share], inv_tok
                )
                inv_ref[rows, lanes] = inv
                now = rounded((base + alphas[point] * diff) * inv * gain)
                window = jnp.concatenate([last[side][point], now], 0)
                last[side][point] = now[CHUNK - GROUP :]
                nows.append(now)
                backs.append(window[GROUP - 1 : GROUP - 1 + CHUNK])
            recent = ((nows[0], backs[1], backs[0]), (nows[1], nows[0], backs[1]))
            for side in range(2):
                rows, upstream = sides[side][0], sides[side][5]
                feats = [sum(taps[f][tap] * recent[side][tap] for tap in range(3)) for f in range(3)]
                k_ref[rows, lanes] = feats[1]
                v_ref[rows, lanes] = feats[2]
                signal_ref[rows, lanes] = (feats[1] * feats[2]).astype(BF16)
                after = slice(cols + point * share, cols + (point + 1) * share)
                signal_ref[rows, after] = (upstream * feats[0]).astype(BF16)


def gradient_kernel(
    points, width, msg_ref, pair_ref, taps_ref, gain_ref,
    signal_ref, k_ref, v_ref, inv_ref, even_ref, odd_ref, even_back_ref, odd_back_ref, spec_ref,
    grad_ref,
    prod_ref, sums_ref,
):
    half = even_ref.shape[1]
    length = 2 * half
    share = pair_ref.shape[2]
    cols = points * share
    n_ctx = msg_ref.shape[0]
    block_half = LANES // 2
    first = (lax.axis_index("ctx") * points + lax.axis_index("path")) * share
    first = pl.multiple_of(first, LANES)
    gain = gain_ref[:, pl.ds(first, share)]
    taps = [taps_ref[f, :, pl.ds(first, share)].astype(F32) for f in range(3)]
    taps = [[taps[f][tap : tap + 1] for tap in range(3)] for f in range(3)]
    alphas = [(point + 0.5) / points for point in range(points)]

    tables = (even_ref, odd_ref)
    backs = (even_back_ref, odd_back_ref)
    blocks = range(half // FREQ_ROWS)
    signals = [slice(kind * cols, (kind + 1) * cols) for kind in range(2)]

    def inverse_rows(kind, index):
        rows = pl.ds(index * FREQ_ROWS, FREQ_ROWS)
        return [
            dot(back[rows, :], prod_ref[side * length : (side + 1) * length, signals[kind]])
            for side, back in enumerate(backs)
        ]

    first_found = [forward_rows(tables, signal_ref, signals[0], index) for index in blocks]
    second_found = []
    for index in blocks:
        second_found.append(forward_rows(tables, signal_ref, signals[1], index))
        multiply_rows(first_found[index], spec_ref, prod_ref, points, 0, index)
    conv = {}
    for index in blocks:
        conv[index] = inverse_rows(0, index)
        multiply_rows(second_found[index], spec_ref, prod_ref, points, 1, index)
    grad_y = {index: inverse_rows(1, index) for index in reversed(blocks)}

    carried = [[jnp.zeros((GROUP, share), F32)] * points for _ in range(3)]
    for index in reversed(blocks):
        found = [conv[index][0], grad_y[index][0], conv[index][1], grad_y[index][1]]
        for part in reversed(range(FREQ_ROWS // CHUNK)):
            start = index * FREQ_ROWS + part * CHUNK
            block = start // block_half
            here = slice(part * CHUNK, (part + 1) * CHUNK)
            sides = []
            for side in range(2):
                rows = pl.ds(side * half + start, CHUNK)
                sent = pl.ds(side * block_half + start % block_half, CHUNK)
                base = pair_ref[1, rows, :].astype(F32)
                diff = pair_ref[0, rows, :].astype(F32) - base
                upstream = msg_ref[block, sent, :].astype(F32)
                sides.append([rows, sent, base, diff, upstream] + [jnp.zeros((CHUNK, share), F32)] * 3)
            for point in range(points):
                lanes = slice(point * share, (point + 1) * share)
                by_tap = []
                for side in range(2):
                    rows, upstream = sides[side][0], sides[side][4]
                    grad_z = found[2 * side + 1][here, lanes]
                    grads = (
                        upstream * found[2 * side][here, lanes],
                        grad_z * v_ref[rows, lanes],
                        grad_z * k_ref[rows, lanes],
                    )
                    by_tap.append([sum(taps[f][tap] * grads[f] for f in range(3)) for tap in range(3)])
                ahead = []
                for slot, value in enumerate((by_tap[0][1], by_tap[0][2], by_tap[1][2])):
                    window = jnp.concatenate([value, carried[slot][point]], 0)
                    carried[slot][point] = value[:GROUP]
                    ahead.append(window[1 : 1 + CHUNK])
                sums = (by_tap[0][0] + by_tap[1][1] + ahead[1], by_tap[1][0] + ahead[0] + ahead[2])
                for side in range(2):
                    rows, _, base, diff, _, total, sum_tok, sum_both = sides[side]
                    inv = inv_ref[rows, lanes]
                    along = inv * sums[side]
                    total = total + along
                    along = along * (base + alphas[point] * diff) * (inv * inv)
                    sum_tok = sum_tok + alphas[point] * along
                    sum_both = sum_both + along
                    sides[side][5:] = [total, sum_tok, sum_both]
            for side in range(2):
                _, sent, _, _, _, total, sum_tok, sum_both = sides[side]
                grad_ref[block, sent, :] = (gain * total).astype(BF16)
                for kind, value in enumerate((gain * sum_tok, gain * (sum_both - sum_tok))):
                    high = value.astype(BF16)
                    into = pl.ds((kind * n_ctx + block) * LANES + side * block_half + start % block_half, CHUNK)
                    sums_ref[into, :share] = high
                    sums_ref[into, share:] = (value - high.astype(F32)).astype(BF16)

    ones = jnp.ones((GROUP, 2 * share), BF16)
    row = lax.dot_general(ones, sums_ref[...], (((1,), (1,)), ((), ())), preferred_element_type=F32)
    row = row[:1] / width
    high = row.astype(BF16).astype(F32)
    for block in range(n_ctx):
        sent = []
        for kind in range(2):
            lanes = slice((kind * n_ctx + block) * LANES, (kind * n_ctx + block + 1) * LANES)
            sent += [high[:, lanes], row[:, lanes] - high[:, lanes]]
        sent.append(jnp.zeros((grad_ref.shape[1] - LANES - len(sent), LANES), F32))
        grad_ref[block, LANES:, :] = jnp.concatenate(sent, 0).astype(BF16)


def partial_kernel(grad_ref, *out_refs):
    rows, _ = out_refs[0].shape
    n_ctx = grad_ref.shape[0]
    each = n_ctx // len(out_refs)
    spare = sum(grad_ref[block, LANES:, :].astype(F32) for block in range(n_ctx))
    sums = [spare[0:1] + spare[1:2], spare[2:3] + spare[3:4]]
    sent = []
    for value in sums:
        high = value.astype(BF16).astype(F32)
        sent += [high, value - high]
    sent.append(jnp.zeros((rows - each * LANES - len(sent), LANES), F32))
    sent = jnp.concatenate(sent, 0).astype(BF16)
    path = lax.axis_index("path")
    for step, ref in enumerate(out_refs):
        dest = path ^ step
        for piece in range(each):
            ref[piece * LANES : (piece + 1) * LANES, :] = grad_ref[dest * each + piece, :LANES, :]
        ref[each * LANES :, :] = sent


def finish_kernel(own_ref, *refs):
    grad_refs, (path_hbm, attr_hbm, path_ref, attr_ref, sems) = refs[:-5], refs[-5:]
    points = len(grad_refs)
    rows, share = grad_refs[0].shape
    pieces = rows // LANES
    spare = sum(ref[pieces * LANES :, :].astype(F32) for ref in grad_refs)
    sums = jnp.concatenate([spare[0:1] + spare[1:2], spare[2:3] + spare[3:4], spare[4:]], 0)
    order = even_first()
    columns = transposed(exact_dot(sums, order, ((1,), (0,))))
    to_tok = columns[:, 0:1]
    to_base = columns[:, 1:2]
    order = order.T.astype(BF16)
    path = lax.axis_index("path")
    copies = []
    for step, ref in enumerate(grad_refs):
        for piece in range(pieces):
            slot = step * pieces + piece
            first = (piece * points + (path ^ step)) * share
            lanes = pl.ds(pl.multiple_of(first, LANES), share)
            tok = own_ref[0, :, lanes].astype(F32)
            base = own_ref[1, :, lanes].astype(F32)
            grad = dot(order, ref[piece * LANES : (piece + 1) * LANES, :])
            grad = (grad - tok * to_tok - base * to_base) / points
            path_ref[slot] = grad
            attr_ref[slot] = (tok - base) * grad
            for kind, (source, target) in enumerate(((path_ref, path_hbm), (attr_ref, attr_hbm))):
                copies.append(
                    pltpu.make_async_copy(source.at[slot], target.at[:, lanes], sems.at[kind, slot])
                )
                copies[-1].start()
    for copy in copies:
        copy.wait()


def any_spec():
    return pl.BlockSpec(memory_space=pl.ANY)


def vmem_spec():
    return pl.BlockSpec(memory_space=pltpu.VMEM)


def hbm_spec():
    return pl.BlockSpec(memory_space=pltpu.HBM)


def call(kernel, ins, outs, scratch, flops, moved, mebibytes):
    return pl.pallas_call(
        kernel,
        in_specs=ins,
        out_specs=[spec for spec, _ in outs],
        out_shape=[shape for _, shape in outs],
        scratch_shapes=scratch,
        compiler_params=pltpu.CompilerParams(vmem_limit_bytes=mebibytes * 2**20),
        cost_estimate=pl.CostEstimate(flops=flops, bytes_accessed=moved, transcendentals=0),
    )


def shape(dims, dtype):
    return jax.ShapeDtypeStruct(dims, dtype)


def kernel_body(tokens, sub_pos, sub_base, embed, norm_gain, fir_taps, long_filter, skip_gain, cotangent):
    n_path, n_ctx = lax.axis_size("path"), lax.axis_size("ctx")
    points = n_path
    tok_rows = tokens.shape[0]
    length = tok_rows * n_ctx
    vocab, width = embed.shape
    share = width // (n_path * n_ctx)
    subs = sub_pos.shape[0] * n_ctx
    own_width = width // n_path
    cols = points * share
    half = length // 2
    tables = dft_tables(length)
    dma = pltpu.SemaphoreType.DMA
    transform_flops = 2 * length * length
    spare = 8

    msg, ids = call(
        pack_kernel,
        [hbm_spec()] * 4,
        [
            (vmem_spec(), shape((n_ctx, tok_rows + spare, share), BF16)),
            (vmem_spec(), shape((spare, LANES), F32)),
        ],
        [
            pltpu.VMEM((1, tok_rows), jnp.int32),
            pltpu.VMEM((1, sub_pos.shape[0]), jnp.int32),
            pltpu.VMEM((1, sub_pos.shape[0]), jnp.int32),
            pltpu.VMEM((tok_rows, n_ctx * share), BF16),
            dma((n_ctx + 3,)),
        ],
        length * share,
        8 * length * share,
        60,
    )(
        tokens.reshape(1, tok_rows),
        sub_pos.reshape(1, -1),
        sub_base.reshape(1, -1),
        cotangent,
    )
    msg = lax.all_to_all(msg, "ctx", 0, 0, tiled=True)

    gain = norm_gain.reshape(1, width)
    skip = skip_gain.reshape(1, n_path * share)
    spec, gram = call(
        prepare_kernel,
        [hbm_spec()] * 5 + [any_spec()],
        [
            (any_spec(), shape((4, half, share), F32)),
            (any_spec(), shape((3 * vocab + vocab // 2, vocab), BF16)),
        ],
        [
            pltpu.VMEM((length, share), F32),
            pltpu.VMEM((length, half), BF16),
            pltpu.VMEM((length, half), BF16),
            pltpu.VMEM((vocab, width), BF16),
            pltpu.VMEM((1, share), F32),
            pltpu.VMEM((vocab, vocab), F32),
            pltpu.VMEM((4, half, share), F32),
            pltpu.VMEM((3 * vocab + vocab // 2, vocab), BF16),
            dma((8,)),
            dma((3 * vocab // LANES + 2,)),
        ],
        2 * vocab * vocab * width,
        2 * vocab * width,
        58,
    )(long_filter, tables[0], tables[1], embed, skip, ids)

    hots, subs_hots, put_hots = call(
        functools.partial(ids_kernel, vocab),
        [vmem_spec()],
        [
            (vmem_spec(), shape((length, vocab), BF16)),
            (vmem_spec(), shape((2 * subs, vocab), BF16)),
            (vmem_spec(), shape((length, 2 * subs), BF16)),
        ],
        [],
        2 * 10**9,
        4 * 10**6,
        8,
    )(msg)
    wide = 4 * LANES
    signal, k_feat, v_feat, inv, pair = call(
        functools.partial(feature_kernel, points),
        [vmem_spec()] * 7 + [hbm_spec()],
        [(vmem_spec(), shape((length, 2 * cols), BF16))]
        + [(vmem_spec(), shape((length, cols), F32))] * 3
        + [(vmem_spec(), shape((2, length, share), BF16))],
        [
            pltpu.VMEM((vocab, wide), BF16),
            pltpu.VMEM((points, subs, LANES), F32),
            pltpu.VMEM((2 * subs, wide), F32),
            pltpu.VMEM((length, 2 * share), F32),
            pltpu.VMEM((length, (2 + points) * share), F32),
            dma,
        ],
        2 * length * vocab * 3 * share,
        2 * vocab * width + 16 * length * cols,
        39,
    )(msg, hots, subs_hots, put_hots, gram, fir_taps, gain, embed)

    grad = call(
        functools.partial(gradient_kernel, points, width),
        [vmem_spec()] * 13,
        [(vmem_spec(), shape((n_ctx, tok_rows + spare, share), BF16))],
        [
            pltpu.VMEM((2 * length, 2 * cols), BF16),
            pltpu.VMEM((2 * length, 2 * share), BF16),
        ],
        4 * transform_flops * cols,
        4 * length * length + 16 * length * cols,
        32,
    )(msg, pair, fir_taps, gain, signal, k_feat, v_feat, inv, *tables, spec)[0]

    own = call(
        own_kernel,
        [vmem_spec(), vmem_spec(), any_spec()],
        [(vmem_spec(), shape((2, tok_rows, own_width), BF16))],
        [],
        4 * tok_rows * vocab * own_width,
        2 * vocab * own_width,
        10,
    )(ids, embed, grad)[0]
    grad = lax.all_to_all(grad, "ctx", 0, 0, tiled=True)
    each = n_ctx // n_path
    parts = call(
        partial_kernel,
        [vmem_spec()],
        [(vmem_spec(), shape((each * tok_rows + spare, share), BF16))] * n_path,
        [],
        spare * LANES * n_ctx,
        4 * length * share,
        4,
    )(grad)
    parts = [
        part if step == 0 else lax.ppermute(part, "path", [(p, p ^ step) for p in range(n_path)])
        for step, part in enumerate(parts)
    ]
    out = shape((tok_rows, own_width), F32)
    return tuple(
        call(
            finish_kernel,
            [vmem_spec()] * (1 + n_path),
            [(any_spec(), out), (any_spec(), out)],
            [pltpu.VMEM((n_path * each, tok_rows, share), F32)] * 2 + [dma((2, n_path * each))],
            8 * tok_rows * own_width,
            14 * tok_rows * own_width,
            8,
        )(own, *parts)
    )


def plain_body(tokens, sub_pos, sub_base, embed, norm_gain, fir_taps, long_filter, skip_gain, cotangent):
    n_path, n_ctx = lax.axis_size("path"), lax.axis_size("ctx")
    path, ctx = lax.axis_index("path"), lax.axis_index("ctx")
    points = n_path
    tok_rows = tokens.shape[0]
    length = tok_rows * n_ctx
    width = embed.shape[1]
    share = width // (n_path * n_ctx)
    own_width = width // n_path
    first = (ctx * n_path + path) * share
    alphas = ((jnp.arange(points, dtype=jnp.int32)).astype(F32) + 0.5) / points
    alphas = alphas[:, None, None]

    local = jnp.arange(tok_rows, dtype=jnp.int32)[:, None] + ctx * tok_rows == sub_pos[None, :]
    put = jnp.sum(jnp.where(local, sub_base[None, :], 0), 1)
    base_ids = jnp.where(jnp.any(local, 1), put, tokens)
    rows_tok = jnp.take(embed, tokens, axis=0).astype(F32)
    rows_base = jnp.take(embed, base_ids, axis=0).astype(F32)
    rows_in = rows_base[None] + alphas * (rows_tok - rows_base)[None]
    inv = lax.rsqrt(jnp.mean(rows_in * rows_in, -1) + EPS)
    inv = lax.all_gather(inv, "ctx", axis=1, tiled=True)[:, :, None]
    all_tok = lax.all_gather(tokens, "ctx", tiled=True)
    all_base = lax.all_gather(base_ids, "ctx", tiled=True)

    cot = cotangent.reshape(tok_rows, n_ctx, n_path, share)
    cot = lax.dynamic_index_in_dim(cot, path, 2, keepdims=False)
    cot = lax.all_to_all(cot.transpose(1, 0, 2), "ctx", 0, 0, tiled=True)
    upstream = cot.reshape(1, length, share).astype(F32)
    mine = lax.dynamic_slice_in_dim(embed, first, share, 1)
    gain = lax.dynamic_slice_in_dim(norm_gain, first, share, 0)
    taps = lax.dynamic_slice_in_dim(fir_taps, first, share, 2).astype(F32)
    filt = lax.dynamic_slice_in_dim(long_filter, path * share, share, 1)
    skip = lax.dynamic_slice_in_dim(skip_gain, path * share, share, 0)

    emb_tok = jnp.take(mine, all_tok, axis=0).astype(F32)
    emb_base = jnp.take(mine, all_base, axis=0).astype(F32)
    inputs = emb_base[None] + alphas * (emb_tok - emb_base)[None]
    normed = rounded(inputs * inv * gain)
    q_feat, k_feat, v_feat = (
        taps[f, 0] * normed + taps[f, 1] * shifted(normed, 1) + taps[f, 2] * shifted(normed, 2)
        for f in range(3)
    )
    filter_spec = spectrum(filt[None])
    conv = rounded(long_conv(rounded(k_feat * v_feat), filter_spec, skip, False))
    grad_z = rounded(long_conv(rounded(upstream * q_feat), filter_spec, skip, True))
    grads = (rounded(upstream * conv), rounded(grad_z * v_feat), rounded(grad_z * k_feat))
    by_tap = [sum(taps[f, tap] * grads[f] for f in range(3)) for tap in range(3)]
    scaled = gain * (by_tap[0] + shifted(by_tap[1], -1) + shifted(by_tap[2], -2))
    grad = jnp.sum(inv * scaled, 0).astype(BF16)
    along = jnp.sum(inputs * scaled, -1, keepdims=True) * inv**3 / width
    part = jnp.stack([jnp.sum(alphas * along, 0)[:, 0], jnp.sum((1.0 - alphas) * along, 0)[:, 0]])
    part = lax.psum(part, ("path", "ctx"))
    part = lax.dynamic_slice_in_dim(part, ctx * tok_rows, tok_rows, 1)

    back = lax.all_to_all(grad.reshape(n_ctx, tok_rows, share), "ctx", 0, 0, tiled=True)
    back = back.reshape(n_path, n_ctx // n_path, tok_rows, share)
    back = lax.all_to_all(back, "path", 0, 0, tiled=True).astype(F32)
    back = back.transpose(2, 1, 0, 3).reshape(tok_rows, own_width)
    own_tok = lax.dynamic_slice_in_dim(rows_tok, path * own_width, own_width, 1)
    own_base = lax.dynamic_slice_in_dim(rows_base, path * own_width, own_width, 1)
    grad = (back - own_tok * part[0][:, None] - own_base * part[1][:, None]) / points
    return (grad, (own_tok - own_base) * grad)


def body(tokens, sub_pos, sub_base, embed, *rest):
    n_path, n_ctx = lax.axis_size("path"), lax.axis_size("ctx")
    tok_rows = tokens.shape[0]
    share = embed.shape[1] // (n_path * n_ctx)
    tables = 4 * (tok_rows * n_ctx) ** 2
    fits = share == LANES and tok_rows == LANES and n_ctx == GROUP and tables <= TABLE_BYTES
    fits = fits and n_ctx % n_path == 0 and n_path & (n_path - 1) == 0
    chosen = kernel_body if fits else plain_body
    return chosen(tokens, sub_pos, sub_base, embed, *rest)


def solution(mesh):
    return jax.shard_map(
        body,
        mesh=mesh,
        in_specs=(
            P("ctx"),
            P("ctx"),
            P("ctx"),
            P(),
            P(),
            P(),
            P(None, "ctx"),
            P("ctx"),
            P("ctx", None),
        ),
        out_specs=(P("ctx", "path"), P("ctx", "path")),
        check_vma=False,
    )
```

```python
import functools

import jax
import jax.numpy as jnp
import ml_dtypes
import numpy as np
from jax import lax
from jax.experimental import pallas as pl
from jax.experimental.pallas import tpu as pltpu
from jax.sharding import PartitionSpec as P

LANES = 128
GROUP = 8
RADIX = 4
LOOK_ROWS = 256
CHUNK = 16
EPS = 1e-06
CANCEL = 0.004
TABLE_BYTES = 2**21
F32 = jnp.float32
BF16 = jnp.bfloat16
precise = lax.Precision.HIGH


def angle_tables(length):
    outer_size = 64
    inner_size = length // outer_size
    outer_idx = jnp.arange(outer_size, dtype=jnp.int32)
    inner_idx = jnp.arange(inner_size, dtype=jnp.int32)
    outer_angle = (
        2.0 * jnp.pi / outer_size
        * (outer_idx[:, None] * outer_idx[None, :] % outer_size).astype(F32)
    )
    inner_angle = (
        2.0 * jnp.pi / inner_size
        * (inner_idx[:, None] * inner_idx[None, :] % inner_size).astype(F32)
    )
    twist_angle = (
        2.0 * jnp.pi / length
        * (outer_idx[:, None] * inner_idx[None, :] % length).astype(F32)
    )
    return (outer_angle, inner_angle, twist_angle)


def complex_table(angle, sign):
    cosine = jnp.cos(angle)
    sine = sign * jnp.sin(angle)
    return jnp.stack([jnp.stack([cosine, sine]), jnp.stack([-sine, cosine])])


def twisted(values, angle, sign):
    cosine = jnp.cos(angle)[None, :, :, None]
    sine = sign * jnp.sin(angle)[None, :, :, None]
    real_part = values[:, 0]
    imag_part = values[:, 1]
    return jnp.stack(
        [real_part * cosine - imag_part * sine, real_part * sine + imag_part * cosine], 1
    )


def spectrum(signal):
    batch, half, width = signal.shape
    length = 2 * half
    outer_angle, inner_angle, twist_angle = angle_tables(length)
    outer_size = outer_angle.shape[0]
    inner_size = inner_angle.shape[0]
    folded = signal.reshape(batch, outer_size // 2, inner_size, width)
    used = outer_angle[:, : outer_size // 2]
    outer_table = jnp.stack([jnp.cos(used), -jnp.sin(used)])
    first = jnp.einsum("rka,pabc->prkbc", outer_table, folded, precision=precise)
    turned = twisted(first, twist_angle, -1.0)
    return jnp.einsum(
        "prkbc,rsbm->pskmc", turned, complex_table(inner_angle, -1.0), precision=precise
    )


def inverse(spec):
    batch, parts, outer_size, inner_size, width = spec.shape
    length = outer_size * inner_size
    outer_angle, inner_angle, twist_angle = angle_tables(length)
    back = jnp.einsum("pskmc,stmb->ptkbc", spec, complex_table(inner_angle, 1.0), precision=precise)
    turned = twisted(back, twist_angle, 1.0)
    used = outer_angle[: outer_size // 2]
    outer_table = jnp.stack([jnp.cos(used), -jnp.sin(used)])
    result = jnp.einsum("rak,prkbc->pabc", outer_table, turned, precision=precise)
    return (result / length).reshape(batch, length // 2, width)


def long_conv(signal, filter_spec, skip_gain, adjoint):
    spec = spectrum(signal)
    sig_real = spec[:, 0]
    sig_imag = spec[:, 1]
    filt_real = filter_spec[:, 0]
    filt_imag = filter_spec[:, 1]
    if adjoint:
        prod_real = sig_real * filt_real + sig_imag * filt_imag
        prod_imag = sig_imag * filt_real - sig_real * filt_imag
    else:
        prod_real = sig_real * filt_real - sig_imag * filt_imag
        prod_imag = sig_real * filt_imag + sig_imag * filt_real
    return inverse(jnp.stack([prod_real, prod_imag], 1)) + skip_gain * signal


def rounded(value):
    return value.astype(BF16).astype(F32)


def shifted(values, step):
    zeros = jnp.zeros_like(values[:, : abs(step)])
    if step > 0:
        return jnp.concatenate([zeros, values[:, :-step]], 1)
    return jnp.concatenate([values[:, -step:], zeros], 1)


@functools.lru_cache(maxsize=None)
def dft_tables(length):
    quarter = length // RADIX
    freq = 4 * np.arange(quarter, dtype=np.int64) + 1
    place = np.arange(quarter, dtype=np.int64)
    there, back = [], []
    for offset in range(RADIX):
        turns = freq[:, None] * (RADIX * place + offset)[None, :] % (4 * length)
        angle = turns * (2.0 * np.pi / (4 * length))
        cosine = np.cos(angle).astype(ml_dtypes.bfloat16)
        sine = np.sin(angle).astype(ml_dtypes.bfloat16)
        there.append(np.concatenate([cosine, sine], 0))
        back.append(np.concatenate([cosine.T, sine.T], 1))
    return (np.stack(there), np.stack(back))


def butterfly(values, sign):
    (r0, s0), (r1, s1), (r2, s2), (r3, s3) = values
    sum_r, sum_s, diff_r, diff_s = r0 + r2, s0 + s2, r0 - r2, s0 - s2
    odd_r, odd_s, turn_r, turn_s = r1 + r3, s1 + s3, r1 - r3, s1 - s3
    ahead = (diff_r + turn_s, diff_s - turn_r)
    behind = (diff_r - turn_s, diff_s + turn_r)
    if sign < 0:
        ahead, behind = behind, ahead
    return ((sum_r + odd_r, sum_s + odd_s), ahead, (sum_r - odd_r, sum_s - odd_s), behind)


def transposed(rows):
    count = rows.shape[0]
    if count < LANES:
        rows = jnp.concatenate([rows, jnp.zeros((LANES - count, LANES), F32)], 0)
    return rows.T


def dot(left, right):
    return jnp.dot(left, right, preferred_element_type=F32)


def exact_dot(left, right, dims):
    return lax.dot_general(
        left, right, (dims, ((), ())), precision=lax.Precision.HIGHEST, preferred_element_type=F32
    )


def iota(dims, axis):
    return lax.broadcasted_iota(jnp.int32, dims, axis)


def by_residue():
    row = iota((LANES, LANES), 0)
    part = LANES // RADIX
    source = RADIX * (row % part) + row // part
    return (iota((LANES, LANES), 1) == source).astype(F32)


def hot(ids, vocab):
    lane = iota(ids.shape, 1).astype(F32)
    parts = [
        (ids == lane + float(column * LANES)).astype(F32).astype(BF16)
        for column in range(vocab // LANES)
    ]
    return jnp.concatenate(parts, 1)


def joined(block, kind):
    return 256.0 * block[2 * kind : 2 * kind + 1] + block[2 * kind + 1 : 2 * kind + 2]


def pack_kernel(
    tok_hbm, pos_hbm, put_hbm, cot_hbm, msg_ref, ids_ref, tok_ref, pos_ref, put_ref, cot_ref, sems
):
    dests, rows, share = msg_ref.shape
    tok_rows = cot_hbm.shape[0]
    n_path = cot_hbm.shape[1] // (dests * share)
    path = lax.axis_index("path")
    moves = [(tok_hbm, tok_ref), (pos_hbm, pos_ref), (put_hbm, put_ref)]
    for dest in range(dests):
        lanes = pl.ds(pl.multiple_of((dest * n_path + path) * share, LANES), share)
        moves.append((cot_hbm.at[:, lanes], cot_ref.at[:, pl.ds(dest * share, share)]))
    copies = [
        pltpu.make_async_copy(source, target, sems.at[index])
        for index, (source, target) in enumerate(moves)
    ]
    for copy in copies:
        copy.start()
    order = by_residue().astype(BF16)
    for copy in copies[:3]:
        copy.wait()
    lists = []
    for ref in (tok_ref, pos_ref, put_ref):
        value = ref[...].astype(F32)
        if value.shape[1] < LANES:
            value = jnp.concatenate([value, jnp.zeros((1, LANES - value.shape[1]), F32)], 1)
        high = jnp.floor(value * (1.0 / 256.0))
        lists += [high, value - 256.0 * high]
    lists.append(jnp.zeros((rows - tok_rows - len(lists), LANES), F32))
    ids = jnp.concatenate(lists, 0)
    ids_ref[...] = ids
    turned = lax.dot_general(
        ids.astype(BF16), order, (((1,), (1,)), ((), ())), preferred_element_type=F32
    )
    ids = jnp.where(iota(ids.shape, 0) < 2, turned, ids).astype(BF16)
    for dest in range(dests):
        msg_ref[dest, tok_rows:, :] = ids
    for copy in copies[3:]:
        copy.wait()
    turned = dot(order, cot_ref[...]).astype(BF16)
    for dest in range(dests):
        msg_ref[dest, :tok_rows, :] = turned[:, dest * share : (dest + 1) * share]


def prepare_kernel(
    filt_hbm, table_hbm, embed_hbm, skip_hbm, after_ref,
    spec_hbm, gram_hbm,
    filt_ref, table_ref, embed_ref, skip_ref, sum_ref, spec_ref, gram_ref, sems, out_sems,
):
    length, share = filt_ref.shape
    quarter = length // RADIX
    vocab, width = embed_ref.shape
    pieces = sems.shape[0] - 3
    wide = width // pieces
    path = lax.axis_index("path")
    lanes = pl.ds(pl.multiple_of(path * share, LANES), share)
    moves = [
        (filt_hbm.at[:, lanes], filt_ref),
        (skip_hbm.at[:, lanes], skip_ref),
        (table_hbm, table_ref),
    ]
    for index in range(pieces):
        lanes = pl.ds(index * wide, wide)
        moves.append((embed_hbm.at[:, lanes], embed_ref.at[:, lanes]))
    copies = [
        pltpu.make_async_copy(source, target, sems.at[index])
        for index, (source, target) in enumerate(moves)
    ]
    for copy in copies:
        copy.start()

    copies[0].wait()
    copies[1].wait()
    filt_ref[0:1, :] = filt_ref[0:1, :] + skip_ref[...]
    parts = []
    for offset in range(RADIX):
        value = filt_ref[pl.ds(offset, quarter, stride=RADIX), :] * (1.0 / length)
        high = value.astype(BF16)
        parts.append(jnp.concatenate([high, (value - high.astype(F32)).astype(BF16)], 1))
    copies[2].wait()
    found = []
    for offset in range(RADIX):
        both = dot(table_ref[offset], parts[offset])
        both = both[:, :share] + both[:, share:]
        found.append((both[:quarter], both[quarter:]))
    for part, (real, imag) in enumerate(butterfly(found, -1)):
        spec_ref[2 * part] = real
        spec_ref[2 * part + 1] = imag
    outs = [pltpu.make_async_copy(spec_ref, spec_hbm, out_sems.at[0])]
    outs[0].start()

    sum_ref[vocab // 2 :, : vocab // 2] = jnp.zeros((vocab // 2, vocab // 2), F32)
    for index in range(pieces):
        copies[3 + index].wait()
        part = embed_ref[:, index * wide : (index + 1) * wide]
        for rows, lanes in ((slice(0, vocab // 2), slice(0, vocab)), (slice(vocab // 2, vocab),) * 2):
            found = lax.dot_general(
                part[rows], part[lanes], (((1,), (1,)), ((), ())), preferred_element_type=F32
            )
            if index == 0:
                sum_ref[rows, lanes] = found
            else:
                sum_ref[rows, lanes] += found
    first = (lax.axis_index("ctx") * lax.axis_size("path") + path) * share
    mine = embed_ref[:, pl.ds(pl.multiple_of(first, LANES), share)]
    same = iota((LANES, LANES), 0) == iota((LANES, LANES), 1)
    lane = iota((LANES, LANES), 1)
    below = 3 * vocab
    for block in range(vocab // LANES):
        rows = slice(block * LANES, (block + 1) * LANES)
        value = sum_ref[rows, :]
        norm = jnp.sum(jnp.where(same, value[:, rows], 0.0), 1, keepdims=True)
        inv = jnp.broadcast_to(lax.rsqrt(norm / width + EPS), (LANES, LANES))
        high = inv.astype(BF16).astype(F32)
        inv = jnp.where(lane < LANES // 2, high, inv - high).astype(BF16)
        side, start = block * LANES // (vocab // 2), block * LANES % (vocab // 2)
        into = slice(below + start, below + start + LANES)
        left = side * (share + LANES)
        gram_ref[into, left : left + share] = mine[rows]
        gram_ref[into, left + share : left + share + LANES] = inv
        for part in range(3):
            high = value.astype(BF16)
            into = slice(part * vocab + block * LANES, part * vocab + (block + 1) * LANES)
            gram_ref[into, :] = high
            value = value - high.astype(F32)
            into = pl.ds(part * vocab + block * LANES, LANES)
            sem = out_sems.at[1 + block * 3 + part]
            outs.append(pltpu.make_async_copy(gram_ref.at[into], gram_hbm.at[into], sem))
            outs[-1].start()
    into = pl.ds(below, vocab // 2)
    outs.append(pltpu.make_async_copy(gram_ref.at[into], gram_hbm.at[into], out_sems.at[out_sems.shape[0] - 1]))
    outs[-1].start()
    for copy in outs:
        copy.wait()


def own_kernel(ids_ref, embed_ref, grad_ref, own_ref):
    vocab = embed_ref.shape[0]
    own_width = own_ref.shape[2]
    lanes = pl.ds(pl.multiple_of(lax.axis_index("path") * own_width, LANES), own_width)
    ids = ids_ref[...]
    columns = transposed(jnp.concatenate([joined(ids, kind) for kind in range(3)], 0))
    tok = jnp.broadcast_to(columns[:, 0:1], (LANES, LANES))
    place = jnp.broadcast_to(joined(ids, 1), (LANES, LANES))
    put = jnp.broadcast_to(joined(ids, 2), (LANES, LANES))
    first = lax.axis_index("ctx") * LANES
    subs = LANES // GROUP
    here = (place == (iota((LANES, LANES), 0) + first).astype(F32)) & (iota((LANES, LANES), 1) < subs)
    found = jnp.max(jnp.where(here, put, -1.0), 1, keepdims=True)
    base = jnp.where(found >= 0.0, found, tok)
    hots = jnp.concatenate([hot(tok, vocab), hot(base, vocab)], 0)
    both = dot(hots, embed_ref[:, lanes]).astype(BF16)
    own_ref[0] = both[:LANES]
    own_ref[1] = both[LANES:]


def multiply_rows(found, spec_ref, prod_ref, points, kind):
    _, quarter, share = spec_ref.shape
    for start in range(0, quarter, CHUNK):
        here = slice(start, start + CHUNK)
        after = slice(quarter + start, quarter + start + CHUNK)
        filt = [(spec_ref[2 * part, here, :], spec_ref[2 * part + 1, here, :]) for part in range(RADIX)]
        for point in range(points):
            lanes = slice(point * share, (point + 1) * share)
            values = butterfly([(value[here, lanes], value[after, lanes]) for value in found], -1)
            prods = []
            for (real, imag), (filt_real, filt_imag) in zip(values, filt):
                if kind == 1:
                    prods.append((real * filt_real + imag * filt_imag, imag * filt_real - real * filt_imag))
                else:
                    prods.append((real * filt_real - imag * filt_imag, imag * filt_real + real * filt_imag))
            lanes = slice((kind * points + point) * share, (kind * points + point + 1) * share)
            for part, (real, imag) in enumerate(butterfly(prods, 1)):
                prod_ref[part, here, lanes] = real.astype(BF16)
                prod_ref[part, after, lanes] = imag.astype(BF16)


def ids_kernel(vocab, msg_ref, hot_ref, subs_ref, put_ref):
    length = hot_ref.shape[0]
    quarter = length // RADIX
    n_ctx = msg_ref.shape[0]
    block_part = LANES // RADIX
    per_block = LANES // GROUP
    subs = n_ctx * per_block
    blocks = [msg_ref[block, LANES:, :].astype(F32) for block in range(n_ctx)]
    toks = transposed(jnp.concatenate([joined(block, 0) for block in blocks], 0))
    spread = sum(
        blocks[block] if block == 0 else pltpu.roll(blocks[block], block * per_block, 1)
        for block in range(n_ctx)
    )
    place = joined(spread, 1)
    put = joined(spread, 2)
    back = jnp.floor(place * (1.0 / RADIX))
    place = back + (place - RADIX * back) * quarter
    columns = transposed(jnp.concatenate([place, put], 0))
    for block in range(n_ctx):
        column = jnp.broadcast_to(toks[:, block : block + 1], (LANES, LANES))
        rows = hot(column, vocab)
        for side in range(RADIX):
            first = side * quarter + block * block_part
            hot_ref[first : first + block_part, :] = rows[side * block_part : (side + 1) * block_part]
    subs_ref[subs:, :] = hot(jnp.broadcast_to(columns[:, 1:2], (subs, LANES)), vocab)
    pick = jnp.concatenate(
        [
            (columns[:, 0:1] == (iota((subs, LANES), 1) + part * LANES).astype(F32)).astype(F32).astype(BF16)
            for part in range(length // LANES)
        ],
        1,
    )
    for index in range(length // LANES):
        row = (iota((LANES, subs), 0) + index * LANES).astype(F32)
        here = (row == place[:, :subs]).astype(F32).astype(BF16)
        put_ref[index * LANES : (index + 1) * LANES, :] = jnp.concatenate([here, here], 1)
    subs_ref[:subs, :] = dot(pick, hot_ref[...]).astype(BF16)


def feature_kernel(
    points, msg_ref, hot_ref, subs_hot_ref, put_ref, gram_ref, taps_ref, gain_ref, embed_hbm,
    signal_ref, k_ref, v_ref, inv_ref, pair_ref,
    embed_ref, sums_ref, found_ref, look_ref, subs_ref, sem,
):
    length = signal_ref.shape[0]
    quarter = length // RADIX
    vocab, width = embed_hbm.shape
    share = pair_ref.shape[2]
    subs = subs_hot_ref.shape[0] // 2
    first = (lax.axis_index("ctx") * points + lax.axis_index("path")) * share
    first = pl.multiple_of(first, LANES)
    below = 3 * vocab
    table = jnp.concatenate(
        [gram_ref[below:, : share + LANES], gram_ref[below:, share + LANES :]], 0
    )

    for index in range(length // LOOK_ROWS):
        rows = pl.ds(index * LOOK_ROWS, LOOK_ROWS)
        look_ref[rows, :] = dot(hot_ref[rows, :], table)

    alphas = [(point + 0.5) / points for point in range(points)]
    hots = subs_hot_ref[...]
    found = dot(jnp.concatenate([hots] * 3, 1), gram_ref[:below, :])
    hot_tok32, hot_base32 = hots[:subs].astype(F32), hots[subs:].astype(F32)
    tok_tok = jnp.sum(found[:subs] * hot_tok32, 1, keepdims=True)
    tok_base = jnp.sum(found[:subs] * hot_base32, 1, keepdims=True)
    base_tok = jnp.sum(found[subs:] * hot_tok32, 1, keepdims=True)
    tok_base = jnp.where(tok_base == 0.0, base_tok, tok_base)
    base_base = jnp.sum(found[subs:] * hot_base32, 1, keepdims=True)
    cancels = jnp.zeros((subs, 1), F32)
    for point in range(points):
        alpha = alphas[point]
        terms = (1.0 - alpha) ** 2 * base_base + alpha**2 * tok_tok
        total = terms + 2.0 * alpha * (1.0 - alpha) * tok_base
        cancels = jnp.maximum(cancels, (total < CANCEL * terms).astype(F32))
        inv = lax.rsqrt(jnp.maximum(total, 0.0) / width + EPS)
        sums_ref[point] = jnp.broadcast_to(inv, (subs, LANES))

    @pl.when(jnp.max(cancels) > 0.5)
    def _():
        sums_ref[...] = jnp.zeros_like(sums_ref)
        wide = found_ref.shape[1]

        @pl.loop(0, width // wide)
        def _(step):
            lanes = pl.ds(pl.multiple_of(step * wide, wide), wide)
            copy = pltpu.make_async_copy(embed_hbm.at[:, lanes], embed_ref, sem)
            copy.start()
            copy.wait()
            found_ref[...] = dot(hots, embed_ref[...])
            for block in range(subs // GROUP):
                rows = slice(block * GROUP, (block + 1) * GROUP)
                sums = [sums_ref[point, rows, :] for point in range(points)]
                for column in range(wide // LANES):
                    cut = slice(column * LANES, (column + 1) * LANES)
                    base = found_ref[subs + block * GROUP : subs + (block + 1) * GROUP, cut]
                    diff = found_ref[rows, cut] - base
                    for point in range(points):
                        value = base + alphas[point] * diff
                        sums[point] = sums[point] + value * value
                for point in range(points):
                    sums_ref[point, rows, :] = sums[point]

        for point in range(points):
            mean = jnp.sum(sums_ref[point], 1, keepdims=True) / width
            sums_ref[point] = jnp.broadcast_to(lax.rsqrt(mean + EPS), (subs, LANES))

    high = [dot(hots[subs:], table[:, :share]), jnp.ones((subs, LANES), F32)]
    low = [jnp.zeros((subs, LANES), F32)] * 2
    for point in range(points):
        inv = sums_ref[point]
        high.append(inv.astype(BF16).astype(F32))
        low.append(inv - high[-1])
    held = jnp.concatenate([jnp.concatenate(high, 1), jnp.concatenate(low, 1)], 0).astype(BF16)
    for index in range(length // LOOK_ROWS):
        rows = pl.ds(index * LOOK_ROWS, LOOK_ROWS)
        subs_ref[rows, :] = dot(put_ref[rows, :], held)

    cols = points * share
    block_part = LANES // RADIX
    last = {side: [jnp.zeros((GROUP, share), F32)] * points for side in (RADIX - 2, RADIX - 1)}
    gain = gain_ref[:, pl.ds(first, share)]
    taps = [taps_ref[f, :, pl.ds(first, share)].astype(F32) for f in range(3)]
    taps = [[taps[f][tap : tap + 1] for tap in range(3)] for f in range(3)]

    for start in range(0, quarter, CHUNK):
        block, inside = start // block_part, start % block_part
        sides = []
        for side in range(RADIX):
            rows = pl.ds(side * quarter + start, CHUNK)
            tok = look_ref[rows, :share]
            inv = look_ref[rows, share:]
            inv = inv + pltpu.roll(inv, LANES // 2, 1)
            chosen = subs_ref[rows, share : 2 * share] > 0.5
            base = jnp.where(chosen, subs_ref[rows, :share], tok)
            pair_ref[0, rows, :] = tok.astype(BF16)
            pair_ref[1, rows, :] = base.astype(BF16)
            sent = pl.ds(side * block_part + inside, CHUNK)
            sides.append((rows, base, tok - base, inv, chosen, msg_ref[block, sent, :].astype(F32)))
        for point in range(points):
            lanes = slice(point * share, (point + 1) * share)
            recent = []
            for rows, base, diff, inv_tok, chosen, _ in sides:
                inv = jnp.where(
                    chosen, subs_ref[rows, (2 + point) * share : (3 + point) * share], inv_tok
                )
                inv_ref[rows, lanes] = inv
                recent.append(rounded((base + alphas[point] * diff) * inv * gain))
            backs = []
            for side in (RADIX - 2, RADIX - 1):
                window = jnp.concatenate([last[side][point], recent[side]], 0)
                last[side][point] = recent[side][CHUNK - GROUP :]
                backs.append(window[GROUP - 1 : GROUP - 1 + CHUNK])
            recent = backs + recent
            for side in range(RADIX):
                rows, upstream = sides[side][0], sides[side][5]
                feats = [sum(taps[f][tap] * recent[side + 2 - tap] for tap in range(3)) for f in range(3)]
                k_ref[rows, lanes] = feats[1]
                v_ref[rows, lanes] = feats[2]
                signal_ref[rows, lanes] = (feats[1] * feats[2]).astype(BF16)
                after = slice(cols + point * share, cols + (point + 1) * share)
                signal_ref[rows, after] = (upstream * feats[0]).astype(BF16)


def gradient_kernel(
    points, width, msg_ref, pair_ref, taps_ref, gain_ref,
    signal_ref, k_ref, v_ref, inv_ref, table_ref, back_ref, spec_ref,
    grad_ref,
    prod_ref, sums_ref,
):
    _, quarter, share = spec_ref.shape
    cols = points * share
    n_ctx = msg_ref.shape[0]
    block_part = LANES // RADIX
    first = (lax.axis_index("ctx") * points + lax.axis_index("path")) * share
    first = pl.multiple_of(first, LANES)
    gain = gain_ref[:, pl.ds(first, share)]
    taps = [taps_ref[f, :, pl.ds(first, share)].astype(F32) for f in range(3)]
    taps = [[taps[f][tap : tap + 1] for tap in range(3)] for f in range(3)]

    found = []
    for kind in range(2):
        signal = slice(kind * cols, (kind + 1) * cols)
        spectra = [
            dot(table_ref[side], signal_ref[side * quarter : (side + 1) * quarter, signal])
            for side in range(RADIX)
        ]
        multiply_rows(spectra, spec_ref, prod_ref, points, kind)
    for kind in range(2):
        signal = slice(kind * cols, (kind + 1) * cols)
        found.append([dot(back_ref[side], prod_ref[side, :, signal]) for side in range(RADIX)])

    carried = [[jnp.zeros((GROUP, share), F32)] * points for _ in range(3)]
    for start in reversed(range(0, quarter, CHUNK)):
        block, inside = start // block_part, start % block_part
        here = slice(start, start + CHUNK)
        sides = []
        for side in range(RADIX):
            rows = pl.ds(side * quarter + start, CHUNK)
            sent = pl.ds(side * block_part + inside, CHUNK)
            upstream = msg_ref[block, sent, :].astype(F32)
            sides.append([rows, sent, upstream] + [jnp.zeros((CHUNK, share), F32)] * 4)
        for point in reversed(range(points)):
            lanes = slice(point * share, (point + 1) * share)
            by_tap = []
            for side in range(RADIX):
                rows, _, upstream = sides[side][:3]
                grad_z = found[1][side][here, lanes]
                grads = (
                    upstream * found[0][side][here, lanes],
                    grad_z * v_ref[rows, lanes],
                    grad_z * k_ref[rows, lanes],
                )
                by_tap.append([sum(taps[f][tap] * grads[f] for f in range(3)) for tap in range(3)])
            ahead = []
            for slot, value in enumerate((by_tap[0][1], by_tap[0][2], by_tap[1][2])):
                window = jnp.concatenate([value, carried[slot][point]], 0)
                carried[slot][point] = value[:GROUP]
                ahead.append(window[1 : 1 + CHUNK])
            by_tap += [[None, ahead[0], ahead[1]], [None, None, ahead[2]]]
            for side in range(RADIX):
                rows, _, _, total, sum0, sum1, sum2 = sides[side]
                inv = inv_ref[rows, lanes]
                along = inv * (by_tap[side][0] + by_tap[side + 1][1] + by_tap[side + 2][2])
                total = total + along
                sum0 = sum0 + along * (inv * inv)
                sum1 = sum1 + sum0
                sides[side][3:] = [total, sum0, sum1, sum2 + sum1]
        for side in range(RADIX):
            rows, sent, _, total, sum0, sum1, sum2 = sides[side]
            base = pair_ref[1, rows, :].astype(F32)
            diff = pair_ref[0, rows, :].astype(F32) - base
            once = (sum1 - 0.5 * sum0) * (1.0 / points)
            twice = (2.0 * (sum2 - sum1) + 0.25 * sum0) * (1.0 / points**2)
            to_tok = base * once + diff * twice
            to_base = base * sum0 + diff * once - to_tok
            grad_ref[block, sent, :] = (gain * total).astype(BF16)
            for kind, value in enumerate((gain * to_tok, gain * to_base)):
                high = value.astype(BF16)
                into = pl.ds((kind * n_ctx + block) * LANES + side * block_part + inside, CHUNK)
                sums_ref[into, :share] = high
                sums_ref[into, share:] = (value - high.astype(F32)).astype(BF16)

    ones = jnp.ones((GROUP, 2 * share), BF16)
    row = lax.dot_general(ones, sums_ref[...], (((1,), (1,)), ((), ())), preferred_element_type=F32)
    row = row[:1] / width
    high = row.astype(BF16).astype(F32)
    for block in range(n_ctx):
        sent = []
        for kind in range(2):
            lanes = slice((kind * n_ctx + block) * LANES, (kind * n_ctx + block + 1) * LANES)
            sent += [high[:, lanes], row[:, lanes] - high[:, lanes]]
        sent.append(jnp.zeros((grad_ref.shape[1] - LANES - len(sent), LANES), F32))
        grad_ref[block, LANES:, :] = jnp.concatenate(sent, 0).astype(BF16)


def partial_kernel(grad_ref, *out_refs):
    rows, _ = out_refs[0].shape
    n_ctx = grad_ref.shape[0]
    each = n_ctx // len(out_refs)
    spare = sum(grad_ref[block, LANES:, :].astype(F32) for block in range(n_ctx))
    sums = [spare[0:1] + spare[1:2], spare[2:3] + spare[3:4]]
    sent = []
    for value in sums:
        high = value.astype(BF16).astype(F32)
        sent += [high, value - high]
    sent.append(jnp.zeros((rows - each * LANES - len(sent), LANES), F32))
    sent = jnp.concatenate(sent, 0).astype(BF16)
    path = lax.axis_index("path")
    for step, ref in enumerate(out_refs):
        dest = path ^ step
        for piece in range(each):
            ref[piece * LANES : (piece + 1) * LANES, :] = grad_ref[dest * each + piece, :LANES, :]
        ref[each * LANES :, :] = sent


def finish_kernel(own_ref, *refs):
    grad_refs, (path_hbm, attr_hbm, path_ref, attr_ref, sems) = refs[:-5], refs[-5:]
    points = len(grad_refs)
    rows, share = grad_refs[0].shape
    pieces = rows // LANES
    spare = sum(ref[pieces * LANES :, :].astype(F32) for ref in grad_refs)
    sums = jnp.concatenate([spare[0:1] + spare[1:2], spare[2:3] + spare[3:4], spare[4:]], 0)
    order = by_residue()
    columns = transposed(exact_dot(sums, order, ((1,), (0,))))
    to_tok = columns[:, 0:1]
    to_base = columns[:, 1:2]
    order = order.T.astype(BF16)
    path = lax.axis_index("path")
    copies = []
    for step, ref in enumerate(grad_refs):
        for piece in range(pieces):
            slot = step * pieces + piece
            first = (piece * points + (path ^ step)) * share
            lanes = pl.ds(pl.multiple_of(first, LANES), share)
            tok = own_ref[0, :, lanes].astype(F32)
            base = own_ref[1, :, lanes].astype(F32)
            grad = dot(order, ref[piece * LANES : (piece + 1) * LANES, :])
            grad = (grad - tok * to_tok - base * to_base) / points
            path_ref[slot] = grad
            attr_ref[slot] = (tok - base) * grad
            for kind, (source, target) in enumerate(((path_ref, path_hbm), (attr_ref, attr_hbm))):
                copies.append(
                    pltpu.make_async_copy(source.at[slot], target.at[:, lanes], sems.at[kind, slot])
                )
                copies[-1].start()
    for copy in copies:
        copy.wait()


def any_spec():
    return pl.BlockSpec(memory_space=pl.ANY)


def vmem_spec():
    return pl.BlockSpec(memory_space=pltpu.VMEM)


def hbm_spec():
    return pl.BlockSpec(memory_space=pltpu.HBM)


def call(kernel, ins, outs, scratch, flops, moved, mebibytes):
    return pl.pallas_call(
        kernel,
        in_specs=ins,
        out_specs=[spec for spec, _ in outs],
        out_shape=[shape for _, shape in outs],
        scratch_shapes=scratch,
        compiler_params=pltpu.CompilerParams(vmem_limit_bytes=mebibytes * 2**20),
        cost_estimate=pl.CostEstimate(flops=flops, bytes_accessed=moved, transcendentals=0),
    )


def shape(dims, dtype):
    return jax.ShapeDtypeStruct(dims, dtype)


def kernel_body(tokens, sub_pos, sub_base, embed, norm_gain, fir_taps, long_filter, skip_gain, cotangent):
    n_path, n_ctx = lax.axis_size("path"), lax.axis_size("ctx")
    points = n_path
    tok_rows = tokens.shape[0]
    length = tok_rows * n_ctx
    vocab, width = embed.shape
    share = width // (n_path * n_ctx)
    subs = sub_pos.shape[0] * n_ctx
    own_width = width // n_path
    cols = points * share
    quarter = length // RADIX
    tables = dft_tables(length)
    dma = pltpu.SemaphoreType.DMA
    transform_flops = length * length
    spare = 8

    msg, ids = call(
        pack_kernel,
        [hbm_spec()] * 4,
        [
            (vmem_spec(), shape((n_ctx, tok_rows + spare, share), BF16)),
            (vmem_spec(), shape((spare, LANES), F32)),
        ],
        [
            pltpu.VMEM((1, tok_rows), jnp.int32),
            pltpu.VMEM((1, sub_pos.shape[0]), jnp.int32),
            pltpu.VMEM((1, sub_pos.shape[0]), jnp.int32),
            pltpu.VMEM((tok_rows, n_ctx * share), BF16),
            dma((n_ctx + 3,)),
        ],
        length * share,
        8 * length * share,
        60,
    )(
        tokens.reshape(1, tok_rows),
        sub_pos.reshape(1, -1),
        sub_base.reshape(1, -1),
        cotangent,
    )
    msg = lax.all_to_all(msg, "ctx", 0, 0, tiled=True)

    gain = norm_gain.reshape(1, width)
    skip = skip_gain.reshape(1, n_path * share)
    spec, gram = call(
        prepare_kernel,
        [hbm_spec()] * 4 + [any_spec()],
        [
            (any_spec(), shape((2 * RADIX, quarter, share), F32)),
            (any_spec(), shape((3 * vocab + vocab // 2, vocab), BF16)),
        ],
        [
            pltpu.VMEM((length, share), F32),
            pltpu.VMEM((RADIX, 2 * quarter, quarter), BF16),
            pltpu.VMEM((vocab, width), BF16),
            pltpu.VMEM((1, share), F32),
            pltpu.VMEM((vocab, vocab), F32),
            pltpu.VMEM((2 * RADIX, quarter, share), F32),
            pltpu.VMEM((3 * vocab + vocab // 2, vocab), BF16),
            dma((7,)),
            dma((3 * vocab // LANES + 2,)),
        ],
        2 * vocab * vocab * width,
        2 * vocab * width,
        58,
    )(long_filter, tables[0], embed, skip, ids)

    hots, subs_hots, put_hots = call(
        functools.partial(ids_kernel, vocab),
        [vmem_spec()],
        [
            (vmem_spec(), shape((length, vocab), BF16)),
            (vmem_spec(), shape((2 * subs, vocab), BF16)),
            (vmem_spec(), shape((length, 2 * subs), BF16)),
        ],
        [],
        2 * 10**9,
        4 * 10**6,
        8,
    )(msg)
    wide = 4 * LANES
    signal, k_feat, v_feat, inv, pair = call(
        functools.partial(feature_kernel, points),
        [vmem_spec()] * 7 + [hbm_spec()],
        [(vmem_spec(), shape((length, 2 * cols), BF16))]
        + [(vmem_spec(), shape((length, cols), F32))] * 3
        + [(vmem_spec(), shape((2, length, share), BF16))],
        [
            pltpu.VMEM((vocab, wide), BF16),
            pltpu.VMEM((points, subs, LANES), F32),
            pltpu.VMEM((2 * subs, wide), F32),
            pltpu.VMEM((length, 2 * share), F32),
            pltpu.VMEM((length, (2 + points) * share), F32),
            dma,
        ],
        2 * length * vocab * 3 * share,
        2 * vocab * width + 16 * length * cols,
        39,
    )(msg, hots, subs_hots, put_hots, gram, fir_taps, gain, embed)

    grad = call(
        functools.partial(gradient_kernel, points, width),
        [vmem_spec()] * 11,
        [(vmem_spec(), shape((n_ctx, tok_rows + spare, share), BF16))],
        [
            pltpu.VMEM((RADIX, 2 * quarter, 2 * cols), BF16),
            pltpu.VMEM((2 * length, 2 * share), BF16),
        ],
        4 * transform_flops * cols,
        4 * length * length + 16 * length * cols,
        32,
    )(msg, pair, fir_taps, gain, signal, k_feat, v_feat, inv, *tables, spec)[0]

    own = call(
        own_kernel,
        [vmem_spec(), vmem_spec(), any_spec()],
        [(vmem_spec(), shape((2, tok_rows, own_width), BF16))],
        [],
        4 * tok_rows * vocab * own_width,
        2 * vocab * own_width,
        10,
    )(ids, embed, grad)[0]
    grad = lax.all_to_all(grad, "ctx", 0, 0, tiled=True)
    each = n_ctx // n_path
    parts = call(
        partial_kernel,
        [vmem_spec()],
        [(vmem_spec(), shape((each * tok_rows + spare, share), BF16))] * n_path,
        [],
        spare * LANES * n_ctx,
        4 * length * share,
        4,
    )(grad)
    parts = [
        part if step == 0 else lax.ppermute(part, "path", [(p, p ^ step) for p in range(n_path)])
        for step, part in enumerate(parts)
    ]
    out = shape((tok_rows, own_width), F32)
    return tuple(
        call(
            finish_kernel,
            [vmem_spec()] * (1 + n_path),
            [(any_spec(), out), (any_spec(), out)],
            [pltpu.VMEM((n_path * each, tok_rows, share), F32)] * 2 + [dma((2, n_path * each))],
            8 * tok_rows * own_width,
            14 * tok_rows * own_width,
            8,
        )(own, *parts)
    )


def plain_body(tokens, sub_pos, sub_base, embed, norm_gain, fir_taps, long_filter, skip_gain, cotangent):
    n_path, n_ctx = lax.axis_size("path"), lax.axis_size("ctx")
    path, ctx = lax.axis_index("path"), lax.axis_index("ctx")
    points = n_path
    tok_rows = tokens.shape[0]
    length = tok_rows * n_ctx
    width = embed.shape[1]
    share = width // (n_path * n_ctx)
    own_width = width // n_path
    first = (ctx * n_path + path) * share
    alphas = ((jnp.arange(points, dtype=jnp.int32)).astype(F32) + 0.5) / points
    alphas = alphas[:, None, None]

    local = jnp.arange(tok_rows, dtype=jnp.int32)[:, None] + ctx * tok_rows == sub_pos[None, :]
    put = jnp.sum(jnp.where(local, sub_base[None, :], 0), 1)
    base_ids = jnp.where(jnp.any(local, 1), put, tokens)
    rows_tok = jnp.take(embed, tokens, axis=0).astype(F32)
    rows_base = jnp.take(embed, base_ids, axis=0).astype(F32)
    rows_in = rows_base[None] + alphas * (rows_tok - rows_base)[None]
    inv = lax.rsqrt(jnp.mean(rows_in * rows_in, -1) + EPS)
    inv = lax.all_gather(inv, "ctx", axis=1, tiled=True)[:, :, None]
    all_tok = lax.all_gather(tokens, "ctx", tiled=True)
    all_base = lax.all_gather(base_ids, "ctx", tiled=True)

    cot = cotangent.reshape(tok_rows, n_ctx, n_path, share)
    cot = lax.dynamic_index_in_dim(cot, path, 2, keepdims=False)
    cot = lax.all_to_all(cot.transpose(1, 0, 2), "ctx", 0, 0, tiled=True)
    upstream = cot.reshape(1, length, share).astype(F32)
    mine = lax.dynamic_slice_in_dim(embed, first, share, 1)
    gain = lax.dynamic_slice_in_dim(norm_gain, first, share, 0)
    taps = lax.dynamic_slice_in_dim(fir_taps, first, share, 2).astype(F32)
    filt = lax.dynamic_slice_in_dim(long_filter, path * share, share, 1)
    skip = lax.dynamic_slice_in_dim(skip_gain, path * share, share, 0)

    emb_tok = jnp.take(mine, all_tok, axis=0).astype(F32)
    emb_base = jnp.take(mine, all_base, axis=0).astype(F32)
    inputs = emb_base[None] + alphas * (emb_tok - emb_base)[None]
    normed = rounded(inputs * inv * gain)
    q_feat, k_feat, v_feat = (
        taps[f, 0] * normed + taps[f, 1] * shifted(normed, 1) + taps[f, 2] * shifted(normed, 2)
        for f in range(3)
    )
    filter_spec = spectrum(filt[None])
    conv = rounded(long_conv(rounded(k_feat * v_feat), filter_spec, skip, False))
    grad_z = rounded(long_conv(rounded(upstream * q_feat), filter_spec, skip, True))
    grads = (rounded(upstream * conv), rounded(grad_z * v_feat), rounded(grad_z * k_feat))
    by_tap = [sum(taps[f, tap] * grads[f] for f in range(3)) for tap in range(3)]
    scaled = gain * (by_tap[0] + shifted(by_tap[1], -1) + shifted(by_tap[2], -2))
    grad = jnp.sum(inv * scaled, 0).astype(BF16)
    along = jnp.sum(inputs * scaled, -1, keepdims=True) * inv**3 / width
    part = jnp.stack([jnp.sum(alphas * along, 0)[:, 0], jnp.sum((1.0 - alphas) * along, 0)[:, 0]])
    part = lax.psum(part, ("path", "ctx"))
    part = lax.dynamic_slice_in_dim(part, ctx * tok_rows, tok_rows, 1)

    back = lax.all_to_all(grad.reshape(n_ctx, tok_rows, share), "ctx", 0, 0, tiled=True)
    back = back.reshape(n_path, n_ctx // n_path, tok_rows, share)
    back = lax.all_to_all(back, "path", 0, 0, tiled=True).astype(F32)
    back = back.transpose(2, 1, 0, 3).reshape(tok_rows, own_width)
    own_tok = lax.dynamic_slice_in_dim(rows_tok, path * own_width, own_width, 1)
    own_base = lax.dynamic_slice_in_dim(rows_base, path * own_width, own_width, 1)
    grad = (back - own_tok * part[0][:, None] - own_base * part[1][:, None]) / points
    return (grad, (own_tok - own_base) * grad)


def body(tokens, sub_pos, sub_base, embed, *rest):
    n_path, n_ctx = lax.axis_size("path"), lax.axis_size("ctx")
    tok_rows = tokens.shape[0]
    share = embed.shape[1] // (n_path * n_ctx)
    tables = 2 * (tok_rows * n_ctx) ** 2
    fits = share == LANES and tok_rows == LANES and n_ctx == GROUP and tables <= TABLE_BYTES
    fits = fits and n_ctx % n_path == 0 and n_path & (n_path - 1) == 0
    chosen = kernel_body if fits else plain_body
    return chosen(tokens, sub_pos, sub_base, embed, *rest)


def solution(mesh):
    return jax.shard_map(
        body,
        mesh=mesh,
        in_specs=(
            P("ctx"),
            P("ctx"),
            P("ctx"),
            P(),
            P(),
            P(),
            P(None, "ctx"),
            P("ctx"),
            P("ctx", None),
        ),
        out_specs=(P("ctx", "path"), P("ctx", "path")),
        check_vma=False,
    )
```

```python
import functools

import jax
import jax.numpy as jnp
import ml_dtypes
import numpy as np
from jax import lax
from jax.experimental import pallas as pl
from jax.experimental.pallas import tpu as pltpu
from jax.sharding import PartitionSpec as P

LANES = 128
GROUP = 8
RADIX = 4
LOOK_ROWS = 256
CHUNK = 16
EPS = 1e-06
CANCEL = 0.004
TABLE_BYTES = 2**21
F32 = jnp.float32
BF16 = jnp.bfloat16
precise = lax.Precision.HIGH


def angle_tables(length):
    outer_size = 64
    inner_size = length // outer_size
    outer_idx = jnp.arange(outer_size, dtype=jnp.int32)
    inner_idx = jnp.arange(inner_size, dtype=jnp.int32)
    outer_angle = (
        2.0 * jnp.pi / outer_size
        * (outer_idx[:, None] * outer_idx[None, :] % outer_size).astype(F32)
    )
    inner_angle = (
        2.0 * jnp.pi / inner_size
        * (inner_idx[:, None] * inner_idx[None, :] % inner_size).astype(F32)
    )
    twist_angle = (
        2.0 * jnp.pi / length
        * (outer_idx[:, None] * inner_idx[None, :] % length).astype(F32)
    )
    return (outer_angle, inner_angle, twist_angle)


def complex_table(angle, sign):
    cosine = jnp.cos(angle)
    sine = sign * jnp.sin(angle)
    return jnp.stack([jnp.stack([cosine, sine]), jnp.stack([-sine, cosine])])


def twisted(values, angle, sign):
    cosine = jnp.cos(angle)[None, :, :, None]
    sine = sign * jnp.sin(angle)[None, :, :, None]
    real_part = values[:, 0]
    imag_part = values[:, 1]
    return jnp.stack(
        [real_part * cosine - imag_part * sine, real_part * sine + imag_part * cosine], 1
    )


def spectrum(signal):
    batch, half, width = signal.shape
    length = 2 * half
    outer_angle, inner_angle, twist_angle = angle_tables(length)
    outer_size = outer_angle.shape[0]
    inner_size = inner_angle.shape[0]
    folded = signal.reshape(batch, outer_size // 2, inner_size, width)
    used = outer_angle[:, : outer_size // 2]
    outer_table = jnp.stack([jnp.cos(used), -jnp.sin(used)])
    first = jnp.einsum("rka,pabc->prkbc", outer_table, folded, precision=precise)
    turned = twisted(first, twist_angle, -1.0)
    return jnp.einsum(
        "prkbc,rsbm->pskmc", turned, complex_table(inner_angle, -1.0), precision=precise
    )


def inverse(spec):
    batch, parts, outer_size, inner_size, width = spec.shape
    length = outer_size * inner_size
    outer_angle, inner_angle, twist_angle = angle_tables(length)
    back = jnp.einsum("pskmc,stmb->ptkbc", spec, complex_table(inner_angle, 1.0), precision=precise)
    turned = twisted(back, twist_angle, 1.0)
    used = outer_angle[: outer_size // 2]
    outer_table = jnp.stack([jnp.cos(used), -jnp.sin(used)])
    result = jnp.einsum("rak,prkbc->pabc", outer_table, turned, precision=precise)
    return (result / length).reshape(batch, length // 2, width)


def long_conv(signal, filter_spec, skip_gain, adjoint):
    spec = spectrum(signal)
    sig_real = spec[:, 0]
    sig_imag = spec[:, 1]
    filt_real = filter_spec[:, 0]
    filt_imag = filter_spec[:, 1]
    if adjoint:
        prod_real = sig_real * filt_real + sig_imag * filt_imag
        prod_imag = sig_imag * filt_real - sig_real * filt_imag
    else:
        prod_real = sig_real * filt_real - sig_imag * filt_imag
        prod_imag = sig_real * filt_imag + sig_imag * filt_real
    return inverse(jnp.stack([prod_real, prod_imag], 1)) + skip_gain * signal


def rounded(value):
    return value.astype(BF16).astype(F32)


def shifted(values, step):
    zeros = jnp.zeros_like(values[:, : abs(step)])
    if step > 0:
        return jnp.concatenate([zeros, values[:, :-step]], 1)
    return jnp.concatenate([values[:, -step:], zeros], 1)


@functools.lru_cache(maxsize=None)
def dft_tables(length):
    quarter = length // RADIX
    freq = 4 * np.arange(quarter, dtype=np.int64) + 1
    place = np.arange(quarter, dtype=np.int64)
    there, back = [], []
    for offset in range(RADIX):
        turns = freq[:, None] * (RADIX * place + offset)[None, :] % (4 * length)
        angle = turns * (2.0 * np.pi / (4 * length))
        cosine = np.cos(angle).astype(ml_dtypes.bfloat16)
        sine = np.sin(angle).astype(ml_dtypes.bfloat16)
        there.append(np.concatenate([cosine, sine], 0))
        back.append(np.concatenate([cosine.T, sine.T], 1))
    return (np.stack(there), np.stack(back))


def butterfly(values, sign):
    (r0, s0), (r1, s1), (r2, s2), (r3, s3) = values
    sum_r, sum_s, diff_r, diff_s = r0 + r2, s0 + s2, r0 - r2, s0 - s2
    odd_r, odd_s, turn_r, turn_s = r1 + r3, s1 + s3, r1 - r3, s1 - s3
    ahead = (diff_r + turn_s, diff_s - turn_r)
    behind = (diff_r - turn_s, diff_s + turn_r)
    if sign < 0:
        ahead, behind = behind, ahead
    return ((sum_r + odd_r, sum_s + odd_s), ahead, (sum_r - odd_r, sum_s - odd_s), behind)


def transposed(rows):
    count = rows.shape[0]
    if count < LANES:
        rows = jnp.concatenate([rows, jnp.zeros((LANES - count, LANES), F32)], 0)
    return rows.T


def dot(left, right):
    return jnp.dot(left, right, preferred_element_type=F32)


def iota(dims, axis):
    return lax.broadcasted_iota(jnp.int32, dims, axis)


def by_residue():
    row = iota((LANES, LANES), 0)
    part = LANES // RADIX
    source = RADIX * (row % part) + row // part
    return (iota((LANES, LANES), 1) == source).astype(F32)


def hot(ids, vocab):
    lane = iota(ids.shape, 1).astype(F32)
    parts = [
        (ids == lane + float(column * LANES)).astype(F32).astype(BF16)
        for column in range(vocab // LANES)
    ]
    return jnp.concatenate(parts, 1)


def joined(block, kind):
    return 256.0 * block[2 * kind : 2 * kind + 1] + block[2 * kind + 1 : 2 * kind + 2]


def pack_kernel(
    tok_hbm, pos_hbm, put_hbm, cot_hbm, msg_ref, ids_ref, tok_ref, pos_ref, put_ref, cot_ref, sems
):
    dests, rows, share = msg_ref.shape
    tok_rows = cot_hbm.shape[0]
    n_path = cot_hbm.shape[1] // (dests * share)
    path = lax.axis_index("path")
    moves = [(tok_hbm, tok_ref), (pos_hbm, pos_ref), (put_hbm, put_ref)]
    for dest in range(dests):
        lanes = pl.ds(pl.multiple_of((dest * n_path + path) * share, LANES), share)
        moves.append((cot_hbm.at[:, lanes], cot_ref.at[:, pl.ds(dest * share, share)]))
    copies = [
        pltpu.make_async_copy(source, target, sems.at[index])
        for index, (source, target) in enumerate(moves)
    ]
    for copy in copies:
        copy.start()
    order = by_residue().astype(BF16)
    for copy in copies[:3]:
        copy.wait()
    lists = []
    for ref in (tok_ref, pos_ref, put_ref):
        value = ref[...].astype(F32)
        if value.shape[1] < LANES:
            value = jnp.concatenate([value, jnp.zeros((1, LANES - value.shape[1]), F32)], 1)
        high = jnp.floor(value * (1.0 / 256.0))
        lists += [high, value - 256.0 * high]
    lists.append(jnp.zeros((rows - tok_rows - len(lists), LANES), F32))
    ids = jnp.concatenate(lists, 0)
    ids_ref[...] = ids
    turned = lax.dot_general(
        ids.astype(BF16), order, (((1,), (1,)), ((), ())), preferred_element_type=F32
    )
    ids = jnp.where(iota(ids.shape, 0) < 2, turned, ids).astype(BF16)
    for dest in range(dests):
        msg_ref[dest, tok_rows:, :] = ids
    for copy in copies[3:]:
        copy.wait()
    turned = dot(order, cot_ref[...]).astype(BF16)
    for dest in range(dests):
        msg_ref[dest, :tok_rows, :] = turned[:, dest * share : (dest + 1) * share]


def prepare_kernel(
    filt_hbm, table_hbm, embed_hbm, skip_hbm, after_ref,
    spec_hbm, gram_hbm,
    filt_ref, table_ref, embed_ref, skip_ref, sum_ref, spec_ref, gram_ref, sems, out_sems,
):
    length, share = filt_ref.shape
    quarter = length // RADIX
    vocab, width = embed_ref.shape
    pieces = sems.shape[0] - 3
    wide = width // pieces
    path = lax.axis_index("path")
    lanes = pl.ds(pl.multiple_of(path * share, LANES), share)
    moves = [
        (filt_hbm.at[:, lanes], filt_ref),
        (skip_hbm.at[:, lanes], skip_ref),
        (table_hbm, table_ref),
    ]
    for index in range(pieces):
        lanes = pl.ds(index * wide, wide)
        moves.append((embed_hbm.at[:, lanes], embed_ref.at[:, lanes]))
    copies = [
        pltpu.make_async_copy(source, target, sems.at[index])
        for index, (source, target) in enumerate(moves)
    ]
    for copy in copies:
        copy.start()

    copies[0].wait()
    copies[1].wait()
    filt_ref[0:1, :] = filt_ref[0:1, :] + skip_ref[...]
    parts = []
    for offset in range(RADIX):
        value = filt_ref[pl.ds(offset, quarter, stride=RADIX), :] * (1.0 / length)
        high = value.astype(BF16)
        parts.append(jnp.concatenate([high, (value - high.astype(F32)).astype(BF16)], 1))
    copies[2].wait()
    found = []
    for offset in range(RADIX):
        both = dot(table_ref[offset], parts[offset])
        both = both[:, :share] + both[:, share:]
        found.append((both[:quarter], both[quarter:]))
    for part, (real, imag) in enumerate(butterfly(found, -1)):
        spec_ref[2 * part] = real
        spec_ref[2 * part + 1] = imag
    outs = [pltpu.make_async_copy(spec_ref, spec_hbm, out_sems.at[0])]
    outs[0].start()

    sum_ref[vocab // 2 :, : vocab // 2] = jnp.zeros((vocab // 2, vocab // 2), F32)
    for index in range(pieces):
        copies[3 + index].wait()
        part = embed_ref[:, index * wide : (index + 1) * wide]
        for rows, lanes in ((slice(0, vocab // 2), slice(0, vocab)), (slice(vocab // 2, vocab),) * 2):
            found = lax.dot_general(
                part[rows], part[lanes], (((1,), (1,)), ((), ())), preferred_element_type=F32
            )
            if index == 0:
                sum_ref[rows, lanes] = found
            else:
                sum_ref[rows, lanes] += found
    first = (lax.axis_index("ctx") * lax.axis_size("path") + path) * share
    mine = embed_ref[:, pl.ds(pl.multiple_of(first, LANES), share)]
    same = iota((LANES, LANES), 0) == iota((LANES, LANES), 1)
    lane = iota((LANES, LANES), 1)
    below = 3 * vocab
    for block in range(vocab // LANES):
        rows = slice(block * LANES, (block + 1) * LANES)
        value = sum_ref[rows, :]
        norm = jnp.sum(jnp.where(same, value[:, rows], 0.0), 1, keepdims=True)
        inv = jnp.broadcast_to(lax.rsqrt(norm / width + EPS), (LANES, LANES))
        high = inv.astype(BF16).astype(F32)
        inv = jnp.where(lane < LANES // 2, high, inv - high).astype(BF16)
        side, start = block * LANES // (vocab // 2), block * LANES % (vocab // 2)
        into = slice(below + start, below + start + LANES)
        left = side * (share + LANES)
        gram_ref[into, left : left + share] = mine[rows]
        gram_ref[into, left + share : left + share + LANES] = inv
        for part in range(3):
            high = value.astype(BF16)
            into = slice(part * vocab + block * LANES, part * vocab + (block + 1) * LANES)
            gram_ref[into, :] = high
            value = value - high.astype(F32)
            into = pl.ds(part * vocab + block * LANES, LANES)
            sem = out_sems.at[1 + block * 3 + part]
            outs.append(pltpu.make_async_copy(gram_ref.at[into], gram_hbm.at[into], sem))
            outs[-1].start()
    into = pl.ds(below, vocab // 2)
    outs.append(pltpu.make_async_copy(gram_ref.at[into], gram_hbm.at[into], out_sems.at[out_sems.shape[0] - 1]))
    outs[-1].start()
    for copy in outs:
        copy.wait()


def own_kernel(ids_ref, embed_ref, grad_ref, own_ref):
    vocab = embed_ref.shape[0]
    own_width = own_ref.shape[2]
    lanes = pl.ds(pl.multiple_of(lax.axis_index("path") * own_width, LANES), own_width)
    ids = ids_ref[...]
    columns = transposed(jnp.concatenate([joined(ids, kind) for kind in range(3)], 0))
    tok = jnp.broadcast_to(columns[:, 0:1], (LANES, LANES))
    place = jnp.broadcast_to(joined(ids, 1), (LANES, LANES))
    put = jnp.broadcast_to(joined(ids, 2), (LANES, LANES))
    first = lax.axis_index("ctx") * LANES
    subs = LANES // GROUP
    here = (place == (iota((LANES, LANES), 0) + first).astype(F32)) & (iota((LANES, LANES), 1) < subs)
    found = jnp.max(jnp.where(here, put, -1.0), 1, keepdims=True)
    base = jnp.where(found >= 0.0, found, tok)
    hots = jnp.concatenate([hot(tok, vocab), hot(base, vocab)], 0)
    both = dot(hots, embed_ref[:, lanes]).astype(BF16)
    own_ref[0] = both[:LANES]
    own_ref[1] = both[LANES:]


def multiply_rows(found, spec_ref, prod_ref, points, kind):
    _, quarter, share = spec_ref.shape
    for start in range(0, quarter, CHUNK):
        here = slice(start, start + CHUNK)
        after = slice(quarter + start, quarter + start + CHUNK)
        filt = [(spec_ref[2 * part, here, :], spec_ref[2 * part + 1, here, :]) for part in range(RADIX)]
        for point in range(points):
            lanes = slice(point * share, (point + 1) * share)
            values = butterfly([(value[here, lanes], value[after, lanes]) for value in found], -1)
            prods = []
            for (real, imag), (filt_real, filt_imag) in zip(values, filt):
                if kind == 1:
                    prods.append((real * filt_real + imag * filt_imag, imag * filt_real - real * filt_imag))
                else:
                    prods.append((real * filt_real - imag * filt_imag, imag * filt_real + real * filt_imag))
            lanes = slice((kind * points + point) * share, (kind * points + point + 1) * share)
            for part, (real, imag) in enumerate(butterfly(prods, 1)):
                prod_ref[part, here, lanes] = real.astype(BF16)
                prod_ref[part, after, lanes] = imag.astype(BF16)


def ids_kernel(vocab, msg_ref, hot_ref, subs_ref, put_ref):
    length = hot_ref.shape[0]
    quarter = length // RADIX
    n_ctx = msg_ref.shape[0]
    block_part = LANES // RADIX
    per_block = LANES // GROUP
    subs = n_ctx * per_block
    blocks = [msg_ref[block, LANES:, :].astype(F32) for block in range(n_ctx)]
    toks = transposed(jnp.concatenate([joined(block, 0) for block in blocks], 0))
    spread = sum(
        blocks[block] if block == 0 else pltpu.roll(blocks[block], block * per_block, 1)
        for block in range(n_ctx)
    )
    place = joined(spread, 1)
    put = joined(spread, 2)
    back = jnp.floor(place * (1.0 / RADIX))
    place = back + (place - RADIX * back) * quarter
    columns = transposed(jnp.concatenate([place, put], 0))
    for block in range(n_ctx):
        column = jnp.broadcast_to(toks[:, block : block + 1], (LANES, LANES))
        rows = hot(column, vocab)
        for side in range(RADIX):
            first = side * quarter + block * block_part
            hot_ref[first : first + block_part, :] = rows[side * block_part : (side + 1) * block_part]
    subs_ref[subs:, :] = hot(jnp.broadcast_to(columns[:, 1:2], (subs, LANES)), vocab)
    pick = jnp.concatenate(
        [
            (columns[:, 0:1] == (iota((subs, LANES), 1) + part * LANES).astype(F32)).astype(F32).astype(BF16)
            for part in range(length // LANES)
        ],
        1,
    )
    for index in range(length // LANES):
        row = (iota((LANES, subs), 0) + index * LANES).astype(F32)
        here = (row == place[:, :subs]).astype(F32).astype(BF16)
        put_ref[index * LANES : (index + 1) * LANES, :] = jnp.concatenate([here, here], 1)
    subs_ref[:subs, :] = dot(pick, hot_ref[...]).astype(BF16)


def feature_kernel(
    points, msg_ref, hot_ref, subs_hot_ref, put_ref, gram_ref, taps_ref, gain_ref, embed_hbm,
    signal_ref, k_ref, v_ref, inv_ref, pair_ref,
    embed_ref, sums_ref, found_ref, look_ref, subs_ref, sem,
):
    length = signal_ref.shape[0]
    quarter = length // RADIX
    vocab, width = embed_hbm.shape
    share = pair_ref.shape[2]
    subs = subs_hot_ref.shape[0] // 2
    first = (lax.axis_index("ctx") * points + lax.axis_index("path")) * share
    first = pl.multiple_of(first, LANES)
    below = 3 * vocab
    table = jnp.concatenate(
        [gram_ref[below:, : share + LANES], gram_ref[below:, share + LANES :]], 0
    )

    for index in range(length // LOOK_ROWS):
        rows = pl.ds(index * LOOK_ROWS, LOOK_ROWS)
        look_ref[rows, :] = dot(hot_ref[rows, :], table)

    alphas = [(point + 0.5) / points for point in range(points)]
    hots = subs_hot_ref[...]
    found = dot(jnp.concatenate([hots] * 3, 1), gram_ref[:below, :])
    hot_tok32, hot_base32 = hots[:subs].astype(F32), hots[subs:].astype(F32)
    tok_tok = jnp.sum(found[:subs] * hot_tok32, 1, keepdims=True)
    tok_base = jnp.sum(found[:subs] * hot_base32, 1, keepdims=True)
    base_tok = jnp.sum(found[subs:] * hot_tok32, 1, keepdims=True)
    tok_base = jnp.where(tok_base == 0.0, base_tok, tok_base)
    base_base = jnp.sum(found[subs:] * hot_base32, 1, keepdims=True)
    cancels = jnp.zeros((subs, 1), F32)
    for point in range(points):
        alpha = alphas[point]
        terms = (1.0 - alpha) ** 2 * base_base + alpha**2 * tok_tok
        total = terms + 2.0 * alpha * (1.0 - alpha) * tok_base
        cancels = jnp.maximum(cancels, (total < CANCEL * terms).astype(F32))
        inv = lax.rsqrt(jnp.maximum(total, 0.0) / width + EPS)
        sums_ref[point] = jnp.broadcast_to(inv, (subs, LANES))

    @pl.when(jnp.max(cancels) > 0.5)
    def _():
        sums_ref[...] = jnp.zeros_like(sums_ref)
        wide = found_ref.shape[1]

        @pl.loop(0, width // wide)
        def _(step):
            lanes = pl.ds(pl.multiple_of(step * wide, wide), wide)
            copy = pltpu.make_async_copy(embed_hbm.at[:, lanes], embed_ref, sem)
            copy.start()
            copy.wait()
            found_ref[...] = dot(hots, embed_ref[...])
            for block in range(subs // GROUP):
                rows = slice(block * GROUP, (block + 1) * GROUP)
                sums = [sums_ref[point, rows, :] for point in range(points)]
                for column in range(wide // LANES):
                    cut = slice(column * LANES, (column + 1) * LANES)
                    base = found_ref[subs + block * GROUP : subs + (block + 1) * GROUP, cut]
                    diff = found_ref[rows, cut] - base
                    for point in range(points):
                        value = base + alphas[point] * diff
                        sums[point] = sums[point] + value * value
                for point in range(points):
                    sums_ref[point, rows, :] = sums[point]

        for point in range(points):
            mean = jnp.sum(sums_ref[point], 1, keepdims=True) / width
            sums_ref[point] = jnp.broadcast_to(lax.rsqrt(mean + EPS), (subs, LANES))

    high = [dot(hots[subs:], table[:, :share]), jnp.ones((subs, LANES), F32)]
    low = [jnp.zeros((subs, LANES), F32)] * 2
    for point in range(points):
        inv = sums_ref[point]
        high.append(inv.astype(BF16).astype(F32))
        low.append(inv - high[-1])
    held = jnp.concatenate([jnp.concatenate(high, 1), jnp.concatenate(low, 1)], 0).astype(BF16)
    for index in range(length // LOOK_ROWS):
        rows = pl.ds(index * LOOK_ROWS, LOOK_ROWS)
        subs_ref[rows, :] = dot(put_ref[rows, :], held)

    cols = points * share
    block_part = LANES // RADIX
    last = {side: [jnp.zeros((GROUP, share), F32)] * points for side in (RADIX - 2, RADIX - 1)}
    gain = gain_ref[:, pl.ds(first, share)]
    taps = [taps_ref[f, :, pl.ds(first, share)].astype(F32) for f in range(3)]
    taps = [[taps[f][tap : tap + 1] for tap in range(3)] for f in range(3)]

    for start in range(0, quarter, CHUNK):
        block, inside = start // block_part, start % block_part
        sides = []
        for side in range(RADIX):
            rows = pl.ds(side * quarter + start, CHUNK)
            tok = look_ref[rows, :share]
            inv = look_ref[rows, share:]
            inv = inv + pltpu.roll(inv, LANES // 2, 1)
            chosen = subs_ref[rows, share : 2 * share] > 0.5
            base = jnp.where(chosen, subs_ref[rows, :share], tok)
            pair_ref[0, rows, :] = tok.astype(BF16)
            pair_ref[1, rows, :] = base.astype(BF16)
            sent = pl.ds(side * block_part + inside, CHUNK)
            sides.append((rows, base, tok - base, inv, chosen, msg_ref[block, sent, :].astype(F32)))
        for point in range(points):
            lanes = slice(point * share, (point + 1) * share)
            recent = []
            for rows, base, diff, inv_tok, chosen, _ in sides:
                inv = jnp.where(
                    chosen, subs_ref[rows, (2 + point) * share : (3 + point) * share], inv_tok
                )
                inv_ref[rows, lanes] = inv
                recent.append(rounded((base + alphas[point] * diff) * inv * gain))
            backs = []
            for side in (RADIX - 2, RADIX - 1):
                window = jnp.concatenate([last[side][point], recent[side]], 0)
                last[side][point] = recent[side][CHUNK - GROUP :]
                backs.append(window[GROUP - 1 : GROUP - 1 + CHUNK])
            recent = backs + recent
            for side in range(RADIX):
                rows, upstream = sides[side][0], sides[side][5]
                feats = [sum(taps[f][tap] * recent[side + 2 - tap] for tap in range(3)) for f in range(3)]
                k_ref[rows, lanes] = feats[1]
                v_ref[rows, lanes] = feats[2]
                signal_ref[rows, lanes] = (feats[1] * feats[2]).astype(BF16)
                after = slice(cols + point * share, cols + (point + 1) * share)
                signal_ref[rows, after] = (upstream * feats[0]).astype(BF16)


def gradient_kernel(
    points, width, msg_ref, pair_ref, taps_ref, gain_ref,
    signal_ref, k_ref, v_ref, inv_ref, table_ref, back_ref, spec_ref,
    grad_ref,
    prod_ref,
):
    _, quarter, share = spec_ref.shape
    cols = points * share
    n_ctx = msg_ref.shape[0]
    block_part = LANES // RADIX
    first = (lax.axis_index("ctx") * points + lax.axis_index("path")) * share
    first = pl.multiple_of(first, LANES)
    gain = gain_ref[:, pl.ds(first, share)]
    taps = [taps_ref[f, :, pl.ds(first, share)].astype(F32) for f in range(3)]
    taps = [[taps[f][tap : tap + 1] for tap in range(3)] for f in range(3)]

    found = []
    for kind in range(2):
        signal = slice(kind * cols, (kind + 1) * cols)
        spectra = [
            dot(table_ref[side], signal_ref[side * quarter : (side + 1) * quarter, signal])
            for side in range(RADIX)
        ]
        multiply_rows(spectra, spec_ref, prod_ref, points, kind)
    for kind in range(2):
        signal = slice(kind * cols, (kind + 1) * cols)
        found.append([dot(back_ref[side], prod_ref[side, :, signal]) for side in range(RADIX)])

    carried = [[jnp.zeros((GROUP, share), F32)] * points for _ in range(3)]
    lane, row = iota((CHUNK, LANES), 1), iota((CHUNK, LANES), 0)
    for start in reversed(range(0, quarter, CHUNK)):
        block, inside = start // block_part, start % block_part
        here = slice(start, start + CHUNK)
        if inside + CHUNK == block_part:
            means = [jnp.zeros((CHUNK, LANES), F32)] * 2
        sides = []
        for side in range(RADIX):
            rows = pl.ds(side * quarter + start, CHUNK)
            sent = pl.ds(side * block_part + inside, CHUNK)
            upstream = msg_ref[block, sent, :].astype(F32)
            sides.append([rows, sent, upstream] + [jnp.zeros((CHUNK, share), F32)] * 4)
        for point in reversed(range(points)):
            lanes = slice(point * share, (point + 1) * share)
            by_tap = []
            for side in range(RADIX):
                rows, _, upstream = sides[side][:3]
                grad_z = found[1][side][here, lanes]
                grads = (
                    upstream * found[0][side][here, lanes],
                    grad_z * v_ref[rows, lanes],
                    grad_z * k_ref[rows, lanes],
                )
                by_tap.append([sum(taps[f][tap] * grads[f] for f in range(3)) for tap in range(3)])
            ahead = []
            for slot, value in enumerate((by_tap[0][1], by_tap[0][2], by_tap[1][2])):
                window = jnp.concatenate([value, carried[slot][point]], 0)
                carried[slot][point] = value[:GROUP]
                ahead.append(window[1 : 1 + CHUNK])
            by_tap += [[None, ahead[0], ahead[1]], [None, None, ahead[2]]]
            for side in range(RADIX):
                rows, _, _, total, sum0, sum1, sum2 = sides[side]
                inv = inv_ref[rows, lanes]
                along = inv * (by_tap[side][0] + by_tap[side + 1][1] + by_tap[side + 2][2])
                total = total + along
                sum0 = sum0 + along * (inv * inv)
                sum1 = sum1 + sum0
                sides[side][3:] = [total, sum0, sum1, sum2 + sum1]
        for side in range(RADIX):
            rows, sent, _, total, sum0, sum1, sum2 = sides[side]
            base = pair_ref[1, rows, :].astype(F32)
            diff = pair_ref[0, rows, :].astype(F32) - base
            once = (sum1 - 0.5 * sum0) * (1.0 / points)
            twice = (2.0 * (sum2 - sum1) + 0.25 * sum0) * (1.0 / points**2)
            to_tok = base * once + diff * twice
            to_base = base * sum0 + diff * once - to_tok
            grad_ref[block, sent, :] = (gain * total).astype(BF16)
            for kind, value in enumerate((gain * to_tok, gain * to_base)):
                value = jnp.sum(value, 1, keepdims=True)
                at = lane == row + (side * block_part + inside)
                means[kind] = means[kind] + jnp.where(at, value, 0.0)
        if inside == 0:
            sent = []
            for value in means:
                value = jnp.sum(value, 0, keepdims=True) / width
                high = value.astype(BF16).astype(F32)
                sent += [high, value - high]
            sent.append(jnp.zeros((grad_ref.shape[1] - LANES - len(sent), LANES), F32))
            grad_ref[block, LANES:, :] = jnp.concatenate(sent, 0).astype(BF16)


def partial_kernel(grad_ref, *out_refs):
    rows, _ = out_refs[0].shape
    n_ctx = grad_ref.shape[0]
    each = n_ctx // len(out_refs)
    spare = sum(grad_ref[block, LANES:, :].astype(F32) for block in range(n_ctx))
    sums = [spare[0:1] + spare[1:2], spare[2:3] + spare[3:4]]
    sent = []
    for value in sums:
        high = value.astype(BF16).astype(F32)
        sent += [high, value - high]
    sent.append(jnp.zeros((rows - each * LANES - len(sent), LANES), F32))
    sent = jnp.concatenate(sent, 0).astype(BF16)
    path = lax.axis_index("path")
    for step, ref in enumerate(out_refs):
        dest = path ^ step
        for piece in range(each):
            ref[piece * LANES : (piece + 1) * LANES, :] = grad_ref[dest * each + piece, :LANES, :]
        ref[each * LANES :, :] = sent


def finish_kernel(own_ref, *refs):
    grad_refs, (path_hbm, attr_hbm, path_ref, attr_ref, sems) = refs[:-5], refs[-5:]
    points = len(grad_refs)
    rows, share = grad_refs[0].shape
    pieces = rows // LANES
    spare = sum(ref[pieces * LANES :, :].astype(F32) for ref in grad_refs)
    lane = iota((LANES, LANES), 1)
    part = LANES // RADIX
    order = (iota((LANES, LANES), 0) == RADIX * (lane % part) + lane // part).astype(F32).astype(BF16)
    left, split = jnp.concatenate([spare[0:1] + spare[1:2], spare[2:3] + spare[3:4]], 0), []
    for _ in range(3):
        split.append(left.astype(BF16).astype(F32))
        left = left - split[-1]
    split = jnp.concatenate(split + [jnp.zeros((2, LANES), F32)], 0).astype(BF16)
    columns = lax.dot_general(order, split, (((1,), (1,)), ((), ())), preferred_element_type=F32)
    to_tok = columns[:, 0:1] + columns[:, 2:3] + columns[:, 4:5]
    to_base = columns[:, 1:2] + columns[:, 3:4] + columns[:, 5:6]
    path = lax.axis_index("path")
    copies = []
    for step, ref in enumerate(grad_refs):
        for piece in range(pieces):
            slot = step * pieces + piece
            first = (piece * points + (path ^ step)) * share
            lanes = pl.ds(pl.multiple_of(first, LANES), share)
            tok = own_ref[0, :, lanes].astype(F32)
            base = own_ref[1, :, lanes].astype(F32)
            grad = dot(order, ref[piece * LANES : (piece + 1) * LANES, :])
            grad = (grad - tok * to_tok - base * to_base) / points
            path_ref[slot] = grad
            attr_ref[slot] = (tok - base) * grad
            for kind, (source, target) in enumerate(((path_ref, path_hbm), (attr_ref, attr_hbm))):
                copies.append(
                    pltpu.make_async_copy(source.at[slot], target.at[:, lanes], sems.at[kind, slot])
                )
                copies[-1].start()
    for copy in copies:
        copy.wait()


def any_spec():
    return pl.BlockSpec(memory_space=pl.ANY)


def vmem_spec():
    return pl.BlockSpec(memory_space=pltpu.VMEM)


def hbm_spec():
    return pl.BlockSpec(memory_space=pltpu.HBM)


def call(kernel, ins, outs, scratch, flops, moved, mebibytes):
    return pl.pallas_call(
        kernel,
        in_specs=ins,
        out_specs=[spec for spec, _ in outs],
        out_shape=[shape for _, shape in outs],
        scratch_shapes=scratch,
        compiler_params=pltpu.CompilerParams(vmem_limit_bytes=mebibytes * 2**20),
        cost_estimate=pl.CostEstimate(flops=flops, bytes_accessed=moved, transcendentals=0),
    )


def shape(dims, dtype):
    return jax.ShapeDtypeStruct(dims, dtype)


def kernel_body(tokens, sub_pos, sub_base, embed, norm_gain, fir_taps, long_filter, skip_gain, cotangent):
    n_path, n_ctx = lax.axis_size("path"), lax.axis_size("ctx")
    points = n_path
    tok_rows = tokens.shape[0]
    length = tok_rows * n_ctx
    vocab, width = embed.shape
    share = width // (n_path * n_ctx)
    subs = sub_pos.shape[0] * n_ctx
    own_width = width // n_path
    cols = points * share
    quarter = length // RADIX
    tables = dft_tables(length)
    dma = pltpu.SemaphoreType.DMA
    transform_flops = length * length
    spare = 8

    msg, ids = call(
        pack_kernel,
        [hbm_spec()] * 4,
        [
            (vmem_spec(), shape((n_ctx, tok_rows + spare, share), BF16)),
            (vmem_spec(), shape((spare, LANES), F32)),
        ],
        [
            pltpu.VMEM((1, tok_rows), jnp.int32),
            pltpu.VMEM((1, sub_pos.shape[0]), jnp.int32),
            pltpu.VMEM((1, sub_pos.shape[0]), jnp.int32),
            pltpu.VMEM((tok_rows, n_ctx * share), BF16),
            dma((n_ctx + 3,)),
        ],
        length * share,
        8 * length * share,
        60,
    )(
        tokens.reshape(1, tok_rows),
        sub_pos.reshape(1, -1),
        sub_base.reshape(1, -1),
        cotangent,
    )
    msg = lax.all_to_all(msg, "ctx", 0, 0, tiled=True)

    gain = norm_gain.reshape(1, width)
    skip = skip_gain.reshape(1, n_path * share)
    spec, gram = call(
        prepare_kernel,
        [hbm_spec()] * 4 + [any_spec()],
        [
            (any_spec(), shape((2 * RADIX, quarter, share), F32)),
            (any_spec(), shape((3 * vocab + vocab // 2, vocab), BF16)),
        ],
        [
            pltpu.VMEM((length, share), F32),
            pltpu.VMEM((RADIX, 2 * quarter, quarter), BF16),
            pltpu.VMEM((vocab, width), BF16),
            pltpu.VMEM((1, share), F32),
            pltpu.VMEM((vocab, vocab), F32),
            pltpu.VMEM((2 * RADIX, quarter, share), F32),
            pltpu.VMEM((3 * vocab + vocab // 2, vocab), BF16),
            dma((7,)),
            dma((3 * vocab // LANES + 2,)),
        ],
        2 * vocab * vocab * width,
        2 * vocab * width,
        58,
    )(long_filter, tables[0], embed, skip, ids)

    hots, subs_hots, put_hots = call(
        functools.partial(ids_kernel, vocab),
        [vmem_spec()],
        [
            (vmem_spec(), shape((length, vocab), BF16)),
            (vmem_spec(), shape((2 * subs, vocab), BF16)),
            (vmem_spec(), shape((length, 2 * subs), BF16)),
        ],
        [],
        2 * 10**9,
        4 * 10**6,
        8,
    )(msg)
    wide = 4 * LANES
    signal, k_feat, v_feat, inv, pair = call(
        functools.partial(feature_kernel, points),
        [vmem_spec()] * 7 + [hbm_spec()],
        [(vmem_spec(), shape((length, 2 * cols), BF16))]
        + [(vmem_spec(), shape((length, cols), F32))] * 3
        + [(vmem_spec(), shape((2, length, share), BF16))],
        [
            pltpu.VMEM((vocab, wide), BF16),
            pltpu.VMEM((points, subs, LANES), F32),
            pltpu.VMEM((2 * subs, wide), F32),
            pltpu.VMEM((length, 2 * share), F32),
            pltpu.VMEM((length, (2 + points) * share), F32),
            dma,
        ],
        2 * length * vocab * 3 * share,
        2 * vocab * width + 16 * length * cols,
        39,
    )(msg, hots, subs_hots, put_hots, gram, fir_taps, gain, embed)

    grad = call(
        functools.partial(gradient_kernel, points, width),
        [vmem_spec()] * 11,
        [(vmem_spec(), shape((n_ctx, tok_rows + spare, share), BF16))],
        [
            pltpu.VMEM((RADIX, 2 * quarter, 2 * cols), BF16),
        ],
        4 * transform_flops * cols,
        4 * length * length + 16 * length * cols,
        32,
    )(msg, pair, fir_taps, gain, signal, k_feat, v_feat, inv, *tables, spec)[0]

    own = call(
        own_kernel,
        [vmem_spec(), vmem_spec(), any_spec()],
        [(vmem_spec(), shape((2, tok_rows, own_width), BF16))],
        [],
        4 * tok_rows * vocab * own_width,
        2 * vocab * own_width,
        10,
    )(ids, embed, grad)[0]
    grad = lax.all_to_all(grad, "ctx", 0, 0, tiled=True)
    each = n_ctx // n_path
    parts = call(
        partial_kernel,
        [vmem_spec()],
        [(vmem_spec(), shape((each * tok_rows + spare, share), BF16))] * n_path,
        [],
        spare * LANES * n_ctx,
        4 * length * share,
        4,
    )(grad)
    parts = [
        part if step == 0 else lax.ppermute(part, "path", [(p, p ^ step) for p in range(n_path)])
        for step, part in enumerate(parts)
    ]
    out = shape((tok_rows, own_width), F32)
    return tuple(
        call(
            finish_kernel,
            [vmem_spec()] * (1 + n_path),
            [(any_spec(), out), (any_spec(), out)],
            [pltpu.VMEM((n_path * each, tok_rows, share), F32)] * 2 + [dma((2, n_path * each))],
            8 * tok_rows * own_width,
            14 * tok_rows * own_width,
            8,
        )(own, *parts)
    )


def plain_body(tokens, sub_pos, sub_base, embed, norm_gain, fir_taps, long_filter, skip_gain, cotangent):
    n_path, n_ctx = lax.axis_size("path"), lax.axis_size("ctx")
    path, ctx = lax.axis_index("path"), lax.axis_index("ctx")
    points = n_path
    tok_rows = tokens.shape[0]
    length = tok_rows * n_ctx
    width = embed.shape[1]
    share = width // (n_path * n_ctx)
    own_width = width // n_path
    first = (ctx * n_path + path) * share
    alphas = ((jnp.arange(points, dtype=jnp.int32)).astype(F32) + 0.5) / points
    alphas = alphas[:, None, None]

    local = jnp.arange(tok_rows, dtype=jnp.int32)[:, None] + ctx * tok_rows == sub_pos[None, :]
    put = jnp.sum(jnp.where(local, sub_base[None, :], 0), 1)
    base_ids = jnp.where(jnp.any(local, 1), put, tokens)
    rows_tok = jnp.take(embed, tokens, axis=0).astype(F32)
    rows_base = jnp.take(embed, base_ids, axis=0).astype(F32)
    rows_in = rows_base[None] + alphas * (rows_tok - rows_base)[None]
    inv = lax.rsqrt(jnp.mean(rows_in * rows_in, -1) + EPS)
    inv = lax.all_gather(inv, "ctx", axis=1, tiled=True)[:, :, None]
    all_tok = lax.all_gather(tokens, "ctx", tiled=True)
    all_base = lax.all_gather(base_ids, "ctx", tiled=True)

    cot = cotangent.reshape(tok_rows, n_ctx, n_path, share)
    cot = lax.dynamic_index_in_dim(cot, path, 2, keepdims=False)
    cot = lax.all_to_all(cot.transpose(1, 0, 2), "ctx", 0, 0, tiled=True)
    upstream = cot.reshape(1, length, share).astype(F32)
    mine = lax.dynamic_slice_in_dim(embed, first, share, 1)
    gain = lax.dynamic_slice_in_dim(norm_gain, first, share, 0)
    taps = lax.dynamic_slice_in_dim(fir_taps, first, share, 2).astype(F32)
    filt = lax.dynamic_slice_in_dim(long_filter, path * share, share, 1)
    skip = lax.dynamic_slice_in_dim(skip_gain, path * share, share, 0)

    emb_tok = jnp.take(mine, all_tok, axis=0).astype(F32)
    emb_base = jnp.take(mine, all_base, axis=0).astype(F32)
    inputs = emb_base[None] + alphas * (emb_tok - emb_base)[None]
    normed = rounded(inputs * inv * gain)
    q_feat, k_feat, v_feat = (
        taps[f, 0] * normed + taps[f, 1] * shifted(normed, 1) + taps[f, 2] * shifted(normed, 2)
        for f in range(3)
    )
    filter_spec = spectrum(filt[None])
    conv = rounded(long_conv(rounded(k_feat * v_feat), filter_spec, skip, False))
    grad_z = rounded(long_conv(rounded(upstream * q_feat), filter_spec, skip, True))
    grads = (rounded(upstream * conv), rounded(grad_z * v_feat), rounded(grad_z * k_feat))
    by_tap = [sum(taps[f, tap] * grads[f] for f in range(3)) for tap in range(3)]
    scaled = gain * (by_tap[0] + shifted(by_tap[1], -1) + shifted(by_tap[2], -2))
    grad = jnp.sum(inv * scaled, 0).astype(BF16)
    along = jnp.sum(inputs * scaled, -1, keepdims=True) * inv**3 / width
    part = jnp.stack([jnp.sum(alphas * along, 0)[:, 0], jnp.sum((1.0 - alphas) * along, 0)[:, 0]])
    part = lax.psum(part, ("path", "ctx"))
    part = lax.dynamic_slice_in_dim(part, ctx * tok_rows, tok_rows, 1)

    back = lax.all_to_all(grad.reshape(n_ctx, tok_rows, share), "ctx", 0, 0, tiled=True)
    back = back.reshape(n_path, n_ctx // n_path, tok_rows, share)
    back = lax.all_to_all(back, "path", 0, 0, tiled=True).astype(F32)
    back = back.transpose(2, 1, 0, 3).reshape(tok_rows, own_width)
    own_tok = lax.dynamic_slice_in_dim(rows_tok, path * own_width, own_width, 1)
    own_base = lax.dynamic_slice_in_dim(rows_base, path * own_width, own_width, 1)
    grad = (back - own_tok * part[0][:, None] - own_base * part[1][:, None]) / points
    return (grad, (own_tok - own_base) * grad)


def body(tokens, sub_pos, sub_base, embed, *rest):
    n_path, n_ctx = lax.axis_size("path"), lax.axis_size("ctx")
    tok_rows = tokens.shape[0]
    share = embed.shape[1] // (n_path * n_ctx)
    tables = 2 * (tok_rows * n_ctx) ** 2
    fits = share == LANES and tok_rows == LANES and n_ctx == GROUP and tables <= TABLE_BYTES
    fits = fits and n_ctx % n_path == 0 and n_path & (n_path - 1) == 0
    chosen = kernel_body if fits else plain_body
    return chosen(tokens, sub_pos, sub_base, embed, *rest)


def solution(mesh):
    return jax.shard_map(
        body,
        mesh=mesh,
        in_specs=(
            P("ctx"),
            P("ctx"),
            P("ctx"),
            P(),
            P(),
            P(),
            P(None, "ctx"),
            P("ctx"),
            P("ctx", None),
        ),
        out_specs=(P("ctx", "path"), P("ctx", "path")),
        check_vma=False,
    )
```

```python
import functools

import jax
import jax.numpy as jnp
import ml_dtypes
import numpy as np
from jax import lax
from jax.experimental import pallas as pl
from jax.experimental.pallas import tpu as pltpu
from jax.sharding import PartitionSpec as P

LANES = 128
GROUP = 8
RADIX = 4
LOOK_ROWS = 256
CHUNK = 16
EPS = 1e-06
CANCEL = 0.004
TABLE_BYTES = 2**21
F32 = jnp.float32
BF16 = jnp.bfloat16
precise = lax.Precision.HIGH


def angle_tables(length):
    outer_size = 64
    inner_size = length // outer_size
    outer_idx = jnp.arange(outer_size, dtype=jnp.int32)
    inner_idx = jnp.arange(inner_size, dtype=jnp.int32)
    outer_angle = (
        2.0 * jnp.pi / outer_size
        * (outer_idx[:, None] * outer_idx[None, :] % outer_size).astype(F32)
    )
    inner_angle = (
        2.0 * jnp.pi / inner_size
        * (inner_idx[:, None] * inner_idx[None, :] % inner_size).astype(F32)
    )
    twist_angle = (
        2.0 * jnp.pi / length
        * (outer_idx[:, None] * inner_idx[None, :] % length).astype(F32)
    )
    return (outer_angle, inner_angle, twist_angle)


def complex_table(angle, sign):
    cosine = jnp.cos(angle)
    sine = sign * jnp.sin(angle)
    return jnp.stack([jnp.stack([cosine, sine]), jnp.stack([-sine, cosine])])


def twisted(values, angle, sign):
    cosine = jnp.cos(angle)[None, :, :, None]
    sine = sign * jnp.sin(angle)[None, :, :, None]
    real_part = values[:, 0]
    imag_part = values[:, 1]
    return jnp.stack(
        [real_part * cosine - imag_part * sine, real_part * sine + imag_part * cosine], 1
    )


def spectrum(signal):
    batch, half, width = signal.shape
    length = 2 * half
    outer_angle, inner_angle, twist_angle = angle_tables(length)
    outer_size = outer_angle.shape[0]
    inner_size = inner_angle.shape[0]
    folded = signal.reshape(batch, outer_size // 2, inner_size, width)
    used = outer_angle[:, : outer_size // 2]
    outer_table = jnp.stack([jnp.cos(used), -jnp.sin(used)])
    first = jnp.einsum("rka,pabc->prkbc", outer_table, folded, precision=precise)
    turned = twisted(first, twist_angle, -1.0)
    return jnp.einsum(
        "prkbc,rsbm->pskmc", turned, complex_table(inner_angle, -1.0), precision=precise
    )


def inverse(spec):
    batch, parts, outer_size, inner_size, width = spec.shape
    length = outer_size * inner_size
    outer_angle, inner_angle, twist_angle = angle_tables(length)
    back = jnp.einsum("pskmc,stmb->ptkbc", spec, complex_table(inner_angle, 1.0), precision=precise)
    turned = twisted(back, twist_angle, 1.0)
    used = outer_angle[: outer_size // 2]
    outer_table = jnp.stack([jnp.cos(used), -jnp.sin(used)])
    result = jnp.einsum("rak,prkbc->pabc", outer_table, turned, precision=precise)
    return (result / length).reshape(batch, length // 2, width)


def long_conv(signal, filter_spec, skip_gain, adjoint):
    spec = spectrum(signal)
    sig_real = spec[:, 0]
    sig_imag = spec[:, 1]
    filt_real = filter_spec[:, 0]
    filt_imag = filter_spec[:, 1]
    if adjoint:
        prod_real = sig_real * filt_real + sig_imag * filt_imag
        prod_imag = sig_imag * filt_real - sig_real * filt_imag
    else:
        prod_real = sig_real * filt_real - sig_imag * filt_imag
        prod_imag = sig_real * filt_imag + sig_imag * filt_real
    return inverse(jnp.stack([prod_real, prod_imag], 1)) + skip_gain * signal


def rounded(value):
    return value.astype(BF16).astype(F32)


def shifted(values, step):
    zeros = jnp.zeros_like(values[:, : abs(step)])
    if step > 0:
        return jnp.concatenate([zeros, values[:, :-step]], 1)
    return jnp.concatenate([values[:, -step:], zeros], 1)


@functools.lru_cache(maxsize=None)
def dft_tables(length):
    quarter = length // RADIX
    freq = 4 * np.arange(quarter, dtype=np.int64) + 1
    place = np.arange(quarter, dtype=np.int64)
    there, back = [], []
    for offset in range(RADIX):
        turns = freq[:, None] * (RADIX * place + offset)[None, :] % (4 * length)
        angle = turns * (2.0 * np.pi / (4 * length))
        cosine = np.cos(angle).astype(ml_dtypes.bfloat16)
        sine = np.sin(angle).astype(ml_dtypes.bfloat16)
        there.append(np.concatenate([cosine, sine], 0))
        back.append(np.concatenate([cosine.T, sine.T], 1))
    return (np.stack(there), np.stack(back))


def butterfly(values, sign):
    (r0, s0), (r1, s1), (r2, s2), (r3, s3) = values
    sum_r, sum_s, diff_r, diff_s = r0 + r2, s0 + s2, r0 - r2, s0 - s2
    odd_r, odd_s, turn_r, turn_s = r1 + r3, s1 + s3, r1 - r3, s1 - s3
    ahead = (diff_r + turn_s, diff_s - turn_r)
    behind = (diff_r - turn_s, diff_s + turn_r)
    if sign < 0:
        ahead, behind = behind, ahead
    return ((sum_r + odd_r, sum_s + odd_s), ahead, (sum_r - odd_r, sum_s - odd_s), behind)


def transposed(rows):
    count = rows.shape[0]
    if count < LANES:
        rows = jnp.concatenate([rows, jnp.zeros((LANES - count, LANES), F32)], 0)
    return rows.T


def dot(left, right):
    return jnp.dot(left, right, preferred_element_type=F32)


def iota(dims, axis):
    return lax.broadcasted_iota(jnp.int32, dims, axis)


def by_residue():
    row = iota((LANES, LANES), 0)
    part = LANES // RADIX
    source = RADIX * (row % part) + row // part
    return (iota((LANES, LANES), 1) == source).astype(F32)


def hot(ids, vocab):
    lane = iota(ids.shape, 1).astype(F32)
    parts = [
        (ids == lane + float(column * LANES)).astype(F32).astype(BF16)
        for column in range(vocab // LANES)
    ]
    return jnp.concatenate(parts, 1)


def joined(block, kind):
    return 256.0 * block[2 * kind : 2 * kind + 1] + block[2 * kind + 1 : 2 * kind + 2]


def pack_kernel(
    tok_hbm, pos_hbm, put_hbm, cot_hbm, msg_ref, ids_ref, tok_ref, pos_ref, put_ref, cot_ref, sems
):
    dests, rows, share = msg_ref.shape
    tok_rows = cot_hbm.shape[0]
    n_path = cot_hbm.shape[1] // (dests * share)
    path = lax.axis_index("path")
    moves = [(tok_hbm, tok_ref), (pos_hbm, pos_ref), (put_hbm, put_ref)]
    for dest in range(dests):
        lanes = pl.ds(pl.multiple_of((dest * n_path + path) * share, LANES), share)
        moves.append((cot_hbm.at[:, lanes], cot_ref.at[:, pl.ds(dest * share, share)]))
    copies = [
        pltpu.make_async_copy(source, target, sems.at[index])
        for index, (source, target) in enumerate(moves)
    ]
    for copy in copies:
        copy.start()
    order = by_residue().astype(BF16)
    for copy in copies[:3]:
        copy.wait()
    lists = []
    for ref in (tok_ref, pos_ref, put_ref):
        value = ref[...].astype(F32)
        if value.shape[1] < LANES:
            value = jnp.concatenate([value, jnp.zeros((1, LANES - value.shape[1]), F32)], 1)
        high = jnp.floor(value * (1.0 / 256.0))
        lists += [high, value - 256.0 * high]
    lists.append(jnp.zeros((rows - tok_rows - len(lists), LANES), F32))
    ids = jnp.concatenate(lists, 0)
    ids_ref[...] = ids
    turned = lax.dot_general(
        ids.astype(BF16), order, (((1,), (1,)), ((), ())), preferred_element_type=F32
    )
    ids = jnp.where(iota(ids.shape, 0) < 2, turned, ids).astype(BF16)
    for dest in range(dests):
        msg_ref[dest, tok_rows:, :] = ids
    for copy in copies[3:]:
        copy.wait()
    turned = dot(order, cot_ref[...]).astype(BF16)
    for dest in range(dests):
        msg_ref[dest, :tok_rows, :] = turned[:, dest * share : (dest + 1) * share]


def prepare_kernel(
    filt_hbm, table_hbm, embed_hbm, skip_hbm, after_ref,
    spec_hbm, gram_hbm,
    filt_ref, table_ref, embed_ref, skip_ref, sum_ref, spec_ref, gram_ref, sems, out_sems,
):
    length, share = filt_ref.shape
    quarter = length // RADIX
    vocab, width = embed_ref.shape
    pieces = sems.shape[0] - 3
    wide = width // pieces
    path = lax.axis_index("path")
    lanes = pl.ds(pl.multiple_of(path * share, LANES), share)
    moves = [
        (filt_hbm.at[:, lanes], filt_ref),
        (skip_hbm.at[:, lanes], skip_ref),
        (table_hbm, table_ref),
    ]
    for index in range(pieces):
        lanes = pl.ds(index * wide, wide)
        moves.append((embed_hbm.at[:, lanes], embed_ref.at[:, lanes]))
    copies = [
        pltpu.make_async_copy(source, target, sems.at[index])
        for index, (source, target) in enumerate(moves)
    ]
    for copy in copies:
        copy.start()

    copies[0].wait()
    copies[1].wait()
    filt_ref[0:1, :] = filt_ref[0:1, :] + skip_ref[...]
    parts = []
    for offset in range(RADIX):
        value = filt_ref[pl.ds(offset, quarter, stride=RADIX), :] * (1.0 / length)
        high = value.astype(BF16)
        parts.append(jnp.concatenate([high, (value - high.astype(F32)).astype(BF16)], 1))
    copies[2].wait()
    found = []
    for offset in range(RADIX):
        both = dot(table_ref[offset], parts[offset])
        both = both[:, :share] + both[:, share:]
        found.append((both[:quarter], both[quarter:]))
    for part, (real, imag) in enumerate(butterfly(found, -1)):
        spec_ref[2 * part] = real
        spec_ref[2 * part + 1] = imag
    outs = [pltpu.make_async_copy(spec_ref, spec_hbm, out_sems.at[0])]
    outs[0].start()

    sum_ref[vocab // 2 :, : vocab // 2] = jnp.zeros((vocab // 2, vocab // 2), F32)
    for index in range(pieces):
        copies[3 + index].wait()
        part = embed_ref[:, index * wide : (index + 1) * wide]
        for rows, lanes in ((slice(0, vocab // 2), slice(0, vocab)), (slice(vocab // 2, vocab),) * 2):
            found = lax.dot_general(
                part[rows], part[lanes], (((1,), (1,)), ((), ())), preferred_element_type=F32
            )
            if index == 0:
                sum_ref[rows, lanes] = found
            else:
                sum_ref[rows, lanes] += found
    first = (lax.axis_index("ctx") * lax.axis_size("path") + path) * share
    mine = embed_ref[:, pl.ds(pl.multiple_of(first, LANES), share)]
    same = iota((LANES, LANES), 0) == iota((LANES, LANES), 1)
    lane = iota((LANES, LANES), 1)
    below = 3 * vocab
    for block in range(vocab // LANES):
        rows = slice(block * LANES, (block + 1) * LANES)
        value = sum_ref[rows, :]
        norm = jnp.sum(jnp.where(same, value[:, rows], 0.0), 1, keepdims=True)
        inv = jnp.broadcast_to(lax.rsqrt(norm / width + EPS), (LANES, LANES))
        high = inv.astype(BF16).astype(F32)
        inv = jnp.where(lane < LANES // 2, high, inv - high).astype(BF16)
        side, start = block * LANES // (vocab // 2), block * LANES % (vocab // 2)
        into = slice(below + start, below + start + LANES)
        left = side * (share + LANES)
        gram_ref[into, left : left + share] = mine[rows]
        gram_ref[into, left + share : left + share + LANES] = inv
        for part in range(3):
            high = value.astype(BF16)
            into = slice(part * vocab + block * LANES, part * vocab + (block + 1) * LANES)
            gram_ref[into, :] = high
            value = value - high.astype(F32)
            into = pl.ds(part * vocab + block * LANES, LANES)
            sem = out_sems.at[1 + block * 3 + part]
            outs.append(pltpu.make_async_copy(gram_ref.at[into], gram_hbm.at[into], sem))
            outs[-1].start()
    into = pl.ds(below, vocab // 2)
    outs.append(pltpu.make_async_copy(gram_ref.at[into], gram_hbm.at[into], out_sems.at[out_sems.shape[0] - 1]))
    outs[-1].start()
    for copy in outs:
        copy.wait()


def own_kernel(ids_ref, embed_ref, grad_ref, own_ref):
    vocab = embed_ref.shape[0]
    own_width = own_ref.shape[2]
    lanes = pl.ds(pl.multiple_of(lax.axis_index("path") * own_width, LANES), own_width)
    ids = ids_ref[...]
    columns = transposed(jnp.concatenate([joined(ids, kind) for kind in range(3)], 0))
    tok = jnp.broadcast_to(columns[:, 0:1], (LANES, LANES))
    place = jnp.broadcast_to(joined(ids, 1), (LANES, LANES))
    put = jnp.broadcast_to(joined(ids, 2), (LANES, LANES))
    first = lax.axis_index("ctx") * LANES
    subs = LANES // GROUP
    here = (place == (iota((LANES, LANES), 0) + first).astype(F32)) & (iota((LANES, LANES), 1) < subs)
    found = jnp.max(jnp.where(here, put, -1.0), 1, keepdims=True)
    base = jnp.where(found >= 0.0, found, tok)
    hots = jnp.concatenate([hot(tok, vocab), hot(base, vocab)], 0)
    both = dot(hots, embed_ref[:, lanes]).astype(BF16)
    own_ref[0] = both[:LANES]
    own_ref[1] = both[LANES:]


def multiply_rows(found, spec_ref, prod_ref, points, kind):
    _, quarter, share = spec_ref.shape
    for start in range(0, quarter, CHUNK):
        here = slice(start, start + CHUNK)
        after = slice(quarter + start, quarter + start + CHUNK)
        filt = [(spec_ref[2 * part, here, :], spec_ref[2 * part + 1, here, :]) for part in range(RADIX)]
        for point in range(points):
            lanes = slice(point * share, (point + 1) * share)
            values = butterfly([(value[here, lanes], value[after, lanes]) for value in found], -1)
            prods = []
            for (real, imag), (filt_real, filt_imag) in zip(values, filt):
                if kind == 1:
                    prods.append((real * filt_real + imag * filt_imag, imag * filt_real - real * filt_imag))
                else:
                    prods.append((real * filt_real - imag * filt_imag, imag * filt_real + real * filt_imag))
            lanes = slice((kind * points + point) * share, (kind * points + point + 1) * share)
            for part, (real, imag) in enumerate(butterfly(prods, 1)):
                prod_ref[part, here, lanes] = real.astype(BF16)
                prod_ref[part, after, lanes] = imag.astype(BF16)


def ids_kernel(vocab, msg_ref, hot_ref, subs_ref, put_ref):
    length = hot_ref.shape[0]
    quarter = length // RADIX
    n_ctx = msg_ref.shape[0]
    block_part = LANES // RADIX
    per_block = LANES // GROUP
    subs = n_ctx * per_block
    blocks = [msg_ref[block, LANES:, :].astype(F32) for block in range(n_ctx)]
    toks = transposed(jnp.concatenate([joined(block, 0) for block in blocks], 0))
    spread = sum(
        blocks[block] if block == 0 else pltpu.roll(blocks[block], block * per_block, 1)
        for block in range(n_ctx)
    )
    place = joined(spread, 1)
    put = joined(spread, 2)
    back = jnp.floor(place * (1.0 / RADIX))
    place = back + (place - RADIX * back) * quarter
    columns = transposed(jnp.concatenate([place, put], 0))
    for block in range(n_ctx):
        column = jnp.broadcast_to(toks[:, block : block + 1], (LANES, LANES))
        rows = hot(column, vocab)
        for side in range(RADIX):
            first = side * quarter + block * block_part
            hot_ref[first : first + block_part, :] = rows[side * block_part : (side + 1) * block_part]
    subs_ref[subs:, :] = hot(jnp.broadcast_to(columns[:, 1:2], (subs, LANES)), vocab)
    pick = jnp.concatenate(
        [
            (columns[:, 0:1] == (iota((subs, LANES), 1) + part * LANES).astype(F32)).astype(F32).astype(BF16)
            for part in range(length // LANES)
        ],
        1,
    )
    for index in range(length // LANES):
        row = (iota((LANES, subs), 0) + index * LANES).astype(F32)
        here = (row == place[:, :subs]).astype(F32).astype(BF16)
        put_ref[index * LANES : (index + 1) * LANES, :] = jnp.concatenate([here, here], 1)
    subs_ref[:subs, :] = dot(pick, hot_ref[...]).astype(BF16)


def feature_kernel(
    points, msg_ref, hot_ref, subs_hot_ref, put_ref, gram_ref, taps_ref, gain_ref, embed_hbm,
    signal_ref, k_ref, v_ref, inv_ref, pair_ref,
    embed_ref, sums_ref, found_ref, look_ref, subs_ref, sem,
):
    length = signal_ref.shape[0]
    quarter = length // RADIX
    vocab, width = embed_hbm.shape
    share = pair_ref.shape[2]
    subs = subs_hot_ref.shape[0] // 2
    first = (lax.axis_index("ctx") * points + lax.axis_index("path")) * share
    first = pl.multiple_of(first, LANES)
    below = 3 * vocab
    table = jnp.concatenate(
        [gram_ref[below:, : share + LANES], gram_ref[below:, share + LANES :]], 0
    )

    for index in range(length // LOOK_ROWS):
        rows = pl.ds(index * LOOK_ROWS, LOOK_ROWS)
        look_ref[rows, :] = dot(hot_ref[rows, :], table)

    alphas = [(point + 0.5) / points for point in range(points)]
    hots = subs_hot_ref[...]
    found = dot(jnp.concatenate([hots] * 3, 1), gram_ref[:below, :])
    hot_tok32, hot_base32 = hots[:subs].astype(F32), hots[subs:].astype(F32)
    tok_tok = jnp.sum(found[:subs] * hot_tok32, 1, keepdims=True)
    tok_base = jnp.sum(found[:subs] * hot_base32, 1, keepdims=True)
    base_tok = jnp.sum(found[subs:] * hot_tok32, 1, keepdims=True)
    tok_base = jnp.where(tok_base == 0.0, base_tok, tok_base)
    base_base = jnp.sum(found[subs:] * hot_base32, 1, keepdims=True)
    cancels = jnp.zeros((subs, 1), F32)
    for point in range(points):
        alpha = alphas[point]
        terms = (1.0 - alpha) ** 2 * base_base + alpha**2 * tok_tok
        total = terms + 2.0 * alpha * (1.0 - alpha) * tok_base
        cancels = jnp.maximum(cancels, (total < CANCEL * terms).astype(F32))
        inv = lax.rsqrt(jnp.maximum(total, 0.0) / width + EPS)
        sums_ref[point] = jnp.broadcast_to(inv, (subs, LANES))

    @pl.when(jnp.max(cancels) > 0.5)
    def _():
        sums_ref[...] = jnp.zeros_like(sums_ref)
        wide = found_ref.shape[1]

        @pl.loop(0, width // wide)
        def _(step):
            lanes = pl.ds(pl.multiple_of(step * wide, wide), wide)
            copy = pltpu.make_async_copy(embed_hbm.at[:, lanes], embed_ref, sem)
            copy.start()
            copy.wait()
            found_ref[...] = dot(hots, embed_ref[...])
            for block in range(subs // GROUP):
                rows = slice(block * GROUP, (block + 1) * GROUP)
                sums = [sums_ref[point, rows, :] for point in range(points)]
                for column in range(wide // LANES):
                    cut = slice(column * LANES, (column + 1) * LANES)
                    base = found_ref[subs + block * GROUP : subs + (block + 1) * GROUP, cut]
                    diff = found_ref[rows, cut] - base
                    for point in range(points):
                        value = base + alphas[point] * diff
                        sums[point] = sums[point] + value * value
                for point in range(points):
                    sums_ref[point, rows, :] = sums[point]

        for point in range(points):
            mean = jnp.sum(sums_ref[point], 1, keepdims=True) / width
            sums_ref[point] = jnp.broadcast_to(lax.rsqrt(mean + EPS), (subs, LANES))

    high = [dot(hots[subs:], table[:, :share]), jnp.ones((subs, LANES), F32)]
    low = [jnp.zeros((subs, LANES), F32)] * 2
    for point in range(points):
        inv = sums_ref[point]
        high.append(inv.astype(BF16).astype(F32))
        low.append(inv - high[-1])
    held = jnp.concatenate([jnp.concatenate(high, 1), jnp.concatenate(low, 1)], 0).astype(BF16)
    for index in range(length // LOOK_ROWS):
        rows = pl.ds(index * LOOK_ROWS, LOOK_ROWS)
        subs_ref[rows, :] = dot(put_ref[rows, :], held)

    cols = points * share
    block_part = LANES // RADIX
    last = {side: [jnp.zeros((GROUP, share), F32)] * points for side in (RADIX - 2, RADIX - 1)}
    gain = gain_ref[:, pl.ds(first, share)]
    taps = [taps_ref[f, :, pl.ds(first, share)].astype(F32) for f in range(3)]
    taps = [[taps[f][tap : tap + 1] for tap in range(3)] for f in range(3)]

    for start in range(0, quarter, CHUNK):
        block, inside = start // block_part, start % block_part
        sides = []
        for side in range(RADIX):
            rows = pl.ds(side * quarter + start, CHUNK)
            tok = look_ref[rows, :share]
            inv = look_ref[rows, share:]
            inv = inv + pltpu.roll(inv, LANES // 2, 1)
            chosen = subs_ref[rows, share : 2 * share] > 0.5
            base = jnp.where(chosen, subs_ref[rows, :share], tok)
            pair_ref[0, rows, :] = tok.astype(BF16)
            pair_ref[1, rows, :] = base.astype(BF16)
            sent = pl.ds(side * block_part + inside, CHUNK)
            upstream = msg_ref[block, sent, :].astype(F32)
            sides.append((rows, gain * base, gain * (tok - base), inv, chosen, upstream))
        for point in range(points):
            lanes = slice(point * share, (point + 1) * share)
            recent = []
            for rows, base, diff, inv_tok, chosen, _ in sides:
                inv = jnp.where(
                    chosen, subs_ref[rows, (2 + point) * share : (3 + point) * share], inv_tok
                )
                inv_ref[rows, lanes] = inv
                recent.append(rounded((base + alphas[point] * diff) * inv))
            backs = []
            for side in (RADIX - 2, RADIX - 1):
                window = jnp.concatenate([last[side][point], recent[side]], 0)
                last[side][point] = recent[side][CHUNK - GROUP :]
                backs.append(window[GROUP - 1 : GROUP - 1 + CHUNK])
            recent = backs + recent
            for side in range(RADIX):
                rows, upstream = sides[side][0], sides[side][5]
                feats = [sum(taps[f][tap] * recent[side + 2 - tap] for tap in range(3)) for f in range(3)]
                k_ref[rows, lanes] = feats[1]
                v_ref[rows, lanes] = feats[2]
                signal_ref[rows, lanes] = (feats[1] * feats[2]).astype(BF16)
                after = slice(cols + point * share, cols + (point + 1) * share)
                signal_ref[rows, after] = (upstream * feats[0]).astype(BF16)


def gradient_kernel(
    points, width, msg_ref, pair_ref, taps_ref, gain_ref,
    signal_ref, k_ref, v_ref, inv_ref, table_ref, back_ref, spec_ref,
    grad_ref,
    prod_ref,
):
    _, quarter, share = spec_ref.shape
    cols = points * share
    n_ctx = msg_ref.shape[0]
    block_part = LANES // RADIX
    first = (lax.axis_index("ctx") * points + lax.axis_index("path")) * share
    first = pl.multiple_of(first, LANES)
    gain = gain_ref[:, pl.ds(first, share)]
    taps = [taps_ref[f, :, pl.ds(first, share)].astype(F32) for f in range(3)]
    taps = [[taps[f][tap : tap + 1] for tap in range(3)] for f in range(3)]

    found = []
    for kind in range(2):
        signal = slice(kind * cols, (kind + 1) * cols)
        spectra = [
            dot(table_ref[side], signal_ref[side * quarter : (side + 1) * quarter, signal])
            for side in range(RADIX)
        ]
        multiply_rows(spectra, spec_ref, prod_ref, points, kind)
    for kind in range(2):
        signal = slice(kind * cols, (kind + 1) * cols)
        found.append([dot(back_ref[side], prod_ref[side, :, signal]) for side in range(RADIX)])

    carried = [[jnp.zeros((GROUP, share), F32)] * points for _ in range(3)]
    lane, row = iota((GROUP, LANES), 1), iota((GROUP, LANES), 0)
    for start in reversed(range(0, quarter, CHUNK)):
        block, inside = start // block_part, start % block_part
        if inside + CHUNK == block_part:
            means = [jnp.zeros((GROUP, LANES), F32)] * 2
        kept = [{} for _ in range(RADIX)]
        for offset in reversed(range(0, CHUNK, GROUP)):
            here = slice(start + offset, start + offset + GROUP)
            sides = []
            for side in range(RADIX):
                rows = slice(side * quarter + start + offset, side * quarter + start + offset + GROUP)
                sent = pl.ds(side * block_part + inside, CHUNK)
                upstream = msg_ref[block, sent, :].astype(F32)[offset : offset + GROUP]
                sides.append([rows, upstream] + [jnp.zeros((GROUP, share), F32)] * 4)
            for point in reversed(range(points)):
                lanes = slice(point * share, (point + 1) * share)
                by_tap = []
                for side in range(RADIX):
                    rows, upstream = sides[side][:2]
                    grad_z = found[1][side][here, lanes]
                    grads = (
                        upstream * found[0][side][here, lanes],
                        grad_z * v_ref[rows, lanes],
                        grad_z * k_ref[rows, lanes],
                    )
                    by_tap.append([sum(taps[f][tap] * grads[f] for f in range(3)) for tap in range(3)])
                ahead = []
                for slot, value in enumerate((by_tap[0][1], by_tap[0][2], by_tap[1][2])):
                    window = jnp.concatenate([value, carried[slot][point]], 0)
                    carried[slot][point] = value
                    ahead.append(window[1 : 1 + GROUP])
                by_tap += [[None, ahead[0], ahead[1]], [None, None, ahead[2]]]
                for side in range(RADIX):
                    rows, _, total, sum0, sum1, sum2 = sides[side]
                    inv = inv_ref[rows, lanes]
                    along = inv * (by_tap[side][0] + by_tap[side + 1][1] + by_tap[side + 2][2])
                    total = total + along
                    sum0 = sum0 + along * (inv * inv)
                    sum1 = sum1 + sum0
                    sides[side][2:] = [total, sum0, sum1, sum2 + sum1]
            for side in range(RADIX):
                _, _, total, sum0, sum1, sum2 = sides[side]
                rows = pl.ds(side * quarter + start, CHUNK)
                base = pair_ref[1, rows, :].astype(F32)[offset : offset + GROUP]
                diff = pair_ref[0, rows, :].astype(F32)[offset : offset + GROUP] - base
                once = (sum1 - 0.5 * sum0) * (1.0 / points)
                twice = (2.0 * (sum2 - sum1) + 0.25 * sum0) * (1.0 / points**2)
                to_tok = base * once + diff * twice
                to_base = base * sum0 + diff * once - to_tok
                kept[side][offset] = gain * total
                for kind, value in enumerate((gain * to_tok, gain * to_base)):
                    value = jnp.sum(value, 1, keepdims=True)
                    at = lane == row + (side * block_part + inside + offset)
                    means[kind] = means[kind] + jnp.where(at, value, 0.0)
        for side in range(RADIX):
            total = jnp.concatenate([kept[side][offset] for offset in range(0, CHUNK, GROUP)], 0)
            grad_ref[block, pl.ds(side * block_part + inside, CHUNK), :] = total.astype(BF16)
        if inside == 0:
            sent = []
            for value in means:
                value = jnp.sum(value, 0, keepdims=True) / width
                high = value.astype(BF16).astype(F32)
                sent += [high, value - high]
            sent.append(jnp.zeros((grad_ref.shape[1] - LANES - len(sent), LANES), F32))
            grad_ref[block, LANES:, :] = jnp.concatenate(sent, 0).astype(BF16)


def partial_kernel(grad_ref, *out_refs):
    rows, _ = out_refs[0].shape
    n_ctx = grad_ref.shape[0]
    each = n_ctx // len(out_refs)
    spare = sum(grad_ref[block, LANES:, :].astype(F32) for block in range(n_ctx))
    sums = [spare[0:1] + spare[1:2], spare[2:3] + spare[3:4]]
    sent = []
    for value in sums:
        high = value.astype(BF16).astype(F32)
        sent += [high, value - high]
    sent.append(jnp.zeros((rows - each * LANES - len(sent), LANES), F32))
    sent = jnp.concatenate(sent, 0).astype(BF16)
    path = lax.axis_index("path")
    for step, ref in enumerate(out_refs):
        dest = path ^ step
        for piece in range(each):
            ref[piece * LANES : (piece + 1) * LANES, :] = grad_ref[dest * each + piece, :LANES, :]
        ref[each * LANES :, :] = sent


def finish_kernel(own_ref, *refs):
    grad_refs, (path_hbm, attr_hbm, path_ref, attr_ref, sems) = refs[:-5], refs[-5:]
    points = len(grad_refs)
    rows, share = grad_refs[0].shape
    pieces = rows // LANES
    spare = sum(ref[pieces * LANES :, :].astype(F32) for ref in grad_refs)
    lane = iota((LANES, LANES), 1)
    part = LANES // RADIX
    order = (iota((LANES, LANES), 0) == RADIX * (lane % part) + lane // part).astype(F32).astype(BF16)
    left, split = jnp.concatenate([spare[0:1] + spare[1:2], spare[2:3] + spare[3:4]], 0), []
    for _ in range(3):
        split.append(left.astype(BF16).astype(F32))
        left = left - split[-1]
    split = jnp.concatenate(split + [jnp.zeros((2, LANES), F32)], 0).astype(BF16)
    columns = lax.dot_general(order, split, (((1,), (1,)), ((), ())), preferred_element_type=F32)
    to_tok = columns[:, 0:1] + columns[:, 2:3] + columns[:, 4:5]
    to_base = columns[:, 1:2] + columns[:, 3:4] + columns[:, 5:6]
    path = lax.axis_index("path")
    copies = []
    for step, ref in enumerate(grad_refs):
        for piece in range(pieces):
            slot = step * pieces + piece
            first = (piece * points + (path ^ step)) * share
            lanes = pl.ds(pl.multiple_of(first, LANES), share)
            tok = own_ref[0, :, lanes].astype(F32)
            base = own_ref[1, :, lanes].astype(F32)
            grad = dot(order, ref[piece * LANES : (piece + 1) * LANES, :])
            grad = (grad - tok * to_tok - base * to_base) / points
            path_ref[slot] = grad
            attr_ref[slot] = (tok - base) * grad
            for kind, (source, target) in enumerate(((path_ref, path_hbm), (attr_ref, attr_hbm))):
                copies.append(
                    pltpu.make_async_copy(source.at[slot], target.at[:, lanes], sems.at[kind, slot])
                )
                copies[-1].start()
    for copy in copies:
        copy.wait()


def any_spec():
    return pl.BlockSpec(memory_space=pl.ANY)


def vmem_spec():
    return pl.BlockSpec(memory_space=pltpu.VMEM)


def hbm_spec():
    return pl.BlockSpec(memory_space=pltpu.HBM)


def call(kernel, ins, outs, scratch, flops, moved, mebibytes):
    return pl.pallas_call(
        kernel,
        in_specs=ins,
        out_specs=[spec for spec, _ in outs],
        out_shape=[shape for _, shape in outs],
        scratch_shapes=scratch,
        compiler_params=pltpu.CompilerParams(vmem_limit_bytes=mebibytes * 2**20),
        cost_estimate=pl.CostEstimate(flops=flops, bytes_accessed=moved, transcendentals=0),
    )


def shape(dims, dtype):
    return jax.ShapeDtypeStruct(dims, dtype)


def kernel_body(tokens, sub_pos, sub_base, embed, norm_gain, fir_taps, long_filter, skip_gain, cotangent):
    n_path, n_ctx = lax.axis_size("path"), lax.axis_size("ctx")
    points = n_path
    tok_rows = tokens.shape[0]
    length = tok_rows * n_ctx
    vocab, width = embed.shape
    share = width // (n_path * n_ctx)
    subs = sub_pos.shape[0] * n_ctx
    own_width = width // n_path
    cols = points * share
    quarter = length // RADIX
    tables = dft_tables(length)
    dma = pltpu.SemaphoreType.DMA
    transform_flops = length * length
    spare = 8

    msg, ids = call(
        pack_kernel,
        [hbm_spec()] * 4,
        [
            (vmem_spec(), shape((n_ctx, tok_rows + spare, share), BF16)),
            (vmem_spec(), shape((spare, LANES), F32)),
        ],
        [
            pltpu.VMEM((1, tok_rows), jnp.int32),
            pltpu.VMEM((1, sub_pos.shape[0]), jnp.int32),
            pltpu.VMEM((1, sub_pos.shape[0]), jnp.int32),
            pltpu.VMEM((tok_rows, n_ctx * share), BF16),
            dma((n_ctx + 3,)),
        ],
        length * share,
        8 * length * share,
        60,
    )(
        tokens.reshape(1, tok_rows),
        sub_pos.reshape(1, -1),
        sub_base.reshape(1, -1),
        cotangent,
    )
    msg = lax.all_to_all(msg, "ctx", 0, 0, tiled=True)

    gain = norm_gain.reshape(1, width)
    skip = skip_gain.reshape(1, n_path * share)
    spec, gram = call(
        prepare_kernel,
        [hbm_spec()] * 4 + [any_spec()],
        [
            (any_spec(), shape((2 * RADIX, quarter, share), F32)),
            (any_spec(), shape((3 * vocab + vocab // 2, vocab), BF16)),
        ],
        [
            pltpu.VMEM((length, share), F32),
            pltpu.VMEM((RADIX, 2 * quarter, quarter), BF16),
            pltpu.VMEM((vocab, width), BF16),
            pltpu.VMEM((1, share), F32),
            pltpu.VMEM((vocab, vocab), F32),
            pltpu.VMEM((2 * RADIX, quarter, share), F32),
            pltpu.VMEM((3 * vocab + vocab // 2, vocab), BF16),
            dma((7,)),
            dma((3 * vocab // LANES + 2,)),
        ],
        2 * vocab * vocab * width,
        2 * vocab * width,
        58,
    )(long_filter, tables[0], embed, skip, ids)

    hots, subs_hots, put_hots = call(
        functools.partial(ids_kernel, vocab),
        [vmem_spec()],
        [
            (vmem_spec(), shape((length, vocab), BF16)),
            (vmem_spec(), shape((2 * subs, vocab), BF16)),
            (vmem_spec(), shape((length, 2 * subs), BF16)),
        ],
        [],
        2 * 10**9,
        4 * 10**6,
        8,
    )(msg)
    wide = 4 * LANES
    signal, k_feat, v_feat, inv, pair = call(
        functools.partial(feature_kernel, points),
        [vmem_spec()] * 7 + [hbm_spec()],
        [(vmem_spec(), shape((length, 2 * cols), BF16))]
        + [(vmem_spec(), shape((length, cols), F32))] * 3
        + [(vmem_spec(), shape((2, length, share), BF16))],
        [
            pltpu.VMEM((vocab, wide), BF16),
            pltpu.VMEM((points, subs, LANES), F32),
            pltpu.VMEM((2 * subs, wide), F32),
            pltpu.VMEM((length, 2 * share), F32),
            pltpu.VMEM((length, (2 + points) * share), F32),
            dma,
        ],
        2 * length * vocab * 3 * share,
        2 * vocab * width + 16 * length * cols,
        39,
    )(msg, hots, subs_hots, put_hots, gram, fir_taps, gain, embed)

    grad = call(
        functools.partial(gradient_kernel, points, width),
        [vmem_spec()] * 11,
        [(vmem_spec(), shape((n_ctx, tok_rows + spare, share), BF16))],
        [
            pltpu.VMEM((RADIX, 2 * quarter, 2 * cols), BF16),
        ],
        4 * transform_flops * cols,
        4 * length * length + 16 * length * cols,
        32,
    )(msg, pair, fir_taps, gain, signal, k_feat, v_feat, inv, *tables, spec)[0]

    own = call(
        own_kernel,
        [vmem_spec(), vmem_spec(), any_spec()],
        [(vmem_spec(), shape((2, tok_rows, own_width), BF16))],
        [],
        4 * tok_rows * vocab * own_width,
        2 * vocab * own_width,
        10,
    )(ids, embed, grad)[0]
    grad = lax.all_to_all(grad, "ctx", 0, 0, tiled=True)
    each = n_ctx // n_path
    parts = call(
        partial_kernel,
        [vmem_spec()],
        [(vmem_spec(), shape((each * tok_rows + spare, share), BF16))] * n_path,
        [],
        spare * LANES * n_ctx,
        4 * length * share,
        4,
    )(grad)
    parts = [
        part if step == 0 else lax.ppermute(part, "path", [(p, p ^ step) for p in range(n_path)])
        for step, part in enumerate(parts)
    ]
    out = shape((tok_rows, own_width), F32)
    return tuple(
        call(
            finish_kernel,
            [vmem_spec()] * (1 + n_path),
            [(any_spec(), out), (any_spec(), out)],
            [pltpu.VMEM((n_path * each, tok_rows, share), F32)] * 2 + [dma((2, n_path * each))],
            8 * tok_rows * own_width,
            14 * tok_rows * own_width,
            8,
        )(own, *parts)
    )


def plain_body(tokens, sub_pos, sub_base, embed, norm_gain, fir_taps, long_filter, skip_gain, cotangent):
    n_path, n_ctx = lax.axis_size("path"), lax.axis_size("ctx")
    path, ctx = lax.axis_index("path"), lax.axis_index("ctx")
    points = n_path
    tok_rows = tokens.shape[0]
    length = tok_rows * n_ctx
    width = embed.shape[1]
    share = width // (n_path * n_ctx)
    own_width = width // n_path
    first = (ctx * n_path + path) * share
    alphas = ((jnp.arange(points, dtype=jnp.int32)).astype(F32) + 0.5) / points
    alphas = alphas[:, None, None]

    local = jnp.arange(tok_rows, dtype=jnp.int32)[:, None] + ctx * tok_rows == sub_pos[None, :]
    put = jnp.sum(jnp.where(local, sub_base[None, :], 0), 1)
    base_ids = jnp.where(jnp.any(local, 1), put, tokens)
    rows_tok = jnp.take(embed, tokens, axis=0).astype(F32)
    rows_base = jnp.take(embed, base_ids, axis=0).astype(F32)
    rows_in = rows_base[None] + alphas * (rows_tok - rows_base)[None]
    inv = lax.rsqrt(jnp.mean(rows_in * rows_in, -1) + EPS)
    inv = lax.all_gather(inv, "ctx", axis=1, tiled=True)[:, :, None]
    all_tok = lax.all_gather(tokens, "ctx", tiled=True)
    all_base = lax.all_gather(base_ids, "ctx", tiled=True)

    cot = cotangent.reshape(tok_rows, n_ctx, n_path, share)
    cot = lax.dynamic_index_in_dim(cot, path, 2, keepdims=False)
    cot = lax.all_to_all(cot.transpose(1, 0, 2), "ctx", 0, 0, tiled=True)
    upstream = cot.reshape(1, length, share).astype(F32)
    mine = lax.dynamic_slice_in_dim(embed, first, share, 1)
    gain = lax.dynamic_slice_in_dim(norm_gain, first, share, 0)
    taps = lax.dynamic_slice_in_dim(fir_taps, first, share, 2).astype(F32)
    filt = lax.dynamic_slice_in_dim(long_filter, path * share, share, 1)
    skip = lax.dynamic_slice_in_dim(skip_gain, path * share, share, 0)

    emb_tok = jnp.take(mine, all_tok, axis=0).astype(F32)
    emb_base = jnp.take(mine, all_base, axis=0).astype(F32)
    inputs = emb_base[None] + alphas * (emb_tok - emb_base)[None]
    normed = rounded(inputs * inv * gain)
    q_feat, k_feat, v_feat = (
        taps[f, 0] * normed + taps[f, 1] * shifted(normed, 1) + taps[f, 2] * shifted(normed, 2)
        for f in range(3)
    )
    filter_spec = spectrum(filt[None])
    conv = rounded(long_conv(rounded(k_feat * v_feat), filter_spec, skip, False))
    grad_z = rounded(long_conv(rounded(upstream * q_feat), filter_spec, skip, True))
    grads = (rounded(upstream * conv), rounded(grad_z * v_feat), rounded(grad_z * k_feat))
    by_tap = [sum(taps[f, tap] * grads[f] for f in range(3)) for tap in range(3)]
    scaled = gain * (by_tap[0] + shifted(by_tap[1], -1) + shifted(by_tap[2], -2))
    grad = jnp.sum(inv * scaled, 0).astype(BF16)
    along = jnp.sum(inputs * scaled, -1, keepdims=True) * inv**3 / width
    part = jnp.stack([jnp.sum(alphas * along, 0)[:, 0], jnp.sum((1.0 - alphas) * along, 0)[:, 0]])
    part = lax.psum(part, ("path", "ctx"))
    part = lax.dynamic_slice_in_dim(part, ctx * tok_rows, tok_rows, 1)

    back = lax.all_to_all(grad.reshape(n_ctx, tok_rows, share), "ctx", 0, 0, tiled=True)
    back = back.reshape(n_path, n_ctx // n_path, tok_rows, share)
    back = lax.all_to_all(back, "path", 0, 0, tiled=True).astype(F32)
    back = back.transpose(2, 1, 0, 3).reshape(tok_rows, own_width)
    own_tok = lax.dynamic_slice_in_dim(rows_tok, path * own_width, own_width, 1)
    own_base = lax.dynamic_slice_in_dim(rows_base, path * own_width, own_width, 1)
    grad = (back - own_tok * part[0][:, None] - own_base * part[1][:, None]) / points
    return (grad, (own_tok - own_base) * grad)


def body(tokens, sub_pos, sub_base, embed, *rest):
    n_path, n_ctx = lax.axis_size("path"), lax.axis_size("ctx")
    tok_rows = tokens.shape[0]
    share = embed.shape[1] // (n_path * n_ctx)
    tables = 2 * (tok_rows * n_ctx) ** 2
    fits = share == LANES and tok_rows == LANES and n_ctx == GROUP and tables <= TABLE_BYTES
    fits = fits and n_ctx % n_path == 0 and n_path & (n_path - 1) == 0
    chosen = kernel_body if fits else plain_body
    return chosen(tokens, sub_pos, sub_base, embed, *rest)


def solution(mesh):
    return jax.shard_map(
        body,
        mesh=mesh,
        in_specs=(
            P("ctx"),
            P("ctx"),
            P("ctx"),
            P(),
            P(),
            P(),
            P(None, "ctx"),
            P("ctx"),
            P("ctx", None),
        ),
        out_specs=(P("ctx", "path"), P("ctx", "path")),
        check_vma=False,
    )
```

```python
import functools

import jax
import jax.numpy as jnp
import ml_dtypes
import numpy as np
from jax import lax
from jax.experimental import pallas as pl
from jax.experimental.pallas import tpu as pltpu
from jax.sharding import PartitionSpec as P

LANES = 128
GROUP = 8
RADIX = 4
LOOK_ROWS = 256
CHUNK = 16
EPS = 1e-06
CANCEL = 0.004
TABLE_BYTES = 2**21
F32 = jnp.float32
BF16 = jnp.bfloat16
precise = lax.Precision.HIGH


def angle_tables(length):
    outer_size = 64
    inner_size = length // outer_size
    outer_idx = jnp.arange(outer_size, dtype=jnp.int32)
    inner_idx = jnp.arange(inner_size, dtype=jnp.int32)
    outer_angle = (
        2.0 * jnp.pi / outer_size
        * (outer_idx[:, None] * outer_idx[None, :] % outer_size).astype(F32)
    )
    inner_angle = (
        2.0 * jnp.pi / inner_size
        * (inner_idx[:, None] * inner_idx[None, :] % inner_size).astype(F32)
    )
    twist_angle = (
        2.0 * jnp.pi / length
        * (outer_idx[:, None] * inner_idx[None, :] % length).astype(F32)
    )
    return (outer_angle, inner_angle, twist_angle)


def complex_table(angle, sign):
    cosine = jnp.cos(angle)
    sine = sign * jnp.sin(angle)
    return jnp.stack([jnp.stack([cosine, sine]), jnp.stack([-sine, cosine])])


def twisted(values, angle, sign):
    cosine = jnp.cos(angle)[None, :, :, None]
    sine = sign * jnp.sin(angle)[None, :, :, None]
    real_part = values[:, 0]
    imag_part = values[:, 1]
    return jnp.stack(
        [real_part * cosine - imag_part * sine, real_part * sine + imag_part * cosine], 1
    )


def spectrum(signal):
    batch, half, width = signal.shape
    length = 2 * half
    outer_angle, inner_angle, twist_angle = angle_tables(length)
    outer_size = outer_angle.shape[0]
    inner_size = inner_angle.shape[0]
    folded = signal.reshape(batch, outer_size // 2, inner_size, width)
    used = outer_angle[:, : outer_size // 2]
    outer_table = jnp.stack([jnp.cos(used), -jnp.sin(used)])
    first = jnp.einsum("rka,pabc->prkbc", outer_table, folded, precision=precise)
    turned = twisted(first, twist_angle, -1.0)
    return jnp.einsum(
        "prkbc,rsbm->pskmc", turned, complex_table(inner_angle, -1.0), precision=precise
    )


def inverse(spec):
    batch, parts, outer_size, inner_size, width = spec.shape
    length = outer_size * inner_size
    outer_angle, inner_angle, twist_angle = angle_tables(length)
    back = jnp.einsum("pskmc,stmb->ptkbc", spec, complex_table(inner_angle, 1.0), precision=precise)
    turned = twisted(back, twist_angle, 1.0)
    used = outer_angle[: outer_size // 2]
    outer_table = jnp.stack([jnp.cos(used), -jnp.sin(used)])
    result = jnp.einsum("rak,prkbc->pabc", outer_table, turned, precision=precise)
    return (result / length).reshape(batch, length // 2, width)


def long_conv(signal, filter_spec, skip_gain, adjoint):
    spec = spectrum(signal)
    sig_real = spec[:, 0]
    sig_imag = spec[:, 1]
    filt_real = filter_spec[:, 0]
    filt_imag = filter_spec[:, 1]
    if adjoint:
        prod_real = sig_real * filt_real + sig_imag * filt_imag
        prod_imag = sig_imag * filt_real - sig_real * filt_imag
    else:
        prod_real = sig_real * filt_real - sig_imag * filt_imag
        prod_imag = sig_real * filt_imag + sig_imag * filt_real
    return inverse(jnp.stack([prod_real, prod_imag], 1)) + skip_gain * signal


def rounded(value):
    return value.astype(BF16).astype(F32)


def shifted(values, step):
    zeros = jnp.zeros_like(values[:, : abs(step)])
    if step > 0:
        return jnp.concatenate([zeros, values[:, :-step]], 1)
    return jnp.concatenate([values[:, -step:], zeros], 1)


@functools.lru_cache(maxsize=None)
def dft_tables(length):
    quarter = length // RADIX
    freq = 4 * np.arange(quarter, dtype=np.int64) + 1
    place = np.arange(quarter, dtype=np.int64)
    there, back = [], []
    for offset in range(RADIX):
        turns = freq[:, None] * (RADIX * place + offset)[None, :] % (4 * length)
        angle = turns * (2.0 * np.pi / (4 * length))
        cosine = np.cos(angle).astype(ml_dtypes.bfloat16)
        sine = np.sin(angle).astype(ml_dtypes.bfloat16)
        there.append(np.concatenate([cosine, sine], 0))
        back.append(np.concatenate([cosine.T, sine.T], 1))
    return (np.stack(there), np.stack(back))


def butterfly(values, sign):
    (r0, s0), (r1, s1), (r2, s2), (r3, s3) = values
    sum_r, sum_s, diff_r, diff_s = r0 + r2, s0 + s2, r0 - r2, s0 - s2
    odd_r, odd_s, turn_r, turn_s = r1 + r3, s1 + s3, r1 - r3, s1 - s3
    ahead = (diff_r + turn_s, diff_s - turn_r)
    behind = (diff_r - turn_s, diff_s + turn_r)
    if sign < 0:
        ahead, behind = behind, ahead
    return ((sum_r + odd_r, sum_s + odd_s), ahead, (sum_r - odd_r, sum_s - odd_s), behind)


def transposed(rows):
    count = rows.shape[0]
    if count < LANES:
        rows = jnp.concatenate([rows, jnp.zeros((LANES - count, LANES), F32)], 0)
    return rows.T


def dot(left, right):
    return jnp.dot(left, right, preferred_element_type=F32)


def iota(dims, axis):
    return lax.broadcasted_iota(jnp.int32, dims, axis)


def by_residue():
    row = iota((LANES, LANES), 0)
    part = LANES // RADIX
    source = RADIX * (row % part) + row // part
    return (iota((LANES, LANES), 1) == source).astype(F32)


def hot(ids, vocab):
    lane = iota(ids.shape, 1).astype(F32)
    parts = [
        (ids == lane + float(column * LANES)).astype(F32).astype(BF16)
        for column in range(vocab // LANES)
    ]
    return jnp.concatenate(parts, 1)


def joined(block, kind):
    return 256.0 * block[2 * kind : 2 * kind + 1] + block[2 * kind + 1 : 2 * kind + 2]


def pack_kernel(
    tok_hbm, pos_hbm, put_hbm, cot_hbm, msg_hbm, ids_ref, tok_ref, pos_ref, put_ref, sent_ref, sems
):
    dests, _, share = msg_hbm.shape
    tok_rows = cot_hbm.shape[0]
    n_path = cot_hbm.shape[1] // (dests * share)
    path = lax.axis_index("path")
    moves = [(tok_hbm, tok_ref), (pos_hbm, pos_ref), (put_hbm, put_ref)]
    for dest in range(dests):
        lanes = pl.ds(pl.multiple_of((dest * n_path + path) * share, LANES), share)
        moves.append((cot_hbm.at[:, lanes], msg_hbm.at[dest, pl.ds(0, tok_rows)]))
    for dest in range(dests):
        moves.append((sent_ref, msg_hbm.at[dest, pl.ds(tok_rows, sent_ref.shape[0])]))
    copies = [
        pltpu.make_async_copy(source, target, sems.at[index])
        for index, (source, target) in enumerate(moves)
    ]
    for copy in copies[: 3 + dests]:
        copy.start()
    for copy in copies[:3]:
        copy.wait()
    lists = []
    for ref in (tok_ref, pos_ref, put_ref):
        value = ref[...].astype(F32)
        if value.shape[1] < LANES:
            value = jnp.concatenate([value, jnp.zeros((1, LANES - value.shape[1]), F32)], 1)
        high = jnp.floor(value * (1.0 / 256.0))
        lists += [high, value - 256.0 * high]
    lists.append(jnp.zeros((ids_ref.shape[0] - len(lists), LANES), F32))
    ids = jnp.concatenate(lists, 0)
    ids_ref[...] = ids
    sent_ref[...] = ids.astype(BF16)
    for copy in copies[3 + dests :]:
        copy.start()
    for copy in copies[3:]:
        copy.wait()


def prepare_kernel(
    filt_hbm, table_hbm, embed_hbm, skip_hbm, after_ref,
    spec_hbm, gram_hbm,
    filt_ref, table_ref, embed_ref, skip_ref, sum_ref, spec_ref, gram_ref, sems, out_sems,
):
    length, share = filt_ref.shape
    quarter = length // RADIX
    vocab, width = embed_ref.shape
    pieces = sems.shape[0] - 3
    wide = width // pieces
    path = lax.axis_index("path")
    lanes = pl.ds(pl.multiple_of(path * share, LANES), share)
    moves = [
        (filt_hbm.at[:, lanes], filt_ref),
        (skip_hbm.at[:, lanes], skip_ref),
        (table_hbm, table_ref),
    ]
    for index in range(pieces):
        lanes = pl.ds(index * wide, wide)
        moves.append((embed_hbm.at[:, lanes], embed_ref.at[:, lanes]))
    copies = [
        pltpu.make_async_copy(source, target, sems.at[index])
        for index, (source, target) in enumerate(moves)
    ]
    for copy in copies:
        copy.start()

    copies[0].wait()
    copies[1].wait()
    filt_ref[0:1, :] = filt_ref[0:1, :] + skip_ref[...]
    parts = []
    for offset in range(RADIX):
        value = filt_ref[pl.ds(offset, quarter, stride=RADIX), :] * (1.0 / length)
        high = value.astype(BF16)
        parts.append(jnp.concatenate([high, (value - high.astype(F32)).astype(BF16)], 1))
    copies[2].wait()
    found = []
    for offset in range(RADIX):
        both = dot(table_ref[offset], parts[offset])
        both = both[:, :share] + both[:, share:]
        found.append((both[:quarter], both[quarter:]))
    for part, (real, imag) in enumerate(butterfly(found, -1)):
        spec_ref[2 * part] = real
        spec_ref[2 * part + 1] = imag
    outs = [pltpu.make_async_copy(spec_ref, spec_hbm, out_sems.at[0])]
    outs[0].start()

    sum_ref[vocab // 2 :, : vocab // 2] = jnp.zeros((vocab // 2, vocab // 2), F32)
    for index in range(pieces):
        copies[3 + index].wait()
        part = embed_ref[:, index * wide : (index + 1) * wide]
        for rows, lanes in ((slice(0, vocab // 2), slice(0, vocab)), (slice(vocab // 2, vocab),) * 2):
            found = lax.dot_general(
                part[rows], part[lanes], (((1,), (1,)), ((), ())), preferred_element_type=F32
            )
            if index == 0:
                sum_ref[rows, lanes] = found
            else:
                sum_ref[rows, lanes] += found
    first = (lax.axis_index("ctx") * lax.axis_size("path") + path) * share
    mine = embed_ref[:, pl.ds(pl.multiple_of(first, LANES), share)]
    same = iota((LANES, LANES), 0) == iota((LANES, LANES), 1)
    lane = iota((LANES, LANES), 1)
    below = 3 * vocab
    for block in range(vocab // LANES):
        rows = slice(block * LANES, (block + 1) * LANES)
        value = sum_ref[rows, :]
        norm = jnp.sum(jnp.where(same, value[:, rows], 0.0), 1, keepdims=True)
        inv = jnp.broadcast_to(lax.rsqrt(norm / width + EPS), (LANES, LANES))
        high = inv.astype(BF16).astype(F32)
        inv = jnp.where(lane < LANES // 2, high, inv - high).astype(BF16)
        side, start = block * LANES // (vocab // 2), block * LANES % (vocab // 2)
        into = slice(below + start, below + start + LANES)
        left = side * (share + LANES)
        gram_ref[into, left : left + share] = mine[rows]
        gram_ref[into, left + share : left + share + LANES] = inv
        for part in range(3):
            high = value.astype(BF16)
            into = slice(part * vocab + block * LANES, part * vocab + (block + 1) * LANES)
            gram_ref[into, :] = high
            value = value - high.astype(F32)
            into = pl.ds(part * vocab + block * LANES, LANES)
            sem = out_sems.at[1 + block * 3 + part]
            outs.append(pltpu.make_async_copy(gram_ref.at[into], gram_hbm.at[into], sem))
            outs[-1].start()
    into = pl.ds(below, vocab // 2)
    outs.append(pltpu.make_async_copy(gram_ref.at[into], gram_hbm.at[into], out_sems.at[out_sems.shape[0] - 1]))
    outs[-1].start()
    for copy in outs:
        copy.wait()


def own_kernel(ids_ref, embed_ref, grad_ref, own_ref):
    vocab = embed_ref.shape[0]
    own_width = own_ref.shape[2]
    lanes = pl.ds(pl.multiple_of(lax.axis_index("path") * own_width, LANES), own_width)
    ids = ids_ref[...]
    columns = transposed(jnp.concatenate([joined(ids, kind) for kind in range(3)], 0))
    tok = jnp.broadcast_to(columns[:, 0:1], (LANES, LANES))
    place = jnp.broadcast_to(joined(ids, 1), (LANES, LANES))
    put = jnp.broadcast_to(joined(ids, 2), (LANES, LANES))
    first = lax.axis_index("ctx") * LANES
    subs = LANES // GROUP
    here = (place == (iota((LANES, LANES), 0) + first).astype(F32)) & (iota((LANES, LANES), 1) < subs)
    found = jnp.max(jnp.where(here, put, -1.0), 1, keepdims=True)
    base = jnp.where(found >= 0.0, found, tok)
    hots = jnp.concatenate([hot(tok, vocab), hot(base, vocab)], 0)
    both = dot(hots, embed_ref[:, lanes]).astype(BF16)
    own_ref[0] = both[:LANES]
    own_ref[1] = both[LANES:]


def multiply_rows(found, spec_ref, prod_ref, points, kind):
    _, quarter, share = spec_ref.shape
    for start in range(0, quarter, CHUNK):
        here = slice(start, start + CHUNK)
        after = slice(quarter + start, quarter + start + CHUNK)
        filt = [(spec_ref[2 * part, here, :], spec_ref[2 * part + 1, here, :]) for part in range(RADIX)]
        for point in range(points):
            lanes = slice(point * share, (point + 1) * share)
            values = butterfly([(value[here, lanes], value[after, lanes]) for value in found], -1)
            prods = []
            for (real, imag), (filt_real, filt_imag) in zip(values, filt):
                if kind == 1:
                    prods.append((real * filt_real + imag * filt_imag, imag * filt_real - real * filt_imag))
                else:
                    prods.append((real * filt_real - imag * filt_imag, imag * filt_real + real * filt_imag))
            lanes = slice((kind * points + point) * share, (kind * points + point + 1) * share)
            for part, (real, imag) in enumerate(butterfly(prods, 1)):
                prod_ref[part, here, lanes] = real.astype(BF16)
                prod_ref[part, after, lanes] = imag.astype(BF16)


def ids_kernel(vocab, msg_ref, cot_ref, hot_ref, subs_ref, put_ref):
    length = hot_ref.shape[0]
    quarter = length // RADIX
    n_ctx = msg_ref.shape[0]
    block_part = LANES // RADIX
    per_block = LANES // GROUP
    subs = n_ctx * per_block
    blocks = [msg_ref[block, LANES:, :].astype(F32) for block in range(n_ctx)]
    order = by_residue().astype(BF16)
    rows = jnp.concatenate([block[part : part + 1] for part in range(2) for block in blocks], 0)
    toks = lax.dot_general(
        order, rows.astype(BF16), (((1,), (1,)), ((), ())), preferred_element_type=F32
    )
    toks = 256.0 * toks[:, :n_ctx] + toks[:, n_ctx:]
    spread = sum(
        blocks[block] if block == 0 else pltpu.roll(blocks[block], block * per_block, 1)
        for block in range(n_ctx)
    )
    place = joined(spread, 1)
    put = joined(spread, 2)
    back = jnp.floor(place * (1.0 / RADIX))
    place = back + (place - RADIX * back) * quarter
    columns = transposed(jnp.concatenate([place, put], 0))
    for block in range(n_ctx):
        column = jnp.broadcast_to(toks[:, block : block + 1], (LANES, LANES))
        rows = hot(column, vocab)
        for side in range(RADIX):
            first = side * quarter + block * block_part
            hot_ref[first : first + block_part, :] = rows[side * block_part : (side + 1) * block_part]
    subs_ref[subs:, :] = hot(jnp.broadcast_to(columns[:, 1:2], (subs, LANES)), vocab)
    pick = jnp.concatenate(
        [
            (columns[:, 0:1] == (iota((subs, LANES), 1) + part * LANES).astype(F32)).astype(F32).astype(BF16)
            for part in range(length // LANES)
        ],
        1,
    )
    for index in range(length // LANES):
        row = (iota((LANES, subs), 0) + index * LANES).astype(F32)
        here = (row == place[:, :subs]).astype(F32).astype(BF16)
        put_ref[index * LANES : (index + 1) * LANES, :] = jnp.concatenate([here, here], 1)
    subs_ref[:subs, :] = dot(pick, hot_ref[...]).astype(BF16)
    cot = jnp.concatenate([msg_ref[block, :LANES, :] for block in range(n_ctx)], 1)
    cot = dot(order, cot).astype(BF16)
    for block in range(n_ctx):
        cot_ref[block] = cot[:, block * LANES : (block + 1) * LANES]


def feature_kernel(
    points, cot_ref, hot_ref, subs_hot_ref, put_ref, gram_ref, taps_ref, gain_ref, embed_hbm,
    signal_ref, k_ref, v_ref, inv_ref, pair_ref,
    embed_ref, sums_ref, found_ref, look_ref, subs_ref, sem,
):
    length = signal_ref.shape[0]
    quarter = length // RADIX
    vocab, width = embed_hbm.shape
    share = pair_ref.shape[2]
    subs = subs_hot_ref.shape[0] // 2
    first = (lax.axis_index("ctx") * points + lax.axis_index("path")) * share
    first = pl.multiple_of(first, LANES)
    below = 3 * vocab
    table = jnp.concatenate(
        [gram_ref[below:, : share + LANES], gram_ref[below:, share + LANES :]], 0
    )

    for index in range(length // LOOK_ROWS):
        rows = pl.ds(index * LOOK_ROWS, LOOK_ROWS)
        look_ref[rows, :] = dot(hot_ref[rows, :], table)

    alphas = [(point + 0.5) / points for point in range(points)]
    hots = subs_hot_ref[...]
    found = dot(jnp.concatenate([hots] * 3, 1), gram_ref[:below, :])
    hot_tok32, hot_base32 = hots[:subs].astype(F32), hots[subs:].astype(F32)
    tok_tok = jnp.sum(found[:subs] * hot_tok32, 1, keepdims=True)
    tok_base = jnp.sum(found[:subs] * hot_base32, 1, keepdims=True)
    base_tok = jnp.sum(found[subs:] * hot_tok32, 1, keepdims=True)
    tok_base = jnp.where(tok_base == 0.0, base_tok, tok_base)
    base_base = jnp.sum(found[subs:] * hot_base32, 1, keepdims=True)
    cancels = jnp.zeros((subs, 1), F32)
    for point in range(points):
        alpha = alphas[point]
        terms = (1.0 - alpha) ** 2 * base_base + alpha**2 * tok_tok
        total = terms + 2.0 * alpha * (1.0 - alpha) * tok_base
        cancels = jnp.maximum(cancels, (total < CANCEL * terms).astype(F32))
        inv = lax.rsqrt(jnp.maximum(total, 0.0) / width + EPS)
        sums_ref[point] = jnp.broadcast_to(inv, (subs, LANES))

    @pl.when(jnp.max(cancels) > 0.5)
    def _():
        sums_ref[...] = jnp.zeros_like(sums_ref)
        wide = found_ref.shape[1]

        @pl.loop(0, width // wide)
        def _(step):
            lanes = pl.ds(pl.multiple_of(step * wide, wide), wide)
            copy = pltpu.make_async_copy(embed_hbm.at[:, lanes], embed_ref, sem)
            copy.start()
            copy.wait()
            found_ref[...] = dot(hots, embed_ref[...])
            for block in range(subs // GROUP):
                rows = slice(block * GROUP, (block + 1) * GROUP)
                sums = [sums_ref[point, rows, :] for point in range(points)]
                for column in range(wide // LANES):
                    cut = slice(column * LANES, (column + 1) * LANES)
                    base = found_ref[subs + block * GROUP : subs + (block + 1) * GROUP, cut]
                    diff = found_ref[rows, cut] - base
                    for point in range(points):
                        value = base + alphas[point] * diff
                        sums[point] = sums[point] + value * value
                for point in range(points):
                    sums_ref[point, rows, :] = sums[point]

        for point in range(points):
            mean = jnp.sum(sums_ref[point], 1, keepdims=True) / width
            sums_ref[point] = jnp.broadcast_to(lax.rsqrt(mean + EPS), (subs, LANES))

    high = [dot(hots[subs:], table[:, :share]), jnp.ones((subs, LANES), F32)]
    low = [jnp.zeros((subs, LANES), F32)] * 2
    for point in range(points):
        inv = sums_ref[point]
        high.append(inv.astype(BF16).astype(F32))
        low.append(inv - high[-1])
    held = jnp.concatenate([jnp.concatenate(high, 1), jnp.concatenate(low, 1)], 0).astype(BF16)
    for index in range(length // LOOK_ROWS):
        rows = pl.ds(index * LOOK_ROWS, LOOK_ROWS)
        subs_ref[rows, :] = dot(put_ref[rows, :], held)

    cols = points * share
    block_part = LANES // RADIX
    last = {side: [jnp.zeros((GROUP, share), F32)] * points for side in (RADIX - 2, RADIX - 1)}
    gain = gain_ref[:, pl.ds(first, share)]
    taps = [taps_ref[f, :, pl.ds(first, share)].astype(F32) for f in range(3)]
    taps = [[taps[f][tap : tap + 1] for tap in range(3)] for f in range(3)]

    for start in range(0, quarter, CHUNK):
        block, inside = start // block_part, start % block_part
        sides = []
        for side in range(RADIX):
            rows = pl.ds(side * quarter + start, CHUNK)
            tok = look_ref[rows, :share]
            inv = look_ref[rows, share:]
            inv = inv + pltpu.roll(inv, LANES // 2, 1)
            chosen = subs_ref[rows, share : 2 * share] > 0.5
            base = jnp.where(chosen, subs_ref[rows, :share], tok)
            pair_ref[0, rows, :] = tok.astype(BF16)
            pair_ref[1, rows, :] = base.astype(BF16)
            sent = pl.ds(side * block_part + inside, CHUNK)
            upstream = cot_ref[block, sent, :].astype(F32)
            sides.append((rows, gain * base, gain * (tok - base), inv, chosen, upstream))
        for point in range(points):
            lanes = slice(point * share, (point + 1) * share)
            recent = []
            for rows, base, diff, inv_tok, chosen, _ in sides:
                inv = jnp.where(
                    chosen, subs_ref[rows, (2 + point) * share : (3 + point) * share], inv_tok
                )
                inv_ref[rows, lanes] = inv
                recent.append(rounded((base + alphas[point] * diff) * inv))
            backs = []
            for side in (RADIX - 2, RADIX - 1):
                window = jnp.concatenate([last[side][point], recent[side]], 0)
                last[side][point] = recent[side][CHUNK - GROUP :]
                backs.append(window[GROUP - 1 : GROUP - 1 + CHUNK])
            recent = backs + recent
            for side in range(RADIX):
                rows, upstream = sides[side][0], sides[side][5]
                feats = [sum(taps[f][tap] * recent[side + 2 - tap] for tap in range(3)) for f in range(3)]
                k_ref[rows, lanes] = feats[1]
                v_ref[rows, lanes] = feats[2]
                signal_ref[rows, lanes] = (feats[1] * feats[2]).astype(BF16)
                after = slice(cols + point * share, cols + (point + 1) * share)
                signal_ref[rows, after] = (upstream * feats[0]).astype(BF16)


def gradient_kernel(
    points, width, cot_ref, pair_ref, taps_ref, gain_ref,
    signal_ref, k_ref, v_ref, inv_ref, table_ref, back_ref, spec_ref,
    grad_ref,
    prod_ref,
):
    _, quarter, share = spec_ref.shape
    cols = points * share
    n_ctx = cot_ref.shape[0]
    block_part = LANES // RADIX
    first = (lax.axis_index("ctx") * points + lax.axis_index("path")) * share
    first = pl.multiple_of(first, LANES)
    gain = gain_ref[:, pl.ds(first, share)]
    taps = [taps_ref[f, :, pl.ds(first, share)].astype(F32) for f in range(3)]
    taps = [[taps[f][tap : tap + 1] for tap in range(3)] for f in range(3)]

    found = []
    for kind in range(2):
        signal = slice(kind * cols, (kind + 1) * cols)
        spectra = [
            dot(table_ref[side], signal_ref[side * quarter : (side + 1) * quarter, signal])
            for side in range(RADIX)
        ]
        multiply_rows(spectra, spec_ref, prod_ref, points, kind)
    for kind in range(2):
        signal = slice(kind * cols, (kind + 1) * cols)
        found.append([dot(back_ref[side], prod_ref[side, :, signal]) for side in range(RADIX)])

    carried = [[jnp.zeros((GROUP, share), F32)] * points for _ in range(3)]
    lane, row = iota((GROUP, LANES), 1), iota((GROUP, LANES), 0)
    for start in reversed(range(0, quarter, CHUNK)):
        block, inside = start // block_part, start % block_part
        if inside + CHUNK == block_part:
            means = [jnp.zeros((GROUP, LANES), F32)] * 2
        kept = [{} for _ in range(RADIX)]
        for offset in reversed(range(0, CHUNK, GROUP)):
            here = slice(start + offset, start + offset + GROUP)
            sides = []
            for side in range(RADIX):
                rows = slice(side * quarter + start + offset, side * quarter + start + offset + GROUP)
                sent = pl.ds(side * block_part + inside, CHUNK)
                upstream = cot_ref[block, sent, :].astype(F32)[offset : offset + GROUP]
                sides.append([rows, upstream] + [jnp.zeros((GROUP, share), F32)] * 4)
            for point in reversed(range(points)):
                lanes = slice(point * share, (point + 1) * share)
                by_tap = []
                for side in range(RADIX):
                    rows, upstream = sides[side][:2]
                    grad_z = found[1][side][here, lanes]
                    grads = (
                        upstream * found[0][side][here, lanes],
                        grad_z * v_ref[rows, lanes],
                        grad_z * k_ref[rows, lanes],
                    )
                    by_tap.append([sum(taps[f][tap] * grads[f] for f in range(3)) for tap in range(3)])
                ahead = []
                for slot, value in enumerate((by_tap[0][1], by_tap[0][2], by_tap[1][2])):
                    window = jnp.concatenate([value, carried[slot][point]], 0)
                    carried[slot][point] = value
                    ahead.append(window[1 : 1 + GROUP])
                by_tap += [[None, ahead[0], ahead[1]], [None, None, ahead[2]]]
                for side in range(RADIX):
                    rows, _, total, sum0, sum1, sum2 = sides[side]
                    inv = inv_ref[rows, lanes]
                    along = inv * (by_tap[side][0] + by_tap[side + 1][1] + by_tap[side + 2][2])
                    total = total + along
                    sum0 = sum0 + along * (inv * inv)
                    sum1 = sum1 + sum0
                    sides[side][2:] = [total, sum0, sum1, sum2 + sum1]
            for side in range(RADIX):
                _, _, total, sum0, sum1, sum2 = sides[side]
                rows = pl.ds(side * quarter + start, CHUNK)
                base = pair_ref[1, rows, :].astype(F32)[offset : offset + GROUP]
                diff = pair_ref[0, rows, :].astype(F32)[offset : offset + GROUP] - base
                once = (sum1 - 0.5 * sum0) * (1.0 / points)
                twice = (2.0 * (sum2 - sum1) + 0.25 * sum0) * (1.0 / points**2)
                to_tok = base * once + diff * twice
                to_base = base * sum0 + diff * once - to_tok
                kept[side][offset] = gain * total
                for kind, value in enumerate((gain * to_tok, gain * to_base)):
                    value = jnp.sum(value, 1, keepdims=True)
                    at = lane == row + (side * block_part + inside + offset)
                    means[kind] = means[kind] + jnp.where(at, value, 0.0)
        for side in range(RADIX):
            total = jnp.concatenate([kept[side][offset] for offset in range(0, CHUNK, GROUP)], 0)
            grad_ref[block, pl.ds(side * block_part + inside, CHUNK), :] = total.astype(BF16)
        if inside == 0:
            sent = []
            for value in means:
                value = jnp.sum(value, 0, keepdims=True) / width
                high = value.astype(BF16).astype(F32)
                sent += [high, value - high]
            sent.append(jnp.zeros((grad_ref.shape[1] - LANES - len(sent), LANES), F32))
            grad_ref[block, LANES:, :] = jnp.concatenate(sent, 0).astype(BF16)


def partial_kernel(grad_ref, *out_refs):
    rows, _ = out_refs[0].shape
    n_ctx = grad_ref.shape[0]
    each = n_ctx // len(out_refs)
    spare = sum(grad_ref[block, LANES:, :].astype(F32) for block in range(n_ctx))
    sums = [spare[0:1] + spare[1:2], spare[2:3] + spare[3:4]]
    sent = []
    for value in sums:
        high = value.astype(BF16).astype(F32)
        sent += [high, value - high]
    sent.append(jnp.zeros((rows - each * LANES - len(sent), LANES), F32))
    sent = jnp.concatenate(sent, 0).astype(BF16)
    path = lax.axis_index("path")
    for step, ref in enumerate(out_refs):
        dest = path ^ step
        for piece in range(each):
            ref[piece * LANES : (piece + 1) * LANES, :] = grad_ref[dest * each + piece, :LANES, :]
        ref[each * LANES :, :] = sent


def finish_kernel(own_ref, *refs):
    grad_refs, (path_hbm, attr_hbm, path_ref, attr_ref, sems) = refs[:-5], refs[-5:]
    points = len(grad_refs)
    rows, share = grad_refs[0].shape
    pieces = rows // LANES
    spare = sum(ref[pieces * LANES :, :].astype(F32) for ref in grad_refs)
    lane = iota((LANES, LANES), 1)
    part = LANES // RADIX
    order = (iota((LANES, LANES), 0) == RADIX * (lane % part) + lane // part).astype(F32).astype(BF16)
    left, split = jnp.concatenate([spare[0:1] + spare[1:2], spare[2:3] + spare[3:4]], 0), []
    for _ in range(3):
        split.append(left.astype(BF16).astype(F32))
        left = left - split[-1]
    split = jnp.concatenate(split + [jnp.zeros((2, LANES), F32)], 0).astype(BF16)
    columns = lax.dot_general(order, split, (((1,), (1,)), ((), ())), preferred_element_type=F32)
    to_tok = columns[:, 0:1] + columns[:, 2:3] + columns[:, 4:5]
    to_base = columns[:, 1:2] + columns[:, 3:4] + columns[:, 5:6]
    path = lax.axis_index("path")
    copies = []
    for step, ref in enumerate(grad_refs):
        for piece in range(pieces):
            slot = step * pieces + piece
            first = (piece * points + (path ^ step)) * share
            lanes = pl.ds(pl.multiple_of(first, LANES), share)
            tok = own_ref[0, :, lanes].astype(F32)
            base = own_ref[1, :, lanes].astype(F32)
            grad = dot(order, ref[piece * LANES : (piece + 1) * LANES, :])
            grad = (grad - tok * to_tok - base * to_base) / points
            path_ref[slot] = grad
            attr_ref[slot] = (tok - base) * grad
            for kind, (source, target) in enumerate(((path_ref, path_hbm), (attr_ref, attr_hbm))):
                copies.append(
                    pltpu.make_async_copy(source.at[slot], target.at[:, lanes], sems.at[kind, slot])
                )
                copies[-1].start()
    for copy in copies:
        copy.wait()


def any_spec():
    return pl.BlockSpec(memory_space=pl.ANY)


def vmem_spec():
    return pl.BlockSpec(memory_space=pltpu.VMEM)


def hbm_spec():
    return pl.BlockSpec(memory_space=pltpu.HBM)


def call(kernel, ins, outs, scratch, flops, moved, mebibytes):
    return pl.pallas_call(
        kernel,
        in_specs=ins,
        out_specs=[spec for spec, _ in outs],
        out_shape=[shape for _, shape in outs],
        scratch_shapes=scratch,
        compiler_params=pltpu.CompilerParams(vmem_limit_bytes=mebibytes * 2**20),
        cost_estimate=pl.CostEstimate(flops=flops, bytes_accessed=moved, transcendentals=0),
    )


def shape(dims, dtype):
    return jax.ShapeDtypeStruct(dims, dtype)


def kernel_body(tokens, sub_pos, sub_base, embed, norm_gain, fir_taps, long_filter, skip_gain, cotangent):
    n_path, n_ctx = lax.axis_size("path"), lax.axis_size("ctx")
    points = n_path
    tok_rows = tokens.shape[0]
    length = tok_rows * n_ctx
    vocab, width = embed.shape
    share = width // (n_path * n_ctx)
    subs = sub_pos.shape[0] * n_ctx
    own_width = width // n_path
    cols = points * share
    quarter = length // RADIX
    tables = dft_tables(length)
    dma = pltpu.SemaphoreType.DMA
    transform_flops = length * length
    spare = 8

    msg, ids = call(
        pack_kernel,
        [hbm_spec()] * 4,
        [
            (any_spec(), shape((n_ctx, tok_rows + 2 * spare, share), BF16)),
            (vmem_spec(), shape((2 * spare, LANES), F32)),
        ],
        [
            pltpu.VMEM((1, tok_rows), jnp.int32),
            pltpu.VMEM((1, sub_pos.shape[0]), jnp.int32),
            pltpu.VMEM((1, sub_pos.shape[0]), jnp.int32),
            pltpu.VMEM((2 * spare, LANES), BF16),
            dma((2 * n_ctx + 3,)),
        ],
        length * share,
        8 * length * share,
        60,
    )(
        tokens.reshape(1, tok_rows),
        sub_pos.reshape(1, -1),
        sub_base.reshape(1, -1),
        cotangent,
    )
    msg = lax.all_to_all(msg, "ctx", 0, 0, tiled=True)

    gain = norm_gain.reshape(1, width)
    skip = skip_gain.reshape(1, n_path * share)
    spec, gram = call(
        prepare_kernel,
        [hbm_spec()] * 4 + [any_spec()],
        [
            (any_spec(), shape((2 * RADIX, quarter, share), F32)),
            (any_spec(), shape((3 * vocab + vocab // 2, vocab), BF16)),
        ],
        [
            pltpu.VMEM((length, share), F32),
            pltpu.VMEM((RADIX, 2 * quarter, quarter), BF16),
            pltpu.VMEM((vocab, width), BF16),
            pltpu.VMEM((1, share), F32),
            pltpu.VMEM((vocab, vocab), F32),
            pltpu.VMEM((2 * RADIX, quarter, share), F32),
            pltpu.VMEM((3 * vocab + vocab // 2, vocab), BF16),
            dma((7,)),
            dma((3 * vocab // LANES + 2,)),
        ],
        2 * vocab * vocab * width,
        2 * vocab * width,
        58,
    )(long_filter, tables[0], embed, skip, ids)

    cot, hots, subs_hots, put_hots = call(
        functools.partial(ids_kernel, vocab),
        [vmem_spec()],
        [
            (vmem_spec(), shape((n_ctx, tok_rows, share), BF16)),
            (vmem_spec(), shape((length, vocab), BF16)),
            (vmem_spec(), shape((2 * subs, vocab), BF16)),
            (vmem_spec(), shape((length, 2 * subs), BF16)),
        ],
        [],
        2 * 10**9,
        4 * 10**6,
        8,
    )(msg)
    wide = 4 * LANES
    signal, k_feat, v_feat, inv, pair = call(
        functools.partial(feature_kernel, points),
        [vmem_spec()] * 7 + [hbm_spec()],
        [(vmem_spec(), shape((length, 2 * cols), BF16))]
        + [(vmem_spec(), shape((length, cols), F32))] * 3
        + [(vmem_spec(), shape((2, length, share), BF16))],
        [
            pltpu.VMEM((vocab, wide), BF16),
            pltpu.VMEM((points, subs, LANES), F32),
            pltpu.VMEM((2 * subs, wide), F32),
            pltpu.VMEM((length, 2 * share), F32),
            pltpu.VMEM((length, (2 + points) * share), F32),
            dma,
        ],
        2 * length * vocab * 3 * share,
        2 * vocab * width + 16 * length * cols,
        39,
    )(cot, hots, subs_hots, put_hots, gram, fir_taps, gain, embed)

    grad = call(
        functools.partial(gradient_kernel, points, width),
        [vmem_spec()] * 11,
        [(vmem_spec(), shape((n_ctx, tok_rows + spare, share), BF16))],
        [
            pltpu.VMEM((RADIX, 2 * quarter, 2 * cols), BF16),
        ],
        4 * transform_flops * cols,
        4 * length * length + 16 * length * cols,
        32,
    )(cot, pair, fir_taps, gain, signal, k_feat, v_feat, inv, *tables, spec)[0]

    own = call(
        own_kernel,
        [vmem_spec(), vmem_spec(), any_spec()],
        [(vmem_spec(), shape((2, tok_rows, own_width), BF16))],
        [],
        4 * tok_rows * vocab * own_width,
        2 * vocab * own_width,
        10,
    )(ids, embed, grad)[0]
    grad = lax.all_to_all(grad, "ctx", 0, 0, tiled=True)
    each = n_ctx // n_path
    parts = call(
        partial_kernel,
        [vmem_spec()],
        [(vmem_spec(), shape((each * tok_rows + spare, share), BF16))] * n_path,
        [],
        spare * LANES * n_ctx,
        4 * length * share,
        4,
    )(grad)
    parts = [
        part if step == 0 else lax.ppermute(part, "path", [(p, p ^ step) for p in range(n_path)])
        for step, part in enumerate(parts)
    ]
    out = shape((tok_rows, own_width), F32)
    return tuple(
        call(
            finish_kernel,
            [vmem_spec()] * (1 + n_path),
            [(any_spec(), out), (any_spec(), out)],
            [pltpu.VMEM((n_path * each, tok_rows, share), F32)] * 2 + [dma((2, n_path * each))],
            8 * tok_rows * own_width,
            14 * tok_rows * own_width,
            8,
        )(own, *parts)
    )


def plain_body(tokens, sub_pos, sub_base, embed, norm_gain, fir_taps, long_filter, skip_gain, cotangent):
    n_path, n_ctx = lax.axis_size("path"), lax.axis_size("ctx")
    path, ctx = lax.axis_index("path"), lax.axis_index("ctx")
    points = n_path
    tok_rows = tokens.shape[0]
    length = tok_rows * n_ctx
    width = embed.shape[1]
    share = width // (n_path * n_ctx)
    own_width = width // n_path
    first = (ctx * n_path + path) * share
    alphas = ((jnp.arange(points, dtype=jnp.int32)).astype(F32) + 0.5) / points
    alphas = alphas[:, None, None]

    local = jnp.arange(tok_rows, dtype=jnp.int32)[:, None] + ctx * tok_rows == sub_pos[None, :]
    put = jnp.sum(jnp.where(local, sub_base[None, :], 0), 1)
    base_ids = jnp.where(jnp.any(local, 1), put, tokens)
    rows_tok = jnp.take(embed, tokens, axis=0).astype(F32)
    rows_base = jnp.take(embed, base_ids, axis=0).astype(F32)
    rows_in = rows_base[None] + alphas * (rows_tok - rows_base)[None]
    inv = lax.rsqrt(jnp.mean(rows_in * rows_in, -1) + EPS)
    inv = lax.all_gather(inv, "ctx", axis=1, tiled=True)[:, :, None]
    all_tok = lax.all_gather(tokens, "ctx", tiled=True)
    all_base = lax.all_gather(base_ids, "ctx", tiled=True)

    cot = cotangent.reshape(tok_rows, n_ctx, n_path, share)
    cot = lax.dynamic_index_in_dim(cot, path, 2, keepdims=False)
    cot = lax.all_to_all(cot.transpose(1, 0, 2), "ctx", 0, 0, tiled=True)
    upstream = cot.reshape(1, length, share).astype(F32)
    mine = lax.dynamic_slice_in_dim(embed, first, share, 1)
    gain = lax.dynamic_slice_in_dim(norm_gain, first, share, 0)
    taps = lax.dynamic_slice_in_dim(fir_taps, first, share, 2).astype(F32)
    filt = lax.dynamic_slice_in_dim(long_filter, path * share, share, 1)
    skip = lax.dynamic_slice_in_dim(skip_gain, path * share, share, 0)

    emb_tok = jnp.take(mine, all_tok, axis=0).astype(F32)
    emb_base = jnp.take(mine, all_base, axis=0).astype(F32)
    inputs = emb_base[None] + alphas * (emb_tok - emb_base)[None]
    normed = rounded(inputs * inv * gain)
    q_feat, k_feat, v_feat = (
        taps[f, 0] * normed + taps[f, 1] * shifted(normed, 1) + taps[f, 2] * shifted(normed, 2)
        for f in range(3)
    )
    filter_spec = spectrum(filt[None])
    conv = rounded(long_conv(rounded(k_feat * v_feat), filter_spec, skip, False))
    grad_z = rounded(long_conv(rounded(upstream * q_feat), filter_spec, skip, True))
    grads = (rounded(upstream * conv), rounded(grad_z * v_feat), rounded(grad_z * k_feat))
    by_tap = [sum(taps[f, tap] * grads[f] for f in range(3)) for tap in range(3)]
    scaled = gain * (by_tap[0] + shifted(by_tap[1], -1) + shifted(by_tap[2], -2))
    grad = jnp.sum(inv * scaled, 0).astype(BF16)
    along = jnp.sum(inputs * scaled, -1, keepdims=True) * inv**3 / width
    part = jnp.stack([jnp.sum(alphas * along, 0)[:, 0], jnp.sum((1.0 - alphas) * along, 0)[:, 0]])
    part = lax.psum(part, ("path", "ctx"))
    part = lax.dynamic_slice_in_dim(part, ctx * tok_rows, tok_rows, 1)

    back = lax.all_to_all(grad.reshape(n_ctx, tok_rows, share), "ctx", 0, 0, tiled=True)
    back = back.reshape(n_path, n_ctx // n_path, tok_rows, share)
    back = lax.all_to_all(back, "path", 0, 0, tiled=True).astype(F32)
    back = back.transpose(2, 1, 0, 3).reshape(tok_rows, own_width)
    own_tok = lax.dynamic_slice_in_dim(rows_tok, path * own_width, own_width, 1)
    own_base = lax.dynamic_slice_in_dim(rows_base, path * own_width, own_width, 1)
    grad = (back - own_tok * part[0][:, None] - own_base * part[1][:, None]) / points
    return (grad, (own_tok - own_base) * grad)


def body(tokens, sub_pos, sub_base, embed, *rest):
    n_path, n_ctx = lax.axis_size("path"), lax.axis_size("ctx")
    tok_rows = tokens.shape[0]
    share = embed.shape[1] // (n_path * n_ctx)
    tables = 2 * (tok_rows * n_ctx) ** 2
    fits = share == LANES and tok_rows == LANES and n_ctx == GROUP and tables <= TABLE_BYTES
    fits = fits and n_ctx % n_path == 0 and n_path & (n_path - 1) == 0
    chosen = kernel_body if fits else plain_body
    return chosen(tokens, sub_pos, sub_base, embed, *rest)


def solution(mesh):
    return jax.shard_map(
        body,
        mesh=mesh,
        in_specs=(
            P("ctx"),
            P("ctx"),
            P("ctx"),
            P(),
            P(),
            P(),
            P(None, "ctx"),
            P("ctx"),
            P("ctx", None),
        ),
        out_specs=(P("ctx", "path"), P("ctx", "path")),
        check_vma=False,
    )
```

```python
import functools

import jax
import jax.numpy as jnp
import ml_dtypes
import numpy as np
from jax import lax
from jax.experimental import pallas as pl
from jax.experimental.pallas import tpu as pltpu
from jax.sharding import PartitionSpec as P

LANES = 128
GROUP = 8
RADIX = 4
LOOK_ROWS = 256
CHUNK = 16
EPS = 1e-06
CANCEL = 0.004
TABLE_BYTES = 2**21
F32 = jnp.float32
BF16 = jnp.bfloat16
precise = lax.Precision.HIGH


def angle_tables(length):
    outer_size = 64
    inner_size = length // outer_size
    outer_idx = jnp.arange(outer_size, dtype=jnp.int32)
    inner_idx = jnp.arange(inner_size, dtype=jnp.int32)
    outer_angle = (
        2.0 * jnp.pi / outer_size
        * (outer_idx[:, None] * outer_idx[None, :] % outer_size).astype(F32)
    )
    inner_angle = (
        2.0 * jnp.pi / inner_size
        * (inner_idx[:, None] * inner_idx[None, :] % inner_size).astype(F32)
    )
    twist_angle = (
        2.0 * jnp.pi / length
        * (outer_idx[:, None] * inner_idx[None, :] % length).astype(F32)
    )
    return (outer_angle, inner_angle, twist_angle)


def complex_table(angle, sign):
    cosine = jnp.cos(angle)
    sine = sign * jnp.sin(angle)
    return jnp.stack([jnp.stack([cosine, sine]), jnp.stack([-sine, cosine])])


def twisted(values, angle, sign):
    cosine = jnp.cos(angle)[None, :, :, None]
    sine = sign * jnp.sin(angle)[None, :, :, None]
    real_part = values[:, 0]
    imag_part = values[:, 1]
    return jnp.stack(
        [real_part * cosine - imag_part * sine, real_part * sine + imag_part * cosine], 1
    )


def spectrum(signal):
    batch, half, width = signal.shape
    length = 2 * half
    outer_angle, inner_angle, twist_angle = angle_tables(length)
    outer_size = outer_angle.shape[0]
    inner_size = inner_angle.shape[0]
    folded = signal.reshape(batch, outer_size // 2, inner_size, width)
    used = outer_angle[:, : outer_size // 2]
    outer_table = jnp.stack([jnp.cos(used), -jnp.sin(used)])
    first = jnp.einsum("rka,pabc->prkbc", outer_table, folded, precision=precise)
    turned = twisted(first, twist_angle, -1.0)
    return jnp.einsum(
        "prkbc,rsbm->pskmc", turned, complex_table(inner_angle, -1.0), precision=precise
    )


def inverse(spec):
    batch, parts, outer_size, inner_size, width = spec.shape
    length = outer_size * inner_size
    outer_angle, inner_angle, twist_angle = angle_tables(length)
    back = jnp.einsum("pskmc,stmb->ptkbc", spec, complex_table(inner_angle, 1.0), precision=precise)
    turned = twisted(back, twist_angle, 1.0)
    used = outer_angle[: outer_size // 2]
    outer_table = jnp.stack([jnp.cos(used), -jnp.sin(used)])
    result = jnp.einsum("rak,prkbc->pabc", outer_table, turned, precision=precise)
    return (result / length).reshape(batch, length // 2, width)


def long_conv(signal, filter_spec, skip_gain, adjoint):
    spec = spectrum(signal)
    sig_real = spec[:, 0]
    sig_imag = spec[:, 1]
    filt_real = filter_spec[:, 0]
    filt_imag = filter_spec[:, 1]
    if adjoint:
        prod_real = sig_real * filt_real + sig_imag * filt_imag
        prod_imag = sig_imag * filt_real - sig_real * filt_imag
    else:
        prod_real = sig_real * filt_real - sig_imag * filt_imag
        prod_imag = sig_real * filt_imag + sig_imag * filt_real
    return inverse(jnp.stack([prod_real, prod_imag], 1)) + skip_gain * signal


def rounded(value):
    return value.astype(BF16).astype(F32)


def shifted(values, step):
    zeros = jnp.zeros_like(values[:, : abs(step)])
    if step > 0:
        return jnp.concatenate([zeros, values[:, :-step]], 1)
    return jnp.concatenate([values[:, -step:], zeros], 1)


@functools.lru_cache(maxsize=None)
def dft_tables(length):
    quarter = length // RADIX
    freq = 4 * np.arange(quarter, dtype=np.int64) + 1
    place = np.arange(quarter, dtype=np.int64)
    there, back = [], []
    for offset in range(RADIX):
        turns = freq[:, None] * (RADIX * place + offset)[None, :] % (4 * length)
        angle = turns * (2.0 * np.pi / (4 * length))
        cosine = np.cos(angle).astype(ml_dtypes.bfloat16)
        sine = np.sin(angle).astype(ml_dtypes.bfloat16)
        there.append(np.concatenate([cosine, sine], 0))
        back.append(np.concatenate([cosine.T, sine.T], 1))
    return (np.stack(there), np.stack(back))


def butterfly(values, sign):
    (r0, s0), (r1, s1), (r2, s2), (r3, s3) = values
    sum_r, sum_s, diff_r, diff_s = r0 + r2, s0 + s2, r0 - r2, s0 - s2
    odd_r, odd_s, turn_r, turn_s = r1 + r3, s1 + s3, r1 - r3, s1 - s3
    ahead = (diff_r + turn_s, diff_s - turn_r)
    behind = (diff_r - turn_s, diff_s + turn_r)
    if sign < 0:
        ahead, behind = behind, ahead
    return ((sum_r + odd_r, sum_s + odd_s), ahead, (sum_r - odd_r, sum_s - odd_s), behind)


def transposed(rows):
    count = rows.shape[0]
    if count < LANES:
        rows = jnp.concatenate([rows, jnp.zeros((LANES - count, LANES), F32)], 0)
    return rows.T


def dot(left, right):
    return jnp.dot(left, right, preferred_element_type=F32)


def iota(dims, axis):
    return lax.broadcasted_iota(jnp.int32, dims, axis)


def by_residue():
    row = iota((LANES, LANES), 0)
    part = LANES // RADIX
    source = RADIX * (row % part) + row // part
    return (iota((LANES, LANES), 1) == source).astype(F32)


def hot(ids, vocab):
    lane = iota(ids.shape, 1).astype(F32)
    parts = [
        (ids == lane + float(column * LANES)).astype(F32).astype(BF16)
        for column in range(vocab // LANES)
    ]
    return jnp.concatenate(parts, 1)


def joined(block, kind):
    return 256.0 * block[2 * kind : 2 * kind + 1] + block[2 * kind + 1 : 2 * kind + 2]


def pack_kernel(
    tok_hbm, pos_hbm, put_hbm, cot_hbm, msg_ref, ids_ref, tok_ref, pos_ref, put_ref, cot_ref, sems
):
    dests, rows, share = msg_ref.shape
    tok_rows = cot_hbm.shape[0]
    n_path = cot_hbm.shape[1] // (dests * share)
    path = lax.axis_index("path")
    moves = [(tok_hbm, tok_ref), (pos_hbm, pos_ref), (put_hbm, put_ref)]
    for dest in range(dests):
        lanes = pl.ds(pl.multiple_of((dest * n_path + path) * share, LANES), share)
        moves.append((cot_hbm.at[:, lanes], cot_ref.at[:, pl.ds(dest * share, share)]))
    copies = [
        pltpu.make_async_copy(source, target, sems.at[index])
        for index, (source, target) in enumerate(moves)
    ]
    for copy in copies:
        copy.start()
    order = by_residue().astype(BF16)
    for copy in copies[:3]:
        copy.wait()
    lists = []
    for ref in (tok_ref, pos_ref, put_ref):
        value = ref[...].astype(F32)
        if value.shape[1] < LANES:
            value = jnp.concatenate([value, jnp.zeros((1, LANES - value.shape[1]), F32)], 1)
        high = jnp.floor(value * (1.0 / 256.0))
        lists += [high, value - 256.0 * high]
    lists.append(jnp.zeros((rows - tok_rows - len(lists), LANES), F32))
    ids = jnp.concatenate(lists, 0)
    ids_ref[...] = ids
    turned = lax.dot_general(
        ids.astype(BF16), order, (((1,), (1,)), ((), ())), preferred_element_type=F32
    )
    ids = jnp.where(iota(ids.shape, 0) < 2, turned, ids).astype(BF16)
    for dest in range(dests):
        msg_ref[dest, tok_rows:, :] = ids
    for copy in copies[3:]:
        copy.wait()
    turned = dot(order, cot_ref[...]).astype(BF16)
    for dest in range(dests):
        msg_ref[dest, :tok_rows, :] = turned[:, dest * share : (dest + 1) * share]


def prepare_kernel(
    filt_hbm, table_hbm, embed_hbm, skip_hbm, after_ref,
    spec_hbm, gram_hbm,
    filt_ref, table_ref, embed_ref, skip_ref, sum_ref, spec_ref, gram_ref, sems, out_sems,
):
    length, share = filt_ref.shape
    quarter = length // RADIX
    vocab, width = embed_ref.shape
    pieces = sems.shape[0] - 3
    wide = width // pieces
    path = lax.axis_index("path")
    lanes = pl.ds(pl.multiple_of(path * share, LANES), share)
    moves = [
        (filt_hbm.at[:, lanes], filt_ref),
        (skip_hbm.at[:, lanes], skip_ref),
        (table_hbm, table_ref),
    ]
    for index in range(pieces):
        lanes = pl.ds(index * wide, wide)
        moves.append((embed_hbm.at[:, lanes], embed_ref.at[:, lanes]))
    copies = [
        pltpu.make_async_copy(source, target, sems.at[index])
        for index, (source, target) in enumerate(moves)
    ]
    for copy in copies:
        copy.start()

    copies[0].wait()
    copies[1].wait()
    filt_ref[0:1, :] = filt_ref[0:1, :] + skip_ref[...]
    parts = []
    for offset in range(RADIX):
        value = filt_ref[pl.ds(offset, quarter, stride=RADIX), :] * (1.0 / length)
        high = value.astype(BF16)
        parts.append(jnp.concatenate([high, (value - high.astype(F32)).astype(BF16)], 1))
    copies[2].wait()
    found = []
    for offset in range(RADIX):
        both = dot(table_ref[offset], parts[offset])
        both = both[:, :share] + both[:, share:]
        found.append((both[:quarter], both[quarter:]))
    for part, (real, imag) in enumerate(butterfly(found, -1)):
        spec_ref[2 * part] = real
        spec_ref[2 * part + 1] = imag
    outs = [pltpu.make_async_copy(spec_ref, spec_hbm, out_sems.at[0])]
    outs[0].start()

    sum_ref[vocab // 2 :, : vocab // 2] = jnp.zeros((vocab // 2, vocab // 2), F32)
    for index in range(pieces):
        copies[3 + index].wait()
        part = embed_ref[:, index * wide : (index + 1) * wide]
        for rows, lanes in ((slice(0, vocab // 2), slice(0, vocab)), (slice(vocab // 2, vocab),) * 2):
            found = lax.dot_general(
                part[rows], part[lanes], (((1,), (1,)), ((), ())), preferred_element_type=F32
            )
            if index == 0:
                sum_ref[rows, lanes] = found
            else:
                sum_ref[rows, lanes] += found
    first = (lax.axis_index("ctx") * lax.axis_size("path") + path) * share
    mine = embed_ref[:, pl.ds(pl.multiple_of(first, LANES), share)]
    same = iota((LANES, LANES), 0) == iota((LANES, LANES), 1)
    lane = iota((LANES, LANES), 1)
    below = 3 * vocab
    for block in range(vocab // LANES):
        rows = slice(block * LANES, (block + 1) * LANES)
        value = sum_ref[rows, :]
        norm = jnp.sum(jnp.where(same, value[:, rows], 0.0), 1, keepdims=True)
        inv = jnp.broadcast_to(lax.rsqrt(norm / width + EPS), (LANES, LANES))
        high = inv.astype(BF16).astype(F32)
        inv = jnp.where(lane < LANES // 2, high, inv - high).astype(BF16)
        side, start = block * LANES // (vocab // 2), block * LANES % (vocab // 2)
        into = slice(below + start, below + start + LANES)
        left = side * (share + LANES)
        gram_ref[into, left : left + share] = mine[rows]
        gram_ref[into, left + share : left + share + LANES] = inv
        for part in range(3):
            high = value.astype(BF16)
            into = slice(part * vocab + block * LANES, part * vocab + (block + 1) * LANES)
            gram_ref[into, :] = high
            value = value - high.astype(F32)
            into = pl.ds(part * vocab + block * LANES, LANES)
            sem = out_sems.at[1 + block * 3 + part]
            outs.append(pltpu.make_async_copy(gram_ref.at[into], gram_hbm.at[into], sem))
            outs[-1].start()
    into = pl.ds(below, vocab // 2)
    outs.append(pltpu.make_async_copy(gram_ref.at[into], gram_hbm.at[into], out_sems.at[out_sems.shape[0] - 1]))
    outs[-1].start()
    for copy in outs:
        copy.wait()


def own_kernel(ids_ref, embed_ref, grad_ref, own_ref):
    vocab = embed_ref.shape[0]
    own_width = own_ref.shape[2]
    lanes = pl.ds(pl.multiple_of(lax.axis_index("path") * own_width, LANES), own_width)
    ids = ids_ref[...]
    columns = transposed(jnp.concatenate([joined(ids, kind) for kind in range(3)], 0))
    tok = jnp.broadcast_to(columns[:, 0:1], (LANES, LANES))
    place = jnp.broadcast_to(joined(ids, 1), (LANES, LANES))
    put = jnp.broadcast_to(joined(ids, 2), (LANES, LANES))
    first = lax.axis_index("ctx") * LANES
    subs = LANES // GROUP
    here = (place == (iota((LANES, LANES), 0) + first).astype(F32)) & (iota((LANES, LANES), 1) < subs)
    found = jnp.max(jnp.where(here, put, -1.0), 1, keepdims=True)
    base = jnp.where(found >= 0.0, found, tok)
    hots = jnp.concatenate([hot(tok, vocab), hot(base, vocab)], 0)
    both = dot(hots, embed_ref[:, lanes]).astype(BF16)
    own_ref[0] = both[:LANES]
    own_ref[1] = both[LANES:]


def multiply_rows(found, spec_ref, prod_ref, points, kind):
    _, quarter, share = spec_ref.shape
    for start in range(0, quarter, CHUNK):
        here = slice(start, start + CHUNK)
        after = slice(quarter + start, quarter + start + CHUNK)
        filt = [(spec_ref[2 * part, here, :], spec_ref[2 * part + 1, here, :]) for part in range(RADIX)]
        for point in range(points):
            lanes = slice(point * share, (point + 1) * share)
            values = butterfly([(value[here, lanes], value[after, lanes]) for value in found], -1)
            prods = []
            for (real, imag), (filt_real, filt_imag) in zip(values, filt):
                if kind == 1:
                    prods.append((real * filt_real + imag * filt_imag, imag * filt_real - real * filt_imag))
                else:
                    prods.append((real * filt_real - imag * filt_imag, imag * filt_real + real * filt_imag))
            lanes = slice((kind * points + point) * share, (kind * points + point + 1) * share)
            for part, (real, imag) in enumerate(butterfly(prods, 1)):
                prod_ref[part, here, lanes] = real.astype(BF16)
                prod_ref[part, after, lanes] = imag.astype(BF16)


def ids_kernel(vocab, msg_ref, hot_ref, subs_ref, put_ref):
    length = hot_ref.shape[0]
    quarter = length // RADIX
    n_ctx = msg_ref.shape[0]
    block_part = LANES // RADIX
    per_block = LANES // GROUP
    subs = n_ctx * per_block
    blocks = [msg_ref[block, LANES:, :].astype(F32) for block in range(n_ctx)]
    toks = transposed(jnp.concatenate([joined(block, 0) for block in blocks], 0))
    spread = sum(
        blocks[block] if block == 0 else pltpu.roll(blocks[block], block * per_block, 1)
        for block in range(n_ctx)
    )
    place = joined(spread, 1)
    put = joined(spread, 2)
    back = jnp.floor(place * (1.0 / RADIX))
    place = back + (place - RADIX * back) * quarter
    columns = transposed(jnp.concatenate([place, put], 0))
    for block in range(n_ctx):
        column = jnp.broadcast_to(toks[:, block : block + 1], (LANES, LANES))
        rows = hot(column, vocab)
        for side in range(RADIX):
            first = side * quarter + block * block_part
            hot_ref[first : first + block_part, :] = rows[side * block_part : (side + 1) * block_part]
    subs_ref[subs:, :] = hot(jnp.broadcast_to(columns[:, 1:2], (subs, LANES)), vocab)
    pick = jnp.concatenate(
        [
            (columns[:, 0:1] == (iota((subs, LANES), 1) + part * LANES).astype(F32)).astype(F32).astype(BF16)
            for part in range(length // LANES)
        ],
        1,
    )
    for index in range(length // LANES):
        row = (iota((LANES, subs), 0) + index * LANES).astype(F32)
        here = (row == place[:, :subs]).astype(F32).astype(BF16)
        put_ref[index * LANES : (index + 1) * LANES, :] = jnp.concatenate([here, here], 1)
    subs_ref[:subs, :] = dot(pick, hot_ref[...]).astype(BF16)


def feature_kernel(
    points, msg_ref, hot_ref, subs_hot_ref, put_ref, gram_ref, taps_ref, gain_ref, embed_hbm,
    signal_ref, k_ref, v_ref, inv_ref, pair_ref,
    embed_ref, sums_ref, found_ref, look_ref, subs_ref, sem,
):
    length = signal_ref.shape[0]
    quarter = length // RADIX
    vocab, width = embed_hbm.shape
    share = pair_ref.shape[2]
    subs = subs_hot_ref.shape[0] // 2
    first = (lax.axis_index("ctx") * points + lax.axis_index("path")) * share
    first = pl.multiple_of(first, LANES)
    below = 3 * vocab
    table = jnp.concatenate(
        [gram_ref[below:, : share + LANES], gram_ref[below:, share + LANES :]], 0
    )

    for index in range(length // LOOK_ROWS):
        rows = pl.ds(index * LOOK_ROWS, LOOK_ROWS)
        look_ref[rows, :] = dot(hot_ref[rows, :], table)

    alphas = [(point + 0.5) / points for point in range(points)]
    hots = subs_hot_ref[...]
    found = dot(jnp.concatenate([hots] * 3, 1), gram_ref[:below, :])
    hot_tok32, hot_base32 = hots[:subs].astype(F32), hots[subs:].astype(F32)
    tok_tok = jnp.sum(found[:subs] * hot_tok32, 1, keepdims=True)
    tok_base = jnp.sum(found[:subs] * hot_base32, 1, keepdims=True)
    base_tok = jnp.sum(found[subs:] * hot_tok32, 1, keepdims=True)
    tok_base = jnp.where(tok_base == 0.0, base_tok, tok_base)
    base_base = jnp.sum(found[subs:] * hot_base32, 1, keepdims=True)
    cancels = jnp.zeros((subs, 1), F32)
    for point in range(points):
        alpha = alphas[point]
        terms = (1.0 - alpha) ** 2 * base_base + alpha**2 * tok_tok
        total = terms + 2.0 * alpha * (1.0 - alpha) * tok_base
        cancels = jnp.maximum(cancels, (total < CANCEL * terms).astype(F32))
        inv = lax.rsqrt(jnp.maximum(total, 0.0) / width + EPS)
        sums_ref[point] = jnp.broadcast_to(inv, (subs, LANES))

    @pl.when(jnp.max(cancels) > 0.5)
    def _():
        sums_ref[...] = jnp.zeros_like(sums_ref)
        wide = found_ref.shape[1]

        @pl.loop(0, width // wide)
        def _(step):
            lanes = pl.ds(pl.multiple_of(step * wide, wide), wide)
            copy = pltpu.make_async_copy(embed_hbm.at[:, lanes], embed_ref, sem)
            copy.start()
            copy.wait()
            found_ref[...] = dot(hots, embed_ref[...])
            for block in range(subs // GROUP):
                rows = slice(block * GROUP, (block + 1) * GROUP)
                sums = [sums_ref[point, rows, :] for point in range(points)]
                for column in range(wide // LANES):
                    cut = slice(column * LANES, (column + 1) * LANES)
                    base = found_ref[subs + block * GROUP : subs + (block + 1) * GROUP, cut]
                    diff = found_ref[rows, cut] - base
                    for point in range(points):
                        value = base + alphas[point] * diff
                        sums[point] = sums[point] + value * value
                for point in range(points):
                    sums_ref[point, rows, :] = sums[point]

        for point in range(points):
            mean = jnp.sum(sums_ref[point], 1, keepdims=True) / width
            sums_ref[point] = jnp.broadcast_to(lax.rsqrt(mean + EPS), (subs, LANES))

    high = [dot(hots[subs:], table[:, :share]), jnp.ones((subs, LANES), F32)]
    low = [jnp.zeros((subs, LANES), F32)] * 2
    for point in range(points):
        inv = sums_ref[point]
        high.append(inv.astype(BF16).astype(F32))
        low.append(inv - high[-1])
    held = jnp.concatenate([jnp.concatenate(high, 1), jnp.concatenate(low, 1)], 0).astype(BF16)
    for index in range(length // LOOK_ROWS):
        rows = pl.ds(index * LOOK_ROWS, LOOK_ROWS)
        subs_ref[rows, :] = dot(put_ref[rows, :], held)

    cols = points * share
    block_part = LANES // RADIX
    last = {side: [jnp.zeros((GROUP, share), F32)] * points for side in (RADIX - 2, RADIX - 1)}
    gain = gain_ref[:, pl.ds(first, share)]
    taps = [taps_ref[f, :, pl.ds(first, share)].astype(F32) for f in range(3)]
    taps = [[taps[f][tap : tap + 1] for tap in range(3)] for f in range(3)]

    for start in range(0, quarter, CHUNK):
        block, inside = start // block_part, start % block_part
        sides = []
        for side in range(RADIX):
            rows = pl.ds(side * quarter + start, CHUNK)
            tok = look_ref[rows, :share]
            inv = look_ref[rows, share:]
            inv = inv + pltpu.roll(inv, LANES // 2, 1)
            chosen = subs_ref[rows, share : 2 * share] > 0.5
            base = jnp.where(chosen, subs_ref[rows, :share], tok)
            pair_ref[0, rows, :] = tok.astype(BF16)
            pair_ref[1, rows, :] = base.astype(BF16)
            sent = pl.ds(side * block_part + inside, CHUNK)
            upstream = msg_ref[block, sent, :].astype(F32)
            sides.append((rows, gain * base, gain * (tok - base), inv, chosen, upstream))
        for point in range(points):
            lanes = slice(point * share, (point + 1) * share)
            recent = []
            for rows, base, diff, inv_tok, chosen, _ in sides:
                inv = jnp.where(
                    chosen, subs_ref[rows, (2 + point) * share : (3 + point) * share], inv_tok
                )
                inv_ref[rows, lanes] = inv
                recent.append(rounded((base + alphas[point] * diff) * inv))
            backs = []
            for side in (RADIX - 2, RADIX - 1):
                window = jnp.concatenate([last[side][point], recent[side]], 0)
                last[side][point] = recent[side][CHUNK - GROUP :]
                backs.append(window[GROUP - 1 : GROUP - 1 + CHUNK])
            recent = backs + recent
            for side in range(RADIX):
                rows, upstream = sides[side][0], sides[side][5]
                feats = [sum(taps[f][tap] * recent[side + 2 - tap] for tap in range(3)) for f in range(3)]
                k_ref[rows, lanes] = feats[1]
                v_ref[rows, lanes] = feats[2]
                signal_ref[rows, lanes] = (feats[1] * feats[2]).astype(BF16)
                after = slice(cols + point * share, cols + (point + 1) * share)
                signal_ref[rows, after] = (upstream * feats[0]).astype(BF16)


def gradient_kernel(
    points, width, msg_ref, pair_ref, taps_ref, gain_ref,
    signal_ref, k_ref, v_ref, inv_ref, table_ref, back_ref, spec_ref,
    grad_ref,
    prod_ref,
):
    _, quarter, share = spec_ref.shape
    cols = points * share
    n_ctx = msg_ref.shape[0]
    block_part = LANES // RADIX
    first = (lax.axis_index("ctx") * points + lax.axis_index("path")) * share
    first = pl.multiple_of(first, LANES)
    gain = gain_ref[:, pl.ds(first, share)]
    taps = [taps_ref[f, :, pl.ds(first, share)].astype(F32) for f in range(3)]
    taps = [[taps[f][tap : tap + 1] for tap in range(3)] for f in range(3)]

    found = []
    for kind in range(2):
        signal = slice(kind * cols, (kind + 1) * cols)
        spectra = [
            dot(table_ref[side], signal_ref[side * quarter : (side + 1) * quarter, signal])
            for side in range(RADIX)
        ]
        multiply_rows(spectra, spec_ref, prod_ref, points, kind)
    for kind in range(2):
        signal = slice(kind * cols, (kind + 1) * cols)
        found.append([dot(back_ref[side], prod_ref[side, :, signal]) for side in range(RADIX)])

    alphas = [(point + 0.5) / points for point in range(points)]
    carried = [[jnp.zeros((GROUP, share), F32)] * points for _ in range(3)]
    lane, row = iota((GROUP, LANES), 1), iota((GROUP, LANES), 0)
    for start in reversed(range(0, quarter, CHUNK)):
        block, inside = start // block_part, start % block_part
        if inside + CHUNK == block_part:
            means = [jnp.zeros((GROUP, LANES), F32)] * 2
        kept = [{} for _ in range(RADIX)]
        for offset in reversed(range(0, CHUNK, GROUP)):
            here = slice(start + offset, start + offset + GROUP)
            sides = []
            for side in range(RADIX):
                rows = slice(side * quarter + start + offset, side * quarter + start + offset + GROUP)
                sent = pl.ds(side * block_part + inside, CHUNK)
                upstream = msg_ref[block, sent, :].astype(F32)[offset : offset + GROUP]
                both = pl.ds(side * quarter + start, CHUNK)
                base = pair_ref[1, both, :].astype(F32)[offset : offset + GROUP]
                diff = pair_ref[0, both, :].astype(F32)[offset : offset + GROUP] - base
                sides.append([rows, upstream, base, diff] + [jnp.zeros((GROUP, share), F32)] * 3)
            for point in reversed(range(points)):
                lanes = slice(point * share, (point + 1) * share)
                by_tap = []
                for side in range(RADIX):
                    rows, upstream = sides[side][:2]
                    grad_z = found[1][side][here, lanes]
                    grads = (
                        upstream * found[0][side][here, lanes],
                        grad_z * v_ref[rows, lanes],
                        grad_z * k_ref[rows, lanes],
                    )
                    by_tap.append([sum(taps[f][tap] * grads[f] for f in range(3)) for tap in range(3)])
                ahead = []
                for slot, value in enumerate((by_tap[0][1], by_tap[0][2], by_tap[1][2])):
                    window = jnp.concatenate([value, carried[slot][point]], 0)
                    carried[slot][point] = value
                    ahead.append(window[1 : 1 + GROUP])
                by_tap += [[None, ahead[0], ahead[1]], [None, None, ahead[2]]]
                for side in range(RADIX):
                    rows, _, base, diff, total, sum_tok, sum_both = sides[side]
                    inv = inv_ref[rows, lanes]
                    along = inv * (by_tap[side][0] + by_tap[side + 1][1] + by_tap[side + 2][2])
                    total = total + along
                    along = along * (base + alphas[point] * diff) * (inv * inv)
                    sides[side][4:] = [total, sum_tok + alphas[point] * along, sum_both + along]
            for side in range(RADIX):
                _, _, _, _, total, sum_tok, sum_both = sides[side]
                kept[side][offset] = gain * total
                for kind, value in enumerate((gain * sum_tok, gain * (sum_both - sum_tok))):
                    value = jnp.sum(value, 1, keepdims=True)
                    at = lane == row + (side * block_part + inside + offset)
                    means[kind] = means[kind] + jnp.where(at, value, 0.0)
        for side in range(RADIX):
            total = jnp.concatenate([kept[side][offset] for offset in range(0, CHUNK, GROUP)], 0)
            grad_ref[block, pl.ds(side * block_part + inside, CHUNK), :] = total.astype(BF16)
        if inside == 0:
            sent = []
            for value in means:
                value = jnp.sum(value, 0, keepdims=True) / width
                high = value.astype(BF16).astype(F32)
                sent += [high, value - high]
            sent.append(jnp.zeros((grad_ref.shape[1] - LANES - len(sent), LANES), F32))
            grad_ref[block, LANES:, :] = jnp.concatenate(sent, 0).astype(BF16)


def partial_kernel(grad_ref, *out_refs):
    rows, _ = out_refs[0].shape
    n_ctx = grad_ref.shape[0]
    each = n_ctx // len(out_refs)
    spare = sum(grad_ref[block, LANES:, :].astype(F32) for block in range(n_ctx))
    sums = [spare[0:1] + spare[1:2], spare[2:3] + spare[3:4]]
    sent = []
    for value in sums:
        high = value.astype(BF16).astype(F32)
        sent += [high, value - high]
    sent.append(jnp.zeros((rows - each * LANES - len(sent), LANES), F32))
    sent = jnp.concatenate(sent, 0).astype(BF16)
    path = lax.axis_index("path")
    for step, ref in enumerate(out_refs):
        dest = path ^ step
        for piece in range(each):
            ref[piece * LANES : (piece + 1) * LANES, :] = grad_ref[dest * each + piece, :LANES, :]
        ref[each * LANES :, :] = sent


def finish_kernel(own_ref, *refs):
    grad_refs, (path_hbm, attr_hbm, path_ref, attr_ref, sems) = refs[:-5], refs[-5:]
    points = len(grad_refs)
    rows, share = grad_refs[0].shape
    pieces = rows // LANES
    spare = sum(ref[pieces * LANES :, :].astype(F32) for ref in grad_refs)
    lane = iota((LANES, LANES), 1)
    part = LANES // RADIX
    order = (iota((LANES, LANES), 0) == RADIX * (lane % part) + lane // part).astype(F32).astype(BF16)
    left, split = jnp.concatenate([spare[0:1] + spare[1:2], spare[2:3] + spare[3:4]], 0), []
    for _ in range(3):
        split.append(left.astype(BF16).astype(F32))
        left = left - split[-1]
    split = jnp.concatenate(split + [jnp.zeros((2, LANES), F32)], 0).astype(BF16)
    columns = lax.dot_general(order, split, (((1,), (1,)), ((), ())), preferred_element_type=F32)
    to_tok = columns[:, 0:1] + columns[:, 2:3] + columns[:, 4:5]
    to_base = columns[:, 1:2] + columns[:, 3:4] + columns[:, 5:6]
    path = lax.axis_index("path")
    copies = []
    for step, ref in enumerate(grad_refs):
        for piece in range(pieces):
            slot = step * pieces + piece
            first = (piece * points + (path ^ step)) * share
            lanes = pl.ds(pl.multiple_of(first, LANES), share)
            tok = own_ref[0, :, lanes].astype(F32)
            base = own_ref[1, :, lanes].astype(F32)
            grad = dot(order, ref[piece * LANES : (piece + 1) * LANES, :])
            grad = (grad - tok * to_tok - base * to_base) / points
            path_ref[slot] = grad
            attr_ref[slot] = (tok - base) * grad
            for kind, (source, target) in enumerate(((path_ref, path_hbm), (attr_ref, attr_hbm))):
                copies.append(
                    pltpu.make_async_copy(source.at[slot], target.at[:, lanes], sems.at[kind, slot])
                )
                copies[-1].start()
    for copy in copies:
        copy.wait()


def any_spec():
    return pl.BlockSpec(memory_space=pl.ANY)


def vmem_spec():
    return pl.BlockSpec(memory_space=pltpu.VMEM)


def hbm_spec():
    return pl.BlockSpec(memory_space=pltpu.HBM)


def call(kernel, ins, outs, scratch, flops, moved, mebibytes):
    return pl.pallas_call(
        kernel,
        in_specs=ins,
        out_specs=[spec for spec, _ in outs],
        out_shape=[shape for _, shape in outs],
        scratch_shapes=scratch,
        compiler_params=pltpu.CompilerParams(vmem_limit_bytes=mebibytes * 2**20),
        cost_estimate=pl.CostEstimate(flops=flops, bytes_accessed=moved, transcendentals=0),
    )


def shape(dims, dtype):
    return jax.ShapeDtypeStruct(dims, dtype)


def kernel_body(tokens, sub_pos, sub_base, embed, norm_gain, fir_taps, long_filter, skip_gain, cotangent):
    n_path, n_ctx = lax.axis_size("path"), lax.axis_size("ctx")
    points = n_path
    tok_rows = tokens.shape[0]
    length = tok_rows * n_ctx
    vocab, width = embed.shape
    share = width // (n_path * n_ctx)
    subs = sub_pos.shape[0] * n_ctx
    own_width = width // n_path
    cols = points * share
    quarter = length // RADIX
    tables = dft_tables(length)
    dma = pltpu.SemaphoreType.DMA
    transform_flops = length * length
    spare = 8

    msg, ids = call(
        pack_kernel,
        [hbm_spec()] * 4,
        [
            (vmem_spec(), shape((n_ctx, tok_rows + spare, share), BF16)),
            (vmem_spec(), shape((spare, LANES), F32)),
        ],
        [
            pltpu.VMEM((1, tok_rows), jnp.int32),
            pltpu.VMEM((1, sub_pos.shape[0]), jnp.int32),
            pltpu.VMEM((1, sub_pos.shape[0]), jnp.int32),
            pltpu.VMEM((tok_rows, n_ctx * share), BF16),
            dma((n_ctx + 3,)),
        ],
        length * share,
        8 * length * share,
        60,
    )(
        tokens.reshape(1, tok_rows),
        sub_pos.reshape(1, -1),
        sub_base.reshape(1, -1),
        cotangent,
    )
    msg = lax.all_to_all(msg, "ctx", 0, 0, tiled=True)

    gain = norm_gain.reshape(1, width)
    skip = skip_gain.reshape(1, n_path * share)
    spec, gram = call(
        prepare_kernel,
        [hbm_spec()] * 4 + [any_spec()],
        [
            (any_spec(), shape((2 * RADIX, quarter, share), F32)),
            (any_spec(), shape((3 * vocab + vocab // 2, vocab), BF16)),
        ],
        [
            pltpu.VMEM((length, share), F32),
            pltpu.VMEM((RADIX, 2 * quarter, quarter), BF16),
            pltpu.VMEM((vocab, width), BF16),
            pltpu.VMEM((1, share), F32),
            pltpu.VMEM((vocab, vocab), F32),
            pltpu.VMEM((2 * RADIX, quarter, share), F32),
            pltpu.VMEM((3 * vocab + vocab // 2, vocab), BF16),
            dma((7,)),
            dma((3 * vocab // LANES + 2,)),
        ],
        2 * vocab * vocab * width,
        2 * vocab * width,
        58,
    )(long_filter, tables[0], embed, skip, ids)

    hots, subs_hots, put_hots = call(
        functools.partial(ids_kernel, vocab),
        [vmem_spec()],
        [
            (vmem_spec(), shape((length, vocab), BF16)),
            (vmem_spec(), shape((2 * subs, vocab), BF16)),
            (vmem_spec(), shape((length, 2 * subs), BF16)),
        ],
        [],
        2 * 10**9,
        4 * 10**6,
        8,
    )(msg)
    wide = 4 * LANES
    signal, k_feat, v_feat, inv, pair = call(
        functools.partial(feature_kernel, points),
        [vmem_spec()] * 7 + [hbm_spec()],
        [(vmem_spec(), shape((length, 2 * cols), BF16))]
        + [(vmem_spec(), shape((length, cols), F32))] * 3
        + [(vmem_spec(), shape((2, length, share), BF16))],
        [
            pltpu.VMEM((vocab, wide), BF16),
            pltpu.VMEM((points, subs, LANES), F32),
            pltpu.VMEM((2 * subs, wide), F32),
            pltpu.VMEM((length, 2 * share), F32),
            pltpu.VMEM((length, (2 + points) * share), F32),
            dma,
        ],
        2 * length * vocab * 3 * share,
        2 * vocab * width + 16 * length * cols,
        39,
    )(msg, hots, subs_hots, put_hots, gram, fir_taps, gain, embed)

    grad = call(
        functools.partial(gradient_kernel, points, width),
        [vmem_spec()] * 11,
        [(vmem_spec(), shape((n_ctx, tok_rows + spare, share), BF16))],
        [
            pltpu.VMEM((RADIX, 2 * quarter, 2 * cols), BF16),
        ],
        4 * transform_flops * cols,
        4 * length * length + 16 * length * cols,
        32,
    )(msg, pair, fir_taps, gain, signal, k_feat, v_feat, inv, *tables, spec)[0]

    own = call(
        own_kernel,
        [vmem_spec(), vmem_spec(), any_spec()],
        [(vmem_spec(), shape((2, tok_rows, own_width), BF16))],
        [],
        4 * tok_rows * vocab * own_width,
        2 * vocab * own_width,
        10,
    )(ids, embed, grad)[0]
    grad = lax.all_to_all(grad, "ctx", 0, 0, tiled=True)
    each = n_ctx // n_path
    parts = call(
        partial_kernel,
        [vmem_spec()],
        [(vmem_spec(), shape((each * tok_rows + spare, share), BF16))] * n_path,
        [],
        spare * LANES * n_ctx,
        4 * length * share,
        4,
    )(grad)
    parts = [
        part if step == 0 else lax.ppermute(part, "path", [(p, p ^ step) for p in range(n_path)])
        for step, part in enumerate(parts)
    ]
    out = shape((tok_rows, own_width), F32)
    return tuple(
        call(
            finish_kernel,
            [vmem_spec()] * (1 + n_path),
            [(any_spec(), out), (any_spec(), out)],
            [pltpu.VMEM((n_path * each, tok_rows, share), F32)] * 2 + [dma((2, n_path * each))],
            8 * tok_rows * own_width,
            14 * tok_rows * own_width,
            8,
        )(own, *parts)
    )


def plain_body(tokens, sub_pos, sub_base, embed, norm_gain, fir_taps, long_filter, skip_gain, cotangent):
    n_path, n_ctx = lax.axis_size("path"), lax.axis_size("ctx")
    path, ctx = lax.axis_index("path"), lax.axis_index("ctx")
    points = n_path
    tok_rows = tokens.shape[0]
    length = tok_rows * n_ctx
    width = embed.shape[1]
    share = width // (n_path * n_ctx)
    own_width = width // n_path
    first = (ctx * n_path + path) * share
    alphas = ((jnp.arange(points, dtype=jnp.int32)).astype(F32) + 0.5) / points
    alphas = alphas[:, None, None]

    local = jnp.arange(tok_rows, dtype=jnp.int32)[:, None] + ctx * tok_rows == sub_pos[None, :]
    put = jnp.sum(jnp.where(local, sub_base[None, :], 0), 1)
    base_ids = jnp.where(jnp.any(local, 1), put, tokens)
    rows_tok = jnp.take(embed, tokens, axis=0).astype(F32)
    rows_base = jnp.take(embed, base_ids, axis=0).astype(F32)
    rows_in = rows_base[None] + alphas * (rows_tok - rows_base)[None]
    inv = lax.rsqrt(jnp.mean(rows_in * rows_in, -1) + EPS)
    inv = lax.all_gather(inv, "ctx", axis=1, tiled=True)[:, :, None]
    all_tok = lax.all_gather(tokens, "ctx", tiled=True)
    all_base = lax.all_gather(base_ids, "ctx", tiled=True)

    cot = cotangent.reshape(tok_rows, n_ctx, n_path, share)
    cot = lax.dynamic_index_in_dim(cot, path, 2, keepdims=False)
    cot = lax.all_to_all(cot.transpose(1, 0, 2), "ctx", 0, 0, tiled=True)
    upstream = cot.reshape(1, length, share).astype(F32)
    mine = lax.dynamic_slice_in_dim(embed, first, share, 1)
    gain = lax.dynamic_slice_in_dim(norm_gain, first, share, 0)
    taps = lax.dynamic_slice_in_dim(fir_taps, first, share, 2).astype(F32)
    filt = lax.dynamic_slice_in_dim(long_filter, path * share, share, 1)
    skip = lax.dynamic_slice_in_dim(skip_gain, path * share, share, 0)

    emb_tok = jnp.take(mine, all_tok, axis=0).astype(F32)
    emb_base = jnp.take(mine, all_base, axis=0).astype(F32)
    inputs = emb_base[None] + alphas * (emb_tok - emb_base)[None]
    normed = rounded(inputs * inv * gain)
    q_feat, k_feat, v_feat = (
        taps[f, 0] * normed + taps[f, 1] * shifted(normed, 1) + taps[f, 2] * shifted(normed, 2)
        for f in range(3)
    )
    filter_spec = spectrum(filt[None])
    conv = rounded(long_conv(rounded(k_feat * v_feat), filter_spec, skip, False))
    grad_z = rounded(long_conv(rounded(upstream * q_feat), filter_spec, skip, True))
    grads = (rounded(upstream * conv), rounded(grad_z * v_feat), rounded(grad_z * k_feat))
    by_tap = [sum(taps[f, tap] * grads[f] for f in range(3)) for tap in range(3)]
    scaled = gain * (by_tap[0] + shifted(by_tap[1], -1) + shifted(by_tap[2], -2))
    grad = jnp.sum(inv * scaled, 0).astype(BF16)
    along = jnp.sum(inputs * scaled, -1, keepdims=True) * inv**3 / width
    part = jnp.stack([jnp.sum(alphas * along, 0)[:, 0], jnp.sum((1.0 - alphas) * along, 0)[:, 0]])
    part = lax.psum(part, ("path", "ctx"))
    part = lax.dynamic_slice_in_dim(part, ctx * tok_rows, tok_rows, 1)

    back = lax.all_to_all(grad.reshape(n_ctx, tok_rows, share), "ctx", 0, 0, tiled=True)
    back = back.reshape(n_path, n_ctx // n_path, tok_rows, share)
    back = lax.all_to_all(back, "path", 0, 0, tiled=True).astype(F32)
    back = back.transpose(2, 1, 0, 3).reshape(tok_rows, own_width)
    own_tok = lax.dynamic_slice_in_dim(rows_tok, path * own_width, own_width, 1)
    own_base = lax.dynamic_slice_in_dim(rows_base, path * own_width, own_width, 1)
    grad = (back - own_tok * part[0][:, None] - own_base * part[1][:, None]) / points
    return (grad, (own_tok - own_base) * grad)


def body(tokens, sub_pos, sub_base, embed, *rest):
    n_path, n_ctx = lax.axis_size("path"), lax.axis_size("ctx")
    tok_rows = tokens.shape[0]
    share = embed.shape[1] // (n_path * n_ctx)
    tables = 2 * (tok_rows * n_ctx) ** 2
    fits = share == LANES and tok_rows == LANES and n_ctx == GROUP and tables <= TABLE_BYTES
    fits = fits and n_ctx % n_path == 0 and n_path & (n_path - 1) == 0
    chosen = kernel_body if fits else plain_body
    return chosen(tokens, sub_pos, sub_base, embed, *rest)


def solution(mesh):
    return jax.shard_map(
        body,
        mesh=mesh,
        in_specs=(
            P("ctx"),
            P("ctx"),
            P("ctx"),
            P(),
            P(),
            P(),
            P(None, "ctx"),
            P("ctx"),
            P("ctx", None),
        ),
        out_specs=(P("ctx", "path"), P("ctx", "path")),
        check_vma=False,
    )
```

```python
import functools

import jax
import jax.numpy as jnp
import ml_dtypes
import numpy as np
from jax import lax
from jax.experimental import pallas as pl
from jax.experimental.pallas import tpu as pltpu
from jax.sharding import PartitionSpec as P

LANES = 128
GROUP = 8
RADIX = 4
LOOK_ROWS = 256
CHUNK = 16
EPS = 1e-06
CANCEL = 0.004
TABLE_BYTES = 2**21
F32 = jnp.float32
BF16 = jnp.bfloat16
precise = lax.Precision.HIGH


def angle_tables(length):
    outer_size = 64
    inner_size = length // outer_size
    outer_idx = jnp.arange(outer_size, dtype=jnp.int32)
    inner_idx = jnp.arange(inner_size, dtype=jnp.int32)
    outer_angle = (
        2.0 * jnp.pi / outer_size
        * (outer_idx[:, None] * outer_idx[None, :] % outer_size).astype(F32)
    )
    inner_angle = (
        2.0 * jnp.pi / inner_size
        * (inner_idx[:, None] * inner_idx[None, :] % inner_size).astype(F32)
    )
    twist_angle = (
        2.0 * jnp.pi / length
        * (outer_idx[:, None] * inner_idx[None, :] % length).astype(F32)
    )
    return (outer_angle, inner_angle, twist_angle)


def complex_table(angle, sign):
    cosine = jnp.cos(angle)
    sine = sign * jnp.sin(angle)
    return jnp.stack([jnp.stack([cosine, sine]), jnp.stack([-sine, cosine])])


def twisted(values, angle, sign):
    cosine = jnp.cos(angle)[None, :, :, None]
    sine = sign * jnp.sin(angle)[None, :, :, None]
    real_part = values[:, 0]
    imag_part = values[:, 1]
    return jnp.stack(
        [real_part * cosine - imag_part * sine, real_part * sine + imag_part * cosine], 1
    )


def spectrum(signal):
    batch, half, width = signal.shape
    length = 2 * half
    outer_angle, inner_angle, twist_angle = angle_tables(length)
    outer_size = outer_angle.shape[0]
    inner_size = inner_angle.shape[0]
    folded = signal.reshape(batch, outer_size // 2, inner_size, width)
    used = outer_angle[:, : outer_size // 2]
    outer_table = jnp.stack([jnp.cos(used), -jnp.sin(used)])
    first = jnp.einsum("rka,pabc->prkbc", outer_table, folded, precision=precise)
    turned = twisted(first, twist_angle, -1.0)
    return jnp.einsum(
        "prkbc,rsbm->pskmc", turned, complex_table(inner_angle, -1.0), precision=precise
    )


def inverse(spec):
    batch, parts, outer_size, inner_size, width = spec.shape
    length = outer_size * inner_size
    outer_angle, inner_angle, twist_angle = angle_tables(length)
    back = jnp.einsum("pskmc,stmb->ptkbc", spec, complex_table(inner_angle, 1.0), precision=precise)
    turned = twisted(back, twist_angle, 1.0)
    used = outer_angle[: outer_size // 2]
    outer_table = jnp.stack([jnp.cos(used), -jnp.sin(used)])
    result = jnp.einsum("rak,prkbc->pabc", outer_table, turned, precision=precise)
    return (result / length).reshape(batch, length // 2, width)


def long_conv(signal, filter_spec, skip_gain, adjoint):
    spec = spectrum(signal)
    sig_real = spec[:, 0]
    sig_imag = spec[:, 1]
    filt_real = filter_spec[:, 0]
    filt_imag = filter_spec[:, 1]
    if adjoint:
        prod_real = sig_real * filt_real + sig_imag * filt_imag
        prod_imag = sig_imag * filt_real - sig_real * filt_imag
    else:
        prod_real = sig_real * filt_real - sig_imag * filt_imag
        prod_imag = sig_real * filt_imag + sig_imag * filt_real
    return inverse(jnp.stack([prod_real, prod_imag], 1)) + skip_gain * signal


def rounded(value):
    return value.astype(BF16).astype(F32)


def shifted(values, step):
    zeros = jnp.zeros_like(values[:, : abs(step)])
    if step > 0:
        return jnp.concatenate([zeros, values[:, :-step]], 1)
    return jnp.concatenate([values[:, -step:], zeros], 1)


@functools.lru_cache(maxsize=None)
def dft_tables(length):
    quarter = length // RADIX
    freq = 4 * np.arange(quarter, dtype=np.int64) + 1
    place = np.arange(quarter, dtype=np.int64)
    there, back = [], []
    for offset in range(RADIX):
        turns = freq[:, None] * (RADIX * place + offset)[None, :] % (4 * length)
        angle = turns * (2.0 * np.pi / (4 * length))
        cosine = np.cos(angle).astype(ml_dtypes.bfloat16)
        sine = np.sin(angle).astype(ml_dtypes.bfloat16)
        there.append(np.concatenate([cosine, sine], 0))
        back.append(np.concatenate([cosine.T, sine.T], 1))
    return (np.stack(there), np.stack(back))


def butterfly(values, sign):
    (r0, s0), (r1, s1), (r2, s2), (r3, s3) = values
    sum_r, sum_s, diff_r, diff_s = r0 + r2, s0 + s2, r0 - r2, s0 - s2
    odd_r, odd_s, turn_r, turn_s = r1 + r3, s1 + s3, r1 - r3, s1 - s3
    ahead = (diff_r + turn_s, diff_s - turn_r)
    behind = (diff_r - turn_s, diff_s + turn_r)
    if sign < 0:
        ahead, behind = behind, ahead
    return ((sum_r + odd_r, sum_s + odd_s), ahead, (sum_r - odd_r, sum_s - odd_s), behind)


def transposed(rows):
    count = rows.shape[0]
    if count < LANES:
        rows = jnp.concatenate([rows, jnp.zeros((LANES - count, LANES), F32)], 0)
    return rows.T


def dot(left, right):
    return jnp.dot(left, right, preferred_element_type=F32)


def iota(dims, axis):
    return lax.broadcasted_iota(jnp.int32, dims, axis)


def by_residue():
    row = iota((LANES, LANES), 0)
    part = LANES // RADIX
    source = RADIX * (row % part) + row // part
    return (iota((LANES, LANES), 1) == source).astype(F32)


def hot(ids, vocab):
    lane = iota(ids.shape, 1).astype(F32)
    parts = [
        (ids == lane + float(column * LANES)).astype(F32).astype(BF16)
        for column in range(vocab // LANES)
    ]
    return jnp.concatenate(parts, 1)


def joined(block, kind):
    return 256.0 * block[2 * kind : 2 * kind + 1] + block[2 * kind + 1 : 2 * kind + 2]


def pack_kernel(
    tok_hbm, pos_hbm, put_hbm, cot_hbm, msg_ref, ids_ref, tok_ref, pos_ref, put_ref, cot_ref, sems
):
    dests, rows, share = msg_ref.shape
    tok_rows = cot_hbm.shape[0]
    n_path = cot_hbm.shape[1] // (dests * share)
    path = lax.axis_index("path")
    moves = [(tok_hbm, tok_ref), (pos_hbm, pos_ref), (put_hbm, put_ref)]
    for dest in range(dests):
        lanes = pl.ds(pl.multiple_of((dest * n_path + path) * share, LANES), share)
        moves.append((cot_hbm.at[:, lanes], cot_ref.at[:, pl.ds(dest * share, share)]))
    copies = [
        pltpu.make_async_copy(source, target, sems.at[index])
        for index, (source, target) in enumerate(moves)
    ]
    for copy in copies:
        copy.start()
    order = by_residue().astype(BF16)
    for copy in copies[:3]:
        copy.wait()
    lists = []
    for ref in (tok_ref, pos_ref, put_ref):
        value = ref[...].astype(F32)
        if value.shape[1] < LANES:
            value = jnp.concatenate([value, jnp.zeros((1, LANES - value.shape[1]), F32)], 1)
        high = jnp.floor(value * (1.0 / 256.0))
        lists += [high, value - 256.0 * high]
    lists.append(jnp.zeros((rows - tok_rows - len(lists), LANES), F32))
    ids = jnp.concatenate(lists, 0)
    ids_ref[...] = ids
    turned = lax.dot_general(
        ids.astype(BF16), order, (((1,), (1,)), ((), ())), preferred_element_type=F32
    )
    ids = jnp.where(iota(ids.shape, 0) < 2, turned, ids).astype(BF16)
    for dest in range(dests):
        msg_ref[dest, tok_rows:, :] = ids
    for copy in copies[3:]:
        copy.wait()
    turned = dot(order, cot_ref[...]).astype(BF16)
    for dest in range(dests):
        msg_ref[dest, :tok_rows, :] = turned[:, dest * share : (dest + 1) * share]


def prepare_kernel(
    filt_hbm, table_hbm, embed_hbm, skip_hbm, after_ref,
    spec_hbm, gram_hbm,
    filt_ref, table_ref, embed_ref, skip_ref, sum_ref, spec_ref, gram_ref, sems, out_sems,
):
    length, share = filt_ref.shape
    quarter = length // RADIX
    vocab, width = embed_ref.shape
    pieces = sems.shape[0] - 3
    wide = width // pieces
    path = lax.axis_index("path")
    lanes = pl.ds(pl.multiple_of(path * share, LANES), share)
    moves = [
        (filt_hbm.at[:, lanes], filt_ref),
        (skip_hbm.at[:, lanes], skip_ref),
        (table_hbm, table_ref),
    ]
    for index in range(pieces):
        lanes = pl.ds(index * wide, wide)
        moves.append((embed_hbm.at[:, lanes], embed_ref.at[:, lanes]))
    copies = [
        pltpu.make_async_copy(source, target, sems.at[index])
        for index, (source, target) in enumerate(moves)
    ]
    for copy in copies:
        copy.start()

    copies[0].wait()
    copies[1].wait()
    filt_ref[0:1, :] = filt_ref[0:1, :] + skip_ref[...]
    parts = []
    for offset in range(RADIX):
        value = filt_ref[pl.ds(offset, quarter, stride=RADIX), :] * (1.0 / length)
        high = value.astype(BF16)
        parts.append(jnp.concatenate([high, (value - high.astype(F32)).astype(BF16)], 1))
    copies[2].wait()
    found = []
    for offset in range(RADIX):
        both = dot(table_ref[offset], parts[offset])
        both = both[:, :share] + both[:, share:]
        found.append((both[:quarter], both[quarter:]))
    for part, (real, imag) in enumerate(butterfly(found, -1)):
        spec_ref[2 * part] = real
        spec_ref[2 * part + 1] = imag
    outs = [pltpu.make_async_copy(spec_ref, spec_hbm, out_sems.at[0])]
    outs[0].start()

    sum_ref[vocab // 2 :, : vocab // 2] = jnp.zeros((vocab // 2, vocab // 2), F32)
    for index in range(pieces):
        copies[3 + index].wait()
        part = embed_ref[:, index * wide : (index + 1) * wide]
        for rows, lanes in ((slice(0, vocab // 2), slice(0, vocab)), (slice(vocab // 2, vocab),) * 2):
            found = lax.dot_general(
                part[rows], part[lanes], (((1,), (1,)), ((), ())), preferred_element_type=F32
            )
            if index == 0:
                sum_ref[rows, lanes] = found
            else:
                sum_ref[rows, lanes] += found
    first = (lax.axis_index("ctx") * lax.axis_size("path") + path) * share
    mine = embed_ref[:, pl.ds(pl.multiple_of(first, LANES), share)]
    same = iota((LANES, LANES), 0) == iota((LANES, LANES), 1)
    lane = iota((LANES, LANES), 1)
    below = 3 * vocab
    for block in range(vocab // LANES):
        rows = slice(block * LANES, (block + 1) * LANES)
        value = sum_ref[rows, :]
        norm = jnp.sum(jnp.where(same, value[:, rows], 0.0), 1, keepdims=True)
        inv = jnp.broadcast_to(lax.rsqrt(norm / width + EPS), (LANES, LANES))
        high = inv.astype(BF16).astype(F32)
        inv = jnp.where(lane < LANES // 2, high, inv - high).astype(BF16)
        side, start = block * LANES // (vocab // 2), block * LANES % (vocab // 2)
        into = slice(below + start, below + start + LANES)
        left = side * (share + LANES)
        gram_ref[into, left : left + share] = mine[rows]
        gram_ref[into, left + share : left + share + LANES] = inv
        for part in range(3):
            high = value.astype(BF16)
            into = slice(part * vocab + block * LANES, part * vocab + (block + 1) * LANES)
            gram_ref[into, :] = high
            value = value - high.astype(F32)
            into = pl.ds(part * vocab + block * LANES, LANES)
            sem = out_sems.at[1 + block * 3 + part]
            outs.append(pltpu.make_async_copy(gram_ref.at[into], gram_hbm.at[into], sem))
            outs[-1].start()
    into = pl.ds(below, vocab // 2)
    outs.append(pltpu.make_async_copy(gram_ref.at[into], gram_hbm.at[into], out_sems.at[out_sems.shape[0] - 1]))
    outs[-1].start()
    for copy in outs:
        copy.wait()


def own_kernel(ids_ref, embed_ref, grad_ref, own_ref):
    vocab = embed_ref.shape[0]
    own_width = own_ref.shape[2]
    lanes = pl.ds(pl.multiple_of(lax.axis_index("path") * own_width, LANES), own_width)
    ids = ids_ref[...]
    columns = transposed(jnp.concatenate([joined(ids, kind) for kind in range(3)], 0))
    tok = jnp.broadcast_to(columns[:, 0:1], (LANES, LANES))
    place = jnp.broadcast_to(joined(ids, 1), (LANES, LANES))
    put = jnp.broadcast_to(joined(ids, 2), (LANES, LANES))
    first = lax.axis_index("ctx") * LANES
    subs = LANES // GROUP
    here = (place == (iota((LANES, LANES), 0) + first).astype(F32)) & (iota((LANES, LANES), 1) < subs)
    found = jnp.max(jnp.where(here, put, -1.0), 1, keepdims=True)
    base = jnp.where(found >= 0.0, found, tok)
    hots = jnp.concatenate([hot(tok, vocab), hot(base, vocab)], 0)
    both = dot(hots, embed_ref[:, lanes]).astype(BF16)
    own_ref[0] = both[:LANES]
    own_ref[1] = both[LANES:]


def multiply_rows(found, spec_ref, prod_ref, points, kind):
    _, quarter, share = spec_ref.shape
    for start in range(0, quarter, CHUNK):
        here = slice(start, start + CHUNK)
        after = slice(quarter + start, quarter + start + CHUNK)
        filt = [(spec_ref[2 * part, here, :], spec_ref[2 * part + 1, here, :]) for part in range(RADIX)]
        for point in range(points):
            lanes = slice((kind * points + point) * share, (kind * points + point + 1) * share)
            values = butterfly([(value[here, lanes], value[after, lanes]) for value in found], -1)
            prods = []
            for (real, imag), (filt_real, filt_imag) in zip(values, filt):
                if kind == 1:
                    prods.append((real * filt_real + imag * filt_imag, imag * filt_real - real * filt_imag))
                else:
                    prods.append((real * filt_real - imag * filt_imag, imag * filt_real + real * filt_imag))
            for part, (real, imag) in enumerate(butterfly(prods, 1)):
                prod_ref[part, here, lanes] = real.astype(BF16)
                prod_ref[part, after, lanes] = imag.astype(BF16)


def ids_kernel(vocab, msg_ref, hot_ref, subs_ref, put_ref):
    length = hot_ref.shape[0]
    quarter = length // RADIX
    n_ctx = msg_ref.shape[0]
    block_part = LANES // RADIX
    per_block = LANES // GROUP
    subs = n_ctx * per_block
    blocks = [msg_ref[block, LANES:, :].astype(F32) for block in range(n_ctx)]
    toks = transposed(jnp.concatenate([joined(block, 0) for block in blocks], 0))
    spread = sum(
        blocks[block] if block == 0 else pltpu.roll(blocks[block], block * per_block, 1)
        for block in range(n_ctx)
    )
    place = joined(spread, 1)
    put = joined(spread, 2)
    back = jnp.floor(place * (1.0 / RADIX))
    place = back + (place - RADIX * back) * quarter
    columns = transposed(jnp.concatenate([place, put], 0))
    for block in range(n_ctx):
        column = jnp.broadcast_to(toks[:, block : block + 1], (LANES, LANES))
        rows = hot(column, vocab)
        for side in range(RADIX):
            first = side * quarter + block * block_part
            hot_ref[first : first + block_part, :] = rows[side * block_part : (side + 1) * block_part]
    subs_ref[subs:, :] = hot(jnp.broadcast_to(columns[:, 1:2], (subs, LANES)), vocab)
    pick = jnp.concatenate(
        [
            (columns[:, 0:1] == (iota((subs, LANES), 1) + part * LANES).astype(F32)).astype(F32).astype(BF16)
            for part in range(length // LANES)
        ],
        1,
    )
    for index in range(length // LANES):
        row = (iota((LANES, subs), 0) + index * LANES).astype(F32)
        here = (row == place[:, :subs]).astype(F32).astype(BF16)
        put_ref[index * LANES : (index + 1) * LANES, :] = jnp.concatenate([here, here], 1)
    subs_ref[:subs, :] = dot(pick, hot_ref[...]).astype(BF16)


def feature_kernel(
    points, msg_ref, hot_ref, subs_hot_ref, put_ref, gram_ref, taps_ref, gain_ref, embed_hbm,
    signal_ref, k_ref, v_ref, inv_ref, pair_ref,
    embed_ref, sums_ref, found_ref, look_ref, subs_ref, sem,
):
    length = signal_ref.shape[0]
    quarter = length // RADIX
    vocab, width = embed_hbm.shape
    share = pair_ref.shape[2]
    subs = subs_hot_ref.shape[0] // 2
    first = (lax.axis_index("ctx") * points + lax.axis_index("path")) * share
    first = pl.multiple_of(first, LANES)
    below = 3 * vocab
    table = jnp.concatenate(
        [gram_ref[below:, : share + LANES], gram_ref[below:, share + LANES :]], 0
    )

    for index in range(length // LOOK_ROWS):
        rows = pl.ds(index * LOOK_ROWS, LOOK_ROWS)
        look_ref[rows, :] = dot(hot_ref[rows, :], table)

    alphas = [(point + 0.5) / points for point in range(points)]
    hots = subs_hot_ref[...]
    found = dot(jnp.concatenate([hots] * 3, 1), gram_ref[:below, :])
    hot_tok32, hot_base32 = hots[:subs].astype(F32), hots[subs:].astype(F32)
    tok_tok = jnp.sum(found[:subs] * hot_tok32, 1, keepdims=True)
    tok_base = jnp.sum(found[:subs] * hot_base32, 1, keepdims=True)
    base_tok = jnp.sum(found[subs:] * hot_tok32, 1, keepdims=True)
    tok_base = jnp.where(tok_base == 0.0, base_tok, tok_base)
    base_base = jnp.sum(found[subs:] * hot_base32, 1, keepdims=True)
    cancels = jnp.zeros((subs, 1), F32)
    for point in range(points):
        alpha = alphas[point]
        terms = (1.0 - alpha) ** 2 * base_base + alpha**2 * tok_tok
        total = terms + 2.0 * alpha * (1.0 - alpha) * tok_base
        cancels = jnp.maximum(cancels, (total < CANCEL * terms).astype(F32))
        inv = lax.rsqrt(jnp.maximum(total, 0.0) / width + EPS)
        sums_ref[point] = jnp.broadcast_to(inv, (subs, LANES))

    @pl.when(jnp.max(cancels) > 0.5)
    def _():
        sums_ref[...] = jnp.zeros_like(sums_ref)
        wide = found_ref.shape[1]

        @pl.loop(0, width // wide)
        def _(step):
            lanes = pl.ds(pl.multiple_of(step * wide, wide), wide)
            copy = pltpu.make_async_copy(embed_hbm.at[:, lanes], embed_ref, sem)
            copy.start()
            copy.wait()
            found_ref[...] = dot(hots, embed_ref[...])
            for block in range(subs // GROUP):
                rows = slice(block * GROUP, (block + 1) * GROUP)
                sums = [sums_ref[point, rows, :] for point in range(points)]
                for column in range(wide // LANES):
                    cut = slice(column * LANES, (column + 1) * LANES)
                    base = found_ref[subs + block * GROUP : subs + (block + 1) * GROUP, cut]
                    diff = found_ref[rows, cut] - base
                    for point in range(points):
                        value = base + alphas[point] * diff
                        sums[point] = sums[point] + value * value
                for point in range(points):
                    sums_ref[point, rows, :] = sums[point]

        for point in range(points):
            mean = jnp.sum(sums_ref[point], 1, keepdims=True) / width
            sums_ref[point] = jnp.broadcast_to(lax.rsqrt(mean + EPS), (subs, LANES))

    high = [dot(hots[subs:], table[:, :share]), jnp.ones((subs, LANES), F32)]
    low = [jnp.zeros((subs, LANES), F32)] * 2
    for point in range(points):
        inv = sums_ref[point]
        high.append(inv.astype(BF16).astype(F32))
        low.append(inv - high[-1])
    held = jnp.concatenate([jnp.concatenate(high, 1), jnp.concatenate(low, 1)], 0).astype(BF16)
    for index in range(length // LOOK_ROWS):
        rows = pl.ds(index * LOOK_ROWS, LOOK_ROWS)
        subs_ref[rows, :] = dot(put_ref[rows, :], held)

    cols = points * share
    block_part = LANES // RADIX
    last = {side: [jnp.zeros((GROUP, share), F32)] * points for side in (RADIX - 2, RADIX - 1)}
    gain = gain_ref[:, pl.ds(first, share)]
    taps = [taps_ref[f, :, pl.ds(first, share)].astype(F32) for f in range(3)]
    taps = [[taps[f][tap : tap + 1] for tap in range(3)] for f in range(3)]

    for start in range(0, quarter, CHUNK):
        block, inside = start // block_part, start % block_part
        sides = []
        for side in range(RADIX):
            rows = pl.ds(side * quarter + start, CHUNK)
            tok = look_ref[rows, :share]
            inv = look_ref[rows, share:]
            inv = inv + pltpu.roll(inv, LANES // 2, 1)
            chosen = subs_ref[rows, share : 2 * share] > 0.5
            base = jnp.where(chosen, subs_ref[rows, :share], tok)
            pair_ref[0, rows, :] = tok.astype(BF16)
            pair_ref[1, rows, :] = base.astype(BF16)
            sent = pl.ds(side * block_part + inside, CHUNK)
            upstream = msg_ref[block, sent, :].astype(F32)
            sides.append((rows, gain * base, gain * (tok - base), inv, chosen, upstream))
        for point in range(points):
            lanes = slice(point * share, (point + 1) * share)
            recent = []
            for rows, base, diff, inv_tok, chosen, _ in sides:
                inv = jnp.where(
                    chosen, subs_ref[rows, (2 + point) * share : (3 + point) * share], inv_tok
                )
                inv_ref[rows, lanes] = inv
                recent.append(rounded((base + alphas[point] * diff) * inv))
            backs = []
            for side in (RADIX - 2, RADIX - 1):
                window = jnp.concatenate([last[side][point], recent[side]], 0)
                last[side][point] = recent[side][CHUNK - GROUP :]
                backs.append(window[GROUP - 1 : GROUP - 1 + CHUNK])
            recent = backs + recent
            for side in range(RADIX):
                rows, upstream = sides[side][0], sides[side][5]
                feats = [sum(taps[f][tap] * recent[side + 2 - tap] for tap in range(3)) for f in range(3)]
                k_ref[rows, lanes] = feats[1]
                v_ref[rows, lanes] = feats[2]
                signal_ref[rows, lanes] = (feats[1] * feats[2]).astype(BF16)
                after = slice(cols + point * share, cols + (point + 1) * share)
                signal_ref[rows, after] = (upstream * feats[0]).astype(BF16)


def gradient_kernel(
    points, width, msg_ref, pair_ref, taps_ref, gain_ref,
    signal_ref, k_ref, v_ref, inv_ref, table_ref, back_ref, spec_ref,
    grad_ref,
    prod_ref,
):
    _, quarter, share = spec_ref.shape
    cols = points * share
    n_ctx = msg_ref.shape[0]
    block_part = LANES // RADIX
    first = (lax.axis_index("ctx") * points + lax.axis_index("path")) * share
    first = pl.multiple_of(first, LANES)
    gain = gain_ref[:, pl.ds(first, share)]
    taps = [taps_ref[f, :, pl.ds(first, share)].astype(F32) for f in range(3)]
    taps = [[taps[f][tap : tap + 1] for tap in range(3)] for f in range(3)]

    spectra = [
        dot(table_ref[side], signal_ref[side * quarter : (side + 1) * quarter, :]) for side in range(RADIX)
    ]
    for kind in range(2):
        multiply_rows(spectra, spec_ref, prod_ref, points, kind)
    found = [dot(back_ref[side], prod_ref[side]) for side in range(RADIX)]

    alphas = [(point + 0.5) / points for point in range(points)]
    carried = [[jnp.zeros((GROUP, share), F32)] * points for _ in range(3)]
    lane, row = iota((GROUP, LANES), 1), iota((GROUP, LANES), 0)
    for start in reversed(range(0, quarter, CHUNK)):
        block, inside = start // block_part, start % block_part
        if inside + CHUNK == block_part:
            means = [jnp.zeros((GROUP, LANES), F32)] * 2
        kept = [{} for _ in range(RADIX)]
        for offset in reversed(range(0, CHUNK, GROUP)):
            here = slice(start + offset, start + offset + GROUP)
            sides = []
            for side in range(RADIX):
                rows = slice(side * quarter + start + offset, side * quarter + start + offset + GROUP)
                sent = pl.ds(side * block_part + inside, CHUNK)
                upstream = msg_ref[block, sent, :].astype(F32)[offset : offset + GROUP]
                both = pl.ds(side * quarter + start, CHUNK)
                base = pair_ref[1, both, :].astype(F32)[offset : offset + GROUP]
                diff = pair_ref[0, both, :].astype(F32)[offset : offset + GROUP] - base
                sides.append([rows, upstream, base, diff] + [jnp.zeros((GROUP, share), F32)] * 3)
            for point in reversed(range(points)):
                lanes = slice(point * share, (point + 1) * share)
                by_tap = []
                for side in range(RADIX):
                    rows, upstream = sides[side][:2]
                    grad_z = found[side][here, cols + point * share : cols + (point + 1) * share]
                    grads = (
                        upstream * found[side][here, lanes],
                        grad_z * v_ref[rows, lanes],
                        grad_z * k_ref[rows, lanes],
                    )
                    by_tap.append([sum(taps[f][tap] * grads[f] for f in range(3)) for tap in range(3)])
                ahead = []
                for slot, value in enumerate((by_tap[0][1], by_tap[0][2], by_tap[1][2])):
                    window = jnp.concatenate([value, carried[slot][point]], 0)
                    carried[slot][point] = value
                    ahead.append(window[1 : 1 + GROUP])
                by_tap += [[None, ahead[0], ahead[1]], [None, None, ahead[2]]]
                for side in range(RADIX):
                    rows, _, base, diff, total, sum_tok, sum_both = sides[side]
                    inv = inv_ref[rows, lanes]
                    along = inv * (by_tap[side][0] + by_tap[side + 1][1] + by_tap[side + 2][2])
                    total = total + along
                    along = along * (base + alphas[point] * diff) * (inv * inv)
                    sides[side][4:] = [total, sum_tok + alphas[point] * along, sum_both + along]
            for side in range(RADIX):
                _, _, _, _, total, sum_tok, sum_both = sides[side]
                kept[side][offset] = gain * total
                for kind, value in enumerate((gain * sum_tok, gain * (sum_both - sum_tok))):
                    value = jnp.sum(value, 1, keepdims=True)
                    at = lane == row + (side * block_part + inside + offset)
                    means[kind] = means[kind] + jnp.where(at, value, 0.0)
        for side in range(RADIX):
            total = jnp.concatenate([kept[side][offset] for offset in range(0, CHUNK, GROUP)], 0)
            grad_ref[block, pl.ds(side * block_part + inside, CHUNK), :] = total.astype(BF16)
        if inside == 0:
            sent = []
            for value in means:
                value = jnp.sum(value, 0, keepdims=True) / width
                high = value.astype(BF16).astype(F32)
                sent += [high, value - high]
            sent.append(jnp.zeros((grad_ref.shape[1] - LANES - len(sent), LANES), F32))
            grad_ref[block, LANES:, :] = jnp.concatenate(sent, 0).astype(BF16)


def partial_kernel(grad_ref, *out_refs):
    rows, _ = out_refs[0].shape
    n_ctx = grad_ref.shape[0]
    each = n_ctx // len(out_refs)
    spare = sum(grad_ref[block, LANES:, :].astype(F32) for block in range(n_ctx))
    sums = [spare[0:1] + spare[1:2], spare[2:3] + spare[3:4]]
    sent = []
    for value in sums:
        high = value.astype(BF16).astype(F32)
        sent += [high, value - high]
    sent.append(jnp.zeros((rows - each * LANES - len(sent), LANES), F32))
    sent = jnp.concatenate(sent, 0).astype(BF16)
    path = lax.axis_index("path")
    for step, ref in enumerate(out_refs):
        dest = path ^ step
        for piece in range(each):
            ref[piece * LANES : (piece + 1) * LANES, :] = grad_ref[dest * each + piece, :LANES, :]
        ref[each * LANES :, :] = sent


def finish_kernel(own_ref, *refs):
    grad_refs, (path_hbm, attr_hbm, path_ref, attr_ref, sems) = refs[:-5], refs[-5:]
    points = len(grad_refs)
    rows, share = grad_refs[0].shape
    pieces = rows // LANES
    spare = sum(ref[pieces * LANES :, :].astype(F32) for ref in grad_refs)
    lane = iota((LANES, LANES), 1)
    part = LANES // RADIX
    order = (iota((LANES, LANES), 0) == RADIX * (lane % part) + lane // part).astype(F32).astype(BF16)
    left, split = jnp.concatenate([spare[0:1] + spare[1:2], spare[2:3] + spare[3:4]], 0), []
    for _ in range(3):
        split.append(left.astype(BF16).astype(F32))
        left = left - split[-1]
    split = jnp.concatenate(split + [jnp.zeros((2, LANES), F32)], 0).astype(BF16)
    columns = lax.dot_general(order, split, (((1,), (1,)), ((), ())), preferred_element_type=F32)
    to_tok = columns[:, 0:1] + columns[:, 2:3] + columns[:, 4:5]
    to_base = columns[:, 1:2] + columns[:, 3:4] + columns[:, 5:6]
    path = lax.axis_index("path")
    copies = []
    for step, ref in enumerate(grad_refs):
        for piece in range(pieces):
            slot = step * pieces + piece
            first = (piece * points + (path ^ step)) * share
            lanes = pl.ds(pl.multiple_of(first, LANES), share)
            tok = own_ref[0, :, lanes].astype(F32)
            base = own_ref[1, :, lanes].astype(F32)
            grad = dot(order, ref[piece * LANES : (piece + 1) * LANES, :])
            grad = (grad - tok * to_tok - base * to_base) / points
            path_ref[slot] = grad
            attr_ref[slot] = (tok - base) * grad
            for kind, (source, target) in enumerate(((path_ref, path_hbm), (attr_ref, attr_hbm))):
                copies.append(
                    pltpu.make_async_copy(source.at[slot], target.at[:, lanes], sems.at[kind, slot])
                )
                copies[-1].start()
    for copy in copies:
        copy.wait()


def any_spec():
    return pl.BlockSpec(memory_space=pl.ANY)


def vmem_spec():
    return pl.BlockSpec(memory_space=pltpu.VMEM)


def hbm_spec():
    return pl.BlockSpec(memory_space=pltpu.HBM)


def call(kernel, ins, outs, scratch, flops, moved, mebibytes):
    return pl.pallas_call(
        kernel,
        in_specs=ins,
        out_specs=[spec for spec, _ in outs],
        out_shape=[shape for _, shape in outs],
        scratch_shapes=scratch,
        compiler_params=pltpu.CompilerParams(vmem_limit_bytes=mebibytes * 2**20),
        cost_estimate=pl.CostEstimate(flops=flops, bytes_accessed=moved, transcendentals=0),
    )


def shape(dims, dtype):
    return jax.ShapeDtypeStruct(dims, dtype)


def kernel_body(tokens, sub_pos, sub_base, embed, norm_gain, fir_taps, long_filter, skip_gain, cotangent):
    n_path, n_ctx = lax.axis_size("path"), lax.axis_size("ctx")
    points = n_path
    tok_rows = tokens.shape[0]
    length = tok_rows * n_ctx
    vocab, width = embed.shape
    share = width // (n_path * n_ctx)
    subs = sub_pos.shape[0] * n_ctx
    own_width = width // n_path
    cols = points * share
    quarter = length // RADIX
    tables = dft_tables(length)
    dma = pltpu.SemaphoreType.DMA
    transform_flops = length * length
    spare = 8

    msg, ids = call(
        pack_kernel,
        [hbm_spec()] * 4,
        [
            (vmem_spec(), shape((n_ctx, tok_rows + spare, share), BF16)),
            (vmem_spec(), shape((spare, LANES), F32)),
        ],
        [
            pltpu.VMEM((1, tok_rows), jnp.int32),
            pltpu.VMEM((1, sub_pos.shape[0]), jnp.int32),
            pltpu.VMEM((1, sub_pos.shape[0]), jnp.int32),
            pltpu.VMEM((tok_rows, n_ctx * share), BF16),
            dma((n_ctx + 3,)),
        ],
        length * share,
        8 * length * share,
        60,
    )(
        tokens.reshape(1, tok_rows),
        sub_pos.reshape(1, -1),
        sub_base.reshape(1, -1),
        cotangent,
    )
    msg = lax.all_to_all(msg, "ctx", 0, 0, tiled=True)

    gain = norm_gain.reshape(1, width)
    skip = skip_gain.reshape(1, n_path * share)
    spec, gram = call(
        prepare_kernel,
        [hbm_spec()] * 4 + [any_spec()],
        [
            (any_spec(), shape((2 * RADIX, quarter, share), F32)),
            (any_spec(), shape((3 * vocab + vocab // 2, vocab), BF16)),
        ],
        [
            pltpu.VMEM((length, share), F32),
            pltpu.VMEM((RADIX, 2 * quarter, quarter), BF16),
            pltpu.VMEM((vocab, width), BF16),
            pltpu.VMEM((1, share), F32),
            pltpu.VMEM((vocab, vocab), F32),
            pltpu.VMEM((2 * RADIX, quarter, share), F32),
            pltpu.VMEM((3 * vocab + vocab // 2, vocab), BF16),
            dma((7,)),
            dma((3 * vocab // LANES + 2,)),
        ],
        2 * vocab * vocab * width,
        2 * vocab * width,
        58,
    )(long_filter, tables[0], embed, skip, ids)

    hots, subs_hots, put_hots = call(
        functools.partial(ids_kernel, vocab),
        [vmem_spec()],
        [
            (vmem_spec(), shape((length, vocab), BF16)),
            (vmem_spec(), shape((2 * subs, vocab), BF16)),
            (vmem_spec(), shape((length, 2 * subs), BF16)),
        ],
        [],
        2 * 10**9,
        4 * 10**6,
        8,
    )(msg)
    wide = 4 * LANES
    signal, k_feat, v_feat, inv, pair = call(
        functools.partial(feature_kernel, points),
        [vmem_spec()] * 7 + [hbm_spec()],
        [(vmem_spec(), shape((length, 2 * cols), BF16))]
        + [(vmem_spec(), shape((length, cols), F32))] * 3
        + [(vmem_spec(), shape((2, length, share), BF16))],
        [
            pltpu.VMEM((vocab, wide), BF16),
            pltpu.VMEM((points, subs, LANES), F32),
            pltpu.VMEM((2 * subs, wide), F32),
            pltpu.VMEM((length, 2 * share), F32),
            pltpu.VMEM((length, (2 + points) * share), F32),
            dma,
        ],
        2 * length * vocab * 3 * share,
        2 * vocab * width + 16 * length * cols,
        39,
    )(msg, hots, subs_hots, put_hots, gram, fir_taps, gain, embed)

    grad = call(
        functools.partial(gradient_kernel, points, width),
        [vmem_spec()] * 11,
        [(vmem_spec(), shape((n_ctx, tok_rows + spare, share), BF16))],
        [
            pltpu.VMEM((RADIX, 2 * quarter, 2 * cols), BF16),
        ],
        4 * transform_flops * cols,
        4 * length * length + 16 * length * cols,
        32,
    )(msg, pair, fir_taps, gain, signal, k_feat, v_feat, inv, *tables, spec)[0]

    own = call(
        own_kernel,
        [vmem_spec(), vmem_spec(), any_spec()],
        [(vmem_spec(), shape((2, tok_rows, own_width), BF16))],
        [],
        4 * tok_rows * vocab * own_width,
        2 * vocab * own_width,
        10,
    )(ids, embed, grad)[0]
    grad = lax.all_to_all(grad, "ctx", 0, 0, tiled=True)
    each = n_ctx // n_path
    parts = call(
        partial_kernel,
        [vmem_spec()],
        [(vmem_spec(), shape((each * tok_rows + spare, share), BF16))] * n_path,
        [],
        spare * LANES * n_ctx,
        4 * length * share,
        4,
    )(grad)
    parts = [
        part if step == 0 else lax.ppermute(part, "path", [(p, p ^ step) for p in range(n_path)])
        for step, part in enumerate(parts)
    ]
    out = shape((tok_rows, own_width), F32)
    return tuple(
        call(
            finish_kernel,
            [vmem_spec()] * (1 + n_path),
            [(any_spec(), out), (any_spec(), out)],
            [pltpu.VMEM((n_path * each, tok_rows, share), F32)] * 2 + [dma((2, n_path * each))],
            8 * tok_rows * own_width,
            14 * tok_rows * own_width,
            8,
        )(own, *parts)
    )


def plain_body(tokens, sub_pos, sub_base, embed, norm_gain, fir_taps, long_filter, skip_gain, cotangent):
    n_path, n_ctx = lax.axis_size("path"), lax.axis_size("ctx")
    path, ctx = lax.axis_index("path"), lax.axis_index("ctx")
    points = n_path
    tok_rows = tokens.shape[0]
    length = tok_rows * n_ctx
    width = embed.shape[1]
    share = width // (n_path * n_ctx)
    own_width = width // n_path
    first = (ctx * n_path + path) * share
    alphas = ((jnp.arange(points, dtype=jnp.int32)).astype(F32) + 0.5) / points
    alphas = alphas[:, None, None]

    local = jnp.arange(tok_rows, dtype=jnp.int32)[:, None] + ctx * tok_rows == sub_pos[None, :]
    put = jnp.sum(jnp.where(local, sub_base[None, :], 0), 1)
    base_ids = jnp.where(jnp.any(local, 1), put, tokens)
    rows_tok = jnp.take(embed, tokens, axis=0).astype(F32)
    rows_base = jnp.take(embed, base_ids, axis=0).astype(F32)
    rows_in = rows_base[None] + alphas * (rows_tok - rows_base)[None]
    inv = lax.rsqrt(jnp.mean(rows_in * rows_in, -1) + EPS)
    inv = lax.all_gather(inv, "ctx", axis=1, tiled=True)[:, :, None]
    all_tok = lax.all_gather(tokens, "ctx", tiled=True)
    all_base = lax.all_gather(base_ids, "ctx", tiled=True)

    cot = cotangent.reshape(tok_rows, n_ctx, n_path, share)
    cot = lax.dynamic_index_in_dim(cot, path, 2, keepdims=False)
    cot = lax.all_to_all(cot.transpose(1, 0, 2), "ctx", 0, 0, tiled=True)
    upstream = cot.reshape(1, length, share).astype(F32)
    mine = lax.dynamic_slice_in_dim(embed, first, share, 1)
    gain = lax.dynamic_slice_in_dim(norm_gain, first, share, 0)
    taps = lax.dynamic_slice_in_dim(fir_taps, first, share, 2).astype(F32)
    filt = lax.dynamic_slice_in_dim(long_filter, path * share, share, 1)
    skip = lax.dynamic_slice_in_dim(skip_gain, path * share, share, 0)

    emb_tok = jnp.take(mine, all_tok, axis=0).astype(F32)
    emb_base = jnp.take(mine, all_base, axis=0).astype(F32)
    inputs = emb_base[None] + alphas * (emb_tok - emb_base)[None]
    normed = rounded(inputs * inv * gain)
    q_feat, k_feat, v_feat = (
        taps[f, 0] * normed + taps[f, 1] * shifted(normed, 1) + taps[f, 2] * shifted(normed, 2)
        for f in range(3)
    )
    filter_spec = spectrum(filt[None])
    conv = rounded(long_conv(rounded(k_feat * v_feat), filter_spec, skip, False))
    grad_z = rounded(long_conv(rounded(upstream * q_feat), filter_spec, skip, True))
    grads = (rounded(upstream * conv), rounded(grad_z * v_feat), rounded(grad_z * k_feat))
    by_tap = [sum(taps[f, tap] * grads[f] for f in range(3)) for tap in range(3)]
    scaled = gain * (by_tap[0] + shifted(by_tap[1], -1) + shifted(by_tap[2], -2))
    grad = jnp.sum(inv * scaled, 0).astype(BF16)
    along = jnp.sum(inputs * scaled, -1, keepdims=True) * inv**3 / width
    part = jnp.stack([jnp.sum(alphas * along, 0)[:, 0], jnp.sum((1.0 - alphas) * along, 0)[:, 0]])
    part = lax.psum(part, ("path", "ctx"))
    part = lax.dynamic_slice_in_dim(part, ctx * tok_rows, tok_rows, 1)

    back = lax.all_to_all(grad.reshape(n_ctx, tok_rows, share), "ctx", 0, 0, tiled=True)
    back = back.reshape(n_path, n_ctx // n_path, tok_rows, share)
    back = lax.all_to_all(back, "path", 0, 0, tiled=True).astype(F32)
    back = back.transpose(2, 1, 0, 3).reshape(tok_rows, own_width)
    own_tok = lax.dynamic_slice_in_dim(rows_tok, path * own_width, own_width, 1)
    own_base = lax.dynamic_slice_in_dim(rows_base, path * own_width, own_width, 1)
    grad = (back - own_tok * part[0][:, None] - own_base * part[1][:, None]) / points
    return (grad, (own_tok - own_base) * grad)


def body(tokens, sub_pos, sub_base, embed, *rest):
    n_path, n_ctx = lax.axis_size("path"), lax.axis_size("ctx")
    tok_rows = tokens.shape[0]
    share = embed.shape[1] // (n_path * n_ctx)
    tables = 2 * (tok_rows * n_ctx) ** 2
    fits = share == LANES and tok_rows == LANES and n_ctx == GROUP and tables <= TABLE_BYTES
    fits = fits and n_ctx % n_path == 0 and n_path & (n_path - 1) == 0
    chosen = kernel_body if fits else plain_body
    return chosen(tokens, sub_pos, sub_base, embed, *rest)


def solution(mesh):
    return jax.shard_map(
        body,
        mesh=mesh,
        in_specs=(
            P("ctx"),
            P("ctx"),
            P("ctx"),
            P(),
            P(),
            P(),
            P(None, "ctx"),
            P("ctx"),
            P("ctx", None),
        ),
        out_specs=(P("ctx", "path"), P("ctx", "path")),
        check_vma=False,
    )
```

```python
import functools

import jax
import jax.numpy as jnp
import ml_dtypes
import numpy as np
from jax import lax
from jax.experimental import pallas as pl
from jax.experimental.pallas import tpu as pltpu
from jax.sharding import PartitionSpec as P

LANES = 128
GROUP = 8
RADIX = 4
LOOK_ROWS = 1024
CHUNK = 16
EPS = 1e-06
CANCEL = 0.004
TABLE_BYTES = 2**21
F32 = jnp.float32
BF16 = jnp.bfloat16
precise = lax.Precision.HIGH


def angle_tables(length):
    outer_size = 64
    inner_size = length // outer_size
    outer_idx = jnp.arange(outer_size, dtype=jnp.int32)
    inner_idx = jnp.arange(inner_size, dtype=jnp.int32)
    outer_angle = (
        2.0 * jnp.pi / outer_size
        * (outer_idx[:, None] * outer_idx[None, :] % outer_size).astype(F32)
    )
    inner_angle = (
        2.0 * jnp.pi / inner_size
        * (inner_idx[:, None] * inner_idx[None, :] % inner_size).astype(F32)
    )
    twist_angle = (
        2.0 * jnp.pi / length
        * (outer_idx[:, None] * inner_idx[None, :] % length).astype(F32)
    )
    return (outer_angle, inner_angle, twist_angle)


def complex_table(angle, sign):
    cosine = jnp.cos(angle)
    sine = sign * jnp.sin(angle)
    return jnp.stack([jnp.stack([cosine, sine]), jnp.stack([-sine, cosine])])


def twisted(values, angle, sign):
    cosine = jnp.cos(angle)[None, :, :, None]
    sine = sign * jnp.sin(angle)[None, :, :, None]
    real_part = values[:, 0]
    imag_part = values[:, 1]
    return jnp.stack(
        [real_part * cosine - imag_part * sine, real_part * sine + imag_part * cosine], 1
    )


def spectrum(signal):
    batch, half, width = signal.shape
    length = 2 * half
    outer_angle, inner_angle, twist_angle = angle_tables(length)
    outer_size = outer_angle.shape[0]
    inner_size = inner_angle.shape[0]
    folded = signal.reshape(batch, outer_size // 2, inner_size, width)
    used = outer_angle[:, : outer_size // 2]
    outer_table = jnp.stack([jnp.cos(used), -jnp.sin(used)])
    first = jnp.einsum("rka,pabc->prkbc", outer_table, folded, precision=precise)
    turned = twisted(first, twist_angle, -1.0)
    return jnp.einsum(
        "prkbc,rsbm->pskmc", turned, complex_table(inner_angle, -1.0), precision=precise
    )


def inverse(spec):
    batch, parts, outer_size, inner_size, width = spec.shape
    length = outer_size * inner_size
    outer_angle, inner_angle, twist_angle = angle_tables(length)
    back = jnp.einsum("pskmc,stmb->ptkbc", spec, complex_table(inner_angle, 1.0), precision=precise)
    turned = twisted(back, twist_angle, 1.0)
    used = outer_angle[: outer_size // 2]
    outer_table = jnp.stack([jnp.cos(used), -jnp.sin(used)])
    result = jnp.einsum("rak,prkbc->pabc", outer_table, turned, precision=precise)
    return (result / length).reshape(batch, length // 2, width)


def long_conv(signal, filter_spec, skip_gain, adjoint):
    spec = spectrum(signal)
    sig_real = spec[:, 0]
    sig_imag = spec[:, 1]
    filt_real = filter_spec[:, 0]
    filt_imag = filter_spec[:, 1]
    if adjoint:
        prod_real = sig_real * filt_real + sig_imag * filt_imag
        prod_imag = sig_imag * filt_real - sig_real * filt_imag
    else:
        prod_real = sig_real * filt_real - sig_imag * filt_imag
        prod_imag = sig_real * filt_imag + sig_imag * filt_real
    return inverse(jnp.stack([prod_real, prod_imag], 1)) + skip_gain * signal


def rounded(value):
    return value.astype(BF16).astype(F32)


def shifted(values, step):
    zeros = jnp.zeros_like(values[:, : abs(step)])
    if step > 0:
        return jnp.concatenate([zeros, values[:, :-step]], 1)
    return jnp.concatenate([values[:, -step:], zeros], 1)


@functools.lru_cache(maxsize=None)
def dft_tables(length):
    quarter = length // RADIX
    freq = 4 * np.arange(quarter, dtype=np.int64) + 1
    place = np.arange(quarter, dtype=np.int64)
    there, back = [], []
    for offset in range(RADIX):
        turns = freq[:, None] * (RADIX * place + offset)[None, :] % (4 * length)
        angle = turns * (2.0 * np.pi / (4 * length))
        cosine = np.cos(angle).astype(ml_dtypes.bfloat16)
        sine = np.sin(angle).astype(ml_dtypes.bfloat16)
        there.append(np.concatenate([cosine, sine], 0))
        back.append(np.concatenate([cosine.T, sine.T], 1))
    return (np.stack(there), np.stack(back))


def butterfly(values, sign):
    (r0, s0), (r1, s1), (r2, s2), (r3, s3) = values
    sum_r, sum_s, diff_r, diff_s = r0 + r2, s0 + s2, r0 - r2, s0 - s2
    odd_r, odd_s, turn_r, turn_s = r1 + r3, s1 + s3, r1 - r3, s1 - s3
    ahead = (diff_r + turn_s, diff_s - turn_r)
    behind = (diff_r - turn_s, diff_s + turn_r)
    if sign < 0:
        ahead, behind = behind, ahead
    return ((sum_r + odd_r, sum_s + odd_s), ahead, (sum_r - odd_r, sum_s - odd_s), behind)


def transposed(rows):
    count = rows.shape[0]
    if count < LANES:
        rows = jnp.concatenate([rows, jnp.zeros((LANES - count, LANES), F32)], 0)
    return rows.T


def dot(left, right):
    return jnp.dot(left, right, preferred_element_type=F32)


def iota(dims, axis):
    return lax.broadcasted_iota(jnp.int32, dims, axis)


def by_residue():
    row = iota((LANES, LANES), 0)
    part = LANES // RADIX
    source = RADIX * (row % part) + row // part
    return (iota((LANES, LANES), 1) == source).astype(F32)


def hot(ids, vocab):
    lane = iota(ids.shape, 1).astype(F32)
    parts = [
        (ids == lane + float(column * LANES)).astype(F32).astype(BF16)
        for column in range(vocab // LANES)
    ]
    return jnp.concatenate(parts, 1)


def joined(block, kind):
    return 256.0 * block[2 * kind : 2 * kind + 1] + block[2 * kind + 1 : 2 * kind + 2]


def pack_kernel(
    tok_hbm, pos_hbm, put_hbm, cot_hbm, msg_ref, ids_ref, tok_ref, pos_ref, put_ref, cot_ref, sems
):
    dests, rows, share = msg_ref.shape
    tok_rows = cot_hbm.shape[0]
    n_path = cot_hbm.shape[1] // (dests * share)
    path = lax.axis_index("path")
    moves = [(tok_hbm, tok_ref), (pos_hbm, pos_ref), (put_hbm, put_ref)]
    for dest in range(dests):
        lanes = pl.ds(pl.multiple_of((dest * n_path + path) * share, LANES), share)
        moves.append((cot_hbm.at[:, lanes], cot_ref.at[:, pl.ds(dest * share, share)]))
    copies = [
        pltpu.make_async_copy(source, target, sems.at[index])
        for index, (source, target) in enumerate(moves)
    ]
    for copy in copies:
        copy.start()
    order = by_residue().astype(BF16)
    for copy in copies[:3]:
        copy.wait()
    lists = []
    for ref in (tok_ref, pos_ref, put_ref):
        value = ref[...].astype(F32)
        if value.shape[1] < LANES:
            value = jnp.concatenate([value, jnp.zeros((1, LANES - value.shape[1]), F32)], 1)
        high = jnp.floor(value * (1.0 / 256.0))
        lists += [high, value - 256.0 * high]
    lists.append(jnp.zeros((rows - tok_rows - len(lists), LANES), F32))
    ids = jnp.concatenate(lists, 0)
    ids_ref[...] = ids
    turned = lax.dot_general(
        ids.astype(BF16), order, (((1,), (1,)), ((), ())), preferred_element_type=F32
    )
    ids = jnp.where(iota(ids.shape, 0) < 2, turned, ids).astype(BF16)
    for dest in range(dests):
        msg_ref[dest, tok_rows:, :] = ids
    for copy in copies[3:]:
        copy.wait()
    turned = dot(order, cot_ref[...]).astype(BF16)
    for dest in range(dests):
        msg_ref[dest, :tok_rows, :] = turned[:, dest * share : (dest + 1) * share]


def prepare_kernel(
    filt_hbm, table_hbm, embed_hbm, skip_hbm, after_ref,
    spec_hbm, gram_hbm,
    filt_ref, table_ref, embed_ref, skip_ref, sum_ref, spec_ref, gram_ref, sems, out_sems,
):
    length, share = filt_ref.shape
    quarter = length // RADIX
    vocab, width = embed_ref.shape
    pieces = sems.shape[0] - 3
    wide = width // pieces
    path = lax.axis_index("path")
    lanes = pl.ds(pl.multiple_of(path * share, LANES), share)
    moves = [
        (filt_hbm.at[:, lanes], filt_ref),
        (skip_hbm.at[:, lanes], skip_ref),
        (table_hbm, table_ref),
    ]
    for index in range(pieces):
        lanes = pl.ds(index * wide, wide)
        moves.append((embed_hbm.at[:, lanes], embed_ref.at[:, lanes]))
    copies = [
        pltpu.make_async_copy(source, target, sems.at[index])
        for index, (source, target) in enumerate(moves)
    ]
    for copy in copies:
        copy.start()

    copies[0].wait()
    copies[1].wait()
    filt_ref[0:1, :] = filt_ref[0:1, :] + skip_ref[...]
    parts = []
    for offset in range(RADIX):
        value = filt_ref[pl.ds(offset, quarter, stride=RADIX), :] * (1.0 / length)
        high = value.astype(BF16)
        parts.append(jnp.concatenate([high, (value - high.astype(F32)).astype(BF16)], 1))
    copies[2].wait()
    found = []
    for offset in range(RADIX):
        both = dot(table_ref[offset], parts[offset])
        both = both[:, :share] + both[:, share:]
        found.append((both[:quarter], both[quarter:]))
    for part, (real, imag) in enumerate(butterfly(found, -1)):
        spec_ref[2 * part] = real
        spec_ref[2 * part + 1] = imag
    outs = [pltpu.make_async_copy(spec_ref, spec_hbm, out_sems.at[0])]
    outs[0].start()

    sum_ref[vocab // 2 :, : vocab // 2] = jnp.zeros((vocab // 2, vocab // 2), F32)
    for index in range(pieces):
        copies[3 + index].wait()
        part = embed_ref[:, index * wide : (index + 1) * wide]
        for rows, lanes in ((slice(0, vocab // 2), slice(0, vocab)), (slice(vocab // 2, vocab),) * 2):
            found = lax.dot_general(
                part[rows], part[lanes], (((1,), (1,)), ((), ())), preferred_element_type=F32
            )
            if index == 0:
                sum_ref[rows, lanes] = found
            else:
                sum_ref[rows, lanes] += found
    first = (lax.axis_index("ctx") * lax.axis_size("path") + path) * share
    mine = embed_ref[:, pl.ds(pl.multiple_of(first, LANES), share)]
    same = iota((LANES, LANES), 0) == iota((LANES, LANES), 1)
    lane = iota((LANES, LANES), 1)
    below = 3 * vocab
    for block in range(vocab // LANES):
        rows = slice(block * LANES, (block + 1) * LANES)
        value = sum_ref[rows, :]
        norm = jnp.sum(jnp.where(same, value[:, rows], 0.0), 1, keepdims=True)
        inv = jnp.broadcast_to(lax.rsqrt(norm / width + EPS), (LANES, LANES))
        high = inv.astype(BF16).astype(F32)
        inv = jnp.where(lane < LANES // 2, high, inv - high).astype(BF16)
        side, start = block * LANES // (vocab // 2), block * LANES % (vocab // 2)
        into = slice(below + start, below + start + LANES)
        left = side * (share + LANES)
        gram_ref[into, left : left + share] = mine[rows]
        gram_ref[into, left + share : left + share + LANES] = inv
        for part in range(3):
            high = value.astype(BF16)
            into = slice(part * vocab + block * LANES, part * vocab + (block + 1) * LANES)
            gram_ref[into, :] = high
            value = value - high.astype(F32)
            into = pl.ds(part * vocab + block * LANES, LANES)
            sem = out_sems.at[1 + block * 3 + part]
            outs.append(pltpu.make_async_copy(gram_ref.at[into], gram_hbm.at[into], sem))
            outs[-1].start()
    into = pl.ds(below, vocab // 2)
    outs.append(pltpu.make_async_copy(gram_ref.at[into], gram_hbm.at[into], out_sems.at[out_sems.shape[0] - 1]))
    outs[-1].start()
    for copy in outs:
        copy.wait()


def own_kernel(ids_ref, embed_ref, grad_ref, own_ref):
    vocab = embed_ref.shape[0]
    own_width = own_ref.shape[2]
    lanes = pl.ds(pl.multiple_of(lax.axis_index("path") * own_width, LANES), own_width)
    ids = ids_ref[...]
    columns = transposed(jnp.concatenate([joined(ids, kind) for kind in range(3)], 0))
    tok = jnp.broadcast_to(columns[:, 0:1], (LANES, LANES))
    place = jnp.broadcast_to(joined(ids, 1), (LANES, LANES))
    put = jnp.broadcast_to(joined(ids, 2), (LANES, LANES))
    first = lax.axis_index("ctx") * LANES
    subs = LANES // GROUP
    here = (place == (iota((LANES, LANES), 0) + first).astype(F32)) & (iota((LANES, LANES), 1) < subs)
    found = jnp.max(jnp.where(here, put, -1.0), 1, keepdims=True)
    base = jnp.where(found >= 0.0, found, tok)
    hots = jnp.concatenate([hot(tok, vocab), hot(base, vocab)], 0)
    both = dot(hots, embed_ref[:, lanes]).astype(BF16)
    own_ref[0] = both[:LANES]
    own_ref[1] = both[LANES:]


def multiply_rows(found, spec_ref, prod_ref, points, kind):
    _, quarter, share = spec_ref.shape
    for start in range(0, quarter, CHUNK):
        here = slice(start, start + CHUNK)
        after = slice(quarter + start, quarter + start + CHUNK)
        filt = [(spec_ref[2 * part, here, :], spec_ref[2 * part + 1, here, :]) for part in range(RADIX)]
        for point in range(points):
            lanes = slice((kind * points + point) * share, (kind * points + point + 1) * share)
            values = butterfly([(value[here, lanes], value[after, lanes]) for value in found], -1)
            prods = []
            for (real, imag), (filt_real, filt_imag) in zip(values, filt):
                if kind == 1:
                    prods.append((real * filt_real + imag * filt_imag, imag * filt_real - real * filt_imag))
                else:
                    prods.append((real * filt_real - imag * filt_imag, imag * filt_real + real * filt_imag))
            for part, (real, imag) in enumerate(butterfly(prods, 1)):
                prod_ref[part, here, lanes] = real.astype(BF16)
                prod_ref[part, after, lanes] = imag.astype(BF16)


def ids_kernel(vocab, msg_ref, hot_ref, subs_ref, put_ref):
    length = hot_ref.shape[0]
    quarter = length // RADIX
    n_ctx = msg_ref.shape[0]
    block_part = LANES // RADIX
    per_block = LANES // GROUP
    subs = n_ctx * per_block
    blocks = [msg_ref[block, LANES:, :].astype(F32) for block in range(n_ctx)]
    toks = transposed(jnp.concatenate([joined(block, 0) for block in blocks], 0))
    spread = sum(
        blocks[block] if block == 0 else pltpu.roll(blocks[block], block * per_block, 1)
        for block in range(n_ctx)
    )
    place = joined(spread, 1)
    put = joined(spread, 2)
    back = jnp.floor(place * (1.0 / RADIX))
    place = back + (place - RADIX * back) * quarter
    columns = transposed(jnp.concatenate([place, put], 0))
    for block in range(n_ctx):
        column = jnp.broadcast_to(toks[:, block : block + 1], (LANES, LANES))
        rows = hot(column, vocab)
        for side in range(RADIX):
            first = side * quarter + block * block_part
            hot_ref[first : first + block_part, :] = rows[side * block_part : (side + 1) * block_part]
    subs_ref[subs:, :] = hot(jnp.broadcast_to(columns[:, 1:2], (subs, LANES)), vocab)
    pick = jnp.concatenate(
        [
            (columns[:, 0:1] == (iota((subs, LANES), 1) + part * LANES).astype(F32)).astype(F32).astype(BF16)
            for part in range(length // LANES)
        ],
        1,
    )
    for index in range(length // LANES):
        row = (iota((LANES, subs), 0) + index * LANES).astype(F32)
        here = (row == place[:, :subs]).astype(F32).astype(BF16)
        put_ref[index * LANES : (index + 1) * LANES, :] = jnp.concatenate([here, here], 1)
    subs_ref[:subs, :] = dot(pick, hot_ref[...]).astype(BF16)


def feature_kernel(
    points, msg_ref, hot_ref, subs_hot_ref, put_ref, gram_ref, taps_ref, gain_ref, embed_hbm,
    signal_ref, k_ref, v_ref, inv_ref, pair_ref,
    embed_ref, sums_ref, found_ref, look_ref, subs_ref, sem,
):
    length = signal_ref.shape[0]
    quarter = length // RADIX
    vocab, width = embed_hbm.shape
    share = pair_ref.shape[2]
    subs = subs_hot_ref.shape[0] // 2
    first = (lax.axis_index("ctx") * points + lax.axis_index("path")) * share
    first = pl.multiple_of(first, LANES)
    below = 3 * vocab
    table = jnp.concatenate(
        [gram_ref[below:, : share + LANES], gram_ref[below:, share + LANES :]], 0
    )

    for index in range(length // LOOK_ROWS):
        rows = pl.ds(index * LOOK_ROWS, LOOK_ROWS)
        look_ref[rows, :] = dot(hot_ref[rows, :], table)

    alphas = [(point + 0.5) / points for point in range(points)]
    hots = subs_hot_ref[...]
    found = dot(jnp.concatenate([hots] * 3, 1), gram_ref[:below, :])
    hot_tok32, hot_base32 = hots[:subs].astype(F32), hots[subs:].astype(F32)
    tok_tok = jnp.sum(found[:subs] * hot_tok32, 1, keepdims=True)
    tok_base = jnp.sum(found[:subs] * hot_base32, 1, keepdims=True)
    base_tok = jnp.sum(found[subs:] * hot_tok32, 1, keepdims=True)
    tok_base = jnp.where(tok_base == 0.0, base_tok, tok_base)
    base_base = jnp.sum(found[subs:] * hot_base32, 1, keepdims=True)
    cancels = jnp.zeros((subs, 1), F32)
    for point in range(points):
        alpha = alphas[point]
        terms = (1.0 - alpha) ** 2 * base_base + alpha**2 * tok_tok
        total = terms + 2.0 * alpha * (1.0 - alpha) * tok_base
        cancels = jnp.maximum(cancels, (total < CANCEL * terms).astype(F32))
        inv = lax.rsqrt(jnp.maximum(total, 0.0) / width + EPS)
        sums_ref[point] = jnp.broadcast_to(inv, (subs, LANES))

    @pl.when(jnp.max(cancels) > 0.5)
    def _():
        sums_ref[...] = jnp.zeros_like(sums_ref)
        wide = found_ref.shape[1]

        @pl.loop(0, width // wide)
        def _(step):
            lanes = pl.ds(pl.multiple_of(step * wide, wide), wide)
            copy = pltpu.make_async_copy(embed_hbm.at[:, lanes], embed_ref, sem)
            copy.start()
            copy.wait()
            found_ref[...] = dot(hots, embed_ref[...])
            for block in range(subs // GROUP):
                rows = slice(block * GROUP, (block + 1) * GROUP)
                sums = [sums_ref[point, rows, :] for point in range(points)]
                for column in range(wide // LANES):
                    cut = slice(column * LANES, (column + 1) * LANES)
                    base = found_ref[subs + block * GROUP : subs + (block + 1) * GROUP, cut]
                    diff = found_ref[rows, cut] - base
                    for point in range(points):
                        value = base + alphas[point] * diff
                        sums[point] = sums[point] + value * value
                for point in range(points):
                    sums_ref[point, rows, :] = sums[point]

        for point in range(points):
            mean = jnp.sum(sums_ref[point], 1, keepdims=True) / width
            sums_ref[point] = jnp.broadcast_to(lax.rsqrt(mean + EPS), (subs, LANES))

    high = [dot(hots[subs:], table[:, :share]), jnp.ones((subs, LANES), F32)]
    low = [jnp.zeros((subs, LANES), F32)] * 2
    for point in range(points):
        inv = sums_ref[point]
        high.append(inv.astype(BF16).astype(F32))
        low.append(inv - high[-1])
    held = jnp.concatenate([jnp.concatenate(high, 1), jnp.concatenate(low, 1)], 0).astype(BF16)
    for index in range(length // LOOK_ROWS):
        rows = pl.ds(index * LOOK_ROWS, LOOK_ROWS)
        subs_ref[rows, :] = dot(put_ref[rows, :], held)

    cols = points * share
    block_part = LANES // RADIX
    last = {side: [jnp.zeros((GROUP, share), F32)] * points for side in (RADIX - 2, RADIX - 1)}
    gain = gain_ref[:, pl.ds(first, share)]
    taps = [taps_ref[f, :, pl.ds(first, share)].astype(F32) for f in range(3)]
    taps = [[taps[f][tap : tap + 1] for tap in range(3)] for f in range(3)]

    for start in range(0, quarter, CHUNK):
        block, inside = start // block_part, start % block_part
        sides = []
        for side in range(RADIX):
            rows = pl.ds(side * quarter + start, CHUNK)
            tok = look_ref[rows, :share]
            inv = look_ref[rows, share:]
            inv = inv + pltpu.roll(inv, LANES // 2, 1)
            chosen = subs_ref[rows, share : 2 * share] > 0.5
            base = jnp.where(chosen, subs_ref[rows, :share], tok)
            pair_ref[0, rows, :] = tok.astype(BF16)
            pair_ref[1, rows, :] = base.astype(BF16)
            sent = pl.ds(side * block_part + inside, CHUNK)
            upstream = msg_ref[block, sent, :].astype(F32)
            sides.append((rows, gain * base, gain * (tok - base), inv, chosen, upstream))
        for point in range(points):
            lanes = slice(point * share, (point + 1) * share)
            recent = []
            for rows, base, diff, inv_tok, chosen, _ in sides:
                inv = jnp.where(
                    chosen, subs_ref[rows, (2 + point) * share : (3 + point) * share], inv_tok
                )
                inv_ref[rows, lanes] = inv
                recent.append(rounded((base + alphas[point] * diff) * inv))
            backs = []
            for side in (RADIX - 2, RADIX - 1):
                window = jnp.concatenate([last[side][point], recent[side]], 0)
                last[side][point] = recent[side][CHUNK - GROUP :]
                backs.append(window[GROUP - 1 : GROUP - 1 + CHUNK])
            recent = backs + recent
            for side in range(RADIX):
                rows, upstream = sides[side][0], sides[side][5]
                feats = [sum(taps[f][tap] * recent[side + 2 - tap] for tap in range(3)) for f in range(3)]
                k_ref[rows, lanes] = feats[1]
                v_ref[rows, lanes] = feats[2]
                signal_ref[rows, lanes] = (feats[1] * feats[2]).astype(BF16)
                after = slice(cols + point * share, cols + (point + 1) * share)
                signal_ref[rows, after] = (upstream * feats[0]).astype(BF16)


def gradient_kernel(
    points, width, msg_ref, pair_ref, taps_ref, gain_ref,
    signal_ref, k_ref, v_ref, inv_ref, table_ref, back_ref, spec_ref,
    grad_ref,
    prod_ref,
):
    _, quarter, share = spec_ref.shape
    cols = points * share
    n_ctx = msg_ref.shape[0]
    block_part = LANES // RADIX
    first = (lax.axis_index("ctx") * points + lax.axis_index("path")) * share
    first = pl.multiple_of(first, LANES)
    gain = gain_ref[:, pl.ds(first, share)]
    taps = [taps_ref[f, :, pl.ds(first, share)].astype(F32) for f in range(3)]
    taps = [[taps[f][tap : tap + 1] for tap in range(3)] for f in range(3)]

    spectra = [
        dot(table_ref[side], signal_ref[side * quarter : (side + 1) * quarter, :]) for side in range(RADIX)
    ]
    for kind in range(2):
        multiply_rows(spectra, spec_ref, prod_ref, points, kind)
    found = [dot(back_ref[side], prod_ref[side]) for side in range(RADIX)]

    alphas = [(point + 0.5) / points for point in range(points)]
    carried = [[jnp.zeros((GROUP, share), F32)] * points for _ in range(3)]
    lane, row = iota((GROUP, LANES), 1), iota((GROUP, LANES), 0)
    for start in reversed(range(0, quarter, CHUNK)):
        block, inside = start // block_part, start % block_part
        if inside + CHUNK == block_part:
            means = [jnp.zeros((GROUP, LANES), F32)] * 2
        kept = [{} for _ in range(RADIX)]
        for offset in reversed(range(0, CHUNK, GROUP)):
            here = slice(start + offset, start + offset + GROUP)
            sides = []
            for side in range(RADIX):
                rows = slice(side * quarter + start + offset, side * quarter + start + offset + GROUP)
                sent = pl.ds(side * block_part + inside, CHUNK)
                upstream = msg_ref[block, sent, :].astype(F32)[offset : offset + GROUP]
                both = pl.ds(side * quarter + start, CHUNK)
                base = pair_ref[1, both, :].astype(F32)[offset : offset + GROUP]
                diff = pair_ref[0, both, :].astype(F32)[offset : offset + GROUP] - base
                sides.append([rows, upstream, base, diff] + [jnp.zeros((GROUP, share), F32)] * 3)
            for point in reversed(range(points)):
                lanes = slice(point * share, (point + 1) * share)
                by_tap = []
                for side in range(RADIX):
                    rows, upstream = sides[side][:2]
                    grad_z = found[side][here, cols + point * share : cols + (point + 1) * share]
                    grads = (
                        upstream * found[side][here, lanes],
                        grad_z * v_ref[rows, lanes],
                        grad_z * k_ref[rows, lanes],
                    )
                    by_tap.append([sum(taps[f][tap] * grads[f] for f in range(3)) for tap in range(3)])
                ahead = []
                for slot, value in enumerate((by_tap[0][1], by_tap[0][2], by_tap[1][2])):
                    window = jnp.concatenate([value, carried[slot][point]], 0)
                    carried[slot][point] = value
                    ahead.append(window[1 : 1 + GROUP])
                by_tap += [[None, ahead[0], ahead[1]], [None, None, ahead[2]]]
                for side in range(RADIX):
                    rows, _, base, diff, total, sum_tok, sum_both = sides[side]
                    inv = inv_ref[rows, lanes]
                    along = inv * (by_tap[side][0] + by_tap[side + 1][1] + by_tap[side + 2][2])
                    total = total + along
                    along = along * (base + alphas[point] * diff) * (inv * inv)
                    sides[side][4:] = [total, sum_tok + alphas[point] * along, sum_both + along]
            for side in range(RADIX):
                _, _, _, _, total, sum_tok, sum_both = sides[side]
                kept[side][offset] = gain * total
                for kind, value in enumerate((gain * sum_tok, gain * (sum_both - sum_tok))):
                    value = jnp.sum(value, 1, keepdims=True)
                    at = lane == row + (side * block_part + inside + offset)
                    means[kind] = means[kind] + jnp.where(at, value, 0.0)
        for side in range(RADIX):
            total = jnp.concatenate([kept[side][offset] for offset in range(0, CHUNK, GROUP)], 0)
            grad_ref[block, pl.ds(side * block_part + inside, CHUNK), :] = total.astype(BF16)
        if inside == 0:
            sent = []
            for value in means:
                value = jnp.sum(value, 0, keepdims=True) / width
                high = value.astype(BF16).astype(F32)
                sent += [high, value - high]
            sent.append(jnp.zeros((grad_ref.shape[1] - LANES - len(sent), LANES), F32))
            grad_ref[block, LANES:, :] = jnp.concatenate(sent, 0).astype(BF16)


def partial_kernel(grad_ref, *out_refs):
    rows, _ = out_refs[0].shape
    n_ctx = grad_ref.shape[0]
    each = n_ctx // len(out_refs)
    spare = sum(grad_ref[block, LANES:, :].astype(F32) for block in range(n_ctx))
    sums = [spare[0:1] + spare[1:2], spare[2:3] + spare[3:4]]
    sent = []
    for value in sums:
        high = value.astype(BF16).astype(F32)
        sent += [high, value - high]
    sent.append(jnp.zeros((rows - each * LANES - len(sent), LANES), F32))
    sent = jnp.concatenate(sent, 0).astype(BF16)
    path = lax.axis_index("path")
    for step, ref in enumerate(out_refs):
        dest = path ^ step
        for piece in range(each):
            ref[piece * LANES : (piece + 1) * LANES, :] = grad_ref[dest * each + piece, :LANES, :]
        ref[each * LANES :, :] = sent


def finish_kernel(own_ref, *refs):
    grad_refs, (path_hbm, attr_hbm, path_ref, attr_ref, sems) = refs[:-5], refs[-5:]
    points = len(grad_refs)
    rows, share = grad_refs[0].shape
    pieces = rows // LANES
    spare = sum(ref[pieces * LANES :, :].astype(F32) for ref in grad_refs)
    lane = iota((LANES, LANES), 1)
    part = LANES // RADIX
    order = (iota((LANES, LANES), 0) == RADIX * (lane % part) + lane // part).astype(F32).astype(BF16)
    left, split = jnp.concatenate([spare[0:1] + spare[1:2], spare[2:3] + spare[3:4]], 0), []
    for _ in range(3):
        split.append(left.astype(BF16).astype(F32))
        left = left - split[-1]
    split = jnp.concatenate(split + [jnp.zeros((2, LANES), F32)], 0).astype(BF16)
    columns = lax.dot_general(order, split, (((1,), (1,)), ((), ())), preferred_element_type=F32)
    to_tok = columns[:, 0:1] + columns[:, 2:3] + columns[:, 4:5]
    to_base = columns[:, 1:2] + columns[:, 3:4] + columns[:, 5:6]
    path = lax.axis_index("path")
    copies = []
    for step, ref in enumerate(grad_refs):
        for piece in range(pieces):
            slot = step * pieces + piece
            first = (piece * points + (path ^ step)) * share
            lanes = pl.ds(pl.multiple_of(first, LANES), share)
            tok = own_ref[0, :, lanes].astype(F32)
            base = own_ref[1, :, lanes].astype(F32)
            grad = dot(order, ref[piece * LANES : (piece + 1) * LANES, :])
            grad = (grad - tok * to_tok - base * to_base) / points
            path_ref[slot] = grad
            attr_ref[slot] = (tok - base) * grad
            for kind, (source, target) in enumerate(((path_ref, path_hbm), (attr_ref, attr_hbm))):
                copies.append(
                    pltpu.make_async_copy(source.at[slot], target.at[:, lanes], sems.at[kind, slot])
                )
                copies[-1].start()
    for copy in copies:
        copy.wait()


def any_spec():
    return pl.BlockSpec(memory_space=pl.ANY)


def vmem_spec():
    return pl.BlockSpec(memory_space=pltpu.VMEM)


def hbm_spec():
    return pl.BlockSpec(memory_space=pltpu.HBM)


def call(kernel, ins, outs, scratch, flops, moved, mebibytes):
    return pl.pallas_call(
        kernel,
        in_specs=ins,
        out_specs=[spec for spec, _ in outs],
        out_shape=[shape for _, shape in outs],
        scratch_shapes=scratch,
        compiler_params=pltpu.CompilerParams(vmem_limit_bytes=mebibytes * 2**20),
        cost_estimate=pl.CostEstimate(flops=flops, bytes_accessed=moved, transcendentals=0),
    )


def shape(dims, dtype):
    return jax.ShapeDtypeStruct(dims, dtype)


def kernel_body(tokens, sub_pos, sub_base, embed, norm_gain, fir_taps, long_filter, skip_gain, cotangent):
    n_path, n_ctx = lax.axis_size("path"), lax.axis_size("ctx")
    points = n_path
    tok_rows = tokens.shape[0]
    length = tok_rows * n_ctx
    vocab, width = embed.shape
    share = width // (n_path * n_ctx)
    subs = sub_pos.shape[0] * n_ctx
    own_width = width // n_path
    cols = points * share
    quarter = length // RADIX
    tables = dft_tables(length)
    dma = pltpu.SemaphoreType.DMA
    transform_flops = length * length
    spare = 8

    msg, ids = call(
        pack_kernel,
        [hbm_spec()] * 4,
        [
            (vmem_spec(), shape((n_ctx, tok_rows + spare, share), BF16)),
            (vmem_spec(), shape((spare, LANES), F32)),
        ],
        [
            pltpu.VMEM((1, tok_rows), jnp.int32),
            pltpu.VMEM((1, sub_pos.shape[0]), jnp.int32),
            pltpu.VMEM((1, sub_pos.shape[0]), jnp.int32),
            pltpu.VMEM((tok_rows, n_ctx * share), BF16),
            dma((n_ctx + 3,)),
        ],
        length * share,
        8 * length * share,
        60,
    )(
        tokens.reshape(1, tok_rows),
        sub_pos.reshape(1, -1),
        sub_base.reshape(1, -1),
        cotangent,
    )
    msg = lax.all_to_all(msg, "ctx", 0, 0, tiled=True)

    gain = norm_gain.reshape(1, width)
    skip = skip_gain.reshape(1, n_path * share)
    spec, gram = call(
        prepare_kernel,
        [hbm_spec()] * 4 + [any_spec()],
        [
            (any_spec(), shape((2 * RADIX, quarter, share), F32)),
            (any_spec(), shape((3 * vocab + vocab // 2, vocab), BF16)),
        ],
        [
            pltpu.VMEM((length, share), F32),
            pltpu.VMEM((RADIX, 2 * quarter, quarter), BF16),
            pltpu.VMEM((vocab, width), BF16),
            pltpu.VMEM((1, share), F32),
            pltpu.VMEM((vocab, vocab), F32),
            pltpu.VMEM((2 * RADIX, quarter, share), F32),
            pltpu.VMEM((3 * vocab + vocab // 2, vocab), BF16),
            dma((7,)),
            dma((3 * vocab // LANES + 2,)),
        ],
        2 * vocab * vocab * width,
        2 * vocab * width,
        58,
    )(long_filter, tables[0], embed, skip, ids)

    hots, subs_hots, put_hots = call(
        functools.partial(ids_kernel, vocab),
        [vmem_spec()],
        [
            (vmem_spec(), shape((length, vocab), BF16)),
            (vmem_spec(), shape((2 * subs, vocab), BF16)),
            (vmem_spec(), shape((length, 2 * subs), BF16)),
        ],
        [],
        2 * 10**9,
        4 * 10**6,
        8,
    )(msg)
    wide = 4 * LANES
    signal, k_feat, v_feat, inv, pair = call(
        functools.partial(feature_kernel, points),
        [vmem_spec()] * 7 + [hbm_spec()],
        [(vmem_spec(), shape((length, 2 * cols), BF16))]
        + [(vmem_spec(), shape((length, cols), F32))] * 3
        + [(vmem_spec(), shape((2, length, share), BF16))],
        [
            pltpu.VMEM((vocab, wide), BF16),
            pltpu.VMEM((points, subs, LANES), F32),
            pltpu.VMEM((2 * subs, wide), F32),
            pltpu.VMEM((length, 2 * share), F32),
            pltpu.VMEM((length, (2 + points) * share), F32),
            dma,
        ],
        2 * length * vocab * 3 * share,
        2 * vocab * width + 16 * length * cols,
        39,
    )(msg, hots, subs_hots, put_hots, gram, fir_taps, gain, embed)

    grad = call(
        functools.partial(gradient_kernel, points, width),
        [vmem_spec()] * 11,
        [(vmem_spec(), shape((n_ctx, tok_rows + spare, share), BF16))],
        [
            pltpu.VMEM((RADIX, 2 * quarter, 2 * cols), BF16),
        ],
        4 * transform_flops * cols,
        4 * length * length + 16 * length * cols,
        32,
    )(msg, pair, fir_taps, gain, signal, k_feat, v_feat, inv, *tables, spec)[0]

    own = call(
        own_kernel,
        [vmem_spec(), vmem_spec(), any_spec()],
        [(vmem_spec(), shape((2, tok_rows, own_width), BF16))],
        [],
        4 * tok_rows * vocab * own_width,
        2 * vocab * own_width,
        10,
    )(ids, embed, grad)[0]
    grad = lax.all_to_all(grad, "ctx", 0, 0, tiled=True)
    each = n_ctx // n_path
    parts = call(
        partial_kernel,
        [vmem_spec()],
        [(vmem_spec(), shape((each * tok_rows + spare, share), BF16))] * n_path,
        [],
        spare * LANES * n_ctx,
        4 * length * share,
        4,
    )(grad)
    parts = [
        part if step == 0 else lax.ppermute(part, "path", [(p, p ^ step) for p in range(n_path)])
        for step, part in enumerate(parts)
    ]
    out = shape((tok_rows, own_width), F32)
    return tuple(
        call(
            finish_kernel,
            [vmem_spec()] * (1 + n_path),
            [(any_spec(), out), (any_spec(), out)],
            [pltpu.VMEM((n_path * each, tok_rows, share), F32)] * 2 + [dma((2, n_path * each))],
            8 * tok_rows * own_width,
            14 * tok_rows * own_width,
            8,
        )(own, *parts)
    )


def plain_body(tokens, sub_pos, sub_base, embed, norm_gain, fir_taps, long_filter, skip_gain, cotangent):
    n_path, n_ctx = lax.axis_size("path"), lax.axis_size("ctx")
    path, ctx = lax.axis_index("path"), lax.axis_index("ctx")
    points = n_path
    tok_rows = tokens.shape[0]
    length = tok_rows * n_ctx
    width = embed.shape[1]
    share = width // (n_path * n_ctx)
    own_width = width // n_path
    first = (ctx * n_path + path) * share
    alphas = ((jnp.arange(points, dtype=jnp.int32)).astype(F32) + 0.5) / points
    alphas = alphas[:, None, None]

    local = jnp.arange(tok_rows, dtype=jnp.int32)[:, None] + ctx * tok_rows == sub_pos[None, :]
    put = jnp.sum(jnp.where(local, sub_base[None, :], 0), 1)
    base_ids = jnp.where(jnp.any(local, 1), put, tokens)
    rows_tok = jnp.take(embed, tokens, axis=0).astype(F32)
    rows_base = jnp.take(embed, base_ids, axis=0).astype(F32)
    rows_in = rows_base[None] + alphas * (rows_tok - rows_base)[None]
    inv = lax.rsqrt(jnp.mean(rows_in * rows_in, -1) + EPS)
    inv = lax.all_gather(inv, "ctx", axis=1, tiled=True)[:, :, None]
    all_tok = lax.all_gather(tokens, "ctx", tiled=True)
    all_base = lax.all_gather(base_ids, "ctx", tiled=True)

    cot = cotangent.reshape(tok_rows, n_ctx, n_path, share)
    cot = lax.dynamic_index_in_dim(cot, path, 2, keepdims=False)
    cot = lax.all_to_all(cot.transpose(1, 0, 2), "ctx", 0, 0, tiled=True)
    upstream = cot.reshape(1, length, share).astype(F32)
    mine = lax.dynamic_slice_in_dim(embed, first, share, 1)
    gain = lax.dynamic_slice_in_dim(norm_gain, first, share, 0)
    taps = lax.dynamic_slice_in_dim(fir_taps, first, share, 2).astype(F32)
    filt = lax.dynamic_slice_in_dim(long_filter, path * share, share, 1)
    skip = lax.dynamic_slice_in_dim(skip_gain, path * share, share, 0)

    emb_tok = jnp.take(mine, all_tok, axis=0).astype(F32)
    emb_base = jnp.take(mine, all_base, axis=0).astype(F32)
    inputs = emb_base[None] + alphas * (emb_tok - emb_base)[None]
    normed = rounded(inputs * inv * gain)
    q_feat, k_feat, v_feat = (
        taps[f, 0] * normed + taps[f, 1] * shifted(normed, 1) + taps[f, 2] * shifted(normed, 2)
        for f in range(3)
    )
    filter_spec = spectrum(filt[None])
    conv = rounded(long_conv(rounded(k_feat * v_feat), filter_spec, skip, False))
    grad_z = rounded(long_conv(rounded(upstream * q_feat), filter_spec, skip, True))
    grads = (rounded(upstream * conv), rounded(grad_z * v_feat), rounded(grad_z * k_feat))
    by_tap = [sum(taps[f, tap] * grads[f] for f in range(3)) for tap in range(3)]
    scaled = gain * (by_tap[0] + shifted(by_tap[1], -1) + shifted(by_tap[2], -2))
    grad = jnp.sum(inv * scaled, 0).astype(BF16)
    along = jnp.sum(inputs * scaled, -1, keepdims=True) * inv**3 / width
    part = jnp.stack([jnp.sum(alphas * along, 0)[:, 0], jnp.sum((1.0 - alphas) * along, 0)[:, 0]])
    part = lax.psum(part, ("path", "ctx"))
    part = lax.dynamic_slice_in_dim(part, ctx * tok_rows, tok_rows, 1)

    back = lax.all_to_all(grad.reshape(n_ctx, tok_rows, share), "ctx", 0, 0, tiled=True)
    back = back.reshape(n_path, n_ctx // n_path, tok_rows, share)
    back = lax.all_to_all(back, "path", 0, 0, tiled=True).astype(F32)
    back = back.transpose(2, 1, 0, 3).reshape(tok_rows, own_width)
    own_tok = lax.dynamic_slice_in_dim(rows_tok, path * own_width, own_width, 1)
    own_base = lax.dynamic_slice_in_dim(rows_base, path * own_width, own_width, 1)
    grad = (back - own_tok * part[0][:, None] - own_base * part[1][:, None]) / points
    return (grad, (own_tok - own_base) * grad)


def body(tokens, sub_pos, sub_base, embed, *rest):
    n_path, n_ctx = lax.axis_size("path"), lax.axis_size("ctx")
    tok_rows = tokens.shape[0]
    share = embed.shape[1] // (n_path * n_ctx)
    tables = 2 * (tok_rows * n_ctx) ** 2
    fits = share == LANES and tok_rows == LANES and n_ctx == GROUP and tables <= TABLE_BYTES
    fits = fits and n_ctx % n_path == 0 and n_path & (n_path - 1) == 0
    chosen = kernel_body if fits else plain_body
    return chosen(tokens, sub_pos, sub_base, embed, *rest)


def solution(mesh):
    return jax.shard_map(
        body,
        mesh=mesh,
        in_specs=(
            P("ctx"),
            P("ctx"),
            P("ctx"),
            P(),
            P(),
            P(),
            P(None, "ctx"),
            P("ctx"),
            P("ctx", None),
        ),
        out_specs=(P("ctx", "path"), P("ctx", "path")),
        check_vma=False,
    )
```
